128 devices in a mesh: fsdp: 4 (over x), context: 16 (over y, z), tensor: 2 (over core).
Axes of the slice: x: 4, y: 4, z: 4, core: 2. Of those that a mesh axis runs over, the one named last changes fastest.
Arguments:
- tokens: bfloat16 [8192, 2560], P(('fsdp', 'context')), may hold values from -6 to 6
- cotangent: bfloat16 [8192, 2560], P(('fsdp', 'context')), may hold values from -6 to 6
- seq_lengths: int32 [4, 3], P('fsdp'), may hold values from 1 to 2048, as said below
- norm_gains: float32 [2, 2560], replicated, may hold values from 0.5 to 1.5
- gains_moment: float32 [2, 2560], replicated, may hold values from -64 to 64
- gains_square: float32 [2, 2560], replicated, may hold values from 491.52 to 1720.32
- recur_params: float32 [8, 2560], P(None, 'tensor'), may hold values from -2 to 9, as said below
- recur_moment: float32 [8, 2560], P(None, 'tensor'), may hold values from -64 to 64
- recur_square: float32 [8, 2560], P(None, 'tensor'), may hold values from 491.52 to 1720.32
- input_proj: float32 [2, 2560, 2560], P(None, ('fsdp', 'context'), 'tensor'), may hold values from -0.125 to 0.125
- input_moment: float32 [2, 2560, 2560], P(None, ('fsdp', 'context'), 'tensor'), may hold values from -64 to 64
- input_square: float32 [2, 2560, 2560], P(None, ('fsdp', 'context'), 'tensor'), may hold values from 491.52 to 1720.32
- gate_blocks: float32 [2, 10, 256, 256], P(None, 'tensor', ('fsdp', 'context')), may hold values from -0.375 to 0.375
- blocks_moment: float32 [2, 10, 256, 256], P(None, 'tensor', ('fsdp', 'context')), may hold values from -4 to 4
- blocks_square: float32 [2, 10, 256, 256], P(None, 'tensor', ('fsdp', 'context')), may hold values from 4.9152 to 17.2032
- output_proj: float32 [2560, 2560], P('tensor', ('fsdp', 'context')), may hold values from -0.3125 to 0.3125
- output_moment: float32 [2560, 2560], P('tensor', ('fsdp', 'context')), may hold values from -64 to 64
- output_square: float32 [2560, 2560], P('tensor', ('fsdp', 'context')), may hold values from 491.52 to 1720.32
- inner_proj: float32 [2, 2560, 7680], P(None, ('fsdp', 'context'), 'tensor'), may hold values from -0.125 to 0.125
- inner_moment: float32 [2, 2560, 7680], P(None, ('fsdp', 'context'), 'tensor'), may hold values from -64 to 64
- inner_square: float32 [2, 2560, 7680], P(None, ('fsdp', 'context'), 'tensor'), may hold values from 491.52 to 1720.32
- down_proj: float32 [7680, 2560], P('tensor', ('fsdp', 'context')), may hold values from -0.0625 to 0.0625
- down_moment: float32 [7680, 2560], P('tensor', ('fsdp', 'context')), may hold values from -64 to 64
- down_square: float32 [7680, 2560], P('tensor', ('fsdp', 'context')), may hold values from 491.52 to 1720.32
Outputs:
- mixed: bfloat16 [8192, 2560], P(('fsdp', 'context'))
- tokens_grad: float32 [8192, 2560], P(('fsdp', 'context'))
- gains_updated: float32 [2, 2560], replicated
- moment_gains: float32 [2, 2560], replicated
- square_gains: float32 [2, 2560], replicated
- recur_updated: float32 [8, 2560], P(None, 'tensor')
- moment_recur: float32 [8, 2560], P(None, 'tensor')
- square_recur: float32 [8, 2560], P(None, 'tensor')
- input_updated: float32 [2, 2560, 2560], P(None, ('fsdp', 'context'), 'tensor')
- moment_input: float32 [2, 2560, 2560], P(None, ('fsdp', 'context'), 'tensor')
- square_input: float32 [2, 2560, 2560], P(None, ('fsdp', 'context'), 'tensor')
- blocks_updated: float32 [2, 10, 256, 256], P(None, 'tensor', ('fsdp', 'context'))
- moment_blocks: float32 [2, 10, 256, 256], P(None, 'tensor', ('fsdp', 'context'))
- square_blocks: float32 [2, 10, 256, 256], P(None, 'tensor', ('fsdp', 'context'))
- output_updated: float32 [2560, 2560], P('tensor', ('fsdp', 'context'))
- moment_output: float32 [2560, 2560], P('tensor', ('fsdp', 'context'))
- square_output: float32 [2560, 2560], P('tensor', ('fsdp', 'context'))
- inner_updated: float32 [2, 2560, 7680], P(None, ('fsdp', 'context'), 'tensor')
- moment_inner: float32 [2, 2560, 7680], P(None, ('fsdp', 'context'), 'tensor')
- square_inner: float32 [2, 2560, 7680], P(None, ('fsdp', 'context'), 'tensor')
- down_updated: float32 [7680, 2560], P('tensor', ('fsdp', 'context'))
- moment_down: float32 [7680, 2560], P('tensor', ('fsdp', 'context'))
- square_down: float32 [7680, 2560], P('tensor', ('fsdp', 'context'))
The draws below stay inside these ranges and needn't reach their ends.
Inputs may be any that keep to these rules, and one draw needn't show every extreme that they name: `seq_lengths`: A group's sequences lie back to back from its first token and their lengths add up to at most 2048; the rest of the group is padding. In every group one sequence has tokens among the first 128 and among the last 128 places. `recur_params`: rows 0 to 6 lie within -2 and 2; row 7 (Lambda) lies within 4 and 9.
All inputs are finite; a program needn't handle non-finite values.
Results may differ from the reference program's by a relative error of at most 0.012.
Values may be sent and summed in bfloat16 or wider, within the bound.
A program may use at most 512 MiB of HBM per device.

```python
import jax
import jax.numpy as jnp
from jax import lax

D = 2560
LRU = 2560
HEADS = 10
FF = 7680
CONV = 4
SEQS = 3
STEP = 10
BLOCK = 256
GROUP = 2048
ROWS = 128
TOKENS = 8192
N_FSDP = 4


def draw_seq_lengths(key, part):
    key = jax.random.fold_in(key, 11)
    keys = jax.random.split(key, 3)
    shorts = jax.random.randint(keys[0], (N_FSDP, SEQS - 1), 1, ROWS // 3 + 1)
    spare = jax.random.randint(keys[1], (N_FSDP, 1), 0, ROWS // 4 + 1)
    longest = GROUP - spare - jnp.sum(shorts, axis=1, keepdims=True)
    chosen = jax.random.randint(keys[2], (N_FSDP, 1), 0, SEQS)
    slots = jnp.arange(SEQS, dtype=jnp.int32)[None, :]
    source = jnp.clip(slots - (slots > chosen).astype(jnp.int32), 0, SEQS - 2)
    picked = jnp.take_along_axis(shorts, source, axis=1)
    return jnp.where(slots == chosen, longest, picked).astype(jnp.int32)


def draw_recur_params(key, part):
    key = jax.random.fold_in(key, 7)
    keys = jax.random.split(key, 2)
    leading = jnp.clip(jax.random.normal(keys[0], (CONV + 3, LRU), jnp.float32) * 0.5, -2.0, 2.0)
    lambdas = jax.random.uniform(keys[1], (1, LRU), jnp.float32, 4.0, 9.0)
    return jnp.concatenate([leading, lambdas], axis=0)


def block_levels(own_key, extent, pieces, smallest, high):
    def one(dim, shards_of):
        draws = jax.random.uniform(jax.random.fold_in(jax.random.fold_in(own_key, 6), dim), (shards_of,), jnp.float32, smallest / len(pieces), high / len(pieces))
        return jnp.repeat(jnp.exp(draws), extent[dim] // shards_of).reshape((-1,) + (1,) * (len(extent) - dim - 1))

    gain = one(*pieces[0])
    for cut in pieces[1:]:
        gain = gain * one(*cut)
    return gain


def scatter_about(stream_key, extent, scale, reach, pieces=(), held_as=jnp.bfloat16):
    drawn = jax.random.normal(stream_key, extent, jnp.float32) * scale
    if len(pieces) > 0:
        drawn = block_levels(stream_key, extent, pieces, -0.22, 0.18) * drawn
    return jnp.clip(drawn, min=-reach, max=reach).astype(held_as)


def setup_inputs(seed: int = 0) -> dict:
    arg_keys = jax.random.split(jax.random.key(seed), 25)
    tokens = scatter_about(arg_keys[0], (TOKENS, D), 1.0, 6.0, ((0, 64),))
    cotangent = scatter_about(arg_keys[1], (TOKENS, D), 1.0, 6.0, ((0, 64),))
    seq_lengths = draw_seq_lengths(jax.random.fold_in(arg_keys[24], 71), 0)
    norm_gains = jnp.clip(1.0 + 0.1 * jax.random.normal(arg_keys[3], (2, D), jnp.float32), 0.5, 1.5)
    gains_moment = scatter_about(arg_keys[4], (2, D), (TOKENS ** 0.5 / 9), 64.0, (), jnp.float32)
    gains_square = jnp.clip(jax.random.uniform(arg_keys[5], (2, D), jnp.float32, 491.52, 1720.32), 491.52, 1720.32)
    recur_params = draw_recur_params(jax.random.fold_in(arg_keys[24], 71), 0)
    recur_moment = scatter_about(arg_keys[7], (CONV + 4, LRU), (TOKENS ** 0.5 / 9), 64.0, ((1, 2),), jnp.float32)
    recur_square = jnp.clip(491.52 + 1228.79996 * jax.random.uniform(arg_keys[8], (CONV + 4, LRU), jnp.float32) ** block_levels(arg_keys[8], (CONV + 4, LRU), ((1, 2),), -0.2, 0.2), 491.52, 1720.32)
    input_proj = scatter_about(arg_keys[9], (2, D, LRU), D ** -0.5, 0.125, ((1, 64), (2, 2)), jnp.float32)
    input_moment = scatter_about(arg_keys[10], (2, D, LRU), (TOKENS ** 0.5 / 9), 64.0, ((1, 64), (2, 2)), jnp.float32)
    input_square = jnp.clip(491.52 + 1228.79996 * jax.random.uniform(arg_keys[11], (2, D, LRU), jnp.float32) ** block_levels(arg_keys[11], (2, D, LRU), ((1, 64), (2, 2)), -0.2, 0.2), 491.52, 1720.32)
    gate_blocks = scatter_about(arg_keys[12], (2, HEADS, BLOCK, BLOCK), BLOCK ** -0.5, 0.375, ((1, 2), (2, 64)), jnp.float32)
    blocks_moment = scatter_about(arg_keys[13], (2, HEADS, BLOCK, BLOCK), (0.1 * TOKENS ** 0.5 / 9), 4.0, ((1, 2), (2, 64)), jnp.float32)
    blocks_square = jnp.clip(4.9152 + 12.287999 * jax.random.uniform(arg_keys[14], (2, HEADS, BLOCK, BLOCK), jnp.float32) ** block_levels(arg_keys[14], (2, HEADS, BLOCK, BLOCK), ((1, 2), (2, 64)), -0.2, 0.2), 4.9152, 17.2032)
    output_proj = scatter_about(arg_keys[15], (LRU, D), (LRU // 8) ** -0.5, 0.3125, ((0, 2), (1, 64)), jnp.float32)
    output_moment = scatter_about(arg_keys[16], (LRU, D), (TOKENS ** 0.5 / 9), 64.0, ((0, 2), (1, 64)), jnp.float32)
    output_square = jnp.clip(491.52 + 1228.79996 * jax.random.uniform(arg_keys[17], (LRU, D), jnp.float32) ** block_levels(arg_keys[17], (LRU, D), ((0, 2), (1, 64)), -0.2, 0.2), 491.52, 1720.32)
    inner_proj = scatter_about(arg_keys[18], (2, D, FF), D ** -0.5, 0.125, ((1, 64), (2, 2)), jnp.float32)
    inner_moment = scatter_about(arg_keys[19], (2, D, FF), (TOKENS ** 0.5 / 9), 64.0, ((1, 64), (2, 2)), jnp.float32)
    inner_square = jnp.clip(491.52 + 1228.79996 * jax.random.uniform(arg_keys[20], (2, D, FF), jnp.float32) ** block_levels(arg_keys[20], (2, D, FF), ((1, 64), (2, 2)), -0.2, 0.2), 491.52, 1720.32)
    down_proj = scatter_about(arg_keys[21], (FF, D), FF ** -0.5, 0.0625, ((0, 2), (1, 64)), jnp.float32)
    down_moment = scatter_about(arg_keys[22], (FF, D), (TOKENS ** 0.5 / 9), 64.0, ((0, 2), (1, 64)), jnp.float32)
    down_square = jnp.clip(491.52 + 1228.79996 * jax.random.uniform(arg_keys[23], (FF, D), jnp.float32) ** block_levels(arg_keys[23], (FF, D), ((0, 2), (1, 64)), -0.2, 0.2), 491.52, 1720.32)
    return dict(tokens=tokens, cotangent=cotangent, seq_lengths=seq_lengths, norm_gains=norm_gains, gains_moment=gains_moment, gains_square=gains_square, recur_params=recur_params, recur_moment=recur_moment, recur_square=recur_square, input_proj=input_proj, input_moment=input_moment, input_square=input_square, gate_blocks=gate_blocks, blocks_moment=blocks_moment, blocks_square=blocks_square, output_proj=output_proj, output_moment=output_moment, output_square=output_square, inner_proj=inner_proj, inner_moment=inner_moment, inner_square=inner_square, down_proj=down_proj, down_moment=down_moment, down_square=down_square)


@jax.custom_vjp
def low(v):
    return lax.optimization_barrier(v.astype(jnp.bfloat16)).astype(jnp.float32)

@jax.custom_vjp
def low_back(v):
    return v

def low_keep(v):
    return (low(v), None)

def low_pass(kept, grad):
    return (grad,)

def back_keep(v):
    return (v, None)

def back_low(kept, grad):
    return (low(grad),)
low.defvjp(low_keep, low_pass)
low_back.defvjp(back_keep, back_low)
norm_eps = 1e-06
beta_one = 0.9
beta_two = 0.95
adam_eps = 1e-08
weight_decay = 0.1
matrix_rate = 0.06
vector_rate = 1.0
gate_scale = 8.0

def product(form, left, right):
    return jnp.einsum(form, left, right, precision=lax.Precision.HIGHEST, preferred_element_type=jnp.float32)

def rms_inverse(values):
    return lax.rsqrt(lax.optimization_barrier(jnp.mean(values * values, axis=-1, keepdims=True)) + norm_eps)

def linear_pair(earlier, later):
    return (earlier[0] * later[0], later[0] * earlier[1] + later[1])

def stream_layout(lengths):
    ends = jnp.cumsum(lengths).astype(jnp.int32)
    places = jnp.arange(GROUP, dtype=jnp.int32)
    segment = lax.optimization_barrier(jnp.sum((places[:, None] >= ends[None, :]).astype(jnp.int32), axis=1)).astype(jnp.int32)
    starts = jnp.concatenate([jnp.zeros((1,), jnp.int32), ends])
    keeping = 1.0 - jnp.any(places[:, None] == starts[None, :], axis=1).astype(jnp.float32)
    valid = (segment < SEQS).astype(jnp.float32)
    return (segment, keeping, valid)

def forward(inputs, gains, recur, in_pair, blocks, out_weight, inner, down, masks, keeping):
    in_pair = low(in_pair)
    blocks = low(blocks)
    out_weight = low(out_weight)
    inner = low(inner)
    down = low(down)
    normed_in = low(inputs * rms_inverse(inputs) * gains[0])
    pre_x = product('gtd,dr->gtr', normed_in, in_pair[0])
    pre_y = product('gtd,dr->gtr', normed_in, in_pair[1])
    branch_x = low(low_back(pre_x))
    gated_y = jax.nn.gelu(low_back(pre_y), approximate=True)
    conv_out = recur[CONV]
    for offset in range(CONV):
        shifted = jnp.pad(branch_x, ((0, 0), (offset, 0), (0, 0)))[:, :GROUP]
        conv_out = conv_out + recur[offset] * masks[offset] * shifted
    conv_low = low(conv_out)
    heads_in = conv_low.reshape(N_FSDP, GROUP, HEADS, BLOCK)
    logit_x = product('gthi,hij->gthj', heads_in, blocks[0]).reshape(N_FSDP, GROUP, LRU) + recur[CONV + 1]
    logit_a = product('gthi,hij->gthj', heads_in, blocks[1]).reshape(N_FSDP, GROUP, LRU) + recur[CONV + 2]
    logit_x = low_back(logit_x)
    logit_a = low_back(logit_a)
    log_decay = -gate_scale * jax.nn.sigmoid(logit_a) * jax.nn.softplus(-recur[CONV + 3])
    decays = jnp.exp(log_decay) * keeping
    driven = (jnp.sqrt(-jnp.expm1(2.0 * log_decay)) * keeping + 1.0 - keeping) * jax.nn.sigmoid(logit_x) * conv_low
    _, hidden = lax.associative_scan(linear_pair, (decays, driven), axis=1)
    mixed_low = low(hidden * gated_y)
    resid = inputs + low_back(product('gtr,rd->gtd', mixed_low, out_weight))
    normed_mid = low(resid * rms_inverse(resid) * gains[1])
    gate_pre = low_back(product('gtd,df->gtf', normed_mid, inner[0]))
    up_pre = low_back(product('gtd,df->gtf', normed_mid, inner[1]))
    inner_low = low(jax.nn.gelu(gate_pre, approximate=True) * up_pre)
    return resid + low_back(product('gtf,fd->gtd', inner_low, down))

def adam_update(weight, moment, square, gradient, rate, shrink):
    moment = beta_one * moment + (1.0 - beta_one) * gradient
    square = beta_two * square + (1.0 - beta_two) * gradient * gradient
    normed = moment / (1.0 - beta_one ** STEP) / (jnp.sqrt(square / (1.0 - beta_two ** STEP)) + adam_eps)
    return (weight - rate * (normed + shrink * weight), moment, square)

def reference(tokens, cotangent, seq_lengths, norm_gains, gains_moment, gains_square, recur_params, recur_moment, recur_square, input_proj, input_moment, input_square, gate_blocks, blocks_moment, blocks_square, output_proj, output_moment, output_square, inner_proj, inner_moment, inner_square, down_proj, down_moment, down_square):
    segment, keeping, valid = jax.vmap(stream_layout)(seq_lengths)
    masks = []
    for offset in range(CONV):
        earlier = jnp.pad(segment, ((0, 0), (offset, 0)), constant_values=-1)[:, :GROUP]
        masks.append((earlier == segment).astype(jnp.float32)[..., None])
    keeping = keeping[..., None]
    inputs = tokens.astype(jnp.float32).reshape(N_FSDP, GROUP, D)
    params = (norm_gains, recur_params, input_proj, gate_blocks, output_proj, inner_proj, down_proj)

    def run(values, gains, recur, in_pair, blocks, out_weight, inner, down):
        return forward(values, gains, recur, in_pair, blocks, out_weight, inner, down, masks, keeping)
    result, pull = jax.vjp(run, inputs, *params)
    incoming = cotangent.astype(jnp.float32).reshape(N_FSDP, GROUP, D) * valid[..., None]
    grads = pull(incoming)
    mixed = result.reshape(TOKENS, D).astype(jnp.bfloat16)
    tokens_grad = grads[0].reshape(TOKENS, D)
    gains_new = adam_update(norm_gains, gains_moment, gains_square, grads[1], vector_rate, 0.0)
    recur_new = adam_update(recur_params, recur_moment, recur_square, grads[2], vector_rate, 0.0)
    input_new = adam_update(input_proj, input_moment, input_square, grads[3], matrix_rate, weight_decay)
    blocks_new = adam_update(gate_blocks, blocks_moment, blocks_square, grads[4], matrix_rate, weight_decay)
    output_new = adam_update(output_proj, output_moment, output_square, grads[5], matrix_rate, weight_decay)
    inner_new = adam_update(inner_proj, inner_moment, inner_square, grads[6], matrix_rate, weight_decay)
    down_new = adam_update(down_proj, down_moment, down_square, grads[7], matrix_rate, weight_decay)
    return (mixed, tokens_grad, gains_new[0], gains_new[1], gains_new[2], recur_new[0], recur_new[1], recur_new[2], input_new[0], input_new[1], input_new[2], blocks_new[0], blocks_new[1], blocks_new[2], output_new[0], output_new[1], output_new[2], inner_new[0], inner_new[1], inner_new[2], down_new[0], down_new[1], down_new[2])
```

```python
import functools

import jax
import jax.numpy as jnp
from jax import lax
from jax.experimental import pallas as pl
from jax.experimental.pallas import tpu as pltpu
from jax.sharding import PartitionSpec as P

STEP = 10

norm_eps = 1e-06
beta_one = 0.9
beta_two = 0.95
adam_eps = 1e-08
weight_decay = 0.1
matrix_rate = 0.06
vector_rate = 1.0
gate_scale = 8.0

bf16, f32 = jnp.bfloat16, jnp.float32
MESH = pl.DeviceIdType.MESH
DIM = 2560
COLS = 3968
SPLIT = 1664
EXT = 2560 + 128
WIDE = EXT + 2560
NT = (((1,), (1,)), ((), ()))
TN = (((0,), (0,)), ((), ()))


def dot(a, b):
    return jnp.dot(a, b, preferred_element_type=f32)


def dot_nt(a, b):
    return lax.dot_general(a, b, NT, preferred_element_type=f32)


def dot_tn(a, b):
    return lax.dot_general(a, b, TN, preferred_element_type=f32)


def many(n, fn):
    def one(i, carry):
        fn(i)
        return carry

    lax.fori_loop(0, n, one, 0)


class Place:
    def __init__(self):
        self.x = lax.axis_index("fsdp")
        self.c = lax.axis_index("context")
        self.t = lax.axis_index("tensor")
        self.y, self.z = lax.div(self.c, 4), lax.rem(self.c, 4)

    def ctx(self, dy, dz):
        return lax.rem(self.y + dy + 4, 4) * 4 + lax.rem(self.z + dz + 4, 4)

    def xs(self, d):
        return lax.rem(self.x + d + 4, 4)

    def along(self, half, d1, d2):
        return self.ctx(d2, d1) if half == 0 else self.ctx(d1, d2)

    def chain(self, d):
        return lax.rem(self.c + d + 16, 16)


class Wire:
    def __init__(self, place, ss, rs):
        self.place, self.ss, self.rs = place, ss, rs
        self.n, self.sent = 0, []

    def send(self, src, dst, **to):
        n = self.n
        self.n += 1
        copy = pltpu.make_async_remote_copy(
            src_ref=src, dst_ref=dst, send_sem=self.ss.at[n], recv_sem=self.rs.at[n],
            device_id=to, device_id_type=MESH,
        )
        copy.start()
        self.sent.append(copy)
        return n

    def recv(self, n, ref):
        pltpu.make_async_remote_copy(
            src_ref=ref, dst_ref=ref, send_sem=self.ss.at[n], recv_sem=self.rs.at[n],
            device_id={"fsdp": self.place.x}, device_id_type=MESH,
        ).wait_recv()

    def finish(self):
        for copy in self.sent:
            copy.wait_send()


class Local:
    def __init__(self, sems):
        self.sems, self.n, self.open = sems, 0, []

    def start(self, src, dst):
        copy = pltpu.make_async_copy(src, dst, self.sems.at[self.n])
        self.n += 1
        copy.start()
        self.open.append(copy)
        return copy

    def wait(self, copy):
        copy.wait()
        self.open = [other for other in self.open if other is not copy]

    def finish(self):
        for copy in self.open:
            copy.wait()


def greet(place, xs=(), ctx=(), chain=(), core=False):
    bar = pltpu.get_barrier_semaphore()
    n = 0
    for d in xs:
        pl.semaphore_signal(bar, inc=1, device_id={"fsdp": place.xs(d)}, device_id_type=MESH)
        n += 1
    for dy, dz in ctx:
        pl.semaphore_signal(bar, inc=1, device_id={"context": place.ctx(dy, dz)}, device_id_type=MESH)
        n += 1
    for d in chain:
        pl.semaphore_signal(bar, inc=1, device_id={"context": place.chain(d)}, device_id_type=MESH)
        n += 1
    if core:
        pl.semaphore_signal(bar, inc=1, device_id={"tensor": 1 - place.t}, device_id_type=MESH)
        n += 1
    pl.semaphore_wait(bar, n)


def row_half(index, half):
    return pl.ds(pl.multiple_of(index * 160 + 80 * half, 16), 80)


def gather_steps(wire, buf, own, at):
    place = wire.place
    width = own.shape[1]
    mid = width // 256 * 128
    LO, HI, FULL = (0, mid), (mid, width), (0, width)

    def ref(i, h, k):
        return buf.at[row_half(i, h), pl.ds(at + k[0], k[1] - k[0])]

    def mine(h):
        return own.at[pl.ds(80 * h, 80), :]

    def send(h, src, i, k, d1, d2):
        return wire.send(src, ref(i, h, k), context=place.along(h, d1, d2))

    st = {}
    for h in (0, 1):
        st[h, 1, 1] = send(h, mine(h), place.c, FULL, 1, 0)
        st[h, 1, -1] = send(h, mine(h), place.c, FULL, -1, 0)
    for h in (0, 1):
        for d in (1, -1):
            st[h, 0, d] = send(h, mine(h), place.c, FULL, 0, d)
    yield
    part = {1: LO, -1: HI}
    for d in (1, -1):
        for h in (0, 1):
            i = place.along(h, -d, 0)
            wire.recv(st[h, 1, d], ref(i, h, FULL))
            st[h, 1, 2 * d] = send(h, ref(i, h, part[d]), i, part[d], d, 0)
            for e in (1, -1):
                st[h, -d + 10, e] = send(h, ref(i, h, FULL), i, FULL, 0, e)
            yield

    def second(h, k, key):
        for d in (1, -1):
            i = place.along(h, k, -d)
            wire.recv(st[h, key, d], ref(i, h, FULL))
            st[h, key, 2 * d] = send(h, ref(i, h, part[d]), i, part[d], 0, d)

    for h in (0, 1):
        second(h, 0, 0)
        yield
    for h in (0, 1):
        i = place.along(h, 2, 0)
        wire.recv(st[h, 1, 2], ref(i, h, LO))
        wire.recv(st[h, 1, -2], ref(i, h, HI))
        for e in (1, -1):
            st[h, 12, e] = send(h, ref(i, h, FULL), i, FULL, 0, e)
        yield
    for k, key in ((-1, 9), (1, 11), (2, 12)):
        for h in (0, 1):
            second(h, k, key)
            yield
    for k, key in ((0, 0), (-1, 9), (1, 11), (2, 12)):
        for h in (0, 1):
            i = place.along(h, k, 2)
            for d in (1, -1):
                wire.recv(st[h, key, 2 * d], ref(i, h, part[d]))
        yield


def rows_gather_steps(wire, src, out, loc):
    place = wire.place
    x, t = place.x, place.t
    width = src.shape[1]
    h = width // 256 * 128
    LO, HI = pl.ds(0, h), pl.ds(h, width - h)
    xp, xm, xo = place.xs(1), place.xs(-1), place.xs(2)
    a = wire.send(src, out.at[x, t], fsdp=xp)
    b = wire.send(src, out.at[x, t], fsdp=xm)
    cores = [(x, wire.send(src, out.at[x, t], tensor=1 - t))]
    own = loc.start(src, out.at[x, t])
    yield
    wire.recv(a, out.at[xm, t])
    e = wire.send(out.at[xm, t, :, LO], out.at[xm, t, :, LO], fsdp=xp)
    cores.append((xm, wire.send(out.at[xm, t], out.at[xm, t], tensor=1 - t)))
    wire.recv(b, out.at[xp, t])
    f = wire.send(out.at[xp, t, :, HI], out.at[xp, t, :, HI], fsdp=xm)
    cores.append((xp, wire.send(out.at[xp, t], out.at[xp, t], tensor=1 - t)))
    yield
    wire.recv(e, out.at[xo, t, :, LO])
    wire.recv(f, out.at[xo, t, :, HI])
    cores.append((xo, wire.send(out.at[xo, t], out.at[xo, t], tensor=1 - t)))
    yield
    for k, n in cores:
        wire.recv(n, out.at[k, 1 - t])
    loc.wait(own)
    yield


def rows_scatter_steps(wire, part, crecv, sums, r1, r2, done):
    place = wire.place
    x, t = place.x, place.t
    R, width = sums.shape[1:]
    h = width // 256 * 128
    LO, HI = pl.ds(0, h), pl.ds(h, width - h)
    xp, xm, xo = place.xs(1), place.xs(-1), place.xs(2)
    cs = []
    for n, k in enumerate((xo, xp, xm, x)):
        cs.append(wire.send(part.at[k, 1 - t], crecv.at[n], tensor=1 - t))

    def rows(fn):
        def one(i):
            fn(pl.ds(pl.multiple_of(i * 16, 16), 16))

        many(R // 16, one)

    def put(n, k, cols, extra=None):
        def fn(r):
            v = part[k, t, r, cols].astype(f32) + crecv[n, r, cols].astype(f32)
            if extra is not None:
                v = v + r1[extra, r, cols].astype(f32)
            sums[n, r, cols] = v.astype(bf16)

        rows(fn)

    yield
    wire.recv(cs[0], crecv.at[0])
    put(0, xo, pl.ds(0, width))
    a = wire.send(sums.at[0, :, LO], r1.at[0, :, LO], fsdp=xp)
    b = wire.send(sums.at[0, :, HI], r1.at[1, :, HI], fsdp=xm)
    wire.recv(cs[1], crecv.at[1])
    put(1, xp, HI)
    e = wire.send(sums.at[1, :, HI], r2.at[0, :, HI], fsdp=xp)
    wire.recv(cs[2], crecv.at[2])
    put(2, xm, LO)
    f = wire.send(sums.at[2, :, LO], r2.at[1, :, LO], fsdp=xm)
    yield
    wire.recv(a, r1.at[0, :, LO])
    put(1, xp, LO, 0)
    g = wire.send(sums.at[1, :, LO], r2.at[0, :, LO], fsdp=xp)
    wire.recv(b, r1.at[1, :, HI])
    put(2, xm, HI, 1)
    i = wire.send(sums.at[2, :, HI], r2.at[1, :, HI], fsdp=xm)
    wire.recv(cs[3], crecv.at[3])
    yield
    wire.recv(e, r2.at[0, :, HI])
    wire.recv(f, r2.at[1, :, LO])
    wire.recv(g, r2.at[0, :, LO])
    wire.recv(i, r2.at[1, :, HI])

    def total(r):
        done(
            r,
            part[x, t, r, :].astype(f32)
            + crecv[3, r, :].astype(f32)
            + r2[0, r, :].astype(f32)
            + r2[1, r, :].astype(f32),
        )

    rows(total)
    yield


def drain(steps):
    for _ in steps:
        pass


def pump(steps, n=1):
    for _ in range(n):
        next(steps, None)


def gelu(v):
    return 0.5 * v * (1.0 + jnp.tanh(0.7978845608028654 * (v + 0.044715 * v * v * v)))


def gelu_and_slope(v):
    u = jnp.tanh(0.7978845608028654 * (v + 0.044715 * v * v * v))
    slope = 0.5 * (1.0 + u) + 0.5 * v * (1.0 - u * u) * (
        0.7978845608028654 * (1.0 + 3 * 0.044715 * v * v)
    )
    return 0.5 * v * (1.0 + u), slope


def one_less_exp(v):
    series = 1.0 + v * (1.0 / 7.0)
    for k in (6.0, 5.0, 4.0, 3.0, 2.0):
        series = 1.0 + v * (1.0 / k) * series
    return jnp.where(v > -0.35, -v * series, 1.0 - jnp.exp(v))


def sigmoid(v):
    return 1.0 / (1.0 + jnp.exp(-v))


def shifted(block, edge, k):
    moved = pltpu.roll(block, k, 0)
    first = jnp.where(
        lax.broadcasted_iota(jnp.int32, edge.shape, 0) < k, pltpu.roll(edge, k, 0), moved[:8]
    )
    return jnp.concatenate([first, moved[8:]], axis=0)


def scan_down(a, b):
    rows = lax.broadcasted_iota(jnp.int32, a.shape, 0)
    s = 1
    while s < a.shape[0]:
        earlier = rows >= s
        pa = jnp.where(earlier, pltpu.roll(a, s, 0), 1.0)
        pb = jnp.where(earlier, pltpu.roll(b, s, 0), 0.0)
        b = b + a * pb
        a = a * pa
        s *= 2
    return a, b


def scan_up(a, b):
    rows = lax.broadcasted_iota(jnp.int32, a.shape, 0)
    n = a.shape[0]
    s = 1
    while s < n:
        later = rows < n - s
        pa = jnp.where(later, pltpu.roll(a, n - s, 0), 1.0)
        pb = jnp.where(later, pltpu.roll(b, n - s, 0), 0.0)
        b = b + a * pb
        a = a * pa
        s *= 2
    return a, b


def selector(g):
    i = lax.broadcasted_iota(jnp.int32, (256, 512), 0)
    j = lax.broadcasted_iota(jnp.int32, (256, 512), 1)
    xx, cc, r = i // 64, (i // 4) % 16, i % 4
    return (j == cc * 32 + xx * 8 + g * 4 + r).astype(f32).astype(bf16)


def gate_matrix(packed, g):
    return dot(selector(g), packed).astype(bf16)


def column(tile):
    return pl.ds(pl.multiple_of(128 + 256 * tile, 128), 256)


def head_count(x):
    return jnp.where(x == 0, 2, 1).astype(jnp.int32)


def lanes(h):
    return pl.ds(pl.multiple_of(h * 256, 256), 256)


def token_rows(g):
    return pl.ds(pl.multiple_of(g * 128, 128), 128)


def recur_terms(lx, la, cl, sp, keep):
    sx, sa = sigmoid(lx), sigmoid(la)
    log_decay = (-gate_scale) * sa * sp
    grown = one_less_exp(2.0 * log_decay)
    root = jnp.sqrt(grown)
    factor = root * keep + 1.0 - keep
    return sx, sa, log_decay, root, factor


def forward_kernel(
    p_ref, a_ref, tok_ref, gain_ref, rec_ref,
    w_out, act_out, lx_out, la_out, hid_out, py_out, low_out, cg_out, nm_out, resid_out,
    xbuf, wide, chunk1, chunk2, w1, act, lx_s, la_s, hid_s, py_s, low_s, halo, cum_s, cg, cin,
    part, crecv, sums, r1, r2, normed, nm, resid, packed, gates,
    ss, rs, ls,
):
    place = Place()
    x, c, t = place.x, place.c, place.t
    greet(place, xs=(1, 2, 3), ctx=((1, 0), (2, 0), (3, 0), (0, 1), (0, 2), (0, 3)), chain=(1, -1), core=True)
    wire, loc = Wire(place, ss, rs), Local(ls)
    nh = head_count(x)

    stages = ((0, SPLIT, chunk1), (SPLIT, COLS, chunk2))
    came = {}

    def spread(s):
        c0, c1, _ = stages[s]
        cs = pl.ds(c0, c1 - c0)
        for d in (1, 3, 2):
            came[s, d] = wire.send(p_ref.at[place.xs(d), :, cs], xbuf.at[x, :, cs], fsdp=place.xs(d))

    def arrange(s):
        c0, c1, chunk = stages[s]
        cs = pl.ds(c0, c1 - c0)
        for d in (1, 3, 2):
            wire.recv(came[s, d], xbuf.at[place.xs(-d), :, cs])

        for k in range(4):
            def take(src, k=k):
                v = src[k, :, cs].astype(f32)
                wide[pl.ds(40 * k, 40), cs] = v[:40]

            pl.when(x == k)(functools.partial(take, p_ref))
            pl.when(x != k)(functools.partial(take, xbuf))
        if s == 0:
            for k in range(4):
                def gate(src, k=k):
                    v = src[k, :, pl.ds(0, 512)].astype(f32)
                    for b in range(4):
                        wide[pl.ds(32 * b + 8 * k, 8), pl.ds(0, 128)] = v[40:, 128 * b : 128 * b + 128]

                pl.when(x == k)(functools.partial(gate, p_ref))
                pl.when(x != k)(functools.partial(gate, xbuf))
        chunk[...] = wide[:, cs].astype(bf16)

    spread(0)
    rows = rows_gather_steps(wire, a_ref, act, loc)
    pump(rows)
    spread(1)
    arrange(0)
    mine = pl.ds(pl.multiple_of(c * 160, 16), 160)
    own1 = loc.start(chunk1, w1.at[mine, :])
    one = gather_steps(wire, w1, chunk1, 0)
    pump(one, 1)
    arrange(1)
    loc.start(chunk2, w_out.at[mine, pl.ds(SPLIT, COLS - SPLIT)])
    pump(one, 2)
    pump(rows)
    pump(one, 2)
    pump(rows)
    pump(one, 2)
    pump(rows)
    pump(one, 4)
    two = gather_steps(wire, w_out, chunk2, SPLIT)
    pump(two, 1)
    drain(one)
    loc.wait(own1)
    drain(rows)
    loc.start(w1, w_out.at[:, pl.ds(0, SPLIT)])
    loc.start(act, act_out)

    def project(h):
        ni = act[:, :, :, pl.ds(0, DIM)].reshape(512, DIM)
        low_s[0, :, lanes(h)] = dot(ni, w1[:, column(h)]).astype(bf16)
        py_s[:, lanes(h)] = dot(ni, w1[:, column(nh + h)])

    many(nh, project)
    before = low_s.at[0].reshape(4, 128, 512)
    hn = wire.send(before.at[:, pl.ds(112, 16), :], halo, context=place.chain(1))
    loc.start(py_s, py_out)
    pump(two, 1)
    for cc in range(16):
        for b in range(4):
            packed[pl.ds(32 * cc, 32), pl.ds(128 * b, 128)] = w1[pl.ds(160 * cc + 32 * b, 32), pl.ds(0, 128)]
    for g in (0, 1):
        gates[g] = gate_matrix(packed[...], g)
    wire.recv(hn, halo)
    pump(two, 1)

    def flags(g, k):
        v = act[pl.ds(g, 1), :, :, pl.ds(DIM, 128)].reshape(128, 128).astype(f32)
        return v[:, k : k + 1]

    cg[c] = jnp.zeros((2, 8, 512), f32)

    def conv(h):
        def group(g):
            bx = low_s[0, token_rows(g), lanes(h)].astype(f32)
            edge = halo[g, :, lanes(h)].astype(f32)[8:]
            out = rec_ref[pl.ds(4, 1), lanes(h)] + rec_ref[pl.ds(0, 1), lanes(h)] * bx
            for k in (1, 2, 3):
                out = out + rec_ref[pl.ds(k, 1), lanes(h)] * (flags(g, 1 + k) * shifted(bx, edge, k))
            low_s[1, token_rows(g), lanes(h)] = out.astype(bf16)

        many(4, group)
        cl = low_s[1, :, lanes(h)]
        lx_s[:, lanes(h)] = dot(cl, gates[0, :, lanes(h)]) + rec_ref[pl.ds(5, 1), lanes(h)]
        la_s[:, lanes(h)] = dot(cl, gates[1, :, lanes(h)]) + rec_ref[pl.ds(6, 1), lanes(h)]

    many(nh, conv)
    loc.start(lx_s, lx_out)
    loc.start(la_s, la_out)
    pump(two, 1)

    def scan(q):
        cols = pl.ds(pl.multiple_of(q * 128, 128), 128)
        for g in range(4):
            r = pl.ds(128 * g, 128)
            keep = flags(g, 1)
            cl = low_s[1, r, cols].astype(f32)
            sx, sa, log_decay, root, factor = recur_terms(
                lx_s[r, cols], la_s[r, cols], cl, rec_ref[pl.ds(7, 1), cols], keep
            )
            a, b = scan_down(jnp.exp(log_decay) * keep, factor * sx * cl)
            cum_s[r, cols] = a
            hid_s[r, cols] = b
            cg[c, 0, pl.ds(g, 1), cols] = a[127:]
            cg[c, 1, pl.ds(g, 1), cols] = b[127:]

    many(2 * nh, scan)
    pump(two, 1)
    ns = [wire.send(cg.at[c], cg.at[c], context=place.ctx(0, d)) for d in (1, 2, 3)]
    for d, n in zip((1, 2, 3), ns):
        wire.recv(n, cg.at[place.ctx(0, -d)])
    line = pl.ds(place.y * 4, 4)
    ns = [wire.send(cg.at[line], cg.at[line], context=place.ctx(d, 0)) for d in (1, 2, 3)]
    pump(two, 1)
    for d, n in zip((1, 2, 3), ns):
        wire.recv(n, cg.at[pl.ds(lax.rem(place.y + 4 - d, 4) * 4, 4)])

    def enter(s, state):
        return cg[s, 0] * state + cg[s, 1]

    cin[...] = lax.fori_loop(0, c, enter, jnp.zeros((8, 512), f32))
    loc.start(cg, cg_out)

    def mix(h):
        for g in range(4):
            r = pl.ds(128 * g, 128)
            hid = hid_s[r, lanes(h)] + cum_s[r, lanes(h)] * cin[pl.ds(g, 1), lanes(h)]
            hid_s[r, lanes(h)] = hid
            low_s[2, r, lanes(h)] = (hid * gelu(py_s[r, lanes(h)])).astype(bf16)

    many(nh, mix)
    loc.start(hid_s, hid_out)
    loc.start(low_s, low_out)
    pump(two, 1)

    def project_out(k, heads):
        def block(n):
            r = pl.ds(pl.multiple_of(n * 512, 512), 512)
            ow = w1[r, pl.ds(128 + 512 * heads, 256 * heads)]
            v = dot_nt(low_s[2, :, pl.ds(0, 256 * heads)], ow)
            part[:, :, :, r] = v.astype(bf16).reshape(4, 2, 64, 512)

        many(5, block)

    pl.when(x == 0)(lambda: project_out(0, 2))
    pl.when(x != 0)(lambda: project_out(0, 1))

    def add_resid(r, total):
        resid[r, :] = tok_ref[r, :] + total

    steps = rows_scatter_steps(wire, part, crecv, sums, r1, r2, add_resid)
    for _ in steps:
        pump(two, 1)
    loc.start(resid, resid_out)

    def norm(i):
        r = pl.ds(pl.multiple_of(i * 16, 16), 16)
        v = resid[r, :]
        inv = lax.rsqrt(jnp.mean(v * v, axis=-1, keepdims=True) + norm_eps)
        normed[r, :] = (v * inv * gain_ref[...]).astype(bf16)

    many(4, norm)
    steps = rows_gather_steps(wire, normed, nm, loc)
    for _ in steps:
        pump(two, 1)
    loc.start(nm, nm_out)
    drain(two)
    wire.finish()
    loc.finish()


def vm(shape, dtype):
    return pltpu.VMEM(shape, dtype)


ANY = pl.BlockSpec(memory_space=pl.ANY)
VM = pl.BlockSpec(memory_space=pltpu.VMEM)


def forward_call(p, a, tok, gain, rec):
    S = jax.ShapeDtypeStruct
    return pl.pallas_call(
        forward_kernel,
        name="recurrent_forward",
        out_shape=(
            S((DIM, COLS), bf16), S((4, 2, 64, WIDE), bf16),
            S((512, 512), f32), S((512, 512), f32), S((512, 512), f32), S((512, 512), f32),
            S((3, 512, 512), bf16), S((16, 2, 8, 512), f32), S((4, 2, 64, DIM), bf16), S((64, DIM), f32),
        ),
        in_specs=[VM] * 5,
        out_specs=[ANY] * 10,
        scratch_shapes=[
            vm((4, 48, COLS), bf16), vm((160, COLS), f32), vm((160, SPLIT), bf16), vm((160, COLS - SPLIT), bf16),
            vm((DIM, SPLIT), bf16), vm((4, 2, 64, WIDE), bf16),
            vm((512, 512), f32), vm((512, 512), f32), vm((512, 512), f32), vm((512, 512), f32),
            vm((3, 512, 512), bf16), vm((4, 16, 512), bf16), vm((512, 512), f32), vm((16, 2, 8, 512), f32), vm((8, 512), f32),
            vm((4, 2, 64, DIM), bf16), vm((4, 64, DIM), bf16), vm((3, 64, DIM), bf16), vm((2, 64, DIM), bf16), vm((2, 64, DIM), bf16),
            vm((64, DIM), bf16), vm((4, 2, 64, DIM), bf16), vm((64, DIM), f32), vm((512, 512), bf16), vm((2, 256, 512), bf16),
            pltpu.SemaphoreType.DMA((140,)), pltpu.SemaphoreType.DMA((140,)), pltpu.SemaphoreType.DMA((20,)),
        ],
        compiler_params=pltpu.CompilerParams(collective_id=0, has_side_effects=True, vmem_limit_bytes=60 << 20),
    )(p, a, tok, gain, rec)


def transpose_rows(src, dst):
    def block(n):
        cols = pl.ds(pl.multiple_of(n * 256, 256), 256)
        dst[cols, :] = src[:, :, :, cols].reshape(512, 256).T

    many(10, block)


def add_sublanes(v):
    return v[:8] + v[8:]


def norm_back(total, value, gain):
    inv = lax.rsqrt(jnp.mean(value * value, axis=-1, keepdims=True) + norm_eps)
    xhat = value * inv
    weighted = total * gain
    inner = jnp.mean(weighted * xhat, axis=-1, keepdims=True)
    return inv * (weighted - xhat * inner), add_sublanes(total * xhat)


def ffn_kernel(
    w_ref, act_ref, nm, resid, gain_ref,
    g_out, mixed_out, gm_out, gres_out, gain_out,
    gl, nmt, glt, wt, gt, pre, low, fo, gmid, part, crecv, sums, r1, r2, normed, gm,
    ss, rs, ls, ws, gs,
):
    place = Place()
    x, t = place.x, place.t
    greet(place, xs=(1, -1), core=True)
    wire, loc = Wire(place, ss, rs), Local(ls)
    nh = head_count(x)
    nf = 5 - nh
    cols = lambda kind, j: column(3 * nh + kind * nf + j)

    def load(j, slot):
        return [pltpu.make_async_copy(w_ref.at[:, cols(k, j)], wt.at[slot, k], ws.at[slot, k]) for k in range(3)]

    def store(j, slot):
        return [pltpu.make_async_copy(gt.at[slot, k], g_out.at[:, cols(k, j)], gs.at[slot, k]) for k in range(3)]

    for cp in load(0, 0):
        cp.start()
    glc = loc.start(act_ref.at[:, :, :, pl.ds(EXT, DIM)], gl)
    transpose_rows(nm, nmt)
    loc.wait(glc)
    transpose_rows(gl, glt)

    def zero(n):
        r = pl.ds(pl.multiple_of(n * 16, 16), 16)
        fo[r, :] = jnp.zeros((16, DIM), f32)
        gmid[r, :] = jnp.zeros((16, DIM), f32)

    many(32, zero)

    def tile(j):
        slot = lax.rem(j, 2)
        for cp in load(j, slot):
            cp.wait()

        @pl.when(j + 1 < nf)
        def _():
            for cp in load(j + 1, 1 - slot):
                cp.start()

        pre[0] = dot(nm[...].reshape(512, DIM), wt[slot, 0])
        pre[1] = dot(nm[...].reshape(512, DIM), wt[slot, 1])
        pre[2] = dot(gl[...].reshape(512, DIM), wt[slot, 2])

        def point(i):
            r = pl.ds(pl.multiple_of(i * 32, 32), 32)
            gated, slope = gelu_and_slope(pre[0, r, :])
            up, gi = pre[1, r, :], pre[2, r, :]
            low[0, r, :] = (gated * up).astype(bf16)
            low[1, r, :] = (gi * up * slope).astype(bf16)
            low[2, r, :] = (gi * gated).astype(bf16)

        many(16, point)

        @pl.when(j >= 2)
        def _():
            for cp in store(j - 2, slot):
                cp.wait()

        def block(n):
            r = pl.ds(pl.multiple_of(n * 512, 512), 512)
            gmid[:, r] += dot_nt(low[1], wt[slot, 0, r, :]) + dot_nt(low[2], wt[slot, 1, r, :])
            fo[:, r] += dot_nt(low[0], wt[slot, 2, r, :])
            gt[slot, 0, r, :] = dot(nmt[r, :], low[1]).astype(bf16)
            gt[slot, 1, r, :] = dot(nmt[r, :], low[2]).astype(bf16)
            gt[slot, 2, r, :] = dot(glt[r, :], low[0]).astype(bf16)

        many(5, block)
        for cp in store(j, slot):
            cp.start()

    many(nf, tile)

    def narrow(n):
        r = pl.ds(pl.multiple_of(n * 64, 64), 64)
        k, u = n // 2, n % 2
        part[0, k, u] = gmid[r, :].astype(bf16)
        part[1, k, u] = fo[r, :].astype(bf16)

    many(8, narrow)
    back = rows_scatter_steps(
        wire, part.at[0], crecv.at[0], sums.at[0], r1.at[0], r2.at[0],
        lambda r, v: gres_step(r, v),
    )

    def gres_step(r, total):
        gx, gain = norm_back(total, resid[r, :], gain_ref[...])
        gr = gl[x, t, r, :].astype(f32) + gx
        fo[r, :] = gr
        normed[r, :] = gr.astype(bf16)
        gmid[pl.ds(0, 8), :] += gain

    ahead = rows_scatter_steps(
        wire, part.at[1], crecv.at[1], sums.at[1], r1.at[1], r2.at[1],
        lambda r, v: mixed_step(r, v),
    )

    def mixed_step(r, total):
        mixed_out[t, r, :] = (resid[r, :] + total).astype(bf16)

    pump(back, 1)
    pump(ahead, 1)
    gmid[pl.ds(0, 8), :] = jnp.zeros((8, DIM), f32)
    drain(back)
    gains = gmid[pl.ds(0, 8), :]
    gain_out[...] = jnp.broadcast_to(jnp.sum(gains, axis=0, keepdims=True), (8, DIM))
    rows = rows_gather_steps(wire, normed, gm, loc)
    pump(rows, 1)
    loc.start(fo.at[pl.ds(0, 64), :], gres_out)
    for _ in rows:
        pump(ahead, 1)
    drain(ahead)
    loc.start(gm, gm_out)
    mn = wire.send(mixed_out.at[t], mixed_out.at[t], tensor=1 - t)
    for n in (2, 1):
        for cp in store(nf - n, lax.rem(nf - n, 2)):
            cp.wait()
    wire.recv(mn, mixed_out.at[1 - t])
    wire.finish()
    loc.finish()


def ffn_call(w, act, nm, resid, gain):
    S = jax.ShapeDtypeStruct
    R = (64, DIM)
    return pl.pallas_call(
        ffn_kernel,
        name="feed_forward",
        out_shape=(S((DIM, COLS), bf16), S((2,) + R, bf16), S((4, 2) + R, bf16), S(R, f32), S((8, DIM), f32)),
        in_specs=[ANY, ANY, VM, VM, VM],
        out_specs=[ANY, VM, ANY, ANY, VM],
        scratch_shapes=[
            vm((4, 2) + R, bf16), vm((DIM, 512), bf16), vm((DIM, 512), bf16), vm((2, 3, DIM, 256), bf16), vm((2, 3, DIM, 256), bf16),
            vm((3, 512, 256), f32), vm((3, 512, 256), bf16), vm((512, DIM), f32), vm((512, DIM), f32),
            vm((2, 4, 2) + R, bf16), vm((2, 4) + R, bf16), vm((2, 3) + R, bf16), vm((2, 2) + R, bf16), vm((2, 2) + R, bf16),
            vm(R, bf16), vm((4, 2) + R, bf16),
            pltpu.SemaphoreType.DMA((40,)), pltpu.SemaphoreType.DMA((40,)), pltpu.SemaphoreType.DMA((8,)),
            pltpu.SemaphoreType.DMA((2, 3)), pltpu.SemaphoreType.DMA((2, 3)),
        ],
        compiler_params=pltpu.CompilerParams(collective_id=1, has_side_effects=True, vmem_limit_bytes=60 << 20),
    )(w, act, nm, resid, gain)


def scatter_steps(wire, loc, g_ref, at, bufs, out_ref, gates):
    gvn, gvo, r1, r2, r3, r4, wide, obuf = bufs
    place = wire.place
    x, c = place.x, place.c
    width = wide.shape[1]
    mid = width // 256 * 128
    LO, HI, FULL = (0, mid), (mid, width), (0, width)
    zero = {1: LO, -1: HI}
    other = {1: HI, -1: LO}

    def gref(h, d1, d2, k):
        return g_ref.at[row_half(place.along(h, d1, d2), h), pl.ds(at + k[0], k[1] - k[0])]

    def cut(k):
        return pl.ds(k[0], k[1] - k[0])

    def short(k):
        return pl.ds(0, k[1] - k[0])

    side = {1: 0, -1: 1}
    order2 = (2, 1, 3, 0)
    st, loads = {}, {}
    for d2 in order2:
        for h in (0, 1):
            for d in (1, -1):
                st[h, 1, d, d2] = wire.send(
                    gref(h, 2, d2, zero[d]), r1.at[h, side[d], d2, :, short(zero[d])], context=place.along(h, d, 0)
                )
    for d2 in order2:
        for h in (0, 1):
            for d in (1, -1):
                loads[h, d, d2] = loc.start(gref(h, d, d2, zero[d]), gvn.at[h, side[d], d2, :, short(zero[d])])
    for d2 in order2:
        for h in (0, 1):
            loads[h, 0, d2] = loc.start(gref(h, 0, d2, FULL), gvo.at[h, d2])
    for d2 in order2:
        for h in (0, 1):
            for d in (1, -1):
                st[h, 2, d, d2] = wire.send(
                    gref(h, d, d2, other[d]), r2.at[h, side[d], d2, :, cut(other[d])], context=place.along(h, d, 0)
                )
    yield

    def add(dst, srcs):
        def one(i):
            r = pl.ds(pl.multiple_of(i * 16, 16), 16)
            v = srcs[0][r, :].astype(f32)
            for s in srcs[1:]:
                v = v + s[r, :].astype(f32)
            dst[r, :] = v.astype(dst.dtype)

        many(5, one)

    for d2 in order2:
        for h in (0, 1):
            for d in (1, -1):
                k = zero[d]
                mine = gvn.at[h, side[d], d2, :, short(k)]
                loc.wait(loads[h, d, d2])
                wire.recv(st[h, 1, d, d2], r1.at[h, side[d], d2, :, short(k)])
                add(mine, [mine, r1.at[h, side[d], d2, :, short(k)]])
                st[h, 3, d, d2] = wire.send(mine, r2.at[h, side[d], d2, :, cut(k)], context=place.along(h, d, 0))
        yield
    for d2 in order2:
        for h in (0, 1):
            own = gvo.at[h, d2]
            loc.wait(loads[h, 0, d2])
            for d in (1, -1):
                wire.recv(st[h, 2, d, d2], r2.at[h, side[d], d2, :, cut(other[d])])
                wire.recv(st[h, 3, d, d2], r2.at[h, side[d], d2, :, cut(zero[d])])
            add(own, [own, r2.at[h, 0, d2], r2.at[h, 1, d2]])
            if d2 == 2:
                for d in (1, -1):
                    st[h, 4, d] = wire.send(
                        own.at[:, cut(zero[d])], r3.at[h, side[d], :, short(zero[d])], context=place.along(h, 0, d)
                    )
            if d2 in (1, 3):
                d = 1 if d2 == 1 else -1
                st[h, 5, d] = wire.send(
                    own.at[:, cut(other[d])], r4.at[h, side[d], :, cut(other[d])], context=place.along(h, 0, d)
                )
        yield
    for h in (0, 1):
        for d in (1, -1):
            k = zero[d]
            mine = gvo.at[h, d % 4, :, cut(k)]
            got = r3.at[h, side[d], :, short(k)]
            wire.recv(st[h, 4, d], got)
            add(mine, [mine, got])
            st[h, 6, d] = wire.send(mine, r4.at[h, side[d], :, cut(k)], context=place.along(h, 0, d))
    yield
    for h in (0, 1):
        for d in (1, -1):
            wire.recv(st[h, 5, d], r4.at[h, side[d], :, cut(other[d])])
            wire.recv(st[h, 6, d], r4.at[h, side[d], :, cut(zero[d])])
        add(wide.at[pl.ds(80 * h, 80), :], [gvo.at[h, 0], r4.at[h, 0], r4.at[h, 1]])
    for k in range(4):
        obuf[k] = jnp.concatenate([wide[pl.ds(40 * k, 40), :], jnp.zeros((8, width), f32)], axis=0).astype(bf16)
        if gates:
            tail = jnp.concatenate([wide[pl.ds(32 * b + 8 * k, 8), pl.ds(0, 128)] for b in range(4)], axis=1)
            obuf[k, :, pl.ds(0, 512)] = jnp.concatenate([wide[pl.ds(40 * k, 40), pl.ds(0, 512)], tail], axis=0).astype(bf16)
    ends = [(d, wire.send(obuf.at[place.xs(d)], out_ref.at[x], fsdp=place.xs(d))) for d in (1, 3, 2)]
    own = loc.start(obuf.at[x], out_ref.at[x])
    yield
    for d, n in ends:
        wire.recv(n, out_ref.at[place.xs(-d)])
    loc.wait(own)
    yield


def scatter_scratch(width):
    hi = width - width // 256 * 128
    return [
        vm((2, 2, 4, 80, hi), bf16), vm((2, 4, 80, width), bf16), vm((2, 2, 4, 80, hi), bf16), vm((2, 2, 4, 80, width), bf16),
        vm((2, 2, 80, hi), bf16), vm((2, 2, 80, width), bf16), vm((160, width), f32), vm((4, 48, width), bf16),
    ]


PLANE = ((1, 0), (3, 0), (0, 1), (0, 3))


def backward_kernel(
    g_ref, w_ref, act_ref, gm, lx_s, la_s, hid_s, py_s, low_s, cg, tok_ref, gres, gain_ref, rec_ref,
    ffn_out, grec_out, tgrad_out, small_out,
    b0, b1, b2, b3, b4, b5, b6, b7,
    w1, ni, nit, flag_s, gmx, gpy, bc, bp, bg, cin, cback, glow, edge, edge_in, edge_out, gpx, gates, packed, dgates,
    gt, gtile, gain_acc, crecv, sums, r1, r2,
    ss, rs, ls, gs,
):
    part, gconv, gdir, gmt = ni, gmx, bc, nit
    place = Place()
    x, c, t = place.x, place.c, place.t
    greet(place, xs=(1, 2, 3), ctx=((1, 0), (2, 0), (3, 0), (0, 1), (0, 2), (0, 3)), chain=(1, -1), core=True)
    wire, loc = Wire(place, ss, rs), Local(ls)
    nh = head_count(x)
    big = scatter_steps(wire, loc, g_ref, SPLIT, (b0, b1, b2, b3, b4, b5, b6, b7), ffn_out, False)
    lw = loc.start(w_ref.at[:, pl.ds(0, SPLIT)], w1)
    ln = loc.start(act_ref.at[:, :, :, pl.ds(0, DIM)], ni)
    lf = loc.start(act_ref.at[:, :, :, pl.ds(DIM, 128)], flag_s)
    pump(big, 1)
    transpose_rows(gm, gmt)
    loc.wait(lw)
    loc.wait(lf)
    pump(big, 1)

    def flags(g, k):
        return flag_s[pl.ds(g, 1)].reshape(128, 128).astype(f32)[:, k : k + 1]

    def send_tile(lhs, rhs, tile, slot, first):
        @pl.when(jnp.logical_not(first))
        def _():
            pltpu.make_async_copy(gt.at[slot], grec_out.at[:, column(0)], gs.at[slot]).wait()

        def block(n):
            r = pl.ds(pl.multiple_of(n * 512, 512), 512)
            gt[slot, r, :] = dot(lhs[r, :], rhs).astype(bf16)

        many(5, block)
        pltpu.make_async_copy(gt.at[slot], grec_out.at[:, column(tile)], gs.at[slot]).start()

    def mixed_back(h):
        gmx[:, lanes(h)] = dot(gm[...].reshape(512, DIM), w1[:, column(2 * nh + h)])

    many(nh, mixed_back)

    bg[c] = jnp.zeros((8, 512), f32)

    def scan(q):
        cols = pl.ds(pl.multiple_of(q * 128, 128), 128)
        for g in range(4):
            r = pl.ds(128 * g, 128)
            gated, slope = gelu_and_slope(py_s[r, cols])
            grad = gmx[r, cols]
            gpy[r, cols] = (grad * hid_s[r, cols] * slope).astype(bf16)
            keep = flags(g, 1)
            dec = jnp.exp((-gate_scale) * sigmoid(la_s[r, cols]) * rec_ref[pl.ds(7, 1), cols]) * keep
            last = lax.broadcasted_iota(jnp.int32, dec.shape, 0) == 127
            a, b = scan_up(jnp.where(last, 1.0, pltpu.roll(dec, 127, 0)), grad * gated)
            bc[r, cols] = a
            bp[r, cols] = b
            bg[c, pl.ds(g, 1), cols] = dec[:1] * b[:1]

    many(2 * nh, scan)
    ns = [wire.send(bg.at[c], bg.at[c], context=place.ctx(0, d)) for d in (1, 2, 3)]
    pump(big, 1)

    def out_tile(h):
        send_tile(gmt, low_s[2, :, lanes(h)], 2 * nh + h, 0, h == 0)

    many(nh, out_tile)
    loc.wait(ln)
    transpose_rows(ni, nit)
    for d, n in zip((1, 2, 3), ns):
        wire.recv(n, bg.at[place.ctx(0, -d)])
    line = pl.ds(place.y * 4, 4)
    ns = [wire.send(bg.at[line], bg.at[line], context=place.ctx(d, 0)) for d in (1, 2, 3)]

    def y_tile(h):
        send_tile(nit, gpy[:, lanes(h)], nh + h, 1, h == 0)

    many(nh, y_tile)
    pump(big, 1)
    for cc in range(16):
        for b in range(4):
            packed[pl.ds(32 * cc, 32), pl.ds(128 * b, 128)] = w1[pl.ds(160 * cc + 32 * b, 32), pl.ds(0, 128)]
    for g in (0, 1):
        gates[g] = gate_matrix(packed[...], g)
    for d, n in zip((1, 2, 3), ns):
        wire.recv(n, bg.at[pl.ds(lax.rem(place.y + 4 - d, 4) * 4, 4)])

    def enter(s, state):
        return cg[s, 0] * state + cg[s, 1]

    cin[...] = lax.fori_loop(0, c, enter, jnp.zeros((8, 512), f32))

    def leave(s, state):
        k = 15 - s
        return cg[k, 0] * state + bg[k]

    cback[...] = lax.fori_loop(0, 15 - c, leave, jnp.zeros((8, 512), f32))
    small_out[...] = jnp.zeros_like(small_out)

    def terms(q):
        cols = pl.ds(pl.multiple_of(q * 128, 128), 128)
        sums_x = jnp.zeros((1, 128), f32)
        sums_a = jnp.zeros((1, 128), f32)
        sums_l = jnp.zeros((1, 128), f32)
        for g in range(4):
            r = pl.ds(128 * g, 128)
            keep = flags(g, 1)
            cl = low_s[1, r, cols].astype(f32)
            sp, dsp = rec_ref[pl.ds(7, 1), cols], rec_ref[pl.ds(8, 1), cols]
            sx, sa, log_decay, root, factor = recur_terms(lx_s[r, cols], la_s[r, cols], cl, sp, keep)
            adj = bp[r, cols] + bc[r, cols] * cback[pl.ds(g, 1), cols]
            hid = hid_s[r, cols]
            first = lax.broadcasted_iota(jnp.int32, hid.shape, 0) == 0
            prev = jnp.where(first, cin[pl.ds(g, 1), cols], pltpu.roll(hid, 1, 0))
            grown = jnp.exp(log_decay)
            gld = keep * grown * (adj * prev - adj * sx * cl * grown / root)
            glx = (adj * factor * cl * sx * (1.0 - sx)).astype(bf16)
            gla = (gld * ((-gate_scale) * sp) * sa * (1.0 - sa)).astype(bf16)
            glow[0, r, cols] = glx
            glow[1, r, cols] = gla
            gdir[r, cols] = adj * factor * sx
            sums_x += jnp.sum(glx.astype(f32), axis=0, keepdims=True)
            sums_a += jnp.sum(gla.astype(f32), axis=0, keepdims=True)
            sums_l += jnp.sum(gld * sa, axis=0, keepdims=True) * (gate_scale * dsp)
        small_out[pl.ds(5, 1), cols] = sums_x
        small_out[pl.ds(6, 1), cols] = sums_a
        small_out[pl.ds(7, 1), cols] = sums_l

    many(2 * nh, terms)
    pump(big, 1)
    before = low_s.at[0].reshape(4, 128, 512)
    hn = wire.send(before.at[:, pl.ds(112, 16), :], edge_in, context=place.chain(1))
    wire.recv(hn, edge_in)

    def conv_back(h):
        cl = low_s[1, :, lanes(h)]
        lx, la = glow[0, :, lanes(h)], glow[1, :, lanes(h)]
        gconv[:, lanes(h)] = (
            gdir[:, lanes(h)] + dot_nt(lx, gates[0, :, lanes(h)]) + dot_nt(la, gates[1, :, lanes(h)])
        )
        dgates[0, :, lanes(h)] = dot_tn(cl, lx).astype(bf16)
        dgates[1, :, lanes(h)] = dot_tn(cl, la).astype(bf16)

        def group(g, taps):
            gc = gconv[token_rows(g), lanes(h)]
            bx = low_s[0, token_rows(g), lanes(h)].astype(f32)
            ahead = edge_in[g, :, lanes(h)].astype(f32)[8:]
            rows = lax.broadcasted_iota(jnp.int32, gc.shape, 0)
            low_rows = lax.broadcasted_iota(jnp.int32, (8, 256), 0)
            out = rec_ref[pl.ds(0, 1), lanes(h)] * gc
            over = jnp.zeros((8, 256), f32)
            new = [taps[0] + jnp.sum(bx * gc, axis=0, keepdims=True)]
            for k in (1, 2, 3):
                masked = flags(g, 1 + k) * gc
                new.append(taps[k] + jnp.sum(shifted(bx, ahead, k) * masked, axis=0, keepdims=True))
                scaled = rec_ref[pl.ds(k, 1), lanes(h)] * masked
                out = out + jnp.where(rows < 128 - k, pltpu.roll(scaled, 128 - k, 0), 0.0)
                over = over + jnp.where(low_rows >= 8 - k, pltpu.roll(scaled[:8], 8 - k, 0), 0.0)
            new.append(taps[4] + jnp.sum(gc, axis=0, keepdims=True))
            gdir[token_rows(g), lanes(h)] = out
            edge[g, :, lanes(h)] = over
            return tuple(new)

        taps = lax.fori_loop(0, 4, group, tuple(jnp.zeros((1, 256), f32) for _ in range(5)))
        for k in range(5):
            small_out[pl.ds(k, 1), lanes(h)] = taps[k]

    many(nh, conv_back)
    en = wire.send(edge, edge_out, context=place.chain(-1))
    pump(big, 1)
    back = (dot_tn(selector(0), dgates[0]) + dot_tn(selector(1), dgates[1])).astype(bf16)
    gtile[...] = jnp.zeros_like(gtile)
    for cc in range(16):
        for b in range(4):
            gtile[pl.ds(160 * cc + 32 * b, 32), :] = back[32 * cc : 32 * cc + 32, 128 * b : 128 * b + 128]
    loc.start(gtile, grec_out.at[:, pl.ds(0, 128)])
    wire.recv(en, edge_out)

    def narrow(h):
        for g in range(4):
            v = gdir[pl.ds(128 * g, 128), lanes(h)]
            tail = v[120:] + edge_out[g, :, lanes(h)]
            gpx[pl.ds(128 * g, 128), lanes(h)] = jnp.concatenate([v[:120], tail], axis=0).astype(bf16)

    many(nh, narrow)

    def norm_grad(heads):
        def block(n):
            r = pl.ds(pl.multiple_of(n * 512, 512), 512)
            v = dot_nt(gpx[:, pl.ds(0, 256 * heads)], w1[r, pl.ds(128, 256 * heads)])
            v = v + dot_nt(gpy[:, pl.ds(0, 256 * heads)], w1[r, pl.ds(128 + 256 * heads, 256 * heads)])
            part[:, :, :, r] = v.astype(bf16).reshape(4, 2, 64, 512)

        many(5, block)

    pl.when(x == 0)(lambda: norm_grad(2))
    pl.when(x != 0)(lambda: norm_grad(1))
    gain_acc[...] = jnp.zeros_like(gain_acc)

    def finish(r, total):
        gx, gain = norm_back(total, tok_ref[r, :], gain_ref[...])
        tgrad_out[t, r, :] = gres[r, :] + gx
        gain_acc[...] += gain

    last = rows_scatter_steps(wire, part, crecv, sums, r1, r2, finish)
    pump(last, 1)

    def x_tile(h):
        send_tile(nit, gpx[:, lanes(h)], h, 0, False)

    many(nh, x_tile)
    for _ in last:
        pump(big, 1)
    small_out[pl.ds(0, 1), pl.ds(512, DIM)] = jnp.sum(gain_acc[...], axis=0, keepdims=True)
    tn = wire.send(tgrad_out.at[t], tgrad_out.at[t], tensor=1 - t)
    drain(big)
    wire.recv(tn, tgrad_out.at[1 - t])
    for slot in (0, 1):
        pltpu.make_async_copy(gt.at[slot], grec_out.at[:, column(0)], gs.at[slot]).wait()
    wire.finish()
    loc.finish()


def backward_call(g, w, act, gm, lx, la, hid, py, low, cg, tok, gres, gain, rec):
    S = jax.ShapeDtypeStruct
    R = (64, DIM)
    F = (512, 512)
    width = COLS - SPLIT
    return pl.pallas_call(
        backward_kernel,
        name="recurrent_backward",
        input_output_aliases={0: 1},
        out_shape=(S((4, 48, width), bf16), S((DIM, COLS), bf16), S((2,) + R, f32), S((8, 512 + DIM), f32)),
        in_specs=[ANY, ANY, ANY] + [VM] * 11,
        out_specs=[VM, ANY, VM, VM],
        scratch_shapes=scatter_scratch(width) + [
            vm((DIM, SPLIT), bf16), vm((4, 2) + R, bf16), vm((DIM, 512), bf16), vm((4, 2, 64, 128), bf16),
            vm(F, f32), vm(F, bf16), vm(F, f32), vm(F, f32), vm((16, 8, 512), f32), vm((8, 512), f32), vm((8, 512), f32),
            vm((2,) + F, bf16), vm((4, 8, 512), f32), vm((4, 16, 512), bf16), vm((4, 8, 512), f32), vm(F, bf16),
            vm((2, 256, 512), bf16), vm(F, bf16), vm((2, 256, 512), bf16),
            vm((2, DIM, 256), bf16), vm((DIM, 128), bf16), vm((8, DIM), f32),
            vm((4,) + R, bf16), vm((3,) + R, bf16), vm((2,) + R, bf16), vm((2,) + R, bf16),
            pltpu.SemaphoreType.DMA((110,)), pltpu.SemaphoreType.DMA((110,)), pltpu.SemaphoreType.DMA((40,)),
            pltpu.SemaphoreType.DMA((2,)),
        ],
        compiler_params=pltpu.CompilerParams(collective_id=2, has_side_effects=True, vmem_limit_bytes=62 << 20),
    )(g, w, act, gm, lx, la, hid, py, low, cg, tok, gres, gain, rec)


def last_kernel(
    g_ref, small_ref, gain_ref, out_ref, recur_out, gains_out,
    b0, b1, b2, b3, b4, b5, b6, b7, small, zin, yin, xin, corein, ss, rs, ls,
):
    place = Place()
    x, c, t = place.x, place.c, place.t
    greet(place, xs=(1, 2, 3), ctx=((1, 0), (2, 0), (3, 0), (0, 1), (0, 2), (0, 3)), core=True)
    wire, loc = Wire(place, ss, rs), Local(ls)
    big = scatter_steps(wire, loc, g_ref, 0, (b0, b1, b2, b3, b4, b5, b6, b7), out_ref, True)
    small[0] = small_ref[...]
    small[0, pl.ds(1, 1), pl.ds(512, DIM)] = gain_ref[pl.ds(0, 1), :]
    ns = [wire.send(small.at[0], zin.at[d - 1], context=place.ctx(0, d)) for d in (1, 2, 3)]
    pump(big, 1)
    for d, n in zip((1, 2, 3), ns):
        wire.recv(n, zin.at[d - 1])
    small[1] = small[0] + zin[0] + zin[1] + zin[2]
    ns = [wire.send(small.at[1], yin.at[d - 1], context=place.ctx(d, 0)) for d in (1, 2, 3)]
    pump(big, 1)
    for d, n in zip((1, 2, 3), ns):
        wire.recv(n, yin.at[d - 1])
    small[2] = small[1] + yin[0] + yin[1] + yin[2]
    ns = [wire.send(small.at[2], xin.at[x], fsdp=place.xs(d)) for d in (1, 2, 3)]
    xin[x] = small[2]
    pump(big, 1)
    for d, n in zip((1, 2, 3), ns):
        wire.recv(n, xin.at[place.xs(-d)])
    for k in range(4):
        recur_out[k] = xin[k, :, pl.ds(0, 512)]
    sums = xin[0] + xin[1] + xin[2] + xin[3]
    small[3] = sums
    n = wire.send(small.at[3], corein, tensor=1 - t)
    pump(big, 1)
    wire.recv(n, corein)
    gains_out[...] = small[3, :, pl.ds(512, DIM)] + corein[:, pl.ds(512, DIM)]
    drain(big)
    wire.finish()
    loc.finish()


def last_call(g, small, gain):
    S = jax.ShapeDtypeStruct
    V = (8, 512 + DIM)
    return pl.pallas_call(
        last_kernel,
        name="recurrent_gradients",
        out_shape=(S((4, 48, SPLIT), bf16), S((4, 8, 512), f32), S((8, DIM), f32)),
        in_specs=[ANY, VM, VM],
        out_specs=[VM, VM, VM],
        scratch_shapes=scatter_scratch(SPLIT) + [
            vm((4,) + V, f32), vm((3,) + V, f32), vm((3,) + V, f32), vm((4,) + V, f32), vm(V, f32),
            pltpu.SemaphoreType.DMA((80,)), pltpu.SemaphoreType.DMA((80,)), pltpu.SemaphoreType.DMA((30,)),
        ],
        compiler_params=pltpu.CompilerParams(collective_id=3, has_side_effects=True, vmem_limit_bytes=48 << 20),
    )(g, small, gain)


def permuted(a):
    return a.reshape(a.shape[:-1] + (4, 16, 40)).swapaxes(-3, -2).reshape(a.shape)


def restored(a):
    return a.reshape(a.shape[:-1] + (16, 4, 40)).swapaxes(-3, -2).reshape(a.shape)


HEAD_START = (0, 2, 3, 4)
HEADS_OF = (2, 1, 1, 1)
FF_START = (0, 768, 1792, 2816)
FF_OF = (768, 1024, 1024, 1024)


def pack_weights(input_proj, gate_blocks, output_proj, inner_proj, down_proj):
    inp, out = input_proj.astype(bf16), output_proj.astype(bf16).T
    inner, down, blocks = inner_proj.astype(bf16), down_proj.astype(bf16).T, gate_blocks.astype(bf16)
    packs = []
    for k in range(4):
        hs = slice(HEAD_START[k] * 256, (HEAD_START[k] + HEADS_OF[k]) * 256)
        fs = slice(FF_START[k], FF_START[k] + FF_OF[k])
        main = jnp.concatenate(
            [jnp.zeros((40, 128), bf16), inp[0][:, hs], inp[1][:, hs], out[:, hs], inner[0][:, fs], inner[1][:, fs], down[:, fs]],
            axis=1,
        )
        g = blocks[:, HEAD_START[k] : HEAD_START[k] + HEADS_OF[k]].swapaxes(1, 2).reshape(8, HEADS_OF[k] * 256)
        packs.append(jnp.concatenate([main, jnp.pad(g, ((0, 0), (0, COLS - g.shape[1])))], axis=0))
    return jnp.stack(packs)


def token_flags(seq_lengths, rows, taps, count):
    margin = taps - 1
    places = lax.axis_index("context") * rows + jnp.arange(-margin, rows, dtype=jnp.int32)
    ends = jnp.cumsum(seq_lengths[0])
    segment = jnp.sum((places[:, None] >= ends[None, :]).astype(jnp.int32), axis=1)
    starts = jnp.concatenate([jnp.zeros((1,), jnp.int32), ends])
    own = places[margin:]
    keeping = 1.0 - jnp.any(own[:, None] == starts[None, :], axis=1).astype(f32)
    valid = (segment[margin:] < count).astype(f32)
    out = [valid, keeping]
    for offset in range(1, taps):
        lower = margin - offset
        same = (segment[lower : lower + rows] == segment[margin:]) & (places[lower : lower + rows] >= 0)
        out.append(same.astype(f32))
    return jnp.stack(out, axis=1)


def prepare(tokens, cotangent, seq_lengths, norm_gains, recur_params, weights):
    x, t = lax.axis_index("fsdp"), lax.axis_index("tensor")
    flags = lax.dynamic_slice_in_dim(token_flags(seq_lengths, tokens.shape[0], 4, 3), t * 64, 64, 0)
    tok = permuted(lax.dynamic_slice_in_dim(tokens, t * 64, 64, 0)).astype(f32)
    cot = permuted(lax.dynamic_slice_in_dim(cotangent, t * 64, 64, 0))
    gains = permuted(norm_gains)
    inv = lax.rsqrt(jnp.mean(tok * tok, axis=-1, keepdims=True) + norm_eps)
    normed = (tok * inv * gains[0]).astype(bf16)
    low = (cot.astype(f32) * flags[:, :1]).astype(bf16)
    a = jnp.concatenate([normed, jnp.pad(flags.astype(bf16), ((0, 0), (0, 123))), low], axis=1)
    start = jnp.where(x == 0, 0, x + 1) * 256
    rec = lax.dynamic_slice_in_dim(jnp.pad(recur_params, ((0, 0), (0, 256))), start, 512, 1)
    rec = jnp.concatenate([rec[:7], jax.nn.softplus(-rec[7:]), jax.nn.sigmoid(-rec[7:]), jnp.zeros((7, 512), f32)], axis=0)
    return pack_weights(*weights), a, tok, gains, rec


def adam_update(weight, moment, square, gradient, rate, shrink):
    moment = beta_one * moment + (1.0 - beta_one) * gradient
    square = beta_two * square + (1.0 - beta_two) * gradient * gradient
    normed = moment / (1.0 - beta_one**STEP) / (jnp.sqrt(square / (1.0 - beta_two**STEP)) + adam_eps)
    return (weight - rate * (normed + shrink * weight), moment, square)


def unpack_gradients(rec, ffn):
    both = jnp.concatenate([rec, ffn], axis=2)
    found = {k: [] for k in ("x", "y", "o", "g", "u", "d", "b")}
    for k in range(4):
        at = 128
        for name, width in [(n, 256 * HEADS_OF[k]) for n in "xyo"] + [(n, FF_OF[k]) for n in "gud"]:
            found[name].append(both[k, :40, at : at + width])
            at += width
        b = both[k, 40:, : 256 * HEADS_OF[k]].reshape(2, 4, HEADS_OF[k], 256).swapaxes(1, 2)
        found["b"].append(b)
    cat = lambda n: jnp.concatenate(found[n], axis=1).astype(f32)
    return (
        jnp.stack([cat("x"), cat("y")]), cat("b"), cat("o").T, jnp.stack([cat("g"), cat("u")]), cat("d").T,
    )


def on_device(
    tokens, cotangent, seq_lengths,
    norm_gains, gains_moment, gains_square, recur_params, recur_moment, recur_square,
    input_proj, input_moment, input_square, gate_blocks, blocks_moment, blocks_square,
    output_proj, output_moment, output_square, inner_proj, inner_moment, inner_square,
    down_proj, down_moment, down_square,
):
    p, a, tok, gains, rec = prepare(
        tokens, cotangent, seq_lengths, norm_gains, recur_params,
        (input_proj, gate_blocks, output_proj, inner_proj, down_proj),
    )
    w, act, lx, la, hid, py, low, cg, nm, resid = forward_call(p, a, tok, gains[1:], rec)
    g, mixed, gm, gres, gain_two = ffn_call(w, act, nm, resid, gains[1:])
    ffn, grec, tgrad, small = backward_call(g, w, act, gm, lx, la, hid, py, low, cg, tok, gres, gains[:1], rec)
    recs, recur, gsum = last_call(grec, small, gain_two)
    input_grad, blocks_grad, output_grad, inner_grad, down_grad = unpack_gradients(recs, ffn)
    recur_grad = jnp.concatenate([recur[k, :, : 256 * HEADS_OF[k]] for k in range(4)], axis=1)
    gains_grad = restored(gsum[:2])
    out = [restored(mixed.reshape(128, DIM)), restored(tgrad.reshape(128, DIM))]
    for w_, m_, s_, q_, rate, shrink in (
        (norm_gains, gains_moment, gains_square, gains_grad, vector_rate, 0.0),
        (recur_params, recur_moment, recur_square, recur_grad, vector_rate, 0.0),
        (input_proj, input_moment, input_square, input_grad, matrix_rate, weight_decay),
        (gate_blocks, blocks_moment, blocks_square, blocks_grad, matrix_rate, weight_decay),
        (output_proj, output_moment, output_square, output_grad, matrix_rate, weight_decay),
        (inner_proj, inner_moment, inner_square, inner_grad, matrix_rate, weight_decay),
        (down_proj, down_moment, down_square, down_grad, matrix_rate, weight_decay),
    ):
        out.extend(adam_update(w_, m_, s_, q_, rate, shrink))
    return tuple(out)


def solution(mesh):
    row = P(("fsdp", "context"), None)
    wide_spec = P(None, ("fsdp", "context"), "tensor")
    tall = P("tensor", ("fsdp", "context"))
    block = P(None, "tensor", ("fsdp", "context"), None)
    params = (P(),) * 3 + (P(None, "tensor"),) * 3 + (wide_spec,) * 3 + (block,) * 3 + (tall,) * 3 + (wide_spec,) * 3 + (tall,) * 3
    return jax.shard_map(
        on_device, mesh=mesh, in_specs=(row, row, P("fsdp", None)) + params, out_specs=(row, row) + params, check_vma=False
    )
```

```python
import functools

import jax
import jax.numpy as jnp
from jax import lax
from jax.experimental import pallas as pl
from jax.experimental.pallas import tpu as pltpu
from jax.sharding import PartitionSpec as P

STEP = 10

norm_eps = 1e-06
beta_one = 0.9
beta_two = 0.95
adam_eps = 1e-08
weight_decay = 0.1
matrix_rate = 0.06
vector_rate = 1.0
gate_scale = 8.0

bf16, f32 = jnp.bfloat16, jnp.float32
MESH = pl.DeviceIdType.MESH
DIM = 2560
COLS = 3968
FIRST, SPLIT = 640, 1664
TRIPLE = 768
EXT = 2560 + 128
NT = (((1,), (1,)), ((), ()))
TN = (((0,), (0,)), ((), ()))


def dot(a, b):
    return jnp.dot(a, b, preferred_element_type=f32)


def dot_nt(a, b):
    return lax.dot_general(a, b, NT, preferred_element_type=f32)


def dot_tn(a, b):
    return lax.dot_general(a, b, TN, preferred_element_type=f32)


def many(n, fn):
    def one(i, carry):
        fn(i)
        return carry

    lax.fori_loop(0, n, one, 0)


class Place:
    def __init__(self):
        self.x = lax.axis_index("fsdp")
        self.c = lax.axis_index("context")
        self.t = lax.axis_index("tensor")
        self.y, self.z = lax.div(self.c, 4), lax.rem(self.c, 4)

    def ctx(self, dy, dz):
        return lax.rem(self.y + dy + 4, 4) * 4 + lax.rem(self.z + dz + 4, 4)

    def xs(self, d):
        return lax.rem(self.x + d + 4, 4)

    def along(self, half, d1, d2):
        return self.ctx(d2, d1) if half == 0 else self.ctx(d1, d2)

    def chain(self, d):
        return lax.rem(self.c + d + 16, 16)


class Wire:
    def __init__(self, place, ss, rs):
        self.place, self.ss, self.rs = place, ss, rs
        self.n, self.sent = 0, []

    def send(self, src, dst, **to):
        n = self.n
        self.n += 1
        copy = pltpu.make_async_remote_copy(
            src_ref=src, dst_ref=dst, send_sem=self.ss.at[n], recv_sem=self.rs.at[n],
            device_id=to, device_id_type=MESH,
        )
        copy.start()
        self.sent.append(copy)
        return n

    def recv(self, n, ref):
        pltpu.make_async_remote_copy(
            src_ref=ref, dst_ref=ref, send_sem=self.ss.at[n], recv_sem=self.rs.at[n],
            device_id={"fsdp": self.place.x}, device_id_type=MESH,
        ).wait_recv()

    def finish(self):
        for copy in self.sent:
            copy.wait_send()


class Local:
    def __init__(self, sems):
        self.sems, self.n, self.open = sems, 0, []

    def start(self, src, dst):
        copy = pltpu.make_async_copy(src, dst, self.sems.at[self.n])
        self.n += 1
        copy.start()
        self.open.append(copy)
        return copy

    def wait(self, copy):
        copy.wait()
        self.open = [other for other in self.open if other is not copy]

    def finish(self):
        for copy in self.open:
            copy.wait()


def greet(place, xs=(), ctx=(), chain=(), core=False):
    bar = pltpu.get_barrier_semaphore()
    n = 0
    for d in xs:
        pl.semaphore_signal(bar, inc=1, device_id={"fsdp": place.xs(d)}, device_id_type=MESH)
        n += 1
    for dy, dz in ctx:
        pl.semaphore_signal(bar, inc=1, device_id={"context": place.ctx(dy, dz)}, device_id_type=MESH)
        n += 1
    for d in chain:
        pl.semaphore_signal(bar, inc=1, device_id={"context": place.chain(d)}, device_id_type=MESH)
        n += 1
    if core:
        pl.semaphore_signal(bar, inc=1, device_id={"tensor": 1 - place.t}, device_id_type=MESH)
        n += 1
    pl.semaphore_wait(bar, n)


def row_half(index, half):
    return pl.ds(pl.multiple_of(index * 160 + 80 * half, 16), 80)


def gather_steps(wire, buf, own, at):
    place = wire.place
    width = own.shape[1]
    mid = width // 256 * 128
    LO, HI, FULL = (0, mid), (mid, width), (0, width)

    def ref(i, h, k):
        return buf.at[row_half(i, h), pl.ds(at + k[0], k[1] - k[0])]

    def mine(h):
        return own.at[pl.ds(80 * h, 80), :]

    def send(h, src, i, k, d1, d2):
        return wire.send(src, ref(i, h, k), context=place.along(h, d1, d2))

    st = {}
    for h in (0, 1):
        st[h, 1, 1] = send(h, mine(h), place.c, FULL, 1, 0)
        st[h, 1, -1] = send(h, mine(h), place.c, FULL, -1, 0)
    for h in (0, 1):
        for d in (1, -1):
            st[h, 0, d] = send(h, mine(h), place.c, FULL, 0, d)
    yield
    part = {1: LO, -1: HI}
    for d in (1, -1):
        for h in (0, 1):
            i = place.along(h, -d, 0)
            wire.recv(st[h, 1, d], ref(i, h, FULL))
            st[h, 1, 2 * d] = send(h, ref(i, h, part[d]), i, part[d], d, 0)
            for e in (1, -1):
                st[h, -d + 10, e] = send(h, ref(i, h, FULL), i, FULL, 0, e)
            yield

    def second(h, k, key):
        for d in (1, -1):
            i = place.along(h, k, -d)
            wire.recv(st[h, key, d], ref(i, h, FULL))
            st[h, key, 2 * d] = send(h, ref(i, h, part[d]), i, part[d], 0, d)

    for h in (0, 1):
        second(h, 0, 0)
        yield
    for h in (0, 1):
        i = place.along(h, 2, 0)
        wire.recv(st[h, 1, 2], ref(i, h, LO))
        wire.recv(st[h, 1, -2], ref(i, h, HI))
        for e in (1, -1):
            st[h, 12, e] = send(h, ref(i, h, FULL), i, FULL, 0, e)
        yield
    for k, key in ((-1, 9), (1, 11), (2, 12)):
        for h in (0, 1):
            second(h, k, key)
            yield
    for k, key in ((0, 0), (-1, 9), (1, 11), (2, 12)):
        for h in (0, 1):
            i = place.along(h, k, 2)
            for d in (1, -1):
                wire.recv(st[h, key, 2 * d], ref(i, h, part[d]))
        yield


def rows_gather_steps(wire, src, out, loc):
    place = wire.place
    x, t = place.x, place.t
    width = src.shape[1]
    h = width // 256 * 128
    LO, HI = pl.ds(0, h), pl.ds(h, width - h)
    xp, xm, xo = place.xs(1), place.xs(-1), place.xs(2)
    a = wire.send(src, out.at[x, t], fsdp=xp)
    b = wire.send(src, out.at[x, t], fsdp=xm)
    cores = [(x, wire.send(src, out.at[x, t], tensor=1 - t))]
    own = loc.start(src, out.at[x, t])
    yield
    wire.recv(a, out.at[xm, t])
    e = wire.send(out.at[xm, t, :, LO], out.at[xm, t, :, LO], fsdp=xp)
    cores.append((xm, wire.send(out.at[xm, t], out.at[xm, t], tensor=1 - t)))
    wire.recv(b, out.at[xp, t])
    f = wire.send(out.at[xp, t, :, HI], out.at[xp, t, :, HI], fsdp=xm)
    cores.append((xp, wire.send(out.at[xp, t], out.at[xp, t], tensor=1 - t)))
    yield
    wire.recv(e, out.at[xo, t, :, LO])
    wire.recv(f, out.at[xo, t, :, HI])
    cores.append((xo, wire.send(out.at[xo, t], out.at[xo, t], tensor=1 - t)))
    yield
    for k, n in cores:
        wire.recv(n, out.at[k, 1 - t])
    loc.wait(own)
    yield


class RowsScatter:
    def __init__(self, wire, part, crecv, sums, r1, r2, piece=512, own=None):
        self.wire, self.part, self.crecv, self.sums, self.r1, self.r2 = wire, part, crecv, sums, r1, r2
        self.piece, self.n = piece, {}
        place = wire.place
        self.x, self.t = place.x, place.t
        self.own = own if own is not None else part.at[:, self.t]
        self.xp, self.xm, self.xo = place.xs(1), place.xs(-1), place.xs(2)

    def cut(self, i):
        at, half = i * self.piece, self.piece // 2
        return pl.ds(at, self.piece), pl.ds(at, half), pl.ds(at + half, half)

    def rows(self, fn):
        many(self.sums.shape[1] // 16, lambda i: fn(pl.ds(pl.multiple_of(i * 16, 16), 16)))

    def put(self, n, k, cols, extra=None):
        def fn(r):
            v = self.own[k, r, cols].astype(f32) + self.crecv[k, r, cols].astype(f32)
            if extra is not None:
                v = v + self.r1[extra, r, cols].astype(f32)
            self.sums[n, r, cols] = v.astype(bf16)

        self.rows(fn)

    def a(self, i):
        cols = self.cut(i)[0]
        self.n["a", i] = self.wire.send(self.part.at[:, 1 - self.t, :, cols], self.crecv.at[:, :, cols], tensor=1 - self.t)

    def b(self, i):
        cols, lo, hi = self.cut(i)
        self.wire.recv(self.n["a", i], self.crecv.at[:, :, cols])
        self.put(0, self.xo, cols)
        self.n["b", i] = self.wire.send(self.sums.at[0, :, lo], self.r1.at[0, :, lo], fsdp=self.xp)
        self.n["c", i] = self.wire.send(self.sums.at[0, :, hi], self.r1.at[1, :, hi], fsdp=self.xm)

    def c(self, i):
        cols, lo, hi = self.cut(i)
        self.wire.recv(self.n["b", i], self.r1.at[0, :, lo])
        self.put(1, self.xp, lo, 0)
        self.put(1, self.xp, hi)
        self.n["d", i] = self.wire.send(self.sums.at[1, :, cols], self.r2.at[0, :, cols], fsdp=self.xp)
        self.wire.recv(self.n["c", i], self.r1.at[1, :, hi])
        self.put(2, self.xm, lo)
        self.put(2, self.xm, hi, 1)
        self.n["e", i] = self.wire.send(self.sums.at[2, :, cols], self.r2.at[1, :, cols], fsdp=self.xm)

    def d(self, i, done):
        cols = self.cut(i)[0]
        self.wire.recv(self.n["d", i], self.r2.at[0, :, cols])
        self.wire.recv(self.n["e", i], self.r2.at[1, :, cols])

        def total(r):
            done(
                cols,
                r,
                self.own[self.x, r, cols].astype(f32)
                + self.crecv[self.x, r, cols].astype(f32)
                + self.r2[0, r, cols].astype(f32)
                + self.r2[1, r, cols].astype(f32),
            )

        self.rows(total)

    def steps(self, compute, done):
        count = self.sums.shape[2] // self.piece
        for i in range(count + 3):
            if i < count:
                compute(i)
                self.a(i)
            if 0 <= i - 1 < count:
                self.b(i - 1)
            if 0 <= i - 2 < count:
                self.c(i - 2)
            if 0 <= i - 3 < count:
                self.d(i - 3, done)
            yield


def drain(steps):
    for _ in steps:
        pass


def pump(steps, n=1):
    for _ in range(n):
        next(steps, None)


def gelu(v):
    return 0.5 * v * (1.0 + jnp.tanh(0.7978845608028654 * (v + 0.044715 * v * v * v)))


def gelu_and_slope(v):
    u = jnp.tanh(0.7978845608028654 * (v + 0.044715 * v * v * v))
    slope = 0.5 * (1.0 + u) + 0.5 * v * (1.0 - u * u) * (
        0.7978845608028654 * (1.0 + 3 * 0.044715 * v * v)
    )
    return 0.5 * v * (1.0 + u), slope


def one_less_exp(v):
    series = 1.0 + v * (1.0 / 7.0)
    for k in (6.0, 5.0, 4.0, 3.0, 2.0):
        series = 1.0 + v * (1.0 / k) * series
    return jnp.where(v > -0.35, -v * series, 1.0 - jnp.exp(v))


def sigmoid(v):
    return 1.0 / (1.0 + jnp.exp(-v))


def shifted(block, edge, k):
    moved = pltpu.roll(block, k, 0)
    first = jnp.where(
        lax.broadcasted_iota(jnp.int32, edge.shape, 0) < k, pltpu.roll(edge, k, 0), moved[:8]
    )
    return jnp.concatenate([first, moved[8:]], axis=0)


def scan_down(a, b):
    rows = lax.broadcasted_iota(jnp.int32, a.shape, 0)
    s = 1
    while s < a.shape[0]:
        earlier = rows >= s
        pa = jnp.where(earlier, pltpu.roll(a, s, 0), 1.0)
        pb = jnp.where(earlier, pltpu.roll(b, s, 0), 0.0)
        b = b + a * pb
        a = a * pa
        s *= 2
    return a, b


def scan_up(a, b):
    rows = lax.broadcasted_iota(jnp.int32, a.shape, 0)
    n = a.shape[0]
    s = 1
    while s < n:
        later = rows < n - s
        pa = jnp.where(later, pltpu.roll(a, n - s, 0), 1.0)
        pb = jnp.where(later, pltpu.roll(b, n - s, 0), 0.0)
        b = b + a * pb
        a = a * pa
        s *= 2
    return a, b


def selector(g):
    i = lax.broadcasted_iota(jnp.int32, (256, 512), 0)
    j = lax.broadcasted_iota(jnp.int32, (256, 512), 1)
    xx, cc, r = i // 64, (i // 4) % 16, i % 4
    return (j == cc * 32 + xx * 8 + g * 4 + r).astype(f32).astype(bf16)


def gate_matrix(packed, g):
    return dot(selector(g), packed).astype(bf16)


def column(tile, tiles=1):
    return pl.ds(pl.multiple_of(128 + 256 * tile, 128), 256 * tiles)


def triple(j):
    return column(jnp.where(j == 3, 3, 6 + 3 * j), 3)


def head_count(x):
    return jnp.where(x == 0, 2, 1).astype(jnp.int32)


def lanes(h):
    return pl.ds(pl.multiple_of(h * 256, 256), 256)


def token_rows(g):
    return pl.ds(pl.multiple_of(g * 128, 128), 128)


def recur_terms(lx, la, cl, sp, keep):
    sx, sa = sigmoid(lx), sigmoid(la)
    log_decay = (-gate_scale) * sa * sp
    grown = one_less_exp(2.0 * log_decay)
    root = jnp.sqrt(grown)
    factor = root * keep + 1.0 - keep
    return sx, sa, log_decay, root, factor


def forward_kernel(
    p_ref, n_ref, cot_ref, tok_ref, gain_ref, rec_ref,
    w_out, act_out, gl_out, lx_out, la_out, hid_out, py_out, low_out, cg_out, nm_out, resid_out,
    xbuf, wide, chunk0, chunk1, chunk2, w1, act, lx_s, la_s, hid_s, py_s, low_s, halo, cum_s, cg, cin,
    part, crecv, sums, r1, r2, normed, resid, packed, gates,
    ss, rs, ls,
):
    place = Place()
    x, c, t = place.x, place.c, place.t
    greet(place, xs=(1, 2, 3), ctx=((1, 0), (2, 0), (3, 0), (0, 1), (0, 2), (0, 3)), chain=(1, -1), core=True)
    wire, loc = Wire(place, ss, rs), Local(ls)
    nh = head_count(x)

    stages = ((0, FIRST, chunk0), (FIRST, SPLIT, chunk1), (SPLIT, COLS, chunk2))
    came = {}

    def spread(s):
        c0, c1, _ = stages[s]
        cs = pl.ds(c0, c1 - c0)
        for d in (2, 1, 3):
            came[s, d] = wire.send(p_ref.at[place.xs(d), :, cs], xbuf.at[x, :, cs], fsdp=place.xs(d))

    def arrange(s):
        c0, c1, chunk = stages[s]
        cs = pl.ds(c0, c1 - c0)
        for d in (1, 3, 2):
            wire.recv(came[s, d], xbuf.at[place.xs(-d), :, cs])

        for k in range(4):
            def take(src, k=k):
                v = src[k, :, cs].astype(f32)
                wide[pl.ds(40 * k, 40), cs] = v[:40]

            pl.when(x == k)(functools.partial(take, p_ref))
            pl.when(x != k)(functools.partial(take, xbuf))
        if s == 0:
            for k in range(4):
                def gate(src, k=k):
                    v = src[k, :, pl.ds(0, 512)].astype(f32)
                    for b in range(4):
                        wide[pl.ds(32 * b + 8 * k, 8), pl.ds(0, 128)] = v[40:, 128 * b : 128 * b + 128]

                pl.when(x == k)(functools.partial(gate, p_ref))
                pl.when(x != k)(functools.partial(gate, xbuf))
        chunk[...] = wide[:, cs].astype(bf16)

    mine = pl.ds(pl.multiple_of(c * 160, 16), 160)
    spread(0)
    spread(1)
    arrange(0)
    rows = rows_gather_steps(wire, n_ref, act, loc)
    pump(rows)
    own0 = loc.start(chunk0, w1.at[mine, pl.ds(0, FIRST)])
    one = gather_steps(wire, w1, chunk0, 0)
    pump(one, 1)
    arrange(1)
    own1 = loc.start(chunk1, w1.at[mine, pl.ds(FIRST, SPLIT - FIRST)])
    two = gather_steps(wire, w1, chunk1, FIRST)
    pump(two, 1)
    spread(2)
    pump(one, 4)
    pump(rows)
    pump(one, 4)
    pump(two, 4)
    pump(rows)
    pump(one, 6)
    pump(two, 2)
    pump(rows)
    drain(one)
    arrange(2)
    loc.start(chunk2, w_out.at[mine, pl.ds(SPLIT, COLS - SPLIT)])
    later = rows_gather_steps(wire, cot_ref, gl_out, loc)
    pump(later)
    pump(two, 4)
    three = gather_steps(wire, w_out, chunk2, SPLIT)
    pump(three, 1)
    pump(two, 4)
    drain(two)
    loc.wait(own0)
    loc.wait(own1)
    drain(rows)
    loc.start(w1, w_out.at[:, pl.ds(0, SPLIT)])
    loc.start(act, act_out)
    two = three

    def project(h):
        ni = act[:, :, :, pl.ds(0, DIM)].reshape(512, DIM)
        low_s[0, :, lanes(h)] = dot(ni, w1[:, column(h)]).astype(bf16)
        py_s[:, lanes(h)] = dot(ni, w1[:, column(nh + h)])

    many(nh, project)
    before = low_s.at[0].reshape(4, 128, 512)
    hn = wire.send(before.at[:, pl.ds(112, 16), :], halo, context=place.chain(1))
    loc.start(py_s, py_out)
    for cc in range(16):
        for b in range(4):
            packed[pl.ds(32 * cc, 32), pl.ds(128 * b, 128)] = w1[pl.ds(160 * cc + 32 * b, 32), pl.ds(0, 128)]
    for g in (0, 1):
        gates[g] = gate_matrix(packed[...], g)
    wire.recv(hn, halo)
    pump(later)

    def flags(g, k):
        v = act[pl.ds(g, 1), :, :, pl.ds(DIM, 128)].reshape(128, 128).astype(f32)
        return v[:, k : k + 1]

    cg[c] = jnp.zeros((2, 8, 512), f32)

    def conv(h):
        def group(g):
            bx = low_s[0, token_rows(g), lanes(h)].astype(f32)
            edge = halo[g, :, lanes(h)].astype(f32)[8:]
            out = rec_ref[pl.ds(4, 1), lanes(h)] + rec_ref[pl.ds(0, 1), lanes(h)] * bx
            for k in (1, 2, 3):
                out = out + rec_ref[pl.ds(k, 1), lanes(h)] * (flags(g, 1 + k) * shifted(bx, edge, k))
            low_s[1, token_rows(g), lanes(h)] = out.astype(bf16)

        many(4, group)
        cl = low_s[1, :, lanes(h)]
        lx_s[:, lanes(h)] = dot(cl, gates[0, :, lanes(h)]) + rec_ref[pl.ds(5, 1), lanes(h)]
        la_s[:, lanes(h)] = dot(cl, gates[1, :, lanes(h)]) + rec_ref[pl.ds(6, 1), lanes(h)]

    many(nh, conv)
    loc.start(lx_s, lx_out)
    loc.start(la_s, la_out)
    pump(later)

    def scan(q):
        cols = pl.ds(pl.multiple_of(q * 128, 128), 128)
        for g in range(4):
            r = pl.ds(128 * g, 128)
            keep = flags(g, 1)
            cl = low_s[1, r, cols].astype(f32)
            sx, sa, log_decay, root, factor = recur_terms(
                lx_s[r, cols], la_s[r, cols], cl, rec_ref[pl.ds(7, 1), cols], keep
            )
            a, b = scan_down(jnp.exp(log_decay) * keep, factor * sx * cl)
            cum_s[r, cols] = a
            hid_s[r, cols] = b
            cg[c, 0, pl.ds(g, 1), cols] = a[127:]
            cg[c, 1, pl.ds(g, 1), cols] = b[127:]

    many(2 * nh, scan)
    ns = [wire.send(cg.at[c], cg.at[c], context=place.ctx(0, d)) for d in (1, 2, 3)]
    for d, n in zip((1, 2, 3), ns):
        wire.recv(n, cg.at[place.ctx(0, -d)])
    line = pl.ds(place.y * 4, 4)
    ns = [wire.send(cg.at[line], cg.at[line], context=place.ctx(d, 0)) for d in (1, 2, 3)]
    pump(two, 1)
    for d, n in zip((1, 2, 3), ns):
        wire.recv(n, cg.at[pl.ds(lax.rem(place.y + 4 - d, 4) * 4, 4)])

    def enter(s, state):
        return cg[s, 0] * state + cg[s, 1]

    cin[...] = lax.fori_loop(0, c, enter, jnp.zeros((8, 512), f32))
    loc.start(cg, cg_out)

    def mix(h):
        for g in range(4):
            r = pl.ds(128 * g, 128)
            hid = hid_s[r, lanes(h)] + cum_s[r, lanes(h)] * cin[pl.ds(g, 1), lanes(h)]
            hid_s[r, lanes(h)] = hid
            low_s[2, r, lanes(h)] = (hid * gelu(py_s[r, lanes(h)])).astype(bf16)

    many(nh, mix)
    loc.start(hid_s, hid_out)
    loc.start(low_s, low_out)
    pump(two, 3)

    drain(later)

    def project_out(n, heads):
        r = pl.ds(512 * n, 512)
        v = dot_nt(low_s[2, :, pl.ds(0, 256 * heads)], w1[r, pl.ds(128 + 512 * heads, 256 * heads)])
        part[:, :, :, r] = v.astype(bf16).reshape(4, 2, 64, 512)

    def project_piece(n):
        pl.when(x == 0)(lambda: project_out(n, 2))
        pl.when(x != 0)(lambda: project_out(n, 1))

    def add_resid(cols, r, total):
        resid[r, cols] = tok_ref[r, cols] + total

    for _ in RowsScatter(wire, part, crecv, sums, r1, r2).steps(project_piece, add_resid):
        pump(two, 1)
    loc.start(resid, resid_out)

    def norm(i):
        r = pl.ds(pl.multiple_of(i * 16, 16), 16)
        v = resid[r, :]
        inv = lax.rsqrt(jnp.mean(v * v, axis=-1, keepdims=True) + norm_eps)
        normed[r, :] = (v * inv * gain_ref[...]).astype(bf16)

    many(4, norm)
    for _ in rows_gather_steps(wire, normed, nm_out, loc):
        pump(two, 1)
    drain(two)
    wire.finish()
    loc.finish()


def vm(shape, dtype):
    return pltpu.VMEM(shape, dtype)


PLANE = ((1, 0), (3, 0), (0, 1), (0, 3))
ANY = pl.BlockSpec(memory_space=pl.ANY)
VM = pl.BlockSpec(memory_space=pltpu.VMEM)


def forward_call(p, n, cot, tok, gain, rec):
    S = jax.ShapeDtypeStruct
    R = (64, DIM)
    F = (512, 512)
    return pl.pallas_call(
        forward_kernel,
        name="recurrent_forward",
        out_shape=(
            S((DIM, COLS), bf16), S((4, 2, 64, EXT), bf16), S((4, 2) + R, bf16),
            S(F, f32), S(F, f32), S(F, f32), S(F, f32),
            S((3,) + F, bf16), S((16, 2, 8, 512), f32), S((4, 2) + R, bf16), S(R, f32),
        ),
        in_specs=[VM] * 6,
        out_specs=[ANY] * 11,
        scratch_shapes=[
            vm((4, 48, COLS), bf16), vm((160, COLS), f32), vm((160, FIRST), bf16), vm((160, SPLIT - FIRST), bf16), vm((160, COLS - SPLIT), bf16),
            vm((DIM, SPLIT), bf16), vm((4, 2, 64, EXT), bf16),
            vm(F, f32), vm(F, f32), vm(F, f32), vm(F, f32),
            vm((3,) + F, bf16), vm((4, 16, 512), bf16), vm(F, f32), vm((16, 2, 8, 512), f32), vm((8, 512), f32),
            vm((4, 2) + R, bf16), vm((4,) + R, bf16), vm((3,) + R, bf16), vm((2,) + R, bf16), vm((2,) + R, bf16),
            vm(R, bf16), vm(R, f32), vm(F, bf16), vm((2, 256, 512), bf16),
            pltpu.SemaphoreType.DMA((200,)), pltpu.SemaphoreType.DMA((200,)), pltpu.SemaphoreType.DMA((20,)),
        ],
        compiler_params=pltpu.CompilerParams(collective_id=0, has_side_effects=True, vmem_limit_bytes=60 << 20),
    )(p, n, cot, tok, gain, rec)


def transpose_rows(src, dst):
    def block(n):
        cols = pl.ds(pl.multiple_of(n * 256, 256), 256)
        dst[cols, :] = src[:, :, :, cols].reshape(512, 256).T

    many(10, block)


def add_sublanes(v):
    return v[:8] + v[8:]


def norm_back(total, value, gain):
    inv = lax.rsqrt(jnp.mean(value * value, axis=-1, keepdims=True) + norm_eps)
    xhat = value * inv
    weighted = total * gain
    inner = jnp.mean(weighted * xhat, axis=-1, keepdims=True)
    return inv * (weighted - xhat * inner), add_sublanes(total * xhat)


def ffn_kernel(
    w_ref, gl_ref, nm, resid, gain_ref,
    g_out, ahead_out, gm_out, gres_out, gain_out, first_out, second_out,
    gl, nmt, glt, wt, gfirst, pre, lowi, lowg, parts, crecv, sums, r1, r2, normed, own_low, gsum,
    a2, a3, a4, a5, a6, a7, d2, d3, d4, d5, d6, d7,
    ss, rs, ls, ws, gs,
):
    place = Place()
    x, t = place.x, place.t
    wire, loc = Wire(place, ss, rs), Local(ls)
    nf = 5 - head_count(x)

    def load(j):
        return pltpu.make_async_copy(w_ref.at[:, triple(j)], wt.at[j], ws.at[j])

    def store(j):
        return pltpu.make_async_copy(wt.at[j], g_out.at[:, triple(j)], gs.at[j])

    glc = loc.start(gl_ref, gl)
    for j in range(3):
        load(j).start()
    pl.when(x != 0)(lambda: load(3).start())
    olc = loc.start(gl_ref.at[x, t], own_low)
    greet(place, xs=(1, -1), ctx=PLANE, core=True)
    transpose_rows(nm, nmt)
    loc.wait(glc)
    loc.wait(olc)
    transpose_rows(gl, glt)

    def tile(j):
        load(j).wait()
        pre[:, pl.ds(0, 512)] = dot(nm[...].reshape(512, DIM), wt[j, :, pl.ds(0, 512)])
        pre[:, pl.ds(512, 256)] = dot(gl[...].reshape(512, DIM), wt[j, :, pl.ds(512, 256)])

        def point(i):
            r = pl.ds(pl.multiple_of(i * 32, 32), 32)
            gated, slope = gelu_and_slope(pre[r, pl.ds(0, 256)])
            up, gi = pre[r, pl.ds(256, 256)], pre[r, pl.ds(512, 256)]
            lowi[j, r, :] = (gated * up).astype(bf16)
            lowg[j, r, pl.ds(0, 256)] = (gi * up * slope).astype(bf16)
            lowg[j, r, pl.ds(256, 256)] = (gi * gated).astype(bf16)

        many(16, point)

    def gradient(j, dst):
        def block(n):
            r = pl.ds(pl.multiple_of(n * 512, 512), 512)
            dst[r, pl.ds(0, 512)] = dot(nmt[r, :], lowg[j]).astype(bf16)
            dst[r, pl.ds(512, 256)] = dot(glt[r, :], lowi[j]).astype(bf16)

        many(5, block)

    tile(0)
    gradient(0, gfirst)
    first = scatter_steps(wire, loc, gfirst, 0, (None, None, a2, a3, a4, a5, a6, a7), first_out, False, True, False)
    pump(first, 1)
    many(nf - 1, lambda j: tile(j + 1))

    def contract(dst, low, cols, n):
        r = pl.ds(512 * n, 512)

        def total(count):
            v = dot_nt(low[0], wt[0, r, cols])
            for j in range(1, count):
                v = v + dot_nt(low[j], wt[j, r, cols])
            dst[:, :, :, r] = v.astype(bf16).reshape(4, 2, 64, 512)

        pl.when(x == 0)(lambda: total(3))
        pl.when(x != 0)(lambda: total(4))

    def keep_sum(cols, r, total):
        gsum[r, cols] = total

    back = RowsScatter(wire, parts, crecv, sums, r1, r2).steps(
        lambda n: contract(parts, lowg, pl.ds(0, 512), n), keep_sum
    )
    pump(first, 4)
    pump(back, 5)
    for n in range(5):
        contract(gl, lowi, pl.ds(512, 256), n)
        if n % 2 == 1:
            pump(back, 1)
    loc.start(gl, ahead_out)
    pump(first, 4)
    gradient(1, wt.at[1])
    second = scatter_steps(wire, loc, wt.at[1], 0, (None, None, d2, d3, d4, d5, d6, d7), second_out, False, True, False)
    pump(second, 1)
    gradient(2, wt.at[2])
    store(2).start()
    drain(back)
    gain_out[...] = jnp.zeros_like(gain_out)

    def resid_back(i):
        r = pl.ds(pl.multiple_of(i * 16, 16), 16)
        gx, gain = norm_back(gsum[r, :], resid[r, :], gain_ref[...])
        gr = own_low[r, :].astype(f32) + gx
        gres_out[r, :] = gr
        normed[r, :] = gr.astype(bf16)
        gain_out[...] += gain

    many(4, resid_back)
    rows = rows_gather_steps(wire, normed, gm_out, loc)
    pump(rows, 1)
    pump(first, 1)

    @pl.when(x != 0)
    def _():
        gradient(3, wt.at[3])
        store(3).start()

    pump(rows, 1)
    pump(second, 4)
    pump(rows, 1)
    pump(first, 1)
    pump(second, 2)
    drain(rows)
    pump(second, 2)
    drain(first)
    drain(second)
    store(2).wait()
    pl.when(x != 0)(lambda: store(3).wait())
    wire.finish()
    loc.finish()


def ffn_call(w, gl, nm, resid, gain):
    S = jax.ShapeDtypeStruct
    R = (64, DIM)
    slices = scatter_scratch(TRIPLE)[2:]
    return pl.pallas_call(
        ffn_kernel,
        name="feed_forward",
        out_shape=(
            S((DIM, COLS), bf16), S((4, 2) + R, bf16), S((4, 2) + R, bf16), S(R, f32), S((8, DIM), f32),
            S((4, 48, TRIPLE), bf16), S((4, 48, TRIPLE), bf16),
        ),
        in_specs=[ANY, ANY, VM, VM, VM],
        out_specs=[ANY, ANY, ANY, VM, VM, ANY, ANY],
        scratch_shapes=[
            vm((4, 2) + R, bf16), vm((DIM, 512), bf16), vm((DIM, 512), bf16), vm((4, DIM, TRIPLE), bf16), vm((DIM, TRIPLE), bf16),
            vm((512, TRIPLE), f32), vm((4, 512, 256), bf16), vm((4, 512, 512), bf16),
            vm((4, 2) + R, bf16), vm((4,) + R, bf16), vm((3,) + R, bf16), vm((2,) + R, bf16), vm((2,) + R, bf16),
            vm(R, bf16), vm(R, bf16), vm(R, f32),
        ] + slices + slices + [
            pltpu.SemaphoreType.DMA((170,)), pltpu.SemaphoreType.DMA((170,)), pltpu.SemaphoreType.DMA((12,)),
            pltpu.SemaphoreType.DMA((4,)), pltpu.SemaphoreType.DMA((4,)),
        ],
        compiler_params=pltpu.CompilerParams(collective_id=1, has_side_effects=True, vmem_limit_bytes=60 << 20),
    )(w, gl, nm, resid, gain)


def scatter_steps(wire, loc, g_ref, at, bufs, out_ref, gates, resident=False, spread=True):
    gvn, gvo, r1, r2, r3, r4, wide, obuf = bufs
    place = wire.place
    x, c = place.x, place.c
    width = wide.shape[1]
    mid = width // 256 * 128
    LO, HI, FULL = (0, mid), (mid, width), (0, width)
    zero = {1: LO, -1: HI}
    other = {1: HI, -1: LO}

    def gref(h, d1, d2, k):
        return g_ref.at[row_half(place.along(h, d1, d2), h), pl.ds(at + k[0], k[1] - k[0])]

    def cut(k):
        return pl.ds(k[0], k[1] - k[0])

    def short(k):
        return pl.ds(0, k[1] - k[0])

    side = {1: 0, -1: 1}
    order2 = (2, 1, 3, 0)
    st, loads = {}, {}
    for d2 in order2:
        for h in (0, 1):
            for d in (1, -1):
                st[h, 1, d, d2] = wire.send(
                    gref(h, 2, d2, zero[d]), r1.at[h, side[d], d2, :, short(zero[d])], context=place.along(h, d, 0)
                )

    def near(h, d, d2):
        if resident:
            return gref(h, d, d2, zero[d])
        return gvn.at[h, side[d], d2, :, short(zero[d])]

    def mine_at(h, d2, k):
        if resident:
            return gref(h, 0, d2, k)
        return gvo.at[h, d2, :, cut(k)]

    if not resident:
        for d2 in order2:
            for h in (0, 1):
                for d in (1, -1):
                    loads[h, d, d2] = loc.start(gref(h, d, d2, zero[d]), near(h, d, d2))
        for d2 in order2:
            for h in (0, 1):
                loads[h, 0, d2] = loc.start(gref(h, 0, d2, FULL), mine_at(h, d2, FULL))
    for d2 in order2:
        for h in (0, 1):
            for d in (1, -1):
                st[h, 2, d, d2] = wire.send(
                    gref(h, d, d2, other[d]), r2.at[h, side[d], d2, :, cut(other[d])], context=place.along(h, d, 0)
                )
    yield

    def add(dst, srcs):
        def one(i):
            r = pl.ds(pl.multiple_of(i * 16, 16), 16)
            v = srcs[0][r, :].astype(f32)
            for s in srcs[1:]:
                v = v + s[r, :].astype(f32)
            dst[r, :] = v.astype(dst.dtype)

        many(5, one)

    for d2 in order2:
        for h in (0, 1):
            for d in (1, -1):
                k = zero[d]
                mine = near(h, d, d2)
                if not resident:
                    loc.wait(loads[h, d, d2])
                wire.recv(st[h, 1, d, d2], r1.at[h, side[d], d2, :, short(k)])
                add(mine, [mine, r1.at[h, side[d], d2, :, short(k)]])
                st[h, 3, d, d2] = wire.send(mine, r2.at[h, side[d], d2, :, cut(k)], context=place.along(h, d, 0))
        yield
    for d2 in order2:
        for h in (0, 1):
            own = mine_at(h, d2, FULL)
            if not resident:
                loc.wait(loads[h, 0, d2])
            for d in (1, -1):
                wire.recv(st[h, 2, d, d2], r2.at[h, side[d], d2, :, cut(other[d])])
                wire.recv(st[h, 3, d, d2], r2.at[h, side[d], d2, :, cut(zero[d])])
            add(own, [own, r2.at[h, 0, d2], r2.at[h, 1, d2]])
            if d2 == 2:
                for d in (1, -1):
                    st[h, 4, d] = wire.send(
                        mine_at(h, d2, zero[d]), r3.at[h, side[d], :, short(zero[d])], context=place.along(h, 0, d)
                    )
            if d2 in (1, 3):
                d = 1 if d2 == 1 else -1
                st[h, 5, d] = wire.send(
                    mine_at(h, d2, other[d]), r4.at[h, side[d], :, cut(other[d])], context=place.along(h, 0, d)
                )
        yield
    for h in (0, 1):
        for d in (1, -1):
            k = zero[d]
            mine = mine_at(h, d % 4, k)
            got = r3.at[h, side[d], :, short(k)]
            wire.recv(st[h, 4, d], got)
            add(mine, [mine, got])
            st[h, 6, d] = wire.send(mine, r4.at[h, side[d], :, cut(k)], context=place.along(h, 0, d))
    yield
    for h in (0, 1):
        for d in (1, -1):
            wire.recv(st[h, 5, d], r4.at[h, side[d], :, cut(other[d])])
            wire.recv(st[h, 6, d], r4.at[h, side[d], :, cut(zero[d])])
        add(wide.at[pl.ds(80 * h, 80), :], [mine_at(h, 0, FULL), r4.at[h, 0], r4.at[h, 1]])
    for k in range(4):
        obuf[k] = jnp.concatenate([wide[pl.ds(40 * k, 40), :], jnp.zeros((8, width), f32)], axis=0).astype(bf16)
        if gates:
            tail = jnp.concatenate([wide[pl.ds(32 * b + 8 * k, 8), pl.ds(0, 128)] for b in range(4)], axis=1)
            obuf[k, :, pl.ds(0, 512)] = jnp.concatenate([wide[pl.ds(40 * k, 40), pl.ds(0, 512)], tail], axis=0).astype(bf16)
    if not spread:
        own = loc.start(obuf, out_ref)
        yield
        loc.wait(own)
        yield
        return
    ends = [(d, wire.send(obuf.at[place.xs(d)], out_ref.at[x], fsdp=place.xs(d))) for d in (1, 3, 2)]
    own = loc.start(obuf.at[x], out_ref.at[x])
    yield
    for d, n in ends:
        wire.recv(n, out_ref.at[place.xs(-d)])
    loc.wait(own)
    yield


def scatter_scratch(width):
    hi = width - width // 256 * 128
    return [
        vm((2, 2, 4, 80, hi), bf16), vm((2, 4, 80, width), bf16), vm((2, 2, 4, 80, hi), bf16), vm((2, 2, 4, 80, width), bf16),
        vm((2, 2, 80, hi), bf16), vm((2, 2, 80, width), bf16), vm((160, width), f32), vm((4, 48, width), bf16),
    ]


def small_steps(wire, mine, zin, yin, xin, corein):
    place = wire.place
    x = place.x
    ns = [wire.send(mine.at[0], zin.at[d - 1], context=place.ctx(0, d)) for d in (1, 2, 3)]
    yield
    for d, n in zip((1, 2, 3), ns):
        wire.recv(n, zin.at[d - 1])
    mine[1] = mine[0] + zin[0] + zin[1] + zin[2]
    ns = [wire.send(mine.at[1], yin.at[d - 1], context=place.ctx(d, 0)) for d in (1, 2, 3)]
    yield
    for d, n in zip((1, 2, 3), ns):
        wire.recv(n, yin.at[d - 1])
    total = mine[1] + yin[0] + yin[1] + yin[2]
    mine[2] = total
    xin[x] = total
    ns = [wire.send(mine.at[2], xin.at[x], fsdp=place.xs(d)) for d in (1, 2, 3)]
    yield
    for d, n in zip((1, 2, 3), ns):
        wire.recv(n, xin.at[place.xs(-d)])
    mine[3] = xin[0] + xin[1] + xin[2] + xin[3]
    n = wire.send(mine.at[3], corein, tensor=1 - place.t)
    yield
    wire.recv(n, corein)
    yield


def fold(dst, row, at):
    for i in range(20):
        dst[pl.ds(i // 3, 1), pl.ds(at + 128 * (i % 3), 128)] = row[:, 128 * i : 128 * i + 128]


def backward_kernel(
    g_ref, w_ref, act_ref, gm_ref, first_ref, second_ref, ahead_ref,
    lx_s, la_s, hid_s, py_s, low_s, cg, tok_ref, gres, resid, gain_ref, rec_ref, gain_two,
    t0_out, t1_out, t2_out, mid_out, last_out, mixed_out, tgrad_out, recur_out, gains_out,
    a0, a1, a2, a3, a4, a5, a6, a7, b2, b3, b4, b5, b6, b7, c2, c3, c4, c5, c6, c7,
    w1, acts, turned, flag_s, gmx, gpy, bc, bp, bg, cin, cback, glow, edge, edge_in, edge_out, gpx, gates, packed, dgates,
    gain_acc, crecv, sums, r1, r2, own_f, crecv_f, sums_f, r1_f, r2_f,
    small, zin, yin, xin, corein, late, zin_l, yin_l, xin_l, corein_l,
    ss, rs, ls, ws,
):
    part, gconv, gdir = acts, gmx, bc
    place = Place()
    x, c, t = place.x, place.c, place.t
    wire, loc = Wire(place, ss, rs), Local(ls)
    nh = head_count(x)
    rest = pl.ds(FIRST + 256, TRIPLE)
    both = pl.ds(0, FIRST + 256)
    lg = loc.start(gm_ref, acts)
    lw = loc.start(w_ref.at[:, both], w1.at[:, both])
    load_w = pltpu.make_async_copy(w_ref.at[:, rest], w1.at[:, rest], ws.at[0])
    load_g = pltpu.make_async_copy(g_ref.at[:, rest], w1.at[:, rest], ws.at[1])
    pl.when(x == 0)(lambda: load_w.start())
    pl.when(x != 0)(lambda: load_g.start())
    lf = loc.start(act_ref.at[:, :, :, pl.ds(DIM, 128)], flag_s)
    lo = loc.start(ahead_ref.at[:, t], own_f)
    greet(place, xs=(1, 2, 3), ctx=((1, 0), (2, 0), (3, 0), (0, 1), (0, 2), (0, 3)), chain=(1, -1), core=True)
    big = scatter_steps(wire, loc, g_ref, SPLIT + 2 * TRIPLE, (a0, a1, a2, a3, a4, a5, a6, a7), t2_out, False)
    pump(big, 1)

    def keep_mixed(cols, r, total):
        mixed_out[t, r, cols] = (resid[r, cols] + total).astype(bf16)

    ahead = RowsScatter(wire, ahead_ref, crecv_f, sums_f, r1_f, r2_f, own=own_f).steps(lambda n: None, keep_mixed)
    fro = []
    for src, dst in ((first_ref, t0_out), (second_ref, t1_out)):
        for d in (2, 1, 3):
            fro.append((d, dst, wire.send(src.at[place.xs(d)], dst.at[x], fsdp=place.xs(d))))
        loc.start(src.at[x], dst.at[x])
    before = low_s.at[0].reshape(4, 128, 512)
    hn = wire.send(before.at[:, pl.ds(112, 16), :], edge_in, context=place.chain(1))
    loc.wait(lg)
    loc.wait(lw)
    loc.wait(lf)
    loc.wait(lo)
    pl.when(x == 0)(lambda: load_w.wait())
    pl.when(x != 0)(lambda: load_g.wait())
    for cc in range(16):
        for b in range(4):
            packed[pl.ds(32 * cc, 32), pl.ds(128 * b, 128)] = w1[pl.ds(160 * cc + 32 * b, 32), pl.ds(0, 128)]
    small[...] = jnp.zeros_like(small)
    late[...] = jnp.zeros_like(late)
    fold(small.at[0], jnp.sum(gain_two[...], axis=0, keepdims=True), 512)

    def flags(g, k):
        return flag_s[pl.ds(g, 1)].reshape(128, 128).astype(f32)[:, k : k + 1]

    def put_tile(rhs, tile):
        def block(n):
            r = pl.ds(pl.multiple_of(n * 512, 512), 512)
            w1[r, column(tile)] = dot(turned[r, :], rhs).astype(bf16)

        many(5, block)

    def mixed_back(h):
        gmx[:, lanes(h)] = dot(acts[...].reshape(512, DIM), w1[:, column(2 * nh + h)])

    many(nh, mixed_back)

    bg[c] = jnp.zeros((8, 512), f32)

    def scan(q):
        cols = pl.ds(pl.multiple_of(q * 128, 128), 128)
        for g in range(4):
            r = pl.ds(128 * g, 128)
            gated, slope = gelu_and_slope(py_s[r, cols])
            grad = gmx[r, cols]
            gpy[r, cols] = (grad * hid_s[r, cols] * slope).astype(bf16)
            keep = flags(g, 1)
            dec = jnp.exp((-gate_scale) * sigmoid(la_s[r, cols]) * rec_ref[pl.ds(7, 1), cols]) * keep
            last = lax.broadcasted_iota(jnp.int32, dec.shape, 0) == 127
            a, b = scan_up(jnp.where(last, 1.0, pltpu.roll(dec, 127, 0)), grad * gated)
            bc[r, cols] = a
            bp[r, cols] = b
            bg[c, pl.ds(g, 1), cols] = dec[:1] * b[:1]

    many(2 * nh, scan)
    ns = [wire.send(bg.at[c], bg.at[c], context=place.ctx(0, d)) for d in (1, 2, 3)]
    transpose_rows(acts, turned)
    ln = loc.start(act_ref.at[:, :, :, pl.ds(0, DIM)], acts)

    many(nh, lambda h: put_tile(low_s[2, :, lanes(h)], 2 * nh + h))
    pump(ahead, 3)
    pump(big, 4)
    for d, n in zip((1, 2, 3), ns):
        wire.recv(n, bg.at[place.ctx(0, -d)])
    line = pl.ds(place.y * 4, 4)
    ns = [wire.send(bg.at[line], bg.at[line], context=place.ctx(d, 0)) for d in (1, 2, 3)]
    for g in (0, 1):
        gates[g] = gate_matrix(packed[...], g)
    loc.wait(ln)
    transpose_rows(acts, turned)

    def norm_grad_y(heads):
        def block(n):
            r = pl.ds(pl.multiple_of(n * 512, 512), 512)
            v = dot_nt(gpy[:, pl.ds(0, 256 * heads)], w1[r, pl.ds(128 + 256 * heads, 256 * heads)])
            part[:, :, :, r] = v.astype(bf16).reshape(4, 2, 64, 512)

        many(5, block)

    pl.when(x == 0)(lambda: norm_grad_y(2))
    pl.when(x != 0)(lambda: norm_grad_y(1))
    many(nh, lambda h: put_tile(gpy[:, lanes(h)], nh + h))
    mid = scatter_steps(wire, loc, w1, FIRST, (None, None, b2, b3, b4, b5, b6, b7), mid_out, False, True)
    pump(mid, 1)
    pump(ahead, 2)
    for d, n in zip((1, 2, 3), ns):
        wire.recv(n, bg.at[pl.ds(lax.rem(place.y + 4 - d, 4) * 4, 4)])

    def enter(s, state):
        return cg[s, 0] * state + cg[s, 1]

    cin[...] = lax.fori_loop(0, c, enter, jnp.zeros((8, 512), f32))

    def leave(s, state):
        k = 15 - s
        return cg[k, 0] * state + bg[k]

    cback[...] = lax.fori_loop(0, 15 - c, leave, jnp.zeros((8, 512), f32))
    def terms(q):
        cols = pl.ds(pl.multiple_of(q * 128, 128), 128)
        sums_x = jnp.zeros((1, 128), f32)
        sums_a = jnp.zeros((1, 128), f32)
        sums_l = jnp.zeros((1, 128), f32)
        for g in range(4):
            r = pl.ds(128 * g, 128)
            keep = flags(g, 1)
            cl = low_s[1, r, cols].astype(f32)
            sp, dsp = rec_ref[pl.ds(7, 1), cols], rec_ref[pl.ds(8, 1), cols]
            sx, sa, log_decay, root, factor = recur_terms(lx_s[r, cols], la_s[r, cols], cl, sp, keep)
            adj = bp[r, cols] + bc[r, cols] * cback[pl.ds(g, 1), cols]
            hid = hid_s[r, cols]
            first = lax.broadcasted_iota(jnp.int32, hid.shape, 0) == 0
            prev = jnp.where(first, cin[pl.ds(g, 1), cols], pltpu.roll(hid, 1, 0))
            grown = jnp.exp(log_decay)
            gld = keep * grown * (adj * prev - adj * sx * cl * grown / root)
            glx = (adj * factor * cl * sx * (1.0 - sx)).astype(bf16)
            gla = (gld * ((-gate_scale) * sp) * sa * (1.0 - sa)).astype(bf16)
            glow[0, r, cols] = glx
            glow[1, r, cols] = gla
            gdir[r, cols] = adj * factor * sx
            sums_x += jnp.sum(glx.astype(f32), axis=0, keepdims=True)
            sums_a += jnp.sum(gla.astype(f32), axis=0, keepdims=True)
            sums_l += jnp.sum(gld * sa, axis=0, keepdims=True) * (gate_scale * dsp)
        small[0, pl.ds(5, 1), cols] = sums_x
        small[0, pl.ds(6, 1), cols] = sums_a
        small[0, pl.ds(7, 1), cols] = sums_l

    many(2 * nh, terms)
    wire.recv(hn, edge_in)

    def conv_back(h):
        cl = low_s[1, :, lanes(h)]
        lx, la = glow[0, :, lanes(h)], glow[1, :, lanes(h)]
        gconv[:, lanes(h)] = (
            gdir[:, lanes(h)] + dot_nt(lx, gates[0, :, lanes(h)]) + dot_nt(la, gates[1, :, lanes(h)])
        )

        def group(g, taps):
            gc = gconv[token_rows(g), lanes(h)]
            bx = low_s[0, token_rows(g), lanes(h)].astype(f32)
            ahead = edge_in[g, :, lanes(h)].astype(f32)[8:]
            rows = lax.broadcasted_iota(jnp.int32, gc.shape, 0)
            low_rows = lax.broadcasted_iota(jnp.int32, (8, 256), 0)
            out = rec_ref[pl.ds(0, 1), lanes(h)] * gc
            over = jnp.zeros((8, 256), f32)
            new = [taps[0] + jnp.sum(bx * gc, axis=0, keepdims=True)]
            for k in (1, 2, 3):
                masked = flags(g, 1 + k) * gc
                new.append(taps[k] + jnp.sum(shifted(bx, ahead, k) * masked, axis=0, keepdims=True))
                scaled = rec_ref[pl.ds(k, 1), lanes(h)] * masked
                out = out + jnp.where(rows < 128 - k, pltpu.roll(scaled, 128 - k, 0), 0.0)
                over = over + jnp.where(low_rows >= 8 - k, pltpu.roll(scaled[:8], 8 - k, 0), 0.0)
            new.append(taps[4] + jnp.sum(gc, axis=0, keepdims=True))
            gdir[token_rows(g), lanes(h)] = out
            edge[g, :, lanes(h)] = over
            return tuple(new)

        taps = lax.fori_loop(0, 4, group, tuple(jnp.zeros((1, 256), f32) for _ in range(5)))
        for k in range(5):
            small[0, pl.ds(k, 1), lanes(h)] = taps[k]

    many(nh, conv_back)
    en = wire.send(edge, edge_out, context=place.chain(-1))

    early = small_steps(wire, small, zin, yin, xin, corein)
    pump(early)
    pump(big, 4)
    pump(ahead, 2)

    def gate_back(h):
        cl = low_s[1, :, lanes(h)]
        dgates[0, :, lanes(h)] = dot_tn(cl, glow[0, :, lanes(h)]).astype(bf16)
        dgates[1, :, lanes(h)] = dot_tn(cl, glow[1, :, lanes(h)]).astype(bf16)

    many(nh, gate_back)
    wire.recv(en, edge_out)

    def narrow(h):
        for g in range(4):
            v = gdir[pl.ds(128 * g, 128), lanes(h)]
            tail = v[120:] + edge_out[g, :, lanes(h)]
            gpx[pl.ds(128 * g, 128), lanes(h)] = jnp.concatenate([v[:120], tail], axis=0).astype(bf16)

    many(nh, narrow)

    def norm_grad(n, heads):
        r = pl.ds(512 * n, 512)
        v = dot_nt(gpx[:, pl.ds(0, 256 * heads)], w1[r, pl.ds(128, 256 * heads)])
        v = v + part[:, :, :, r].reshape(512, 512).astype(f32)
        part[:, :, :, r] = v.astype(bf16).reshape(4, 2, 64, 512)

    def norm_piece(n):
        pl.when(x == 0)(lambda: norm_grad(n, 2))
        pl.when(x != 0)(lambda: norm_grad(n, 1))

    def keep_sum(cols, r, total):
        tgrad_out[t, r, cols] = total

    final = RowsScatter(wire, part, crecv, sums, r1, r2).steps(norm_piece, keep_sum)
    pump(final, 2)
    pump(mid, 4)
    pump(final, 3)
    many(nh, lambda h: put_tile(gpx[:, lanes(h)], h))
    back = (dot_tn(selector(0), dgates[0]) + dot_tn(selector(1), dgates[1])).astype(bf16)
    for cc in range(16):
        for b in range(4):
            w1[pl.ds(160 * cc + 32 * b, 32), pl.ds(0, 128)] = back[32 * cc : 32 * cc + 32, 128 * b : 128 * b + 128]
    last = scatter_steps(wire, loc, w1, 0, (None, None, c2, c3, c4, c5, c6, c7), last_out, True, True)
    pump(last, 1)
    pump(final, 1)
    pump(early)
    pump(big, 1)
    pump(final, 1)
    pump(early)
    drain(final)
    gain_acc[...] = jnp.zeros_like(gain_acc)

    def finish(i):
        r = pl.ds(pl.multiple_of(i * 16, 16), 16)
        gx, gain = norm_back(tgrad_out[t, r, :], tok_ref[r, :], gain_ref[...])
        tgrad_out[t, r, :] = gres[r, :] + gx
        gain_acc[...] += gain

    many(4, finish)
    tn = wire.send(tgrad_out.at[t], tgrad_out.at[t], tensor=1 - t)
    fold(late.at[0], jnp.sum(gain_acc[...], axis=0, keepdims=True), 0)
    tail = small_steps(wire, late, zin_l, yin_l, xin_l, corein_l)
    pump(tail)
    pump(ahead, 1)
    pump(mid, 4)
    pump(early)
    pump(tail)
    pump(big, 1)
    pump(last, 4)
    drain(ahead)
    mn = wire.send(mixed_out.at[t], mixed_out.at[t], tensor=1 - t)
    pump(tail)
    pump(mid, 1)
    pump(early)
    pump(last, 4)
    pump(tail)
    drain(big)
    pump(mid, 1)
    pump(last, 1)
    drain(mid)
    drain(tail)
    drain(early)
    for k in range(4):
        recur_out[k] = xin[k, :, pl.ds(0, 512)]
    gains_out[0] = late[3] + corein_l[...]
    gains_out[1] = small[3, :, pl.ds(512, 384)] + corein[:, pl.ds(512, 384)]
    drain(last)
    for d, dst, n in fro:
        wire.recv(n, dst.at[place.xs(-d)])
    wire.recv(mn, mixed_out.at[1 - t])
    wire.recv(tn, tgrad_out.at[1 - t])
    wire.finish()
    loc.finish()


def backward_call(g, w, act, gm, first, second, ahead, lx, la, hid, py, low, cg, tok, gres, resid, gain, rec, gain_two):
    S = jax.ShapeDtypeStruct
    R = (64, DIM)
    F = (512, 512)
    E, L = (8, 896), (8, 384)
    slices = lambda n: S((4, 48, n), bf16)
    return pl.pallas_call(
        backward_kernel,
        name="recurrent_backward",
        out_shape=(
            slices(TRIPLE), slices(TRIPLE), slices(TRIPLE), slices(SPLIT - FIRST), slices(FIRST),
            S((2,) + R, bf16), S((2,) + R, f32), S((4, 8, 512), f32), S((2,) + L, f32),
        ),
        in_specs=[ANY] * 7 + [VM] * 12,
        out_specs=[ANY, ANY, ANY, ANY, ANY, VM, VM, VM, VM],
        scratch_shapes=scatter_scratch(TRIPLE) + scatter_scratch(SPLIT - FIRST)[2:] + scatter_scratch(FIRST)[2:] + [
            vm((DIM, SPLIT), bf16), vm((4, 2) + R, bf16), vm((DIM, 512), bf16), vm((4, 2, 64, 128), bf16),
            vm(F, f32), vm(F, bf16), vm(F, f32), vm(F, f32), vm((16, 8, 512), f32), vm((8, 512), f32), vm((8, 512), f32),
            vm((2,) + F, bf16), vm((4, 8, 512), f32), vm((4, 16, 512), bf16), vm((4, 8, 512), f32), vm(F, bf16),
            vm((2, 256, 512), bf16), vm(F, bf16), vm((2, 256, 512), bf16), vm((8, DIM), f32),
            vm((4,) + R, bf16), vm((3,) + R, bf16), vm((2,) + R, bf16), vm((2,) + R, bf16),
            vm((4,) + R, bf16), vm((4,) + R, bf16), vm((3,) + R, bf16), vm((2,) + R, bf16), vm((2,) + R, bf16),
            vm((4,) + E, f32), vm((3,) + E, f32), vm((3,) + E, f32), vm((4,) + E, f32), vm(E, f32),
            vm((4,) + L, f32), vm((3,) + L, f32), vm((3,) + L, f32), vm((4,) + L, f32), vm(L, f32),
            pltpu.SemaphoreType.DMA((310,)), pltpu.SemaphoreType.DMA((310,)), pltpu.SemaphoreType.DMA((60,)),
            pltpu.SemaphoreType.DMA((2,)),
        ],
        compiler_params=pltpu.CompilerParams(collective_id=2, has_side_effects=True, vmem_limit_bytes=62 << 20),
    )(g, w, act, gm, first, second, ahead, lx, la, hid, py, low, cg, tok, gres, resid, gain, rec, gain_two)


HEAD_START = (0, 2, 3, 4)
HEADS_OF = (2, 1, 1, 1)
FF_START = (0, 768, 1792, 2816)
TILE_ORDER = ((0, 1, 2), (3, 0, 1, 2), (3, 0, 1, 2), (3, 0, 1, 2))


def adam_update(weight, moment, square, gradient, rate, shrink):
    moment = beta_one * moment + (1.0 - beta_one) * gradient
    square = beta_two * square + (1.0 - beta_two) * gradient * gradient
    normed = moment / (1.0 - beta_one**STEP) / (jnp.sqrt(square / (1.0 - beta_two**STEP)) + adam_eps)
    return (weight - rate * (normed + shrink * weight), moment, square)


def restored_tile(get, q, shape):
    lane = lax.broadcasted_iota(jnp.int32, shape, len(shape) - 1)
    out = jnp.zeros(shape, f32)
    at = 128 * q
    while at < 128 * q + 128:
        m = at // 40
        source = 40 * (4 * (m % 16) + m // 16) + at - 40 * m
        p = source // 128
        stop = min(40 * m + 40, 128 * q + 128, at + 128 * p + 128 - source)
        turn = (at - 128 * q - (source - 128 * p)) % 128
        v = get(p)
        if turn:
            v = pltpu.roll(v, turn, len(shape) - 1)
        out = jnp.where((lane >= at - 128 * q) & (lane < stop - 128 * q), v, out)
        at = stop
    return out


def update_kernel(
    last, mid, t0, t1, t2, recur, gains, mixed, tgrad, *refs,
):
    params, outs = refs[:21], refs[21:]
    mixed_out, tgrad_out = outs[:2]

    def group(n):
        return params[3 * n : 3 * n + 3], outs[2 + 3 * n : 5 + 3 * n]

    def update(n, index, grad, rate=matrix_rate, shrink=weight_decay):
        old, new = group(n)
        values = adam_update(*(ref[index] for ref in old), grad, rate, shrink)
        for ref, value in zip(new, values):
            ref[index] = value

    def piece(k, tile):
        if tile < 2:
            ref, at = last, 128 + 256 * tile
        elif tile < 6:
            ref, at = mid, 256 * (tile - 2)
        else:
            ref, at = (t0, t1, t2)[(tile - 6) // 3], 256 * ((tile - 6) % 3)
        return ref[k, :, pl.ds(at, 256)].astype(f32)

    for k in range(4):
        for h in range(HEADS_OF[k]):
            nh = HEADS_OF[k]
            at = 256 * (HEAD_START[k] + h)
            update(2, (0, slice(None), pl.ds(at, 256)), piece(k, h)[:40])
            update(2, (1, slice(None), pl.ds(at, 256)), piece(k, nh + h)[:40])
            update(4, (slice(None), pl.ds(at, 256)), piece(k, 2 * nh + h)[:40])
            b = last[k, :, pl.ds(256 * h, 256)].astype(f32)[40:]
            for g in (0, 1):
                update(3, (g, HEAD_START[k] + h), b[4 * g : 4 * g + 4])
        for j in TILE_ORDER[k]:
            tile = 3 if j == 3 else 6 + 3 * j
            at = FF_START[k] + 256 * j
            update(5, (0, slice(None), pl.ds(at, 256)), piece(k, tile)[:40])
            update(5, (1, slice(None), pl.ds(at, 256)), piece(k, tile + 1)[:40])
            update(6, (slice(None), pl.ds(at, 256)), piece(k, tile + 2)[:40])
        n = 256 * HEADS_OF[k]
        update(1, (slice(None), pl.ds(256 * HEAD_START[k], n)), recur[k, :, pl.ds(0, n)], vector_rate, 0.0)

    for n in (0, 1):
        for q in range(20):
            grad = restored_tile(lambda p: gains[n, pl.ds(p // 3, 1), pl.ds(128 * (p % 3), 128)], q, (1, 128))
            update(0, (pl.ds(n, 1), pl.ds(128 * q, 128)), grad, vector_rate, 0.0)

    def restore(i):
        t = i // 4
        r = pl.ds(pl.multiple_of((i % 4) * 16, 16), 16)
        dst = pl.ds(pl.multiple_of(i * 16, 16), 16)
        for q in range(20):
            cols = pl.ds(128 * q, 128)
            mixed_out[dst, cols] = restored_tile(lambda p: mixed[t, r, pl.ds(128 * p, 128)].astype(f32), q, (16, 128)).astype(bf16)
            tgrad_out[dst, cols] = restored_tile(lambda p: tgrad[t, r, pl.ds(128 * p, 128)], q, (16, 128))

    many(8, restore)


def update_call(pieces, recur, gains, mixed, tgrad, params):
    shapes = [jax.ShapeDtypeStruct(v.shape, v.dtype) for v in params]
    outs = [jax.ShapeDtypeStruct((128, DIM), bf16), jax.ShapeDtypeStruct((128, DIM), f32)] + shapes
    return pl.pallas_call(
        update_kernel,
        name="optimizer_step",
        out_shape=tuple(outs),
        in_specs=[VM] * (9 + len(params)),
        out_specs=tuple([VM] * len(outs)),
        compiler_params=pltpu.CompilerParams(vmem_limit_bytes=56 << 20),
    )(*pieces, recur, gains, mixed, tgrad, *params)


def permuted(a):
    return a.reshape(a.shape[:-1] + (4, 16, 40)).swapaxes(-3, -2).reshape(a.shape)


def restored(a):
    return a.reshape(a.shape[:-1] + (16, 4, 40)).swapaxes(-3, -2).reshape(a.shape)


def pack_weights(input_proj, gate_blocks, output_proj, inner_proj, down_proj):
    inp, out = input_proj.astype(bf16), output_proj.astype(bf16).T
    inner, down, blocks = inner_proj.astype(bf16), down_proj.astype(bf16).T, gate_blocks.astype(bf16)
    packs = []
    for k in range(4):
        hs = slice(HEAD_START[k] * 256, (HEAD_START[k] + HEADS_OF[k]) * 256)
        main = [jnp.zeros((40, 128), bf16), inp[0][:, hs], inp[1][:, hs], out[:, hs]]
        for j in TILE_ORDER[k]:
            f = slice(FF_START[k] + 256 * j, FF_START[k] + 256 * j + 256)
            main += [inner[0][:, f], inner[1][:, f], down[:, f]]
        main = jnp.concatenate(main, axis=1)
        g = blocks[:, HEAD_START[k] : HEAD_START[k] + HEADS_OF[k]].swapaxes(1, 2).reshape(8, HEADS_OF[k] * 256)
        packs.append(jnp.concatenate([main, jnp.pad(g, ((0, 0), (0, COLS - g.shape[1])))], axis=0))
    return jnp.stack(packs)


def token_flags(seq_lengths, rows, taps, count):
    margin = taps - 1
    places = lax.axis_index("context") * rows + jnp.arange(-margin, rows, dtype=jnp.int32)
    ends = jnp.cumsum(seq_lengths[0])
    segment = jnp.sum((places[:, None] >= ends[None, :]).astype(jnp.int32), axis=1)
    starts = jnp.concatenate([jnp.zeros((1,), jnp.int32), ends])
    own = places[margin:]
    keeping = 1.0 - jnp.any(own[:, None] == starts[None, :], axis=1).astype(f32)
    valid = (segment[margin:] < count).astype(f32)
    out = [valid, keeping]
    for offset in range(1, taps):
        lower = margin - offset
        same = (segment[lower : lower + rows] == segment[margin:]) & (places[lower : lower + rows] >= 0)
        out.append(same.astype(f32))
    return jnp.stack(out, axis=1)


def prepare(tokens, cotangent, seq_lengths, norm_gains, recur_params, weights):
    x, t = lax.axis_index("fsdp"), lax.axis_index("tensor")
    flags = lax.dynamic_slice_in_dim(token_flags(seq_lengths, tokens.shape[0], 4, 3), t * 64, 64, 0)
    tok = permuted(lax.dynamic_slice_in_dim(tokens, t * 64, 64, 0)).astype(f32)
    cot = permuted(lax.dynamic_slice_in_dim(cotangent, t * 64, 64, 0))
    gains = permuted(norm_gains)
    inv = lax.rsqrt(jnp.mean(tok * tok, axis=-1, keepdims=True) + norm_eps)
    normed = (tok * inv * gains[0]).astype(bf16)
    low = (cot.astype(f32) * flags[:, :1]).astype(bf16)
    normed = jnp.concatenate([normed, jnp.pad(flags.astype(bf16), ((0, 0), (0, 123)))], axis=1)
    start = jnp.where(x == 0, 0, x + 1) * 256
    rec = lax.dynamic_slice_in_dim(jnp.pad(recur_params, ((0, 0), (0, 256))), start, 512, 1)
    rec = jnp.concatenate([rec[:7], jax.nn.softplus(-rec[7:]), jax.nn.sigmoid(-rec[7:]), jnp.zeros((7, 512), f32)], axis=0)
    return pack_weights(*weights), normed, low, tok, gains, rec


def on_device(
    tokens, cotangent, seq_lengths,
    norm_gains, gains_moment, gains_square, recur_params, recur_moment, recur_square,
    input_proj, input_moment, input_square, gate_blocks, blocks_moment, blocks_square,
    output_proj, output_moment, output_square, inner_proj, inner_moment, inner_square,
    down_proj, down_moment, down_square,
):
    p, normed, cot, tok, gains, rec = prepare(
        tokens, cotangent, seq_lengths, norm_gains, recur_params,
        (input_proj, gate_blocks, output_proj, inner_proj, down_proj),
    )
    w, act, gl, lx, la, hid, py, low, cg, nm, resid = forward_call(p, normed, cot, tok, gains[1:], rec)
    g, ahead, gm, gres, gain_two, first, second = ffn_call(w, gl, nm, resid, gains[1:])
    t0, t1, t2, mid, last, mixed, tgrad, recur, gsum = backward_call(
        g, w, act, gm, first, second, ahead, lx, la, hid, py, low, cg, tok, gres, resid, gains[:1], rec, gain_two
    )
    params = (
        norm_gains, gains_moment, gains_square, recur_params, recur_moment, recur_square,
        input_proj, input_moment, input_square, gate_blocks, blocks_moment, blocks_square,
        output_proj.T, output_moment.T, output_square.T, inner_proj, inner_moment, inner_square,
        down_proj.T, down_moment.T, down_square.T,
    )
    out = update_call((last, mid, t0, t1, t2), recur, gsum, mixed, tgrad, params)
    return out[:14] + tuple(v.T for v in out[14:17]) + out[17:20] + tuple(v.T for v in out[20:])


def solution(mesh):
    row = P(("fsdp", "context"), None)
    wide_spec = P(None, ("fsdp", "context"), "tensor")
    tall = P("tensor", ("fsdp", "context"))
    block = P(None, "tensor", ("fsdp", "context"), None)
    params = (P(),) * 3 + (P(None, "tensor"),) * 3 + (wide_spec,) * 3 + (block,) * 3 + (tall,) * 3 + (wide_spec,) * 3 + (tall,) * 3
    return jax.shard_map(
        on_device, mesh=mesh, in_specs=(row, row, P("fsdp", None)) + params, out_specs=(row, row) + params, check_vma=False
    )
```

```python
import functools

import jax
import jax.numpy as jnp
from jax import lax
from jax.experimental import pallas as pl
from jax.experimental.pallas import tpu as pltpu
from jax.sharding import PartitionSpec as P

STEP = 10

norm_eps = 1e-06
beta_one = 0.9
beta_two = 0.95
adam_eps = 1e-08
weight_decay = 0.1
matrix_rate = 0.06
vector_rate = 1.0
gate_scale = 8.0

bf16, f32 = jnp.bfloat16, jnp.float32
MESH = pl.DeviceIdType.MESH
DIM = 2560
COLS = 3968
FIRST, SPLIT = 640, 1664
TRIPLE = 768
EXT = 2560 + 128
NT = (((1,), (1,)), ((), ()))
TN = (((0,), (0,)), ((), ()))


def dot(a, b):
    return jnp.dot(a, b, preferred_element_type=f32)


def dot_nt(a, b):
    return lax.dot_general(a, b, NT, preferred_element_type=f32)


def dot_tn(a, b):
    return lax.dot_general(a, b, TN, preferred_element_type=f32)


def many(n, fn):
    def one(i, carry):
        fn(i)
        return carry

    lax.fori_loop(0, n, one, 0)


class Place:
    def __init__(self):
        self.x = lax.axis_index("fsdp")
        self.c = lax.axis_index("context")
        self.t = lax.axis_index("tensor")
        self.y, self.z = lax.div(self.c, 4), lax.rem(self.c, 4)

    def ctx(self, dy, dz):
        return lax.rem(self.y + dy + 4, 4) * 4 + lax.rem(self.z + dz + 4, 4)

    def xs(self, d):
        return lax.rem(self.x + d + 4, 4)

    def along(self, half, d1, d2):
        return self.ctx(d2, d1) if half == 0 else self.ctx(d1, d2)

    def chain(self, d):
        return lax.rem(self.c + d + 16, 16)


class Wire:
    def __init__(self, place, ss, rs):
        self.place, self.ss, self.rs = place, ss, rs
        self.n, self.sent = 0, []

    def send(self, src, dst, **to):
        n = self.n
        self.n += 1
        copy = pltpu.make_async_remote_copy(
            src_ref=src, dst_ref=dst, send_sem=self.ss.at[n], recv_sem=self.rs.at[n],
            device_id=to, device_id_type=MESH,
        )
        copy.start()
        self.sent.append(copy)
        return n

    def recv(self, n, ref):
        pltpu.make_async_remote_copy(
            src_ref=ref, dst_ref=ref, send_sem=self.ss.at[n], recv_sem=self.rs.at[n],
            device_id={"fsdp": self.place.x}, device_id_type=MESH,
        ).wait_recv()

    def finish(self):
        for copy in self.sent:
            copy.wait_send()


class Local:
    def __init__(self, sems):
        self.sems, self.n, self.open = sems, 0, []

    def start(self, src, dst):
        copy = pltpu.make_async_copy(src, dst, self.sems.at[self.n])
        self.n += 1
        copy.start()
        self.open.append(copy)
        return copy

    def wait(self, copy):
        copy.wait()
        self.open = [other for other in self.open if other is not copy]

    def finish(self):
        for copy in self.open:
            copy.wait()


def greet(place, xs=(), ctx=(), chain=(), core=False):
    bar = pltpu.get_barrier_semaphore()
    n = 0
    for d in xs:
        pl.semaphore_signal(bar, inc=1, device_id={"fsdp": place.xs(d)}, device_id_type=MESH)
        n += 1
    for dy, dz in ctx:
        pl.semaphore_signal(bar, inc=1, device_id={"context": place.ctx(dy, dz)}, device_id_type=MESH)
        n += 1
    for d in chain:
        pl.semaphore_signal(bar, inc=1, device_id={"context": place.chain(d)}, device_id_type=MESH)
        n += 1
    if core:
        pl.semaphore_signal(bar, inc=1, device_id={"tensor": 1 - place.t}, device_id_type=MESH)
        n += 1
    pl.semaphore_wait(bar, n)


def chunk_rows(index, half):
    return pl.ds(pl.multiple_of(index * 160 + 80 * half, 16), 80)


def line_of(ref, place, half, d, cols):
    grid = ref.reshape(4, 4, 160, ref.shape[1])
    rows = pl.ds(80 * half, 80)
    if half == 0:
        return grid.at[:, lax.rem(place.z + d + 4, 4), rows, cols]
    return grid.at[lax.rem(place.y + d + 4, 4), :, rows, cols]


def gather_steps(wire, buf, own, at):
    place = wire.place
    width = own.shape[1]
    mid = width // 256 * 128
    FULL = pl.ds(at, width)
    part = {1: pl.ds(at, mid), -1: pl.ds(at + mid, width - mid)}

    def ref(h, d, cols):
        return buf.at[chunk_rows(place.along(h, d, 0), h), cols]

    def second_line(h, d, cols):
        grid = buf.reshape(4, 4, 160, buf.shape[1])
        rows = pl.ds(80 * h, 80)
        if h == 0:
            return grid.at[lax.rem(place.y + d + 4, 4), :, rows, cols]
        return grid.at[:, lax.rem(place.z + d + 4, 4), rows, cols]

    st = {}
    for h in (0, 1):
        for d in (1, -1):
            st[h, 1, d] = wire.send(own.at[pl.ds(80 * h, 80), :], ref(h, 0, FULL), context=place.along(h, d, 0))
    yield
    for d in (1, -1):
        for h in (0, 1):
            wire.recv(st[h, 1, d], ref(h, -d, FULL))
            st[h, 2, d] = wire.send(ref(h, -d, part[d]), ref(h, -d, part[d]), context=place.along(h, d, 0))
    yield
    for h in (0, 1):
        for d in (1, -1):
            wire.recv(st[h, 2, d], ref(h, 2, part[d]))
        for k in (1, -1):
            for d in (1, -1):
                cols = part[k * d]
                st[h, 3, d, k] = wire.send(second_line(h, 0, cols), second_line(h, 0, cols), context=place.along(h, 0, d))
    yield
    for h in (0, 1):
        for d in (1, -1):
            wire.recv(st[h, 3, d, 1], second_line(h, -d, part[d]))
            st[h, 4, d] = wire.send(second_line(h, -d, part[d]), second_line(h, -d, part[d]), context=place.along(h, 0, d))
    yield
    for h in (0, 1):
        for d in (1, -1):
            wire.recv(st[h, 3, d, -1], second_line(h, -d, part[-d]))
    for h in (0, 1):
        for d in (1, -1):
            wire.recv(st[h, 4, d], second_line(h, 2, part[d]))
    yield


def rows_gather_steps(wire, src, out, loc):
    place = wire.place
    x, t = place.x, place.t
    width = src.shape[1]
    h = width // 256 * 128
    LO, HI = pl.ds(0, h), pl.ds(h, width - h)
    xp, xm, xo = place.xs(1), place.xs(-1), place.xs(2)
    def hop(ref, piece, cols, d):
        return wire.send(ref, out.at[piece, t, :, cols], fsdp=place.xs(d))

    a = hop(src.at[:, LO], x, LO, 1)
    b = hop(src.at[:, HI], x, HI, -1)
    aa = hop(src.at[:, HI], x, HI, 1)
    bb = hop(src.at[:, LO], x, LO, -1)
    cores = [(x, wire.send(src, out.at[x, t], tensor=1 - t))]
    own = loc.start(src, out.at[x, t])
    yield
    wire.recv(a, out.at[xm, t, :, LO])
    e = hop(out.at[xm, t, :, LO], xm, LO, 1)
    wire.recv(b, out.at[xp, t, :, HI])
    f = hop(out.at[xp, t, :, HI], xp, HI, -1)
    yield
    wire.recv(aa, out.at[xm, t, :, HI])
    cores.append((xm, wire.send(out.at[xm, t], out.at[xm, t], tensor=1 - t)))
    wire.recv(bb, out.at[xp, t, :, LO])
    cores.append((xp, wire.send(out.at[xp, t], out.at[xp, t], tensor=1 - t)))
    yield
    wire.recv(e, out.at[xo, t, :, LO])
    wire.recv(f, out.at[xo, t, :, HI])
    cores.append((xo, wire.send(out.at[xo, t], out.at[xo, t], tensor=1 - t)))
    yield
    for k, n in cores:
        wire.recv(n, out.at[k, 1 - t])
    loc.wait(own)
    yield


class RowsScatter:
    def __init__(self, wire, part, crecv, sums, r1, r2, piece=512, own=None):
        self.wire, self.part, self.crecv, self.sums, self.r1, self.r2 = wire, part, crecv, sums, r1, r2
        self.piece, self.n = piece, {}
        place = wire.place
        self.x, self.t = place.x, place.t
        self.own = own if own is not None else part.at[:, self.t]
        self.xp, self.xm, self.xo = place.xs(1), place.xs(-1), place.xs(2)

    def cut(self, i):
        at, half = i * self.piece, self.piece // 2
        return pl.ds(at, self.piece), pl.ds(at, half), pl.ds(at + half, half)

    def rows(self, fn):
        for i in (0, 1):
            fn(pl.ds(32 * i, 32))

    def put(self, n, k, cols, extra=None):
        def fn(r):
            v = self.own[k, r, cols].astype(f32) + self.crecv[k, r, cols].astype(f32)
            if extra is not None:
                v = v + self.r1[extra, r, cols].astype(f32)
            self.sums[n, r, cols] = v.astype(bf16)

        self.rows(fn)

    def a(self, i):
        cols = self.cut(i)[0]
        self.n["a", i] = self.wire.send(self.part.at[:, 1 - self.t, :, cols], self.crecv.at[:, :, cols], tensor=1 - self.t)

    def b(self, i):
        cols, lo, hi = self.cut(i)
        self.wire.recv(self.n["a", i], self.crecv.at[:, :, cols])
        self.put(0, self.xo, cols)
        self.n["b", i] = self.wire.send(self.sums.at[0, :, lo], self.r1.at[0, :, lo], fsdp=self.xp)
        self.n["c", i] = self.wire.send(self.sums.at[0, :, hi], self.r1.at[1, :, hi], fsdp=self.xm)

    def c(self, i):
        cols, lo, hi = self.cut(i)
        self.wire.recv(self.n["b", i], self.r1.at[0, :, lo])
        self.put(1, self.xp, lo, 0)
        self.put(1, self.xp, hi)
        self.n["d", i] = self.wire.send(self.sums.at[1, :, cols], self.r2.at[0, :, cols], fsdp=self.xp)
        self.wire.recv(self.n["c", i], self.r1.at[1, :, hi])
        self.put(2, self.xm, lo)
        self.put(2, self.xm, hi, 1)
        self.n["e", i] = self.wire.send(self.sums.at[2, :, cols], self.r2.at[1, :, cols], fsdp=self.xm)

    def d(self, i, done):
        cols = self.cut(i)[0]
        self.wire.recv(self.n["d", i], self.r2.at[0, :, cols])
        self.wire.recv(self.n["e", i], self.r2.at[1, :, cols])

        def total(r):
            done(
                cols,
                r,
                self.own[self.x, r, cols].astype(f32)
                + self.crecv[self.x, r, cols].astype(f32)
                + self.r2[0, r, cols].astype(f32)
                + self.r2[1, r, cols].astype(f32),
            )

        self.rows(total)

    def steps(self, compute, done):
        count = self.sums.shape[2] // self.piece
        for i in range(count + 3):
            if i < count:
                compute(i)
                self.a(i)
            if 0 <= i - 1 < count:
                self.b(i - 1)
            if 0 <= i - 2 < count:
                self.c(i - 2)
            if 0 <= i - 3 < count:
                self.d(i - 3, done)
            yield


def drain(steps):
    for _ in steps:
        pass


def pump(steps, n=1):
    for _ in range(n):
        next(steps, None)


def gelu(v):
    return 0.5 * v * (1.0 + jnp.tanh(0.7978845608028654 * (v + 0.044715 * v * v * v)))


def gelu_and_slope(v):
    u = jnp.tanh(0.7978845608028654 * (v + 0.044715 * v * v * v))
    slope = 0.5 * (1.0 + u) + 0.5 * v * (1.0 - u * u) * (
        0.7978845608028654 * (1.0 + 3 * 0.044715 * v * v)
    )
    return 0.5 * v * (1.0 + u), slope


def one_less_exp(v):
    series = 1.0 + v * (1.0 / 7.0)
    for k in (6.0, 5.0, 4.0, 3.0, 2.0):
        series = 1.0 + v * (1.0 / k) * series
    return jnp.where(v > -0.35, -v * series, 1.0 - jnp.exp(v))


def sigmoid(v):
    return 1.0 / (1.0 + jnp.exp(-v))


def shifted(block, edge, k):
    moved = pltpu.roll(block, k, 0)
    first = jnp.where(
        lax.broadcasted_iota(jnp.int32, edge.shape, 0) < k, pltpu.roll(edge, k, 0), moved[:8]
    )
    return jnp.concatenate([first, moved[8:]], axis=0)


def scan_down(a, b):
    rows = lax.broadcasted_iota(jnp.int32, a.shape, 0)
    s = 1
    while s < a.shape[0]:
        earlier = rows >= s
        pa = jnp.where(earlier, pltpu.roll(a, s, 0), 1.0)
        pb = jnp.where(earlier, pltpu.roll(b, s, 0), 0.0)
        b = b + a * pb
        a = a * pa
        s *= 2
    return a, b


def scan_up(a, b):
    rows = lax.broadcasted_iota(jnp.int32, a.shape, 0)
    n = a.shape[0]
    s = 1
    while s < n:
        later = rows < n - s
        pa = jnp.where(later, pltpu.roll(a, n - s, 0), 1.0)
        pb = jnp.where(later, pltpu.roll(b, n - s, 0), 0.0)
        b = b + a * pb
        a = a * pa
        s *= 2
    return a, b


def selector(g):
    i = lax.broadcasted_iota(jnp.int32, (256, 512), 0)
    j = lax.broadcasted_iota(jnp.int32, (256, 512), 1)
    xx, cc, r = i // 64, (i // 4) % 16, i % 4
    return (j == cc * 32 + xx * 8 + g * 4 + r).astype(f32).astype(bf16)


def gate_matrix(packed, g):
    return dot(selector(g), packed).astype(bf16)


def column(tile, tiles=1):
    return pl.ds(pl.multiple_of(128 + 256 * tile, 128), 256 * tiles)


def triple(j):
    return column(jnp.where(j == 3, 3, 6 + 3 * j), 3)


def head_count(x):
    return jnp.where(x == 0, 2, 1).astype(jnp.int32)


def lanes(h):
    return pl.ds(pl.multiple_of(h * 256, 256), 256)


def token_rows(g):
    return pl.ds(pl.multiple_of(g * 128, 128), 128)


def recur_terms(lx, la, cl, sp, keep):
    sx, sa = sigmoid(lx), sigmoid(la)
    log_decay = (-gate_scale) * sa * sp
    grown = one_less_exp(2.0 * log_decay)
    root = jnp.sqrt(grown)
    factor = root * keep + 1.0 - keep
    return sx, sa, log_decay, root, factor


def forward_kernel(
    p_ref, n_ref, cot_ref, tok_ref, gain_ref, rec_ref,
    w_out, act_out, gl_out, lx_out, la_out, hid_out, py_out, low_out, cg_out, nm_out, resid_out,
    xbuf, wide, chunk0, chunk1, chunk2, w1, act, lx_s, la_s, hid_s, py_s, low_s, halo, cum_s, cg, cin,
    part, crecv, sums, r1, r2, normed, resid, packed, gates,
    ss, rs, ls,
):
    place = Place()
    x, c, t = place.x, place.c, place.t
    greet(place, xs=(1, 2, 3), ctx=((1, 0), (2, 0), (3, 0), (0, 1), (0, 2), (0, 3)), chain=(1, -1), core=True)
    wire, loc = Wire(place, ss, rs), Local(ls)
    nh = head_count(x)

    stages = ((0, FIRST, chunk0), (FIRST, SPLIT, chunk1), (SPLIT, COLS, chunk2))
    came = {}

    def spread(s):
        c0, c1, _ = stages[s]
        cs = pl.ds(c0, c1 - c0)
        for d in (2, 1, 3):
            came[s, d] = wire.send(p_ref.at[place.xs(d), :, cs], xbuf.at[x, :, cs], fsdp=place.xs(d))

    def arrange(s):
        c0, c1, chunk = stages[s]
        cs = pl.ds(c0, c1 - c0)
        for d in (1, 3, 2):
            wire.recv(came[s, d], xbuf.at[place.xs(-d), :, cs])

        for k in range(4):
            def take(src, k=k):
                v = src[k, :, cs].astype(f32)
                wide[pl.ds(40 * k, 40), cs] = v[:40]

            pl.when(x == k)(functools.partial(take, p_ref))
            pl.when(x != k)(functools.partial(take, xbuf))
        if s == 0:
            for k in range(4):
                def gate(src, k=k):
                    v = src[k, :, pl.ds(0, 512)].astype(f32)
                    for b in range(4):
                        wide[pl.ds(32 * b + 8 * k, 8), pl.ds(0, 128)] = v[40:, 128 * b : 128 * b + 128]

                pl.when(x == k)(functools.partial(gate, p_ref))
                pl.when(x != k)(functools.partial(gate, xbuf))
        chunk[...] = wide[:, cs].astype(bf16)

    mine = pl.ds(pl.multiple_of(c * 160, 16), 160)
    spread(0)
    arrange(0)
    own0 = loc.start(chunk0, w1.at[mine, pl.ds(0, FIRST)])
    one = gather_steps(wire, w1, chunk0, 0)
    pump(one)
    spread(1)
    rows = rows_gather_steps(wire, n_ref, act, loc)
    pump(rows)
    pump(one)
    arrange(1)
    own1 = loc.start(chunk1, w1.at[mine, pl.ds(FIRST, SPLIT - FIRST)])
    two = gather_steps(wire, w1, chunk1, FIRST)
    pump(two)
    loc.wait(own0)
    pump(one)
    spread(2)
    pump(rows)
    pump(two)
    pump(one)
    pump(rows)
    loc.wait(own1)
    pump(two)
    pump(rows)
    drain(one)
    drain(rows)
    loc.start(act, act_out)
    later = rows_gather_steps(wire, cot_ref, gl_out, loc)

    def project_x(h):
        ni = act[:, :, :, pl.ds(0, DIM)].reshape(512, DIM)
        low_s[0, :, lanes(h)] = dot(ni, w1[:, column(h)]).astype(bf16)

    many(nh, project_x)
    before = low_s.at[0].reshape(4, 128, 512)
    hn = wire.send(before.at[:, pl.ds(112, 16), :], halo, context=place.chain(1))
    for cc in range(16):
        for b in range(4):
            packed[pl.ds(32 * cc, 32), pl.ds(128 * b, 128)] = w1[pl.ds(160 * cc + 32 * b, 32), pl.ds(0, 128)]
    for g in (0, 1):
        gates[g] = gate_matrix(packed[...], g)
    wire.recv(hn, halo)

    def flags(g, k):
        v = act[pl.ds(g, 1), :, :, pl.ds(DIM, 128)].reshape(128, 128).astype(f32)
        return v[:, k : k + 1]

    cg[c] = jnp.zeros((2, 8, 512), f32)

    def conv(h):
        def group(g):
            bx = low_s[0, token_rows(g), lanes(h)].astype(f32)
            edge = halo[g, :, lanes(h)].astype(f32)[8:]
            out = rec_ref[pl.ds(4, 1), lanes(h)] + rec_ref[pl.ds(0, 1), lanes(h)] * bx
            for k in (1, 2, 3):
                out = out + rec_ref[pl.ds(k, 1), lanes(h)] * (flags(g, 1 + k) * shifted(bx, edge, k))
            low_s[1, token_rows(g), lanes(h)] = out.astype(bf16)

        many(4, group)
        cl = low_s[1, :, lanes(h)]
        lx_s[:, lanes(h)] = dot(cl, gates[0, :, lanes(h)]) + rec_ref[pl.ds(5, 1), lanes(h)]
        la_s[:, lanes(h)] = dot(cl, gates[1, :, lanes(h)]) + rec_ref[pl.ds(6, 1), lanes(h)]

    many(nh, conv)
    loc.start(lx_s, lx_out)
    loc.start(la_s, la_out)
    pump(later)
    pump(two)

    def scan(q):
        cols = pl.ds(pl.multiple_of(q * 128, 128), 128)
        for g in range(4):
            r = pl.ds(128 * g, 128)
            keep = flags(g, 1)
            cl = low_s[1, r, cols].astype(f32)
            sx, sa, log_decay, root, factor = recur_terms(
                lx_s[r, cols], la_s[r, cols], cl, rec_ref[pl.ds(7, 1), cols], keep
            )
            a, b = scan_down(jnp.exp(log_decay) * keep, factor * sx * cl)
            cum_s[r, cols] = a
            hid_s[r, cols] = b
            cg[c, 0, pl.ds(g, 1), cols] = a[127:]
            cg[c, 1, pl.ds(g, 1), cols] = b[127:]

    many(2 * nh, scan)
    ns = [wire.send(cg.at[c], cg.at[c], context=place.ctx(0, d)) for d in (1, 2, 3)]
    for d, n in zip((1, 2, 3), ns):
        wire.recv(n, cg.at[place.ctx(0, -d)])
    line = pl.ds(place.y * 4, 4)
    ns = [wire.send(cg.at[line], cg.at[line], context=place.ctx(d, 0)) for d in (1, 2, 3)]
    arrange(2)
    own2 = loc.start(chunk2, w_out.at[mine, pl.ds(SPLIT, COLS - SPLIT)])
    for d, n in zip((1, 2, 3), ns):
        wire.recv(n, cg.at[pl.ds(lax.rem(place.y + 4 - d, 4) * 4, 4)])

    def enter(s, state):
        return cg[s, 0] * state + cg[s, 1]

    cin[...] = lax.fori_loop(0, c, enter, jnp.zeros((8, 512), f32))
    loc.start(cg, cg_out)

    pump(later)
    three = gather_steps(wire, w_out, chunk2, SPLIT)
    pump(three)
    drain(two)
    pump(three)
    loc.start(w1, w_out.at[:, pl.ds(0, SPLIT)])
    two = three

    def project_y(h):
        ni = act[:, :, :, pl.ds(0, DIM)].reshape(512, DIM)
        py_s[:, lanes(h)] = dot(ni, w1[:, column(nh + h)])

    many(nh, project_y)
    loc.start(py_s, py_out)
    pump(later)

    def mix(h):
        for g in range(4):
            r = pl.ds(128 * g, 128)
            hid = hid_s[r, lanes(h)] + cum_s[r, lanes(h)] * cin[pl.ds(g, 1), lanes(h)]
            hid_s[r, lanes(h)] = hid
            low_s[2, r, lanes(h)] = (hid * gelu(py_s[r, lanes(h)])).astype(bf16)

    many(nh, mix)
    loc.start(hid_s, hid_out)
    loc.start(low_s, low_out)
    loc.wait(own2)
    pump(two)

    drain(later)

    def project_out(n, heads):
        r = pl.ds(512 * n, 512)
        v = dot_nt(low_s[2, :, pl.ds(0, 256 * heads)], w1[r, pl.ds(128 + 512 * heads, 256 * heads)])
        part[:, :, :, r] = v.astype(bf16).reshape(4, 2, 64, 512)

    def project_piece(n):
        pl.when(x == 0)(lambda: project_out(n, 2))
        pl.when(x != 0)(lambda: project_out(n, 1))

    def add_resid(cols, r, total):
        resid[r, cols] = tok_ref[r, cols] + total

    drain(RowsScatter(wire, part, crecv, sums, r1, r2).steps(project_piece, add_resid))
    pump(two)
    loc.start(resid, resid_out)

    def norm(i):
        r = pl.ds(pl.multiple_of(i * 16, 16), 16)
        v = resid[r, :]
        inv = lax.rsqrt(jnp.mean(v * v, axis=-1, keepdims=True) + norm_eps)
        normed[r, :] = (v * inv * gain_ref[pl.ds(1, 1), :]).astype(bf16)

    many(4, norm)
    drain(rows_gather_steps(wire, normed, nm_out, loc))
    drain(two)
    wire.finish()
    loc.finish()


def vm(shape, dtype):
    return pltpu.VMEM(shape, dtype)


PLANE = ((1, 0), (3, 0), (0, 1), (0, 3))
ANY = pl.BlockSpec(memory_space=pl.ANY)
VM = pl.BlockSpec(memory_space=pltpu.VMEM)


def forward_call(p, n, cot, tok, gain, rec):
    S = jax.ShapeDtypeStruct
    R = (64, DIM)
    F = (512, 512)
    return pl.pallas_call(
        forward_kernel,
        name="recurrent_forward",
        out_shape=(
            S((DIM, COLS), bf16), S((4, 2, 64, EXT), bf16), S((4, 2) + R, bf16),
            S(F, f32), S(F, f32), S(F, f32), S(F, f32),
            S((3,) + F, bf16), S((16, 2, 8, 512), f32), S((4, 2) + R, bf16), S(R, f32),
        ),
        in_specs=[VM] * 6,
        out_specs=[ANY] * 11,
        scratch_shapes=[
            vm((4, 48, COLS), bf16), vm((160, COLS), f32), vm((160, FIRST), bf16), vm((160, SPLIT - FIRST), bf16), vm((160, COLS - SPLIT), bf16),
            vm((DIM, SPLIT), bf16), vm((4, 2, 64, EXT), bf16),
            vm(F, f32), vm(F, f32), vm(F, f32), vm(F, f32),
            vm((3,) + F, bf16), vm((4, 16, 512), bf16), vm(F, f32), vm((16, 2, 8, 512), f32), vm((8, 512), f32),
            vm((4, 2) + R, bf16), vm((4,) + R, bf16), vm((3,) + R, bf16), vm((2,) + R, bf16), vm((2,) + R, bf16),
            vm(R, bf16), vm(R, f32), vm(F, bf16), vm((2, 256, 512), bf16),
            pltpu.SemaphoreType.DMA((200,)), pltpu.SemaphoreType.DMA((200,)), pltpu.SemaphoreType.DMA((20,)),
        ],
        compiler_params=pltpu.CompilerParams(collective_id=0, has_side_effects=True, vmem_limit_bytes=60 << 20),
    )(p, n, cot, tok, gain, rec)


def transpose_rows(src, dst):
    def block(n):
        cols = pl.ds(pl.multiple_of(n * 256, 256), 256)
        dst[cols, :] = src[:, :, :, cols].reshape(512, 256).T

    many(10, block)


def add_sublanes(v):
    return v[:8] + v[8:]


def norm_back(total, value, gain):
    inv = lax.rsqrt(jnp.mean(value * value, axis=-1, keepdims=True) + norm_eps)
    xhat = value * inv
    weighted = total * gain
    inner = jnp.mean(weighted * xhat, axis=-1, keepdims=True)
    return inv * (weighted - xhat * inner), add_sublanes(total * xhat)


def ffn_kernel(
    w_ref, gl_ref, nm, resid, gain_ref,
    g_out, ahead_out, gm_out, gres_out, gain_out, first_out, second_out,
    gl, nmt, glt, wt, gfirst, gsecond, pre, lowi, lowg, parts, crecv, sums, r1, r2, normed, own_low, gsum,
    a2, a3, a4, a5, a6, a7, d2, d3, d4, d5, d6, d7,
    ss, rs, ls, ws, gs,
):
    place = Place()
    x, t = place.x, place.t
    wire, loc = Wire(place, ss, rs), Local(ls)
    nf = 5 - head_count(x)

    def load(j):
        return pltpu.make_async_copy(w_ref.at[:, triple(j)], wt.at[j], ws.at[j])

    def store(j):
        return pltpu.make_async_copy(wt.at[j], g_out.at[:, triple(j)], gs.at[j])

    glc = loc.start(gl_ref, gl)
    for j in range(3):
        load(j).start()
    pl.when(x != 0)(lambda: load(3).start())
    olc = loc.start(gl_ref.at[x, t], own_low)
    greet(place, xs=(1, -1), ctx=PLANE, core=True)
    transpose_rows(nm, nmt)
    loc.wait(glc)
    loc.wait(olc)
    transpose_rows(gl, glt)

    def tile(j):
        load(j).wait()
        pre[:, pl.ds(0, 512)] = dot(nm[...].reshape(512, DIM), wt[j, :, pl.ds(0, 512)])
        pre[:, pl.ds(512, 256)] = dot(gl[...].reshape(512, DIM), wt[j, :, pl.ds(512, 256)])

        def point(i):
            r = pl.ds(pl.multiple_of(i * 32, 32), 32)
            gated, slope = gelu_and_slope(pre[r, pl.ds(0, 256)])
            up, gi = pre[r, pl.ds(256, 256)], pre[r, pl.ds(512, 256)]
            lowi[j, r, :] = (gated * up).astype(bf16)
            lowg[j, r, pl.ds(0, 256)] = (gi * up * slope).astype(bf16)
            lowg[j, r, pl.ds(256, 256)] = (gi * gated).astype(bf16)

        many(16, point)

    def gradient(j, dst):
        def block(n):
            r = pl.ds(pl.multiple_of(n * 512, 512), 512)
            dst[r, pl.ds(0, 512)] = dot(nmt[r, :], lowg[j]).astype(bf16)
            dst[r, pl.ds(512, 256)] = dot(glt[r, :], lowi[j]).astype(bf16)

        many(5, block)

    tile(0)
    gradient(0, gfirst)
    first = scatter_steps(wire, loc, gfirst, 0, (None, None, a2, a3, a4, a5, a6, a7), first_out, False, True, False)
    pump(first, 1)
    tile(1)
    gradient(1, gsecond)
    second = scatter_steps(wire, loc, gsecond, 0, (None, None, d2, d3, d4, d5, d6, d7), second_out, False, True, False)
    pump(second, 1)
    many(nf - 2, lambda j: tile(j + 2))

    def contract(dst, low, cols, n):
        r = pl.ds(512 * n, 512)

        def total(count):
            v = dot_nt(low[0], wt[0, r, cols])
            for j in range(1, count):
                v = v + dot_nt(low[j], wt[j, r, cols])
            dst[:, :, :, r] = v.astype(bf16).reshape(4, 2, 64, 512)

        pl.when(x == 0)(lambda: total(3))
        pl.when(x != 0)(lambda: total(4))

    def keep_sum(cols, r, total):
        gsum[r, cols] = total

    back = RowsScatter(wire, parts, crecv, sums, r1, r2).steps(
        lambda n: contract(parts, lowg, pl.ds(0, 512), n), keep_sum
    )
    pump(first, 4)
    pump(back, 5)
    for n in range(5):
        contract(gl, lowi, pl.ds(512, 256), n)
        if n % 2 == 1:
            pump(back, 1)
    loc.start(gl, ahead_out)
    pump(first, 4)
    gradient(2, wt.at[2])
    store(2).start()
    drain(back)
    gain_out[...] = jnp.zeros_like(gain_out)

    def resid_back(i):
        r = pl.ds(pl.multiple_of(i * 16, 16), 16)
        gx, gain = norm_back(gsum[r, :], resid[r, :], gain_ref[pl.ds(1, 1), :])
        gr = own_low[r, :].astype(f32) + gx
        gres_out[r, :] = gr
        normed[r, :] = gr.astype(bf16)
        gain_out[...] += gain

    many(4, resid_back)
    rows = rows_gather_steps(wire, normed, gm_out, loc)
    pump(rows, 1)
    pump(second, 4)
    pump(rows, 1)

    @pl.when(x != 0)
    def _():
        gradient(3, wt.at[3])
        store(3).start()

    pump(rows, 1)
    pump(first, 1)
    drain(rows)
    pump(second, 4)
    pump(first, 1)
    pump(second, 1)
    drain(first)
    drain(second)
    store(2).wait()
    pl.when(x != 0)(lambda: store(3).wait())
    wire.finish()
    loc.finish()


def ffn_call(w, gl, nm, resid, gain):
    S = jax.ShapeDtypeStruct
    R = (64, DIM)
    slices = scatter_scratch(TRIPLE)[2:]
    return pl.pallas_call(
        ffn_kernel,
        name="feed_forward",
        out_shape=(
            S((DIM, COLS), bf16), S((4, 2) + R, bf16), S((4, 2) + R, bf16), S(R, f32), S((8, DIM), f32),
            S((4, 48, TRIPLE), bf16), S((4, 48, TRIPLE), bf16),
        ),
        in_specs=[ANY, ANY, VM, VM, VM],
        out_specs=[ANY, ANY, ANY, VM, VM, ANY, ANY],
        scratch_shapes=[
            vm((4, 2) + R, bf16), vm((DIM, 512), bf16), vm((DIM, 512), bf16), vm((4, DIM, TRIPLE), bf16), vm((DIM, TRIPLE), bf16), vm((DIM, TRIPLE), bf16),
            vm((512, TRIPLE), f32), vm((4, 512, 256), bf16), vm((4, 512, 512), bf16),
            vm((4, 2) + R, bf16), vm((4,) + R, bf16), vm((3,) + R, bf16), vm((2,) + R, bf16), vm((2,) + R, bf16),
            vm(R, bf16), vm(R, bf16), vm(R, f32),
        ] + slices + slices + [
            pltpu.SemaphoreType.DMA((170,)), pltpu.SemaphoreType.DMA((170,)), pltpu.SemaphoreType.DMA((12,)),
            pltpu.SemaphoreType.DMA((4,)), pltpu.SemaphoreType.DMA((4,)),
        ],
        compiler_params=pltpu.CompilerParams(collective_id=1, has_side_effects=True, vmem_limit_bytes=60 << 20),
    )(w, gl, nm, resid, gain)


def scatter_steps(wire, loc, g_ref, at, bufs, out_ref, gates, resident=False, spread=True):
    gvn, gvo, r1, r2, r3, r4, wide, obuf = bufs
    place = wire.place
    x, c = place.x, place.c
    width = wide.shape[1]
    mid = width // 256 * 128
    LO, HI, FULL = (0, mid), (mid, width), (0, width)
    zero = {1: LO, -1: HI}
    other = {1: HI, -1: LO}

    def cut(k):
        return pl.ds(k[0], k[1] - k[0])

    def short(k):
        return pl.ds(0, k[1] - k[0])

    def wide_cut(k):
        return pl.ds(at + k[0], k[1] - k[0])

    def group(h, d, k):
        return line_of(g_ref, place, h, d, wide_cut(k))

    def index(h, d, q):
        return q * 4 + lax.rem(place.z + d + 4, 4) if h == 0 else lax.rem(place.y + d + 4, 4) * 4 + q

    side = {1: 0, -1: 1}
    ends = {0: place.y, 1: place.z}
    st, loads = {}, {}

    class Piece:
        def __init__(self, h, d, k, ref):
            self.h, self.d, self.k, self.ref = h, d, k, ref

        def at(self, q, half):
            c0, c1 = self.k
            if half is not None:
                c0, c1 = (c0, mid) if half == 0 else (mid, c1)
            if resident:
                return g_ref, chunk_rows(index(self.h, self.d, q), self.h), wide_cut((c0, c1))
            return self.ref.at[q], pl.ds(0, 80), (short((c0, c1)) if self.d else cut((c0, c1)))

    def add_near(piece, got):
        def one(q):
            ref, r, cols = piece.at(q, None)
            ref[r, cols] = ref[r, cols] + got[q]

        many(4, one)

    def add_own(piece, srcs):
        def one(q):
            for half in (0, 1):
                ref, r, cols = piece.at(q, half)
                v = ref[r, cols].astype(f32)
                for s in srcs:
                    v = v + s[q, :, cut((LO, HI)[half])].astype(f32)
                ref[r, cols] = v.astype(bf16)

        many(4, one)

    def mine_at(h, q, k):
        if resident:
            return g_ref.at[chunk_rows(index(h, 0, q), h), wide_cut(k)]
        return gvo.at[h, q, :, cut(k)]

    for h in (0, 1):
        for d in (1, -1):
            k = zero[d]
            st[h, 1, d] = wire.send(group(h, 2, k), r1.at[h, side[d], :, :, short(k)], context=place.along(h, d, 0))
    if not resident:
        for h in (0, 1):
            for d in (1, -1):
                loads[h, d] = loc.start(group(h, d, zero[d]), gvn.at[h, side[d], :, :, short(zero[d])])
        for h in (0, 1):
            loads[h, 0] = loc.start(group(h, 0, FULL), gvo.at[h])
    for h in (0, 1):
        for d in (1, -1):
            k = other[d]
            st[h, 2, d] = wire.send(group(h, d, k), r2.at[h, side[d], :, :, cut(k)], context=place.along(h, d, 0))
    yield

    def add(dst, srcs):
        def one(i):
            r = pl.ds(pl.multiple_of(i * 16, 16), 16)
            v = srcs[0][r, :].astype(f32)
            for s in srcs[1:]:
                v = v + s[r, :].astype(f32)
            dst[r, :] = v.astype(dst.dtype)

        many(5, one)

    for h in (0, 1):
        for d in (1, -1):
            k = zero[d]
            if not resident:
                loc.wait(loads[h, d])
            got = r1.at[h, side[d], :, :, short(k)]
            wire.recv(st[h, 1, d], got)
            piece = Piece(h, d, k, None if resident else gvn.at[h, side[d]])
            add_near(piece, got)
            src = group(h, d, k) if resident else gvn.at[h, side[d], :, :, short(k)]
            st[h, 3, d] = wire.send(src, r2.at[h, side[d], :, :, cut(k)], context=place.along(h, d, 0))
            yield
    for h in (0, 1):
        if not resident:
            loc.wait(loads[h, 0])
        for d in (1, -1):
            wire.recv(st[h, 2, d], r2.at[h, side[d], :, :, cut(other[d])])
            wire.recv(st[h, 3, d], r2.at[h, side[d], :, :, cut(zero[d])])
        add_own(Piece(h, 0, FULL, None if resident else gvo.at[h]), [r2.at[h, 0], r2.at[h, 1]])
        far = lax.rem(ends[h] + 2, 4)
        for d in (1, -1):
            st[h, 4, d] = wire.send(
                mine_at(h, far, zero[d]), r3.at[h, side[d], :, short(zero[d])], context=place.along(h, 0, d)
            )
        for d in (1, -1):
            near = lax.rem(ends[h] + d + 4, 4)
            st[h, 5, d] = wire.send(
                mine_at(h, near, other[d]), r4.at[h, side[d], :, cut(other[d])], context=place.along(h, 0, d)
            )
        yield
        yield
    for h in (0, 1):
        for d in (1, -1):
            k = zero[d]
            mine = mine_at(h, lax.rem(ends[h] + d + 4, 4), k)
            got = r3.at[h, side[d], :, short(k)]
            wire.recv(st[h, 4, d], got)
            add(mine, [mine, got])
            st[h, 6, d] = wire.send(mine, r4.at[h, side[d], :, cut(k)], context=place.along(h, 0, d))
    yield
    for h in (0, 1):
        for d in (1, -1):
            wire.recv(st[h, 5, d], r4.at[h, side[d], :, cut(other[d])])
            wire.recv(st[h, 6, d], r4.at[h, side[d], :, cut(zero[d])])
        add(wide.at[pl.ds(80 * h, 80), :], [mine_at(h, ends[h], FULL), r4.at[h, 0], r4.at[h, 1]])
    for k in range(4):
        obuf[k] = jnp.concatenate([wide[pl.ds(40 * k, 40), :], jnp.zeros((8, width), f32)], axis=0).astype(bf16)
        if gates:
            tail = jnp.concatenate([wide[pl.ds(32 * b + 8 * k, 8), pl.ds(0, 128)] for b in range(4)], axis=1)
            obuf[k, :, pl.ds(0, 512)] = jnp.concatenate([wide[pl.ds(40 * k, 40), pl.ds(0, 512)], tail], axis=0).astype(bf16)
    if not spread:
        own = loc.start(obuf, out_ref)
        yield
        loc.wait(own)
        yield
        return
    sent = [(d, wire.send(obuf.at[place.xs(d)], out_ref.at[x], fsdp=place.xs(d))) for d in (1, 3, 2)]
    own = loc.start(obuf.at[x], out_ref.at[x])
    yield
    for d, n in sent:
        wire.recv(n, out_ref.at[place.xs(-d)])
    loc.wait(own)
    yield


def scatter_scratch(width):
    hi = width - width // 256 * 128
    return [
        vm((2, 2, 4, 80, hi), bf16), vm((2, 4, 80, width), bf16), vm((2, 2, 4, 80, hi), bf16), vm((2, 2, 4, 80, width), bf16),
        vm((2, 2, 80, hi), bf16), vm((2, 2, 80, width), bf16), vm((160, width), f32), vm((4, 48, width), bf16),
    ]


def small_steps(wire, mine, zin, yin, xin, corein):
    place = wire.place
    x = place.x
    ns = [wire.send(mine.at[0], zin.at[d - 1], context=place.ctx(0, d)) for d in (1, 2, 3)]
    yield
    for d, n in zip((1, 2, 3), ns):
        wire.recv(n, zin.at[d - 1])
    mine[1] = mine[0] + zin[0] + zin[1] + zin[2]
    ns = [wire.send(mine.at[1], yin.at[d - 1], context=place.ctx(d, 0)) for d in (1, 2, 3)]
    yield
    for d, n in zip((1, 2, 3), ns):
        wire.recv(n, yin.at[d - 1])
    total = mine[1] + yin[0] + yin[1] + yin[2]
    mine[2] = total
    xin[x] = total
    ns = [wire.send(mine.at[2], xin.at[x], fsdp=place.xs(d)) for d in (1, 2, 3)]
    yield
    for d, n in zip((1, 2, 3), ns):
        wire.recv(n, xin.at[place.xs(-d)])
    mine[3] = xin[0] + xin[1] + xin[2] + xin[3]
    n = wire.send(mine.at[3], corein, tensor=1 - place.t)
    yield
    wire.recv(n, corein)
    yield


def fold(dst, row, at):
    for i in range(20):
        dst[pl.ds(i // 3, 1), pl.ds(at + 128 * (i % 3), 128)] = row[:, 128 * i : 128 * i + 128]


def backward_kernel(
    g_ref, w_ref, act_ref, gm_ref, first_ref, second_ref, ahead_ref,
    lx_ref, la_ref, hid_ref, py_ref, low_ref, cg, tok_ref, gres, resid, gain_ref, rec_ref, gain_two,
    t0_out, t1_out, t2_out, mid_out, last_out, mixed_out, tgrad_out, recur_out, gains_out,
    a0, a1, a2, a3, a4, a5, a6, a7, b2, b3, b4, b5, b6, b7, c2, c3, c4, c5, c6, c7,
    w1, acts, turned, flag_s, gmx, gpy, bc, bp, bg, cin, cback, glow, edge, edge_in, edge_out, gpx, gates, packed, dgates,
    gain_acc, crecv, sums, r1, r2, own_f, crecv_f, sums_f, r1_f, r2_f,
    small, zin, yin, xin, corein, late, zin_l, yin_l, xin_l, corein_l,
    lx_s, la_s, hid_s, py_s, low_s, glast,
    ss, rs, ls, ws,
):
    part, gconv, gdir = acts, gmx, bc
    place = Place()
    x, c, t = place.x, place.c, place.t
    wire, loc = Wire(place, ss, rs), Local(ls)
    nh = head_count(x)
    rest = pl.ds(FIRST + 256, TRIPLE)
    both = pl.ds(0, FIRST + 256)
    lg = loc.start(gm_ref, acts)
    lw = loc.start(w_ref.at[:, both], w1.at[:, both])
    load_w = pltpu.make_async_copy(w_ref.at[:, rest], w1.at[:, rest], ws.at[0])
    load_g = pltpu.make_async_copy(g_ref.at[:, rest], w1.at[:, rest], ws.at[1])
    pl.when(x == 0)(lambda: load_w.start())
    pl.when(x != 0)(lambda: load_g.start())
    lf = loc.start(act_ref.at[:, :, :, pl.ds(DIM, 128)], flag_s)
    li = [loc.start(a, b) for a, b in ((low_ref, low_s), (py_ref, py_s), (hid_ref, hid_s), (la_ref, la_s), (lx_ref, lx_s))]
    lo = loc.start(ahead_ref.at[:, t], own_f)
    greet(place, xs=(1, 2, 3), ctx=((1, 0), (2, 0), (3, 0), (0, 1), (0, 2), (0, 3)), chain=(1, -1), core=True)
    big = scatter_steps(wire, loc, g_ref, SPLIT + 2 * TRIPLE, (a0, a1, a2, a3, a4, a5, a6, a7), t2_out, False)
    pump(big, 1)

    def keep_mixed(cols, r, total):
        mixed_out[t, r, cols] = (resid[r, cols] + total).astype(bf16)

    ahead = RowsScatter(wire, ahead_ref, crecv_f, sums_f, r1_f, r2_f, own=own_f).steps(lambda n: None, keep_mixed)
    fro = []
    for src, dst in ((first_ref, t0_out), (second_ref, t1_out)):
        for d in (2, 1, 3):
            fro.append((d, dst, wire.send(src.at[place.xs(d)], dst.at[x], fsdp=place.xs(d))))
        loc.start(src.at[x], dst.at[x])
    for copy in li:
        loc.wait(copy)
    before = low_s.at[0].reshape(4, 128, 512)
    hn = wire.send(before.at[:, pl.ds(112, 16), :], edge_in, context=place.chain(1))
    loc.wait(lg)
    loc.wait(lw)
    loc.wait(lf)
    loc.wait(lo)
    pl.when(x == 0)(lambda: load_w.wait())
    pl.when(x != 0)(lambda: load_g.wait())
    for cc in range(16):
        for b in range(4):
            packed[pl.ds(32 * cc, 32), pl.ds(128 * b, 128)] = w1[pl.ds(160 * cc + 32 * b, 32), pl.ds(0, 128)]
    small[...] = jnp.zeros_like(small)
    late[...] = jnp.zeros_like(late)
    fold(small.at[0], jnp.sum(gain_two[...], axis=0, keepdims=True), 512)

    def flags(g, k):
        return flag_s[pl.ds(g, 1)].reshape(128, 128).astype(f32)[:, k : k + 1]

    def put_tile(rhs, dst, cols):
        def block(n):
            r = pl.ds(pl.multiple_of(n * 512, 512), 512)
            dst[r, cols] = dot(turned[r, :], rhs).astype(bf16)

        many(5, block)

    def mixed_back(h):
        gmx[:, lanes(h)] = dot(acts[...].reshape(512, DIM), w1[:, column(2 * nh + h)])

    many(nh, mixed_back)

    bg[c] = jnp.zeros((8, 512), f32)

    def scan(q):
        cols = pl.ds(pl.multiple_of(q * 128, 128), 128)
        for g in range(4):
            r = pl.ds(128 * g, 128)
            gated, slope = gelu_and_slope(py_s[r, cols])
            grad = gmx[r, cols]
            gpy[r, cols] = (grad * hid_s[r, cols] * slope).astype(bf16)
            keep = flags(g, 1)
            dec = jnp.exp((-gate_scale) * sigmoid(la_s[r, cols]) * rec_ref[pl.ds(7, 1), cols]) * keep
            last = lax.broadcasted_iota(jnp.int32, dec.shape, 0) == 127
            a, b = scan_up(jnp.where(last, 1.0, pltpu.roll(dec, 127, 0)), grad * gated)
            bc[r, cols] = a
            bp[r, cols] = b
            bg[c, pl.ds(g, 1), cols] = dec[:1] * b[:1]

    many(2 * nh, scan)
    ns = [wire.send(bg.at[c], bg.at[c], context=place.ctx(0, d)) for d in (1, 2, 3)]
    pump(ahead, 2)
    transpose_rows(acts, turned)
    ln = loc.start(act_ref.at[:, :, :, pl.ds(0, DIM)], acts)

    many(nh, lambda h: put_tile(low_s[2, :, lanes(h)], w1, column(2 * nh + h)))
    pump(ahead, 2)
    pump(big, 4)
    for d, n in zip((1, 2, 3), ns):
        wire.recv(n, bg.at[place.ctx(0, -d)])
    line = pl.ds(place.y * 4, 4)
    ns = [wire.send(bg.at[line], bg.at[line], context=place.ctx(d, 0)) for d in (1, 2, 3)]
    for g in (0, 1):
        gates[g] = gate_matrix(packed[...], g)
    loc.wait(ln)
    transpose_rows(acts, turned)

    def norm_grad_y(heads):
        def block(n):
            r = pl.ds(pl.multiple_of(n * 512, 512), 512)
            v = dot_nt(gpy[:, pl.ds(0, 256 * heads)], w1[r, pl.ds(128 + 256 * heads, 256 * heads)])
            part[:, :, :, r] = v.astype(bf16).reshape(4, 2, 64, 512)

        many(5, block)

    pl.when(x == 0)(lambda: norm_grad_y(2))
    pl.when(x != 0)(lambda: norm_grad_y(1))
    pl.when(x == 0)(lambda: many(2, lambda h: put_tile(gpy[:, lanes(h)], w1, column(2 + h))))
    pl.when(x != 0)(lambda: put_tile(gpy[:, pl.ds(0, 256)], glast, pl.ds(384, 256)))
    mid = scatter_steps(wire, loc, w1, FIRST, (None, None, b2, b3, b4, b5, b6, b7), mid_out, False, True)
    pump(mid, 1)
    pump(ahead, 2)
    for d, n in zip((1, 2, 3), ns):
        wire.recv(n, bg.at[pl.ds(lax.rem(place.y + 4 - d, 4) * 4, 4)])

    def enter(s, state):
        return cg[s, 0] * state + cg[s, 1]

    cin[...] = lax.fori_loop(0, c, enter, jnp.zeros((8, 512), f32))

    def leave(s, state):
        k = 15 - s
        return cg[k, 0] * state + bg[k]

    cback[...] = lax.fori_loop(0, 15 - c, leave, jnp.zeros((8, 512), f32))
    def terms(q):
        cols = pl.ds(pl.multiple_of(q * 128, 128), 128)
        sums_x = jnp.zeros((1, 128), f32)
        sums_a = jnp.zeros((1, 128), f32)
        sums_l = jnp.zeros((1, 128), f32)
        for g in range(4):
            r = pl.ds(128 * g, 128)
            keep = flags(g, 1)
            cl = low_s[1, r, cols].astype(f32)
            sp, dsp = rec_ref[pl.ds(7, 1), cols], rec_ref[pl.ds(8, 1), cols]
            sx, sa, log_decay, root, factor = recur_terms(lx_s[r, cols], la_s[r, cols], cl, sp, keep)
            adj = bp[r, cols] + bc[r, cols] * cback[pl.ds(g, 1), cols]
            hid = hid_s[r, cols]
            first = lax.broadcasted_iota(jnp.int32, hid.shape, 0) == 0
            prev = jnp.where(first, cin[pl.ds(g, 1), cols], pltpu.roll(hid, 1, 0))
            grown = jnp.exp(log_decay)
            gld = keep * grown * (adj * prev - adj * sx * cl * grown / root)
            glx = (adj * factor * cl * sx * (1.0 - sx)).astype(bf16)
            gla = (gld * ((-gate_scale) * sp) * sa * (1.0 - sa)).astype(bf16)
            glow[0, r, cols] = glx
            glow[1, r, cols] = gla
            gdir[r, cols] = adj * factor * sx
            sums_x += jnp.sum(glx.astype(f32), axis=0, keepdims=True)
            sums_a += jnp.sum(gla.astype(f32), axis=0, keepdims=True)
            sums_l += jnp.sum(gld * sa, axis=0, keepdims=True) * (gate_scale * dsp)
        small[0, pl.ds(5, 1), cols] = sums_x
        small[0, pl.ds(6, 1), cols] = sums_a
        small[0, pl.ds(7, 1), cols] = sums_l

    many(2 * nh, terms)
    wire.recv(hn, edge_in)

    def conv_back(h):
        cl = low_s[1, :, lanes(h)]
        lx, la = glow[0, :, lanes(h)], glow[1, :, lanes(h)]
        gconv[:, lanes(h)] = (
            gdir[:, lanes(h)] + dot_nt(lx, gates[0, :, lanes(h)]) + dot_nt(la, gates[1, :, lanes(h)])
        )

        def group(g, taps):
            gc = gconv[token_rows(g), lanes(h)]
            bx = low_s[0, token_rows(g), lanes(h)].astype(f32)
            ahead = edge_in[g, :, lanes(h)].astype(f32)[8:]
            rows = lax.broadcasted_iota(jnp.int32, gc.shape, 0)
            low_rows = lax.broadcasted_iota(jnp.int32, (8, 256), 0)
            out = rec_ref[pl.ds(0, 1), lanes(h)] * gc
            over = jnp.zeros((8, 256), f32)
            new = [taps[0] + jnp.sum(bx * gc, axis=0, keepdims=True)]
            for k in (1, 2, 3):
                masked = flags(g, 1 + k) * gc
                new.append(taps[k] + jnp.sum(shifted(bx, ahead, k) * masked, axis=0, keepdims=True))
                scaled = rec_ref[pl.ds(k, 1), lanes(h)] * masked
                out = out + jnp.where(rows < 128 - k, pltpu.roll(scaled, 128 - k, 0), 0.0)
                over = over + jnp.where(low_rows >= 8 - k, pltpu.roll(scaled[:8], 8 - k, 0), 0.0)
            new.append(taps[4] + jnp.sum(gc, axis=0, keepdims=True))
            gdir[token_rows(g), lanes(h)] = out
            edge[g, :, lanes(h)] = over
            return tuple(new)

        taps = lax.fori_loop(0, 4, group, tuple(jnp.zeros((1, 256), f32) for _ in range(5)))
        for k in range(5):
            small[0, pl.ds(k, 1), lanes(h)] = taps[k]

    many(nh, conv_back)
    en = wire.send(edge, edge_out, context=place.chain(-1))

    early = small_steps(wire, small, zin, yin, xin, corein)
    pump(early)
    pump(big, 4)
    pump(ahead, 2)

    def gate_back(h):
        cl = low_s[1, :, lanes(h)]
        dgates[0, :, lanes(h)] = dot_tn(cl, glow[0, :, lanes(h)]).astype(bf16)
        dgates[1, :, lanes(h)] = dot_tn(cl, glow[1, :, lanes(h)]).astype(bf16)

    many(nh, gate_back)
    wire.recv(en, edge_out)

    def narrow(h):
        for g in range(4):
            v = gdir[pl.ds(128 * g, 128), lanes(h)]
            tail = v[120:] + edge_out[g, :, lanes(h)]
            gpx[pl.ds(128 * g, 128), lanes(h)] = jnp.concatenate([v[:120], tail], axis=0).astype(bf16)

    many(nh, narrow)

    def norm_grad(n, heads):
        r = pl.ds(512 * n, 512)
        v = dot_nt(gpx[:, pl.ds(0, 256 * heads)], w1[r, pl.ds(128, 256 * heads)])
        v = v + part[:, :, :, r].reshape(512, 512).astype(f32)
        part[:, :, :, r] = v.astype(bf16).reshape(4, 2, 64, 512)

    def norm_piece(n):
        pl.when(x == 0)(lambda: norm_grad(n, 2))
        pl.when(x != 0)(lambda: norm_grad(n, 1))

    def keep_sum(cols, r, total):
        tgrad_out[t, r, cols] = total

    pump(mid, 4)
    many(nh, lambda h: put_tile(gpx[:, lanes(h)], glast, column(h)))
    back = (dot_tn(selector(0), dgates[0]) + dot_tn(selector(1), dgates[1])).astype(bf16)
    glast[:, pl.ds(0, 128)] = jnp.zeros((DIM, 128), bf16)
    for cc in range(16):
        for b in range(4):
            glast[pl.ds(160 * cc + 32 * b, 32), pl.ds(0, 128)] = back[32 * cc : 32 * cc + 32, 128 * b : 128 * b + 128]
    last = scatter_steps(wire, loc, glast, 0, (None, None, c2, c3, c4, c5, c6, c7), last_out, True, True)
    pump(last, 1)
    final = RowsScatter(wire, part, crecv, sums, r1, r2).steps(norm_piece, keep_sum)
    pump(final, 5)
    pump(early)
    pump(big, 1)
    pump(final, 1)
    pump(last, 4)
    pump(early)
    pump(final, 1)
    drain(final)
    gain_acc[...] = jnp.zeros_like(gain_acc)

    def finish(i):
        r = pl.ds(pl.multiple_of(i * 16, 16), 16)
        gx, gain = norm_back(tgrad_out[t, r, :], tok_ref[r, :], gain_ref[pl.ds(0, 1), :])
        tgrad_out[t, r, :] = gres[r, :] + gx
        gain_acc[...] += gain

    many(4, finish)
    tn = wire.send(tgrad_out.at[t], tgrad_out.at[t], tensor=1 - t)
    fold(late.at[0], jnp.sum(gain_acc[...], axis=0, keepdims=True), 0)
    tail = small_steps(wire, late, zin_l, yin_l, xin_l, corein_l)
    pump(tail)
    pump(mid, 4)
    pump(early)
    pump(tail)
    pump(last, 4)
    pump(big, 1)
    pump(tail)
    pump(mid, 1)
    pump(early)
    pump(last, 1)
    pump(tail)
    drain(ahead)
    mn = wire.send(mixed_out.at[t], mixed_out.at[t], tensor=1 - t)
    pump(mid, 1)
    pump(last, 1)
    drain(big)
    drain(mid)
    drain(tail)
    drain(early)
    for k in range(4):
        recur_out[k] = xin[k, :, pl.ds(0, 512)]
    gains_out[0] = late[3] + corein_l[...]
    gains_out[1] = small[3, :, pl.ds(512, 384)] + corein[:, pl.ds(512, 384)]
    drain(last)
    for d, dst, n in fro:
        wire.recv(n, dst.at[place.xs(-d)])
    wire.recv(mn, mixed_out.at[1 - t])
    wire.recv(tn, tgrad_out.at[1 - t])
    wire.finish()
    loc.finish()


def backward_call(g, w, act, gm, first, second, ahead, lx, la, hid, py, low, cg, tok, gres, resid, gain, rec, gain_two):
    S = jax.ShapeDtypeStruct
    R = (64, DIM)
    F = (512, 512)
    E, L = (8, 896), (8, 384)
    slices = lambda n: S((4, 48, n), bf16)
    return pl.pallas_call(
        backward_kernel,
        name="recurrent_backward",
        out_shape=(
            slices(TRIPLE), slices(TRIPLE), slices(TRIPLE), slices(SPLIT - FIRST), slices(FIRST),
            S((2,) + R, bf16), S((2,) + R, f32), S((4, 8, 512), f32), S((2,) + L, f32),
        ),
        in_specs=[ANY] * 12 + [VM] * 7,
        out_specs=[ANY, ANY, ANY, ANY, ANY, VM, VM, VM, VM],
        scratch_shapes=scatter_scratch(TRIPLE) + scatter_scratch(SPLIT - FIRST)[2:] + scatter_scratch(FIRST)[2:] + [
            vm((DIM, SPLIT), bf16), vm((4, 2) + R, bf16), vm((DIM, 512), bf16), vm((4, 2, 64, 128), bf16),
            vm(F, f32), vm(F, bf16), vm(F, f32), vm(F, f32), vm((16, 8, 512), f32), vm((8, 512), f32), vm((8, 512), f32),
            vm((2,) + F, bf16), vm((4, 8, 512), f32), vm((4, 16, 512), bf16), vm((4, 8, 512), f32), vm(F, bf16),
            vm((2, 256, 512), bf16), vm(F, bf16), vm((2, 256, 512), bf16), vm((8, DIM), f32),
            vm((4,) + R, bf16), vm((3,) + R, bf16), vm((2,) + R, bf16), vm((2,) + R, bf16),
            vm((4,) + R, bf16), vm((4,) + R, bf16), vm((3,) + R, bf16), vm((2,) + R, bf16), vm((2,) + R, bf16),
            vm((4,) + E, f32), vm((3,) + E, f32), vm((3,) + E, f32), vm((4,) + E, f32), vm(E, f32),
            vm((4,) + L, f32), vm((3,) + L, f32), vm((3,) + L, f32), vm((4,) + L, f32), vm(L, f32),
            vm(F, f32), vm(F, f32), vm(F, f32), vm(F, f32), vm((3,) + F, bf16), vm((DIM, FIRST), bf16),
            pltpu.SemaphoreType.DMA((310,)), pltpu.SemaphoreType.DMA((310,)), pltpu.SemaphoreType.DMA((60,)),
            pltpu.SemaphoreType.DMA((2,)),
        ],
        compiler_params=pltpu.CompilerParams(collective_id=2, has_side_effects=True, vmem_limit_bytes=62 << 20),
    )(g, w, act, gm, first, second, ahead, lx, la, hid, py, low, cg, tok, gres, resid, gain, rec, gain_two)


HEAD_START = (0, 2, 3, 4)
HEADS_OF = (2, 1, 1, 1)
FF_START = (0, 768, 1792, 2816)
TILE_ORDER = ((0, 1, 2), (3, 0, 1, 2), (3, 0, 1, 2), (3, 0, 1, 2))


def adam_update(weight, moment, square, gradient, rate, shrink):
    moment = beta_one * moment + (1.0 - beta_one) * gradient
    square = beta_two * square + (1.0 - beta_two) * gradient * gradient
    normed = (moment * (1.0 / (1.0 - beta_one**STEP))) / (jnp.sqrt(square * (1.0 / (1.0 - beta_two**STEP))) + adam_eps)
    return (weight - rate * (normed + shrink * weight), moment, square)


def restored_tile(get, q, shape):
    lane = lax.broadcasted_iota(jnp.int32, shape, len(shape) - 1)
    out = jnp.zeros(shape, f32)
    at = 128 * q
    while at < 128 * q + 128:
        m = at // 40
        source = 40 * (4 * (m % 16) + m // 16) + at - 40 * m
        p = source // 128
        stop = min(40 * m + 40, 128 * q + 128, at + 128 * p + 128 - source)
        turn = (at - 128 * q - (source - 128 * p)) % 128
        v = get(p)
        if turn:
            v = pltpu.roll(v, turn, len(shape) - 1)
        out = jnp.where((lane >= at - 128 * q) & (lane < stop - 128 * q), v, out)
        at = stop
    return out


def update_kernel(
    last, mid, t0, t1, t2, recur, gains, mixed, tgrad, *refs,
):
    params, outs = refs[:21], refs[21:]
    mixed_out, tgrad_out = outs[:2]

    def group(n):
        return params[3 * n : 3 * n + 3], outs[2 + 3 * n : 5 + 3 * n]

    def update(n, index, grad, rate=matrix_rate, shrink=weight_decay):
        old, new = group(n)
        values = adam_update(*(ref[index] for ref in old), grad, rate, shrink)
        for ref, value in zip(new, values):
            ref[index] = value

    def piece(k, tile):
        if tile < 2:
            ref, at = last, 128 + 256 * tile
        elif tile < 6:
            ref, at = mid, 256 * (tile - 2)
        else:
            ref, at = (t0, t1, t2)[(tile - 6) // 3], 256 * ((tile - 6) % 3)
        return ref[k, :, pl.ds(at, 256)].astype(f32)

    for k in range(4):
        for h in range(HEADS_OF[k]):
            nh = HEADS_OF[k]
            at = 256 * (HEAD_START[k] + h)
            update(2, (0, slice(None), pl.ds(at, 256)), piece(k, h)[:40])
            update(2, (1, slice(None), pl.ds(at, 256)), piece(k, nh + h)[:40])
            update(4, (slice(None), pl.ds(at, 256)), piece(k, 2 * nh + h)[:40])
            b = last[k, :, pl.ds(256 * h, 256)].astype(f32)[40:]
            for g in (0, 1):
                update(3, (g, HEAD_START[k] + h), b[4 * g : 4 * g + 4])
        for j in TILE_ORDER[k]:
            tile = 3 if j == 3 else 6 + 3 * j
            at = FF_START[k] + 256 * j
            update(5, (0, slice(None), pl.ds(at, 256)), piece(k, tile)[:40])
            update(5, (1, slice(None), pl.ds(at, 256)), piece(k, tile + 1)[:40])
            update(6, (slice(None), pl.ds(at, 256)), piece(k, tile + 2)[:40])
        n = 256 * HEADS_OF[k]
        update(1, (slice(None), pl.ds(256 * HEAD_START[k], n)), recur[k, :, pl.ds(0, n)], vector_rate, 0.0)

    for n in (0, 1):
        for q in range(20):
            grad = restored_tile(lambda p: gains[n, pl.ds(p // 3, 1), pl.ds(128 * (p % 3), 128)], q, (1, 128))
            update(0, (pl.ds(n, 1), pl.ds(128 * q, 128)), grad, vector_rate, 0.0)

    def restore(i):
        t = i // 4
        r = pl.ds(pl.multiple_of((i % 4) * 16, 16), 16)
        dst = pl.ds(pl.multiple_of(i * 16, 16), 16)
        for q in range(20):
            cols = pl.ds(128 * q, 128)
            mixed_out[dst, cols] = restored_tile(lambda p: mixed[t, r, pl.ds(128 * p, 128)].astype(f32), q, (16, 128)).astype(bf16)
            tgrad_out[dst, cols] = restored_tile(lambda p: tgrad[t, r, pl.ds(128 * p, 128)], q, (16, 128))

    many(8, restore)


def update_call(pieces, recur, gains, mixed, tgrad, params):
    shapes = [jax.ShapeDtypeStruct(v.shape, v.dtype) for v in params]
    outs = [jax.ShapeDtypeStruct((128, DIM), bf16), jax.ShapeDtypeStruct((128, DIM), f32)] + shapes
    return pl.pallas_call(
        update_kernel,
        name="optimizer_step",
        out_shape=tuple(outs),
        in_specs=[VM] * (9 + len(params)),
        out_specs=tuple([VM] * len(outs)),
        compiler_params=pltpu.CompilerParams(vmem_limit_bytes=56 << 20),
    )(*pieces, recur, gains, mixed, tgrad, *params)


def permuted(a):
    return a.reshape(a.shape[:-1] + (4, 16, 40)).swapaxes(-3, -2).reshape(a.shape)


def restored(a):
    return a.reshape(a.shape[:-1] + (16, 4, 40)).swapaxes(-3, -2).reshape(a.shape)


def pack_weights(input_proj, gate_blocks, output_proj, inner_proj, down_proj):
    inp, out = input_proj.astype(bf16), output_proj.astype(bf16).T
    inner, down, blocks = inner_proj.astype(bf16), down_proj.astype(bf16).T, gate_blocks.astype(bf16)
    packs = []
    for k in range(4):
        hs = slice(HEAD_START[k] * 256, (HEAD_START[k] + HEADS_OF[k]) * 256)
        main = [jnp.zeros((40, 128), bf16), inp[0][:, hs], inp[1][:, hs], out[:, hs]]
        for j in TILE_ORDER[k]:
            f = slice(FF_START[k] + 256 * j, FF_START[k] + 256 * j + 256)
            main += [inner[0][:, f], inner[1][:, f], down[:, f]]
        main = jnp.concatenate(main, axis=1)
        g = blocks[:, HEAD_START[k] : HEAD_START[k] + HEADS_OF[k]].swapaxes(1, 2).reshape(8, HEADS_OF[k] * 256)
        packs.append(jnp.concatenate([main, jnp.pad(g, ((0, 0), (0, COLS - g.shape[1])))], axis=0))
    return jnp.stack(packs)


def token_flags(seq_lengths, rows, first):
    place = first + lax.broadcasted_iota(jnp.int32, (rows, 128), 0)
    lane = lax.broadcasted_iota(jnp.int32, (rows, 128), 1)
    ends = [seq_lengths[0, 0]]
    for k in (1, 2):
        ends.append(ends[-1] + seq_lengths[0, k])

    def segment(p):
        return sum((p >= e).astype(jnp.int32) for e in ends)

    here = segment(place)
    fresh = place == 0
    for e in ends:
        fresh = fresh | (place == e)
    back = place - (lane - 1)
    same = (segment(back) == here) & (back >= 0) & (lane < 5)
    flag = jnp.where(lane == 0, here < 3, jnp.where(lane == 1, ~fresh, same))
    return flag.astype(f32)


def prepare(tokens, cotangent, seq_lengths, norm_gains, recur_params, weights):
    x, t = lax.axis_index("fsdp"), lax.axis_index("tensor")
    flags = token_flags(seq_lengths, 64, lax.axis_index("context") * 128 + t * 64)
    tok = permuted(lax.dynamic_slice_in_dim(tokens, t * 64, 64, 0)).astype(f32)
    cot = permuted(lax.dynamic_slice_in_dim(cotangent, t * 64, 64, 0))
    gains = permuted(norm_gains)
    inv = lax.rsqrt(jnp.mean(tok * tok, axis=-1, keepdims=True) + norm_eps)
    normed = (tok * inv * gains[0]).astype(bf16)
    low = (cot.astype(f32) * flags[:, :1]).astype(bf16)
    normed = jnp.concatenate([normed, flags.astype(bf16)], axis=1)
    start = jnp.where(x == 0, 0, x + 1) * 256
    rec = lax.dynamic_slice_in_dim(jnp.pad(recur_params, ((0, 0), (0, 256))), start, 512, 1)
    rec = jnp.concatenate([rec[:7], jax.nn.softplus(-rec[7:]), jax.nn.sigmoid(-rec[7:]), jnp.zeros((7, 512), f32)], axis=0)
    return pack_weights(*weights), normed, low, tok, gains, rec


def on_device(
    tokens, cotangent, seq_lengths,
    norm_gains, gains_moment, gains_square, recur_params, recur_moment, recur_square,
    input_proj, input_moment, input_square, gate_blocks, blocks_moment, blocks_square,
    output_proj, output_moment, output_square, inner_proj, inner_moment, inner_square,
    down_proj, down_moment, down_square,
):
    p, normed, cot, tok, gains, rec = prepare(
        tokens, cotangent, seq_lengths, norm_gains, recur_params,
        (input_proj, gate_blocks, output_proj, inner_proj, down_proj),
    )
    w, act, gl, lx, la, hid, py, low, cg, nm, resid = forward_call(p, normed, cot, tok, gains, rec)
    g, ahead, gm, gres, gain_two, first, second = ffn_call(w, gl, nm, resid, gains)
    t0, t1, t2, mid, last, mixed, tgrad, recur, gsum = backward_call(
        g, w, act, gm, first, second, ahead, lx, la, hid, py, low, cg, tok, gres, resid, gains, rec, gain_two
    )
    params = (
        norm_gains, gains_moment, gains_square, recur_params, recur_moment, recur_square,
        input_proj, input_moment, input_square, gate_blocks, blocks_moment, blocks_square,
        output_proj.T, output_moment.T, output_square.T, inner_proj, inner_moment, inner_square,
        down_proj.T, down_moment.T, down_square.T,
    )
    out = update_call((last, mid, t0, t1, t2), recur, gsum, mixed, tgrad, params)
    return out[:14] + tuple(v.T for v in out[14:17]) + out[17:20] + tuple(v.T for v in out[20:])


def solution(mesh):
    row = P(("fsdp", "context"), None)
    wide_spec = P(None, ("fsdp", "context"), "tensor")
    tall = P("tensor", ("fsdp", "context"))
    block = P(None, "tensor", ("fsdp", "context"), None)
    params = (P(),) * 3 + (P(None, "tensor"),) * 3 + (wide_spec,) * 3 + (block,) * 3 + (tall,) * 3 + (wide_spec,) * 3 + (tall,) * 3
    return jax.shard_map(
        on_device, mesh=mesh, in_specs=(row, row, P("fsdp", None)) + params, out_specs=(row, row) + params, check_vma=False
    )
```

```python
import functools

import jax
import jax.numpy as jnp
from jax import lax
from jax.experimental import pallas as pl
from jax.experimental.pallas import tpu as pltpu
from jax.sharding import PartitionSpec as P

STEP = 10

norm_eps = 1e-06
beta_one = 0.9
beta_two = 0.95
adam_eps = 1e-08
weight_decay = 0.1
matrix_rate = 0.06
vector_rate = 1.0
gate_scale = 8.0

bf16, f32 = jnp.bfloat16, jnp.float32
MESH = pl.DeviceIdType.MESH
DIM = 2560
COLS = 3968
FIRST, SPLIT = 640, 1664
TRIPLE = 768
EXT = 2560 + 128
NT = (((1,), (1,)), ((), ()))
TN = (((0,), (0,)), ((), ()))


def dot(a, b):
    return jnp.dot(a, b, preferred_element_type=f32)


def dot_nt(a, b):
    return lax.dot_general(a, b, NT, preferred_element_type=f32)


def dot_tn(a, b):
    return lax.dot_general(a, b, TN, preferred_element_type=f32)


def many(n, fn):
    def one(i, carry):
        fn(i)
        return carry

    lax.fori_loop(0, n, one, 0)


class Place:
    def __init__(self):
        self.x = lax.axis_index("fsdp")
        self.c = lax.axis_index("context")
        self.t = lax.axis_index("tensor")
        self.y, self.z = lax.div(self.c, 4), lax.rem(self.c, 4)

    def ctx(self, dy, dz):
        return lax.rem(self.y + dy + 4, 4) * 4 + lax.rem(self.z + dz + 4, 4)

    def xs(self, d):
        return lax.rem(self.x + d + 4, 4)

    def along(self, half, d1, d2):
        return self.ctx(d2, d1) if half == 0 else self.ctx(d1, d2)

    def chain(self, d):
        return lax.rem(self.c + d + 16, 16)


class Wire:
    def __init__(self, place, ss, rs):
        self.place, self.ss, self.rs = place, ss, rs
        self.n, self.sent = 0, []

    def send(self, src, dst, **to):
        n = self.n
        self.n += 1
        copy = pltpu.make_async_remote_copy(
            src_ref=src, dst_ref=dst, send_sem=self.ss.at[n], recv_sem=self.rs.at[n],
            device_id=to, device_id_type=MESH,
        )
        copy.start()
        self.sent.append(copy)
        return n

    def recv(self, n, ref):
        pltpu.make_async_remote_copy(
            src_ref=ref, dst_ref=ref, send_sem=self.ss.at[n], recv_sem=self.rs.at[n],
            device_id={"fsdp": self.place.x}, device_id_type=MESH,
        ).wait_recv()

    def finish(self):
        for copy in self.sent:
            copy.wait_send()


class Local:
    def __init__(self, sems):
        self.sems, self.n, self.open = sems, 0, []

    def start(self, src, dst):
        copy = pltpu.make_async_copy(src, dst, self.sems.at[self.n])
        self.n += 1
        copy.start()
        self.open.append(copy)
        return copy

    def wait(self, copy):
        copy.wait()
        self.open = [other for other in self.open if other is not copy]

    def finish(self):
        for copy in self.open:
            copy.wait()


def greet(place, xs=(), ctx=(), chain=(), core=False, between=None):
    bar = pltpu.get_barrier_semaphore()
    n = 0
    for d in xs:
        pl.semaphore_signal(bar, inc=1, device_id={"fsdp": place.xs(d)}, device_id_type=MESH)
        n += 1
    for dy, dz in ctx:
        pl.semaphore_signal(bar, inc=1, device_id={"context": place.ctx(dy, dz)}, device_id_type=MESH)
        n += 1
    for d in chain:
        pl.semaphore_signal(bar, inc=1, device_id={"context": place.chain(d)}, device_id_type=MESH)
        n += 1
    if core:
        pl.semaphore_signal(bar, inc=1, device_id={"tensor": 1 - place.t}, device_id_type=MESH)
        n += 1
    if between is not None:
        between()
    pl.semaphore_wait(bar, n)


def chunk_rows(index, half):
    return pl.ds(pl.multiple_of(index * 160 + 80 * half, 16), 80)


def line_of(ref, place, half, d, cols):
    grid = ref.reshape(4, 4, 160, ref.shape[1])
    rows = pl.ds(80 * half, 80)
    if half == 0:
        return grid.at[:, lax.rem(place.z + d + 4, 4), rows, cols]
    return grid.at[lax.rem(place.y + d + 4, 4), :, rows, cols]


def gather_steps(wire, buf, own, at):
    place = wire.place
    width = own.shape[1]
    mid = width // 256 * 128
    FULL = pl.ds(at, width)
    part = {1: pl.ds(at, mid), -1: pl.ds(at + mid, width - mid)}

    def ref(h, d, cols):
        return buf.at[chunk_rows(place.along(h, d, 0), h), cols]

    def second_line(h, d, cols):
        grid = buf.reshape(4, 4, 160, buf.shape[1])
        rows = pl.ds(80 * h, 80)
        if h == 0:
            return grid.at[lax.rem(place.y + d + 4, 4), :, rows, cols]
        return grid.at[:, lax.rem(place.z + d + 4, 4), rows, cols]

    st = {}
    for h in (0, 1):
        for d in (1, -1):
            st[h, 1, d] = wire.send(own.at[pl.ds(80 * h, 80), :], ref(h, 0, FULL), context=place.along(h, d, 0))
    yield
    for d in (1, -1):
        for h in (0, 1):
            wire.recv(st[h, 1, d], ref(h, -d, FULL))
            st[h, 2, d] = wire.send(ref(h, -d, part[d]), ref(h, -d, part[d]), context=place.along(h, d, 0))
    yield
    for h in (0, 1):
        for d in (1, -1):
            wire.recv(st[h, 2, d], ref(h, 2, part[d]))
        for k in (1, -1):
            for d in (1, -1):
                cols = part[k * d]
                st[h, 3, d, k] = wire.send(second_line(h, 0, cols), second_line(h, 0, cols), context=place.along(h, 0, d))
    yield
    for h in (0, 1):
        for d in (1, -1):
            wire.recv(st[h, 3, d, 1], second_line(h, -d, part[d]))
            st[h, 4, d] = wire.send(second_line(h, -d, part[d]), second_line(h, -d, part[d]), context=place.along(h, 0, d))
    yield
    for h in (0, 1):
        for d in (1, -1):
            wire.recv(st[h, 3, d, -1], second_line(h, -d, part[-d]))
    for h in (0, 1):
        for d in (1, -1):
            wire.recv(st[h, 4, d], second_line(h, 2, part[d]))
    yield


def rows_gather_steps(wire, src, out, loc):
    place = wire.place
    x, t = place.x, place.t
    width = src.shape[1]
    h = width // 256 * 128
    LO, HI = pl.ds(0, h), pl.ds(h, width - h)
    xp, xm, xo = place.xs(1), place.xs(-1), place.xs(2)
    def hop(ref, piece, cols, d):
        return wire.send(ref, out.at[piece, t, :, cols], fsdp=place.xs(d))

    a = hop(src.at[:, LO], x, LO, 1)
    b = hop(src.at[:, HI], x, HI, -1)
    aa = hop(src.at[:, HI], x, HI, 1)
    bb = hop(src.at[:, LO], x, LO, -1)
    cores = [(x, wire.send(src, out.at[x, t], tensor=1 - t))]
    own = loc.start(src, out.at[x, t])
    yield
    wire.recv(a, out.at[xm, t, :, LO])
    e = hop(out.at[xm, t, :, LO], xm, LO, 1)
    wire.recv(b, out.at[xp, t, :, HI])
    f = hop(out.at[xp, t, :, HI], xp, HI, -1)
    yield
    wire.recv(aa, out.at[xm, t, :, HI])
    cores.append((xm, wire.send(out.at[xm, t], out.at[xm, t], tensor=1 - t)))
    wire.recv(bb, out.at[xp, t, :, LO])
    cores.append((xp, wire.send(out.at[xp, t], out.at[xp, t], tensor=1 - t)))
    yield
    wire.recv(e, out.at[xo, t, :, LO])
    wire.recv(f, out.at[xo, t, :, HI])
    cores.append((xo, wire.send(out.at[xo, t], out.at[xo, t], tensor=1 - t)))
    yield
    for k, n in cores:
        wire.recv(n, out.at[k, 1 - t])
    loc.wait(own)
    yield


class RowsScatter:
    def __init__(self, wire, part, crecv, sums, r1, r2, piece=512, own=None):
        self.wire, self.part, self.crecv, self.sums, self.r1, self.r2 = wire, part, crecv, sums, r1, r2
        self.piece, self.n = piece, {}
        place = wire.place
        self.x, self.t = place.x, place.t
        self.own = own if own is not None else part.at[:, self.t]
        self.xp, self.xm, self.xo = place.xs(1), place.xs(-1), place.xs(2)

    def cut(self, i):
        at, half = i * self.piece, self.piece // 2
        return pl.ds(at, self.piece), pl.ds(at, half), pl.ds(at + half, half)

    def rows(self, fn):
        for i in (0, 1):
            fn(pl.ds(32 * i, 32))

    def put(self, n, k, cols, extra=None):
        def fn(r):
            v = self.own[k, r, cols].astype(f32) + self.crecv[k, r, cols].astype(f32)
            if extra is not None:
                v = v + self.r1[extra, r, cols].astype(f32)
            self.sums[n, r, cols] = v.astype(bf16)

        self.rows(fn)

    def a(self, i):
        cols = self.cut(i)[0]
        self.n["a", i] = self.wire.send(self.part.at[:, 1 - self.t, :, cols], self.crecv.at[:, :, cols], tensor=1 - self.t)

    def b(self, i):
        cols, lo, hi = self.cut(i)
        self.wire.recv(self.n["a", i], self.crecv.at[:, :, cols])
        self.put(0, self.xo, cols)
        self.n["b", i] = self.wire.send(self.sums.at[0, :, lo], self.r1.at[0, :, lo], fsdp=self.xp)
        self.n["c", i] = self.wire.send(self.sums.at[0, :, hi], self.r1.at[1, :, hi], fsdp=self.xm)

    def c(self, i):
        cols, lo, hi = self.cut(i)
        self.wire.recv(self.n["b", i], self.r1.at[0, :, lo])
        self.put(1, self.xp, lo, 0)
        self.put(1, self.xp, hi)
        self.n["d", i] = self.wire.send(self.sums.at[1, :, cols], self.r2.at[0, :, cols], fsdp=self.xp)
        self.wire.recv(self.n["c", i], self.r1.at[1, :, hi])
        self.put(2, self.xm, lo)
        self.put(2, self.xm, hi, 1)
        self.n["e", i] = self.wire.send(self.sums.at[2, :, cols], self.r2.at[1, :, cols], fsdp=self.xm)

    def d(self, i, done):
        cols = self.cut(i)[0]
        self.wire.recv(self.n["d", i], self.r2.at[0, :, cols])
        self.wire.recv(self.n["e", i], self.r2.at[1, :, cols])

        def total(r):
            done(
                cols,
                r,
                self.own[self.x, r, cols].astype(f32)
                + self.crecv[self.x, r, cols].astype(f32)
                + self.r2[0, r, cols].astype(f32)
                + self.r2[1, r, cols].astype(f32),
            )

        self.rows(total)

    def steps(self, compute, done):
        count = self.sums.shape[2] // self.piece
        for i in range(count + 3):
            if i < count:
                compute(i)
                self.a(i)
            if 0 <= i - 1 < count:
                self.b(i - 1)
            if 0 <= i - 2 < count:
                self.c(i - 2)
            if 0 <= i - 3 < count:
                self.d(i - 3, done)
            yield


def drain(steps):
    for _ in steps:
        pass


def pump(steps, n=1):
    for _ in range(n):
        next(steps, None)


def gelu(v):
    return 0.5 * v * (1.0 + jnp.tanh(0.7978845608028654 * (v + 0.044715 * v * v * v)))


def gelu_and_slope(v):
    u = jnp.tanh(0.7978845608028654 * (v + 0.044715 * v * v * v))
    slope = 0.5 * (1.0 + u) + 0.5 * v * (1.0 - u * u) * (
        0.7978845608028654 * (1.0 + 3 * 0.044715 * v * v)
    )
    return 0.5 * v * (1.0 + u), slope


def one_less_exp(v):
    series = 1.0 + v * (1.0 / 7.0)
    for k in (6.0, 5.0, 4.0, 3.0, 2.0):
        series = 1.0 + v * (1.0 / k) * series
    return jnp.where(v > -0.35, -v * series, 1.0 - jnp.exp(v))


def sigmoid(v):
    return 1.0 / (1.0 + jnp.exp(-v))


def shifted(block, edge, k):
    moved = pltpu.roll(block, k, 0)
    first = jnp.where(
        lax.broadcasted_iota(jnp.int32, edge.shape, 0) < k, pltpu.roll(edge, k, 0), moved[:8]
    )
    return jnp.concatenate([first, moved[8:]], axis=0)


def scan_down(a, b):
    rows = lax.broadcasted_iota(jnp.int32, a.shape, 0)
    s = 1
    while s < a.shape[0]:
        earlier = rows >= s
        pa = jnp.where(earlier, pltpu.roll(a, s, 0), 1.0)
        pb = jnp.where(earlier, pltpu.roll(b, s, 0), 0.0)
        b = b + a * pb
        a = a * pa
        s *= 2
    return a, b


def scan_up(a, b):
    rows = lax.broadcasted_iota(jnp.int32, a.shape, 0)
    n = a.shape[0]
    s = 1
    while s < n:
        later = rows < n - s
        pa = jnp.where(later, pltpu.roll(a, n - s, 0), 1.0)
        pb = jnp.where(later, pltpu.roll(b, n - s, 0), 0.0)
        b = b + a * pb
        a = a * pa
        s *= 2
    return a, b


def selector(g):
    i = lax.broadcasted_iota(jnp.int32, (256, 512), 0)
    j = lax.broadcasted_iota(jnp.int32, (256, 512), 1)
    xx, cc, r = i // 64, (i // 4) % 16, i % 4
    return (j == cc * 32 + xx * 8 + g * 4 + r).astype(f32).astype(bf16)


def gate_matrix(packed, g):
    return dot(selector(g), packed).astype(bf16)


def column(tile, tiles=1):
    return pl.ds(pl.multiple_of(128 + 256 * tile, 128), 256 * tiles)


def triple(j):
    return column(jnp.where(j == 3, 3, 6 + 3 * j), 3)


def head_count(x):
    return jnp.where(x == 0, 2, 1).astype(jnp.int32)


def lanes(h):
    return pl.ds(pl.multiple_of(h * 256, 256), 256)


def token_rows(g):
    return pl.ds(pl.multiple_of(g * 128, 128), 128)


def recur_terms(lx, la, cl, sp, keep):
    sx, sa = sigmoid(lx), sigmoid(la)
    log_decay = (-gate_scale) * sa * sp
    grown = one_less_exp(2.0 * log_decay)
    root = jnp.sqrt(grown)
    factor = root * keep + 1.0 - keep
    return sx, sa, log_decay, root, factor


HEAD_START = (0, 2, 3, 4)
HEADS_OF = (2, 1, 1, 1)
FF_START = (0, 768, 1792, 2816)
TILE_ORDER = ((0, 1, 2), (3, 0, 1, 2), (3, 0, 1, 2), (3, 0, 1, 2))


def restored_granule(m):
    return 4 * (m % 16) + m // 16


def permuted_granule(m):
    return 16 * (m % 4) + m // 4


def moved_tile(get, q, shape, granule):
    lane = lax.broadcasted_iota(jnp.int32, shape, len(shape) - 1)
    out = jnp.zeros(shape, f32)
    at = 128 * q
    while at < 128 * q + 128:
        m = at // 40
        source = 40 * granule(m) + at - 40 * m
        p = source // 128
        stop = min(40 * m + 40, 128 * q + 128, at + 128 * p + 128 - source)
        turn = (at - 128 * q - (source - 128 * p)) % 128
        v = get(p)
        if turn:
            v = pltpu.roll(v, turn, len(shape) - 1)
        out = jnp.where((lane >= at - 128 * q) & (lane < stop - 128 * q), v, out)
        at = stop
    return out


def segment_of(place, ends):
    return sum((place >= e).astype(jnp.int32) for e in ends)


def forward_kernel(
    seq_ref, tokens, cotangent, gains, rec_ref, inp, blocks, outp, inner, down,
    w_out, act_out, gl_out, tok_out, gains_out, lx_out, la_out, hid_out, py_out, low_out, cg_out, nm_out, resid_out,
    xbuf, wide, chunk0, chunk1, chunk2, w1, act, lx_s, la_s, hid_s, py_s, low_s, halo, cum_s, cg, cin,
    part, crecv, sums, r1, r2, normed, resid, packed, gates,
    p_ref, n_ref, cot_ref, tok_ref, gain_ref,
    ss, rs, ls,
):
    place = Place()
    x, c, t = place.x, place.c, place.t
    wire, loc = Wire(place, ss, rs), Local(ls)
    nh = head_count(x)

    def weight_tile(k, tile):
        heads = HEADS_OF[k]
        if tile < 3 * heads:
            at = 256 * (HEAD_START[k] + tile % heads)
            ref = (inp.at[0], inp.at[1], outp)[tile // heads]
        else:
            kind = (tile - 6) % 3 if tile >= 6 else tile - 3
            j = (tile - 6) // 3 if tile >= 6 else 3
            at = FF_START[k] + 256 * j
            ref = (inner.at[0], inner.at[1], down)[kind]
        return ref[:, pl.ds(at, 256)]

    def pack(first, count):
        for k in range(4):
            for tile in range(first, first + count):
                v = jnp.concatenate([weight_tile(k, tile), jnp.zeros((8, 256), f32)], axis=0)
                p_ref[k, :, pl.ds(128 + 256 * tile, 256)] = v.astype(bf16)

    def pack_first():
        for k in range(4):
            heads = HEADS_OF[k]
            rows = [
                jnp.concatenate([blocks[g, HEAD_START[k] + h] for h in range(heads)] + [jnp.zeros((4, 512 - 256 * heads), f32)] * (heads < 2), axis=1)
                for g in (0, 1)
            ]
            gate = jnp.concatenate([jnp.concatenate(rows, axis=0), jnp.zeros((8, 128), f32)], axis=1)
            main = jnp.concatenate([jnp.zeros((40, 128), f32), weight_tile(k, 0), weight_tile(k, 1)], axis=1)
            p_ref[k, :, pl.ds(0, FIRST)] = jnp.concatenate([main, gate], axis=0).astype(bf16)

    def prepare():
        pack_first()
        for n in (0, 1):
            for q in range(20):
                gain_ref[pl.ds(n, 1), pl.ds(128 * q, 128)] = moved_tile(
                    lambda p: gains[pl.ds(n, 1), pl.ds(128 * p, 128)], q, (1, 128), permuted_granule
                )
        ends = [seq_ref[0, 0]]
        for k in (1, 2):
            ends.append(ends[-1] + seq_ref[0, k])

        def rows(i):
            src = pl.ds(pl.multiple_of(t * 64 + 16 * i, 16), 16)
            r = pl.ds(pl.multiple_of(16 * i, 16), 16)
            where = c * 128 + t * 64 + 16 * i + lax.broadcasted_iota(jnp.int32, (16, 128), 0)
            lane = lax.broadcasted_iota(jnp.int32, (16, 128), 1)
            here = segment_of(where, ends)
            valid = (here < 3).astype(f32)
            fresh = (where == 0).astype(f32)
            for e in ends:
                fresh = jnp.maximum(fresh, (where == e).astype(f32))
            back = where - (lane - 1)
            same = (segment_of(back, ends) == here).astype(f32) * (back >= 0).astype(f32) * (lane < 5).astype(f32)
            flag = jnp.where(lane == 0, valid, jnp.where(lane == 1, 1.0 - fresh, same))
            n_ref[r, pl.ds(DIM, 128)] = flag.astype(bf16)
            for q in range(20):
                cols = pl.ds(128 * q, 128)
                tok_ref[r, cols] = moved_tile(lambda p: tokens[src, pl.ds(128 * p, 128)].astype(f32), q, (16, 128), permuted_granule)
                cot = moved_tile(lambda p: cotangent[src, pl.ds(128 * p, 128)].astype(f32), q, (16, 128), permuted_granule)
                cot_ref[r, cols] = (cot * valid).astype(bf16)
            v = tok_ref[r, :]
            inv = lax.rsqrt(jnp.mean(v * v, axis=-1, keepdims=True) + norm_eps)
            n_ref[r, pl.ds(0, DIM)] = (v * inv * gain_ref[pl.ds(0, 1), :]).astype(bf16)

        many(4, rows)

    greet(
        place, xs=(1, 2, 3), ctx=((1, 0), (2, 0), (3, 0), (0, 1), (0, 2), (0, 3)), chain=(1, -1), core=True, between=prepare
    )
    loc.start(tok_ref, tok_out)
    loc.start(gain_ref, gains_out)

    stages = ((0, FIRST, chunk0), (FIRST, SPLIT, chunk1), (SPLIT, COLS, chunk2))
    came = {}

    def spread(s):
        c0, c1, _ = stages[s]
        cs = pl.ds(c0, c1 - c0)
        for d in (2, 1, 3):
            came[s, d] = wire.send(p_ref.at[place.xs(d), :, cs], xbuf.at[x, :, cs], fsdp=place.xs(d))

    def arrange(s):
        c0, c1, chunk = stages[s]
        cs = pl.ds(c0, c1 - c0)
        for d in (1, 3, 2):
            wire.recv(came[s, d], xbuf.at[place.xs(-d), :, cs])

        for k in range(4):
            def take(src, k=k):
                v = src[k, :, cs].astype(f32)
                wide[pl.ds(40 * k, 40), cs] = v[:40]

            pl.when(x == k)(functools.partial(take, p_ref))
            pl.when(x != k)(functools.partial(take, xbuf))
        if s == 0:
            for k in range(4):
                def gate(src, k=k):
                    v = src[k, :, pl.ds(0, 512)].astype(f32)
                    for b in range(4):
                        wide[pl.ds(32 * b + 8 * k, 8), pl.ds(0, 128)] = v[40:, 128 * b : 128 * b + 128]

                pl.when(x == k)(functools.partial(gate, p_ref))
                pl.when(x != k)(functools.partial(gate, xbuf))
        chunk[...] = wide[:, cs].astype(bf16)

    mine = pl.ds(pl.multiple_of(c * 160, 16), 160)
    spread(0)
    pack(2, 4)
    spread(1)
    pack(6, 9)
    arrange(0)
    own0 = loc.start(chunk0, w1.at[mine, pl.ds(0, FIRST)])
    one = gather_steps(wire, w1, chunk0, 0)
    pump(one)
    rows = rows_gather_steps(wire, n_ref, act, loc)
    pump(rows)
    pump(one)
    arrange(1)
    own1 = loc.start(chunk1, w1.at[mine, pl.ds(FIRST, SPLIT - FIRST)])
    two = gather_steps(wire, w1, chunk1, FIRST)
    pump(two)
    loc.wait(own0)
    pump(one)
    spread(2)
    pump(rows)
    pump(two)
    pump(one)
    pump(rows)
    loc.wait(own1)
    pump(two)
    pump(rows)
    drain(one)
    drain(rows)
    loc.start(act, act_out)
    later = rows_gather_steps(wire, cot_ref, gl_out, loc)

    def project_x(h):
        ni = act[:, :, :, pl.ds(0, DIM)].reshape(512, DIM)
        low_s[0, :, lanes(h)] = dot(ni, w1[:, column(h)]).astype(bf16)

    many(nh, project_x)
    before = low_s.at[0].reshape(4, 128, 512)
    hn = wire.send(before.at[:, pl.ds(112, 16), :], halo, context=place.chain(1))
    for cc in range(16):
        for b in range(4):
            packed[pl.ds(32 * cc, 32), pl.ds(128 * b, 128)] = w1[pl.ds(160 * cc + 32 * b, 32), pl.ds(0, 128)]
    for g in (0, 1):
        gates[g] = gate_matrix(packed[...], g)
    wire.recv(hn, halo)

    def flags(g, k):
        v = act[pl.ds(g, 1), :, :, pl.ds(DIM, 128)].reshape(128, 128).astype(f32)
        return v[:, k : k + 1]

    cg[c] = jnp.zeros((2, 8, 512), f32)

    def conv(h):
        def group(g):
            bx = low_s[0, token_rows(g), lanes(h)].astype(f32)
            edge = halo[g, :, lanes(h)].astype(f32)[8:]
            out = rec_ref[pl.ds(4, 1), lanes(h)] + rec_ref[pl.ds(0, 1), lanes(h)] * bx
            for k in (1, 2, 3):
                out = out + rec_ref[pl.ds(k, 1), lanes(h)] * (flags(g, 1 + k) * shifted(bx, edge, k))
            low_s[1, token_rows(g), lanes(h)] = out.astype(bf16)

        many(4, group)
        cl = low_s[1, :, lanes(h)]
        lx_s[:, lanes(h)] = dot(cl, gates[0, :, lanes(h)]) + rec_ref[pl.ds(5, 1), lanes(h)]
        la_s[:, lanes(h)] = dot(cl, gates[1, :, lanes(h)]) + rec_ref[pl.ds(6, 1), lanes(h)]

    many(nh, conv)
    loc.start(lx_s, lx_out)
    loc.start(la_s, la_out)
    pump(later)
    pump(two)

    def scan(q):
        cols = pl.ds(pl.multiple_of(q * 128, 128), 128)
        for g in range(4):
            r = pl.ds(128 * g, 128)
            keep = flags(g, 1)
            cl = low_s[1, r, cols].astype(f32)
            sx, sa, log_decay, root, factor = recur_terms(
                lx_s[r, cols], la_s[r, cols], cl, rec_ref[pl.ds(7, 1), cols], keep
            )
            a, b = scan_down(jnp.exp(log_decay) * keep, factor * sx * cl)
            cum_s[r, cols] = a
            hid_s[r, cols] = b
            cg[c, 0, pl.ds(g, 1), cols] = a[127:]
            cg[c, 1, pl.ds(g, 1), cols] = b[127:]

    many(2 * nh, scan)
    ns = [wire.send(cg.at[c], cg.at[c], context=place.ctx(0, d)) for d in (1, 2, 3)]
    for d, n in zip((1, 2, 3), ns):
        wire.recv(n, cg.at[place.ctx(0, -d)])
    line = pl.ds(place.y * 4, 4)
    ns = [wire.send(cg.at[line], cg.at[line], context=place.ctx(d, 0)) for d in (1, 2, 3)]
    arrange(2)
    own2 = loc.start(chunk2, w_out.at[mine, pl.ds(SPLIT, COLS - SPLIT)])
    for d, n in zip((1, 2, 3), ns):
        wire.recv(n, cg.at[pl.ds(lax.rem(place.y + 4 - d, 4) * 4, 4)])

    def enter(s, state):
        return cg[s, 0] * state + cg[s, 1]

    cin[...] = lax.fori_loop(0, c, enter, jnp.zeros((8, 512), f32))
    loc.start(cg, cg_out)

    pump(later)
    three = gather_steps(wire, w_out, chunk2, SPLIT)
    pump(three)
    drain(two)
    pump(three)
    loc.start(w1, w_out.at[:, pl.ds(0, SPLIT)])
    two = three

    def project_y(h):
        ni = act[:, :, :, pl.ds(0, DIM)].reshape(512, DIM)
        py_s[:, lanes(h)] = dot(ni, w1[:, column(nh + h)])

    many(nh, project_y)
    loc.start(py_s, py_out)
    pump(later)

    def mix(h):
        for g in range(4):
            r = pl.ds(128 * g, 128)
            hid = hid_s[r, lanes(h)] + cum_s[r, lanes(h)] * cin[pl.ds(g, 1), lanes(h)]
            hid_s[r, lanes(h)] = hid
            low_s[2, r, lanes(h)] = (hid * gelu(py_s[r, lanes(h)])).astype(bf16)

    many(nh, mix)
    loc.start(hid_s, hid_out)
    loc.start(low_s, low_out)
    loc.wait(own2)
    pump(two)

    drain(later)

    def project_out(n, heads):
        r = pl.ds(512 * n, 512)
        v = dot_nt(low_s[2, :, pl.ds(0, 256 * heads)], w1[r, pl.ds(128 + 512 * heads, 256 * heads)])
        part[:, :, :, r] = v.astype(bf16).reshape(4, 2, 64, 512)

    def project_piece(n):
        pl.when(x == 0)(lambda: project_out(n, 2))
        pl.when(x != 0)(lambda: project_out(n, 1))

    def add_resid(cols, r, total):
        resid[r, cols] = tok_ref[r, cols] + total

    drain(RowsScatter(wire, part, crecv, sums, r1, r2).steps(project_piece, add_resid))
    pump(two)
    loc.start(resid, resid_out)

    def norm(i):
        r = pl.ds(pl.multiple_of(i * 16, 16), 16)
        v = resid[r, :]
        inv = lax.rsqrt(jnp.mean(v * v, axis=-1, keepdims=True) + norm_eps)
        normed[r, :] = (v * inv * gain_ref[pl.ds(1, 1), :]).astype(bf16)

    many(4, norm)
    drain(rows_gather_steps(wire, normed, nm_out, loc))
    drain(two)
    wire.finish()
    loc.finish()


def vm(shape, dtype):
    return pltpu.VMEM(shape, dtype)


PLANE = ((1, 0), (3, 0), (0, 1), (0, 3))
ANY = pl.BlockSpec(memory_space=pl.ANY)
VM = pl.BlockSpec(memory_space=pltpu.VMEM)


def forward_call(seq, tokens, cotangent, gains, rec, inp, blocks, outp, inner, down):
    S = jax.ShapeDtypeStruct
    R = (64, DIM)
    F = (512, 512)
    return pl.pallas_call(
        forward_kernel,
        name="recurrent_forward",
        out_shape=(
            S((DIM, COLS), bf16), S((4, 2, 64, EXT), bf16), S((4, 2) + R, bf16), S(R, f32), S((2, DIM), f32),
            S(F, f32), S(F, f32), S(F, f32), S(F, f32),
            S((3,) + F, bf16), S((16, 2, 8, 512), f32), S((4, 2) + R, bf16), S(R, f32),
        ),
        in_specs=[pl.BlockSpec(memory_space=pltpu.SMEM)] + [VM] * 9,
        out_specs=[ANY] * 13,
        scratch_shapes=[
            vm((4, 48, COLS), bf16), vm((160, COLS), f32), vm((160, FIRST), bf16), vm((160, SPLIT - FIRST), bf16), vm((160, COLS - SPLIT), bf16),
            vm((DIM, SPLIT), bf16), vm((4, 2, 64, EXT), bf16),
            vm(F, f32), vm(F, f32), vm(F, f32), vm(F, f32),
            vm((3,) + F, bf16), vm((4, 16, 512), bf16), vm(F, f32), vm((16, 2, 8, 512), f32), vm((8, 512), f32),
            vm((4, 2) + R, bf16), vm((4,) + R, bf16), vm((3,) + R, bf16), vm((2,) + R, bf16), vm((2,) + R, bf16),
            vm(R, bf16), vm(R, f32), vm(F, bf16), vm((2, 256, 512), bf16),
            vm((4, 48, COLS), bf16), vm((64, EXT), bf16), vm(R, bf16), vm(R, f32), vm((2, DIM), f32),
            pltpu.SemaphoreType.DMA((160,)), pltpu.SemaphoreType.DMA((160,)), pltpu.SemaphoreType.DMA((20,)),
        ],
        compiler_params=pltpu.CompilerParams(collective_id=0, has_side_effects=True, vmem_limit_bytes=60 << 20),
    )(seq, tokens, cotangent, gains, rec, inp, blocks, outp, inner, down)


def transpose_rows(src, dst):
    def block(n):
        cols = pl.ds(pl.multiple_of(n * 256, 256), 256)
        dst[cols, :] = src[:, :, :, cols].reshape(512, 256).T

    many(10, block)


def add_sublanes(v):
    return v[:8] + v[8:]


def norm_back(total, value, gain):
    inv = lax.rsqrt(jnp.mean(value * value, axis=-1, keepdims=True) + norm_eps)
    xhat = value * inv
    weighted = total * gain
    inner = jnp.mean(weighted * xhat, axis=-1, keepdims=True)
    return inv * (weighted - xhat * inner), add_sublanes(total * xhat)


def ffn_kernel(
    w_ref, gl_ref, nm, resid, gain_ref,
    g_out, ahead_out, gm_out, gres_out, gain_out, first_out, second_out,
    gl, nmt, glt, wt, gfirst, gsecond, pre, lowi, lowg, parts, crecv, sums, r1, r2, normed, own_low, gsum,
    a2, a3, a4, a5, a6, a7, d2, d3, d4, d5, d6, d7,
    ss, rs, ls, ws, gs,
):
    place = Place()
    x, t = place.x, place.t
    wire, loc = Wire(place, ss, rs), Local(ls)
    nf = 5 - head_count(x)

    def load(j):
        return pltpu.make_async_copy(w_ref.at[:, triple(j)], wt.at[j], ws.at[j])

    def store(j):
        return pltpu.make_async_copy(wt.at[j], g_out.at[:, triple(j)], gs.at[j])

    glc = loc.start(gl_ref, gl)
    for j in range(3):
        load(j).start()
    pl.when(x != 0)(lambda: load(3).start())
    olc = loc.start(gl_ref.at[x, t], own_low)
    greet(place, xs=(1, -1), ctx=PLANE, core=True)
    transpose_rows(nm, nmt)
    loc.wait(glc)
    loc.wait(olc)
    transpose_rows(gl, glt)

    def tile(j):
        load(j).wait()
        pre[:, pl.ds(0, 512)] = dot(nm[...].reshape(512, DIM), wt[j, :, pl.ds(0, 512)])
        pre[:, pl.ds(512, 256)] = dot(gl[...].reshape(512, DIM), wt[j, :, pl.ds(512, 256)])

        def point(i):
            r = pl.ds(pl.multiple_of(i * 32, 32), 32)
            gated, slope = gelu_and_slope(pre[r, pl.ds(0, 256)])
            up, gi = pre[r, pl.ds(256, 256)], pre[r, pl.ds(512, 256)]
            lowi[j, r, :] = (gated * up).astype(bf16)
            lowg[j, r, pl.ds(0, 256)] = (gi * up * slope).astype(bf16)
            lowg[j, r, pl.ds(256, 256)] = (gi * gated).astype(bf16)

        many(16, point)

    def gradient(j, dst):
        def block(n):
            r = pl.ds(pl.multiple_of(n * 512, 512), 512)
            dst[r, pl.ds(0, 512)] = dot(nmt[r, :], lowg[j]).astype(bf16)
            dst[r, pl.ds(512, 256)] = dot(glt[r, :], lowi[j]).astype(bf16)

        many(5, block)

    tile(0)
    gradient(0, gfirst)
    first = scatter_steps(wire, loc, gfirst, 0, (None, None, a2, a3, a4, a5, a6, a7), first_out, False, True, False)
    pump(first, 1)
    tile(1)
    gradient(1, gsecond)
    second = scatter_steps(wire, loc, gsecond, 0, (None, None, d2, d3, d4, d5, d6, d7), second_out, False, True, False)
    pump(second, 1)
    many(nf - 2, lambda j: tile(j + 2))

    def contract(dst, low, cols, n):
        r = pl.ds(512 * n, 512)

        def total(count):
            v = dot_nt(low[0], wt[0, r, cols])
            for j in range(1, count):
                v = v + dot_nt(low[j], wt[j, r, cols])
            dst[:, :, :, r] = v.astype(bf16).reshape(4, 2, 64, 512)

        pl.when(x == 0)(lambda: total(3))
        pl.when(x != 0)(lambda: total(4))

    def keep_sum(cols, r, total):
        gsum[r, cols] = total

    back = RowsScatter(wire, parts, crecv, sums, r1, r2).steps(
        lambda n: contract(parts, lowg, pl.ds(0, 512), n), keep_sum
    )
    pump(first, 4)
    pump(back, 5)
    for n in range(5):
        contract(gl, lowi, pl.ds(512, 256), n)
        if n % 2 == 1:
            pump(back, 1)
    loc.start(gl, ahead_out)
    pump(first, 4)
    gradient(2, wt.at[2])
    store(2).start()
    drain(back)
    gain_out[...] = jnp.zeros_like(gain_out)

    def resid_back(i):
        r = pl.ds(pl.multiple_of(i * 16, 16), 16)
        gx, gain = norm_back(gsum[r, :], resid[r, :], gain_ref[pl.ds(1, 1), :])
        gr = own_low[r, :].astype(f32) + gx
        gres_out[r, :] = gr
        normed[r, :] = gr.astype(bf16)
        gain_out[...] += gain

    many(4, resid_back)
    rows = rows_gather_steps(wire, normed, gm_out, loc)
    pump(rows, 1)
    pump(second, 4)
    pump(rows, 1)

    @pl.when(x != 0)
    def _():
        gradient(3, wt.at[3])
        store(3).start()

    pump(rows, 1)
    pump(first, 1)
    drain(rows)
    pump(second, 4)
    pump(first, 1)
    pump(second, 1)
    drain(first)
    drain(second)
    store(2).wait()
    pl.when(x != 0)(lambda: store(3).wait())
    wire.finish()
    loc.finish()


def ffn_call(w, gl, nm, resid, gain):
    S = jax.ShapeDtypeStruct
    R = (64, DIM)
    slices = scatter_scratch(TRIPLE)[2:]
    return pl.pallas_call(
        ffn_kernel,
        name="feed_forward",
        out_shape=(
            S((DIM, COLS), bf16), S((4, 2) + R, bf16), S((4, 2) + R, bf16), S(R, f32), S((8, DIM), f32),
            S((4, 48, TRIPLE), bf16), S((4, 48, TRIPLE), bf16),
        ),
        in_specs=[ANY, ANY, VM, VM, VM],
        out_specs=[ANY, ANY, ANY, VM, VM, ANY, ANY],
        scratch_shapes=[
            vm((4, 2) + R, bf16), vm((DIM, 512), bf16), vm((DIM, 512), bf16), vm((4, DIM, TRIPLE), bf16), vm((DIM, TRIPLE), bf16), vm((DIM, TRIPLE), bf16),
            vm((512, TRIPLE), f32), vm((4, 512, 256), bf16), vm((4, 512, 512), bf16),
            vm((4, 2) + R, bf16), vm((4,) + R, bf16), vm((3,) + R, bf16), vm((2,) + R, bf16), vm((2,) + R, bf16),
            vm(R, bf16), vm(R, bf16), vm(R, f32),
        ] + slices + slices + [
            pltpu.SemaphoreType.DMA((170,)), pltpu.SemaphoreType.DMA((170,)), pltpu.SemaphoreType.DMA((12,)),
            pltpu.SemaphoreType.DMA((4,)), pltpu.SemaphoreType.DMA((4,)),
        ],
        compiler_params=pltpu.CompilerParams(collective_id=1, has_side_effects=True, vmem_limit_bytes=60 << 20),
    )(w, gl, nm, resid, gain)


def scatter_steps(wire, loc, g_ref, at, bufs, out_ref, gates, resident=False, spread=True):
    gvn, gvo, r1, r2, r3, r4, wide, obuf = bufs
    place = wire.place
    x, c = place.x, place.c
    width = wide.shape[1]
    mid = width // 256 * 128
    LO, HI, FULL = (0, mid), (mid, width), (0, width)
    zero = {1: LO, -1: HI}
    other = {1: HI, -1: LO}

    def cut(k):
        return pl.ds(k[0], k[1] - k[0])

    def short(k):
        return pl.ds(0, k[1] - k[0])

    def wide_cut(k):
        return pl.ds(at + k[0], k[1] - k[0])

    def group(h, d, k):
        return line_of(g_ref, place, h, d, wide_cut(k))

    def index(h, d, q):
        return q * 4 + lax.rem(place.z + d + 4, 4) if h == 0 else lax.rem(place.y + d + 4, 4) * 4 + q

    side = {1: 0, -1: 1}
    ends = {0: place.y, 1: place.z}
    st, loads = {}, {}

    class Piece:
        def __init__(self, h, d, k, ref):
            self.h, self.d, self.k, self.ref = h, d, k, ref

        def at(self, q, half):
            c0, c1 = self.k
            if half is not None:
                c0, c1 = (c0, mid) if half == 0 else (mid, c1)
            if resident:
                return g_ref, chunk_rows(index(self.h, self.d, q), self.h), wide_cut((c0, c1))
            return self.ref.at[q], pl.ds(0, 80), (short((c0, c1)) if self.d else cut((c0, c1)))

    def add_near(piece, got):
        def one(q):
            ref, r, cols = piece.at(q, None)
            ref[r, cols] = ref[r, cols] + got[q]

        many(4, one)

    def add_own(piece, srcs):
        def one(q):
            for half in (0, 1):
                ref, r, cols = piece.at(q, half)
                v = ref[r, cols].astype(f32)
                for s in srcs:
                    v = v + s[q, :, cut((LO, HI)[half])].astype(f32)
                ref[r, cols] = v.astype(bf16)

        many(4, one)

    def mine_at(h, q, k):
        if resident:
            return g_ref.at[chunk_rows(index(h, 0, q), h), wide_cut(k)]
        return gvo.at[h, q, :, cut(k)]

    for h in (0, 1):
        for d in (1, -1):
            k = zero[d]
            st[h, 1, d] = wire.send(group(h, 2, k), r1.at[h, side[d], :, :, short(k)], context=place.along(h, d, 0))
    if not resident:
        for h in (0, 1):
            for d in (1, -1):
                loads[h, d] = loc.start(group(h, d, zero[d]), gvn.at[h, side[d], :, :, short(zero[d])])
        for h in (0, 1):
            loads[h, 0] = loc.start(group(h, 0, FULL), gvo.at[h])
    for h in (0, 1):
        for d in (1, -1):
            k = other[d]
            st[h, 2, d] = wire.send(group(h, d, k), r2.at[h, side[d], :, :, cut(k)], context=place.along(h, d, 0))
    yield

    def add(dst, srcs):
        def one(i):
            r = pl.ds(pl.multiple_of(i * 16, 16), 16)
            v = srcs[0][r, :].astype(f32)
            for s in srcs[1:]:
                v = v + s[r, :].astype(f32)
            dst[r, :] = v.astype(dst.dtype)

        many(5, one)

    for h in (0, 1):
        for d in (1, -1):
            k = zero[d]
            if not resident:
                loc.wait(loads[h, d])
            got = r1.at[h, side[d], :, :, short(k)]
            wire.recv(st[h, 1, d], got)
            piece = Piece(h, d, k, None if resident else gvn.at[h, side[d]])
            add_near(piece, got)
            src = group(h, d, k) if resident else gvn.at[h, side[d], :, :, short(k)]
            st[h, 3, d] = wire.send(src, r2.at[h, side[d], :, :, cut(k)], context=place.along(h, d, 0))
            yield
    for h in (0, 1):
        if not resident:
            loc.wait(loads[h, 0])
        for d in (1, -1):
            wire.recv(st[h, 2, d], r2.at[h, side[d], :, :, cut(other[d])])
            wire.recv(st[h, 3, d], r2.at[h, side[d], :, :, cut(zero[d])])
        add_own(Piece(h, 0, FULL, None if resident else gvo.at[h]), [r2.at[h, 0], r2.at[h, 1]])
        far = lax.rem(ends[h] + 2, 4)
        for d in (1, -1):
            st[h, 4, d] = wire.send(
                mine_at(h, far, zero[d]), r3.at[h, side[d], :, short(zero[d])], context=place.along(h, 0, d)
            )
        for d in (1, -1):
            near = lax.rem(ends[h] + d + 4, 4)
            st[h, 5, d] = wire.send(
                mine_at(h, near, other[d]), r4.at[h, side[d], :, cut(other[d])], context=place.along(h, 0, d)
            )
        yield
        yield
    for h in (0, 1):
        for d in (1, -1):
            k = zero[d]
            mine = mine_at(h, lax.rem(ends[h] + d + 4, 4), k)
            got = r3.at[h, side[d], :, short(k)]
            wire.recv(st[h, 4, d], got)
            add(mine, [mine, got])
            st[h, 6, d] = wire.send(mine, r4.at[h, side[d], :, cut(k)], context=place.along(h, 0, d))
    yield
    for h in (0, 1):
        for d in (1, -1):
            wire.recv(st[h, 5, d], r4.at[h, side[d], :, cut(other[d])])
            wire.recv(st[h, 6, d], r4.at[h, side[d], :, cut(zero[d])])
        add(wide.at[pl.ds(80 * h, 80), :], [mine_at(h, ends[h], FULL), r4.at[h, 0], r4.at[h, 1]])
    for k in range(4):
        obuf[k] = jnp.concatenate([wide[pl.ds(40 * k, 40), :], jnp.zeros((8, width), f32)], axis=0).astype(bf16)
        if gates:
            tail = jnp.concatenate([wide[pl.ds(32 * b + 8 * k, 8), pl.ds(0, 128)] for b in range(4)], axis=1)
            obuf[k, :, pl.ds(0, 512)] = jnp.concatenate([wide[pl.ds(40 * k, 40), pl.ds(0, 512)], tail], axis=0).astype(bf16)
    if not spread:
        own = loc.start(obuf, out_ref)
        yield
        loc.wait(own)
        yield
        return
    sent = [(d, wire.send(obuf.at[place.xs(d)], out_ref.at[x], fsdp=place.xs(d))) for d in (1, 3, 2)]
    own = loc.start(obuf.at[x], out_ref.at[x])
    yield
    for d, n in sent:
        wire.recv(n, out_ref.at[place.xs(-d)])
    loc.wait(own)
    yield


def scatter_scratch(width):
    hi = width - width // 256 * 128
    return [
        vm((2, 2, 4, 80, hi), bf16), vm((2, 4, 80, width), bf16), vm((2, 2, 4, 80, hi), bf16), vm((2, 2, 4, 80, width), bf16),
        vm((2, 2, 80, hi), bf16), vm((2, 2, 80, width), bf16), vm((160, width), f32), vm((4, 48, width), bf16),
    ]


def small_steps(wire, mine, zin, yin, xin, corein):
    place = wire.place
    x = place.x
    ns = [wire.send(mine.at[0], zin.at[d - 1], context=place.ctx(0, d)) for d in (1, 2, 3)]
    yield
    for d, n in zip((1, 2, 3), ns):
        wire.recv(n, zin.at[d - 1])
    mine[1] = mine[0] + zin[0] + zin[1] + zin[2]
    ns = [wire.send(mine.at[1], yin.at[d - 1], context=place.ctx(d, 0)) for d in (1, 2, 3)]
    yield
    for d, n in zip((1, 2, 3), ns):
        wire.recv(n, yin.at[d - 1])
    total = mine[1] + yin[0] + yin[1] + yin[2]
    mine[2] = total
    xin[x] = total
    ns = [wire.send(mine.at[2], xin.at[x], fsdp=place.xs(d)) for d in (1, 2, 3)]
    yield
    for d, n in zip((1, 2, 3), ns):
        wire.recv(n, xin.at[place.xs(-d)])
    mine[3] = xin[0] + xin[1] + xin[2] + xin[3]
    n = wire.send(mine.at[3], corein, tensor=1 - place.t)
    yield
    wire.recv(n, corein)
    yield


def fold(dst, row, at):
    for i in range(20):
        dst[pl.ds(i // 3, 1), pl.ds(at + 128 * (i % 3), 128)] = row[:, 128 * i : 128 * i + 128]


def backward_kernel(
    g_ref, w_ref, act_ref, gm_ref, first_ref, second_ref, ahead_ref,
    lx_ref, la_ref, hid_ref, py_ref, low_ref, cg, tok_ref, gres, resid, gain_ref, rec_ref, gain_two,
    t0_out, t1_out, t2_out, mid_out, last_out, mixed_out, tgrad_out, recur_out, gains_out,
    a0, a1, a2, a3, a4, a5, a6, a7, b2, b3, b4, b5, b6, b7, c2, c3, c4, c5, c6, c7,
    w1, acts, turned, flag_s, gmx, gpy, bc, bp, bg, cin, cback, glow, edge, edge_in, edge_out, gpx, gates, packed, dgates,
    gain_acc, crecv, sums, r1, r2, own_f, crecv_f, sums_f, r1_f, r2_f,
    small, zin, yin, xin, corein, late, zin_l, yin_l, xin_l, corein_l,
    lx_s, la_s, hid_s, py_s, low_s, glast,
    ss, rs, ls, ws,
):
    part, gconv, gdir = acts, gmx, bc
    place = Place()
    x, c, t = place.x, place.c, place.t
    wire, loc = Wire(place, ss, rs), Local(ls)
    nh = head_count(x)
    rest = pl.ds(FIRST + 256, TRIPLE)
    both = pl.ds(0, FIRST + 256)
    lg = loc.start(gm_ref, acts)
    lw = loc.start(w_ref.at[:, both], w1.at[:, both])
    load_w = pltpu.make_async_copy(w_ref.at[:, rest], w1.at[:, rest], ws.at[0])
    load_g = pltpu.make_async_copy(g_ref.at[:, rest], w1.at[:, rest], ws.at[1])
    pl.when(x == 0)(lambda: load_w.start())
    pl.when(x != 0)(lambda: load_g.start())
    lf = loc.start(act_ref.at[:, :, :, pl.ds(DIM, 128)], flag_s)
    li = [loc.start(a, b) for a, b in ((low_ref, low_s), (py_ref, py_s), (hid_ref, hid_s), (la_ref, la_s), (lx_ref, lx_s))]
    lo = loc.start(ahead_ref.at[:, t], own_f)
    greet(place, xs=(1, 2, 3), ctx=((1, 0), (2, 0), (3, 0), (0, 1), (0, 2), (0, 3)), chain=(1, -1), core=True)
    big = scatter_steps(wire, loc, g_ref, SPLIT + 2 * TRIPLE, (a0, a1, a2, a3, a4, a5, a6, a7), t2_out, False)
    pump(big, 1)

    def keep_mixed(cols, r, total):
        mixed_out[t, r, cols] = (resid[r, cols] + total).astype(bf16)

    ahead = RowsScatter(wire, ahead_ref, crecv_f, sums_f, r1_f, r2_f, own=own_f).steps(lambda n: None, keep_mixed)
    fro = []
    for src, dst in ((first_ref, t0_out), (second_ref, t1_out)):
        for d in (2, 1, 3):
            fro.append((d, dst, wire.send(src.at[place.xs(d)], dst.at[x], fsdp=place.xs(d))))
        loc.start(src.at[x], dst.at[x])
    for copy in li:
        loc.wait(copy)
    before = low_s.at[0].reshape(4, 128, 512)
    hn = wire.send(before.at[:, pl.ds(112, 16), :], edge_in, context=place.chain(1))
    loc.wait(lg)
    loc.wait(lw)
    loc.wait(lf)
    loc.wait(lo)
    pl.when(x == 0)(lambda: load_w.wait())
    pl.when(x != 0)(lambda: load_g.wait())
    for cc in range(16):
        for b in range(4):
            packed[pl.ds(32 * cc, 32), pl.ds(128 * b, 128)] = w1[pl.ds(160 * cc + 32 * b, 32), pl.ds(0, 128)]
    small[...] = jnp.zeros_like(small)
    late[...] = jnp.zeros_like(late)
    fold(small.at[0], jnp.sum(gain_two[...], axis=0, keepdims=True), 512)

    def flags(g, k):
        return flag_s[pl.ds(g, 1)].reshape(128, 128).astype(f32)[:, k : k + 1]

    def put_tile(rhs, dst, cols):
        def block(n):
            r = pl.ds(pl.multiple_of(n * 512, 512), 512)
            dst[r, cols] = dot(turned[r, :], rhs).astype(bf16)

        many(5, block)

    def mixed_back(h):
        gmx[:, lanes(h)] = dot(acts[...].reshape(512, DIM), w1[:, column(2 * nh + h)])

    many(nh, mixed_back)

    bg[c] = jnp.zeros((8, 512), f32)

    def scan(q):
        cols = pl.ds(pl.multiple_of(q * 128, 128), 128)
        for g in range(4):
            r = pl.ds(128 * g, 128)
            gated, slope = gelu_and_slope(py_s[r, cols])
            grad = gmx[r, cols]
            gpy[r, cols] = (grad * hid_s[r, cols] * slope).astype(bf16)
            keep = flags(g, 1)
            dec = jnp.exp((-gate_scale) * sigmoid(la_s[r, cols]) * rec_ref[pl.ds(7, 1), cols]) * keep
            last = lax.broadcasted_iota(jnp.int32, dec.shape, 0) == 127
            a, b = scan_up(jnp.where(last, 1.0, pltpu.roll(dec, 127, 0)), grad * gated)
            bc[r, cols] = a
            bp[r, cols] = b
            bg[c, pl.ds(g, 1), cols] = dec[:1] * b[:1]

    many(2 * nh, scan)
    ns = [wire.send(bg.at[c], bg.at[c], context=place.ctx(0, d)) for d in (1, 2, 3)]
    pump(ahead, 2)
    transpose_rows(acts, turned)
    ln = loc.start(act_ref.at[:, :, :, pl.ds(0, DIM)], acts)

    many(nh, lambda h: put_tile(low_s[2, :, lanes(h)], w1, column(2 * nh + h)))
    pump(ahead, 2)
    pump(big, 4)
    for d, n in zip((1, 2, 3), ns):
        wire.recv(n, bg.at[place.ctx(0, -d)])
    line = pl.ds(place.y * 4, 4)
    ns = [wire.send(bg.at[line], bg.at[line], context=place.ctx(d, 0)) for d in (1, 2, 3)]
    for g in (0, 1):
        gates[g] = gate_matrix(packed[...], g)
    loc.wait(ln)
    transpose_rows(acts, turned)

    def norm_grad_y(heads):
        def block(n):
            r = pl.ds(pl.multiple_of(n * 512, 512), 512)
            v = dot_nt(gpy[:, pl.ds(0, 256 * heads)], w1[r, pl.ds(128 + 256 * heads, 256 * heads)])
            part[:, :, :, r] = v.astype(bf16).reshape(4, 2, 64, 512)

        many(5, block)

    pl.when(x == 0)(lambda: norm_grad_y(2))
    pl.when(x != 0)(lambda: norm_grad_y(1))
    pl.when(x == 0)(lambda: many(2, lambda h: put_tile(gpy[:, lanes(h)], w1, column(2 + h))))
    pl.when(x != 0)(lambda: put_tile(gpy[:, pl.ds(0, 256)], glast, pl.ds(384, 256)))
    mid = scatter_steps(wire, loc, w1, FIRST, (None, None, b2, b3, b4, b5, b6, b7), mid_out, False, True)
    pump(mid, 1)
    pump(ahead, 2)
    for d, n in zip((1, 2, 3), ns):
        wire.recv(n, bg.at[pl.ds(lax.rem(place.y + 4 - d, 4) * 4, 4)])

    def enter(s, state):
        return cg[s, 0] * state + cg[s, 1]

    cin[...] = lax.fori_loop(0, c, enter, jnp.zeros((8, 512), f32))

    def leave(s, state):
        k = 15 - s
        return cg[k, 0] * state + bg[k]

    cback[...] = lax.fori_loop(0, 15 - c, leave, jnp.zeros((8, 512), f32))
    def terms(q):
        cols = pl.ds(pl.multiple_of(q * 128, 128), 128)
        sums_x = jnp.zeros((1, 128), f32)
        sums_a = jnp.zeros((1, 128), f32)
        sums_l = jnp.zeros((1, 128), f32)
        for g in range(4):
            r = pl.ds(128 * g, 128)
            keep = flags(g, 1)
            cl = low_s[1, r, cols].astype(f32)
            sp, dsp = rec_ref[pl.ds(7, 1), cols], rec_ref[pl.ds(8, 1), cols]
            sx, sa, log_decay, root, factor = recur_terms(lx_s[r, cols], la_s[r, cols], cl, sp, keep)
            adj = bp[r, cols] + bc[r, cols] * cback[pl.ds(g, 1), cols]
            hid = hid_s[r, cols]
            first = lax.broadcasted_iota(jnp.int32, hid.shape, 0) == 0
            prev = jnp.where(first, cin[pl.ds(g, 1), cols], pltpu.roll(hid, 1, 0))
            grown = jnp.exp(log_decay)
            gld = keep * grown * (adj * prev - adj * sx * cl * grown / root)
            glx = (adj * factor * cl * sx * (1.0 - sx)).astype(bf16)
            gla = (gld * ((-gate_scale) * sp) * sa * (1.0 - sa)).astype(bf16)
            glow[0, r, cols] = glx
            glow[1, r, cols] = gla
            gdir[r, cols] = adj * factor * sx
            sums_x += jnp.sum(glx.astype(f32), axis=0, keepdims=True)
            sums_a += jnp.sum(gla.astype(f32), axis=0, keepdims=True)
            sums_l += jnp.sum(gld * sa, axis=0, keepdims=True) * (gate_scale * dsp)
        small[0, pl.ds(5, 1), cols] = sums_x
        small[0, pl.ds(6, 1), cols] = sums_a
        small[0, pl.ds(7, 1), cols] = sums_l

    many(2 * nh, terms)
    wire.recv(hn, edge_in)

    def conv_back(h):
        cl = low_s[1, :, lanes(h)]
        lx, la = glow[0, :, lanes(h)], glow[1, :, lanes(h)]
        gconv[:, lanes(h)] = (
            gdir[:, lanes(h)] + dot_nt(lx, gates[0, :, lanes(h)]) + dot_nt(la, gates[1, :, lanes(h)])
        )

        def group(g, taps):
            gc = gconv[token_rows(g), lanes(h)]
            bx = low_s[0, token_rows(g), lanes(h)].astype(f32)
            ahead = edge_in[g, :, lanes(h)].astype(f32)[8:]
            rows = lax.broadcasted_iota(jnp.int32, gc.shape, 0)
            low_rows = lax.broadcasted_iota(jnp.int32, (8, 256), 0)
            out = rec_ref[pl.ds(0, 1), lanes(h)] * gc
            over = jnp.zeros((8, 256), f32)
            new = [taps[0] + jnp.sum(bx * gc, axis=0, keepdims=True)]
            for k in (1, 2, 3):
                masked = flags(g, 1 + k) * gc
                new.append(taps[k] + jnp.sum(shifted(bx, ahead, k) * masked, axis=0, keepdims=True))
                scaled = rec_ref[pl.ds(k, 1), lanes(h)] * masked
                out = out + jnp.where(rows < 128 - k, pltpu.roll(scaled, 128 - k, 0), 0.0)
                over = over + jnp.where(low_rows >= 8 - k, pltpu.roll(scaled[:8], 8 - k, 0), 0.0)
            new.append(taps[4] + jnp.sum(gc, axis=0, keepdims=True))
            gdir[token_rows(g), lanes(h)] = out
            edge[g, :, lanes(h)] = over
            return tuple(new)

        taps = lax.fori_loop(0, 4, group, tuple(jnp.zeros((1, 256), f32) for _ in range(5)))
        for k in range(5):
            small[0, pl.ds(k, 1), lanes(h)] = taps[k]

    many(nh, conv_back)
    en = wire.send(edge, edge_out, context=place.chain(-1))

    early = small_steps(wire, small, zin, yin, xin, corein)
    pump(early)
    pump(big, 4)
    pump(ahead, 2)

    def gate_back(h):
        cl = low_s[1, :, lanes(h)]
        dgates[0, :, lanes(h)] = dot_tn(cl, glow[0, :, lanes(h)]).astype(bf16)
        dgates[1, :, lanes(h)] = dot_tn(cl, glow[1, :, lanes(h)]).astype(bf16)

    many(nh, gate_back)
    wire.recv(en, edge_out)

    def narrow(h):
        for g in range(4):
            v = gdir[pl.ds(128 * g, 128), lanes(h)]
            tail = v[120:] + edge_out[g, :, lanes(h)]
            gpx[pl.ds(128 * g, 128), lanes(h)] = jnp.concatenate([v[:120], tail], axis=0).astype(bf16)

    many(nh, narrow)

    def norm_grad(n, heads):
        r = pl.ds(512 * n, 512)
        v = dot_nt(gpx[:, pl.ds(0, 256 * heads)], w1[r, pl.ds(128, 256 * heads)])
        v = v + part[:, :, :, r].reshape(512, 512).astype(f32)
        part[:, :, :, r] = v.astype(bf16).reshape(4, 2, 64, 512)

    def norm_piece(n):
        pl.when(x == 0)(lambda: norm_grad(n, 2))
        pl.when(x != 0)(lambda: norm_grad(n, 1))

    def keep_sum(cols, r, total):
        tgrad_out[t, r, cols] = total

    pump(mid, 4)
    many(nh, lambda h: put_tile(gpx[:, lanes(h)], glast, column(h)))
    back = (dot_tn(selector(0), dgates[0]) + dot_tn(selector(1), dgates[1])).astype(bf16)
    glast[:, pl.ds(0, 128)] = jnp.zeros((DIM, 128), bf16)
    for cc in range(16):
        for b in range(4):
            glast[pl.ds(160 * cc + 32 * b, 32), pl.ds(0, 128)] = back[32 * cc : 32 * cc + 32, 128 * b : 128 * b + 128]
    last = scatter_steps(wire, loc, glast, 0, (None, None, c2, c3, c4, c5, c6, c7), last_out, True, True)
    pump(last, 1)
    final = RowsScatter(wire, part, crecv, sums, r1, r2).steps(norm_piece, keep_sum)
    pump(final, 5)
    pump(early)
    pump(big, 1)
    pump(final, 1)
    pump(last, 4)
    pump(early)
    pump(final, 1)
    drain(final)
    gain_acc[...] = jnp.zeros_like(gain_acc)

    def finish(i):
        r = pl.ds(pl.multiple_of(i * 16, 16), 16)
        gx, gain = norm_back(tgrad_out[t, r, :], tok_ref[r, :], gain_ref[pl.ds(0, 1), :])
        tgrad_out[t, r, :] = gres[r, :] + gx
        gain_acc[...] += gain

    many(4, finish)
    tn = wire.send(tgrad_out.at[t], tgrad_out.at[t], tensor=1 - t)
    fold(late.at[0], jnp.sum(gain_acc[...], axis=0, keepdims=True), 0)
    tail = small_steps(wire, late, zin_l, yin_l, xin_l, corein_l)
    pump(tail)
    pump(mid, 4)
    pump(early)
    pump(tail)
    pump(last, 4)
    pump(big, 1)
    pump(tail)
    pump(mid, 1)
    pump(early)
    pump(last, 1)
    pump(tail)
    drain(ahead)
    mn = wire.send(mixed_out.at[t], mixed_out.at[t], tensor=1 - t)
    pump(mid, 1)
    pump(last, 1)
    drain(big)
    drain(mid)
    drain(tail)
    drain(early)
    for k in range(4):
        recur_out[k] = xin[k, :, pl.ds(0, 512)]
    gains_out[0] = late[3] + corein_l[...]
    gains_out[1] = small[3, :, pl.ds(512, 384)] + corein[:, pl.ds(512, 384)]
    drain(last)
    for d, dst, n in fro:
        wire.recv(n, dst.at[place.xs(-d)])
    wire.recv(mn, mixed_out.at[1 - t])
    wire.recv(tn, tgrad_out.at[1 - t])
    wire.finish()
    loc.finish()


def backward_call(g, w, act, gm, first, second, ahead, lx, la, hid, py, low, cg, tok, gres, resid, gain, rec, gain_two):
    S = jax.ShapeDtypeStruct
    R = (64, DIM)
    F = (512, 512)
    E, L = (8, 896), (8, 384)
    slices = lambda n: S((4, 48, n), bf16)
    return pl.pallas_call(
        backward_kernel,
        name="recurrent_backward",
        out_shape=(
            slices(TRIPLE), slices(TRIPLE), slices(TRIPLE), slices(SPLIT - FIRST), slices(FIRST),
            S((2,) + R, bf16), S((2,) + R, f32), S((4, 8, 512), f32), S((2,) + L, f32),
        ),
        in_specs=[ANY] * 12 + [VM] * 7,
        out_specs=[ANY, ANY, ANY, ANY, ANY, VM, VM, VM, VM],
        scratch_shapes=scatter_scratch(TRIPLE) + scatter_scratch(SPLIT - FIRST)[2:] + scatter_scratch(FIRST)[2:] + [
            vm((DIM, SPLIT), bf16), vm((4, 2) + R, bf16), vm((DIM, 512), bf16), vm((4, 2, 64, 128), bf16),
            vm(F, f32), vm(F, bf16), vm(F, f32), vm(F, f32), vm((16, 8, 512), f32), vm((8, 512), f32), vm((8, 512), f32),
            vm((2,) + F, bf16), vm((4, 8, 512), f32), vm((4, 16, 512), bf16), vm((4, 8, 512), f32), vm(F, bf16),
            vm((2, 256, 512), bf16), vm(F, bf16), vm((2, 256, 512), bf16), vm((8, DIM), f32),
            vm((4,) + R, bf16), vm((3,) + R, bf16), vm((2,) + R, bf16), vm((2,) + R, bf16),
            vm((4,) + R, bf16), vm((4,) + R, bf16), vm((3,) + R, bf16), vm((2,) + R, bf16), vm((2,) + R, bf16),
            vm((4,) + E, f32), vm((3,) + E, f32), vm((3,) + E, f32), vm((4,) + E, f32), vm(E, f32),
            vm((4,) + L, f32), vm((3,) + L, f32), vm((3,) + L, f32), vm((4,) + L, f32), vm(L, f32),
            vm(F, f32), vm(F, f32), vm(F, f32), vm(F, f32), vm((3,) + F, bf16), vm((DIM, FIRST), bf16),
            pltpu.SemaphoreType.DMA((310,)), pltpu.SemaphoreType.DMA((310,)), pltpu.SemaphoreType.DMA((60,)),
            pltpu.SemaphoreType.DMA((2,)),
        ],
        compiler_params=pltpu.CompilerParams(collective_id=2, has_side_effects=True, vmem_limit_bytes=62 << 20),
    )(g, w, act, gm, first, second, ahead, lx, la, hid, py, low, cg, tok, gres, resid, gain, rec, gain_two)


def adam_update(weight, moment, square, gradient, rate, shrink):
    moment = beta_one * moment + (1.0 - beta_one) * gradient
    square = beta_two * square + (1.0 - beta_two) * gradient * gradient
    normed = (moment * (1.0 / (1.0 - beta_one**STEP))) / (jnp.sqrt(square * (1.0 / (1.0 - beta_two**STEP))) + adam_eps)
    return (weight - rate * (normed + shrink * weight), moment, square)


def update_kernel(
    last, mid, t0, t1, t2, recur, gains, mixed, tgrad, *refs,
):
    ins, outs, held, fresh, ls, ss = refs[:21], refs[21:44], refs[44:56], refs[56:68], refs[68], refs[69]
    mixed_out, tgrad_out = outs[:2]
    big = (2, 5, 4, 6)
    loads, stores = {}, {}
    for i, n in enumerate(big):
        for k in range(3):
            loads[n, k] = pltpu.make_async_copy(ins[3 * n + k], held[3 * i + k], ls.at[3 * i + k])
            loads[n, k].start()
            stores[n, k] = pltpu.make_async_copy(fresh[3 * i + k], outs[2 + 3 * n + k], ss.at[3 * i + k])

    def group(n):
        if n in big:
            i = big.index(n)
            return held[3 * i : 3 * i + 3], fresh[3 * i : 3 * i + 3]
        return ins[3 * n : 3 * n + 3], outs[2 + 3 * n : 5 + 3 * n]

    def ready(n):
        for k in range(3):
            loads[n, k].wait()

    def leave(n):
        for k in range(3):
            stores[n, k].start()

    def update(n, index, grad, rate=matrix_rate, shrink=weight_decay):
        old, new = group(n)
        values = adam_update(*(ref[index] for ref in old), grad, rate, shrink)
        for ref, value in zip(new, values):
            ref[index] = value

    def piece(k, tile):
        if tile < 2:
            ref, at = last, 128 + 256 * tile
        elif tile < 6:
            ref, at = mid, 256 * (tile - 2)
        else:
            ref, at = (t0, t1, t2)[(tile - 6) // 3], 256 * ((tile - 6) % 3)
        return ref[k, :, pl.ds(at, 256)].astype(f32)

    ready(2)
    for k in range(4):
        for h in range(HEADS_OF[k]):
            nh = HEADS_OF[k]
            at = 256 * (HEAD_START[k] + h)
            update(2, (0, slice(None), pl.ds(at, 256)), piece(k, h)[:40])
            update(2, (1, slice(None), pl.ds(at, 256)), piece(k, nh + h)[:40])
            b = last[k, :, pl.ds(256 * h, 256)].astype(f32)[40:]
            for g in (0, 1):
                update(3, (g, HEAD_START[k] + h), b[4 * g : 4 * g + 4])
        n = 256 * HEADS_OF[k]
        update(1, (slice(None), pl.ds(256 * HEAD_START[k], n)), recur[k, :, pl.ds(0, n)], vector_rate, 0.0)
    leave(2)
    ready(5)
    for k in range(4):
        for j in TILE_ORDER[k]:
            tile = 3 if j == 3 else 6 + 3 * j
            at = FF_START[k] + 256 * j
            update(5, (0, slice(None), pl.ds(at, 256)), piece(k, tile)[:40])
            update(5, (1, slice(None), pl.ds(at, 256)), piece(k, tile + 1)[:40])
    leave(5)
    ready(4)
    for k in range(4):
        for h in range(HEADS_OF[k]):
            at = 256 * (HEAD_START[k] + h)
            update(4, (slice(None), pl.ds(at, 256)), piece(k, 2 * HEADS_OF[k] + h)[:40])
    leave(4)
    ready(6)
    for k in range(4):
        for j in TILE_ORDER[k]:
            tile = 3 if j == 3 else 6 + 3 * j
            update(6, (slice(None), pl.ds(FF_START[k] + 256 * j, 256)), piece(k, tile + 2)[:40])
    leave(6)

    for n in (0, 1):
        for q in range(20):
            grad = moved_tile(lambda p: gains[n, pl.ds(p // 3, 1), pl.ds(128 * (p % 3), 128)], q, (1, 128), restored_granule)
            update(0, (pl.ds(n, 1), pl.ds(128 * q, 128)), grad, vector_rate, 0.0)

    def restore(i):
        t = i // 4
        r = pl.ds(pl.multiple_of((i % 4) * 16, 16), 16)
        dst = pl.ds(pl.multiple_of(i * 16, 16), 16)
        for q in range(20):
            cols = pl.ds(128 * q, 128)
            mixed_out[dst, cols] = moved_tile(lambda p: mixed[t, r, pl.ds(128 * p, 128)].astype(f32), q, (16, 128), restored_granule).astype(bf16)
            tgrad_out[dst, cols] = moved_tile(lambda p: tgrad[t, r, pl.ds(128 * p, 128)], q, (16, 128), restored_granule)

    many(8, restore)
    for n in big:
        for k in range(3):
            stores[n, k].wait()


def update_call(pieces, recur, gains, mixed, tgrad, params):
    shapes = [jax.ShapeDtypeStruct(v.shape, v.dtype) for v in params]
    outs = [jax.ShapeDtypeStruct((128, DIM), bf16), jax.ShapeDtypeStruct((128, DIM), f32)] + shapes
    place = [VM if n in (0, 1, 3) else ANY for n in range(7) for _ in range(3)]
    held = [vm(params[3 * n + k].shape, f32) for n in (2, 5, 4, 6) for k in range(3)]
    return pl.pallas_call(
        update_kernel,
        name="optimizer_step",
        out_shape=tuple(outs),
        in_specs=[VM] * 9 + place,
        out_specs=tuple([VM, VM] + place),
        scratch_shapes=held + held + [pltpu.SemaphoreType.DMA((12,)), pltpu.SemaphoreType.DMA((12,))],
        compiler_params=pltpu.CompilerParams(vmem_limit_bytes=56 << 20),
    )(*pieces, recur, gains, mixed, tgrad, *params)


def recurrent_rows(recur_params):
    x = lax.axis_index("fsdp")
    start = jnp.where(x == 0, 0, x + 1) * 256
    rec = lax.dynamic_slice_in_dim(jnp.pad(recur_params, ((0, 0), (0, 256))), start, 512, 1)
    return jnp.concatenate(
        [rec[:7], jax.nn.softplus(-rec[7:]), jax.nn.sigmoid(-rec[7:]), jnp.zeros((7, 512), f32)], axis=0
    )


def on_device(
    tokens, cotangent, seq_lengths,
    norm_gains, gains_moment, gains_square, recur_params, recur_moment, recur_square,
    input_proj, input_moment, input_square, gate_blocks, blocks_moment, blocks_square,
    output_proj, output_moment, output_square, inner_proj, inner_moment, inner_square,
    down_proj, down_moment, down_square,
):
    rec = recurrent_rows(recur_params)
    w, act, gl, tok, gains, lx, la, hid, py, low, cg, nm, resid = forward_call(
        seq_lengths, tokens, cotangent, norm_gains, rec, input_proj, gate_blocks, output_proj.T, inner_proj, down_proj.T
    )
    g, ahead, gm, gres, gain_two, first, second = ffn_call(w, gl, nm, resid, gains)
    t0, t1, t2, mid, last, mixed, tgrad, recur, gsum = backward_call(
        g, w, act, gm, first, second, ahead, lx, la, hid, py, low, cg, tok, gres, resid, gains, rec, gain_two
    )
    params = (
        norm_gains, gains_moment, gains_square, recur_params, recur_moment, recur_square,
        input_proj, input_moment, input_square, gate_blocks, blocks_moment, blocks_square,
        output_proj.T, output_moment.T, output_square.T, inner_proj, inner_moment, inner_square,
        down_proj.T, down_moment.T, down_square.T,
    )
    out = update_call((last, mid, t0, t1, t2), recur, gsum, mixed, tgrad, params)
    return out[:14] + tuple(v.T for v in out[14:17]) + out[17:20] + tuple(v.T for v in out[20:])


def solution(mesh):
    row = P(("fsdp", "context"), None)
    wide_spec = P(None, ("fsdp", "context"), "tensor")
    tall = P("tensor", ("fsdp", "context"))
    block = P(None, "tensor", ("fsdp", "context"), None)
    params = (P(),) * 3 + (P(None, "tensor"),) * 3 + (wide_spec,) * 3 + (block,) * 3 + (tall,) * 3 + (wide_spec,) * 3 + (tall,) * 3
    return jax.shard_map(
        on_device, mesh=mesh, in_specs=(row, row, P("fsdp", None)) + params, out_specs=(row, row) + params, check_vma=False
    )
```

```python
import functools

import jax
import jax.numpy as jnp
from jax import lax
from jax.experimental import pallas as pl
from jax.experimental.pallas import tpu as pltpu
from jax.sharding import PartitionSpec as P

STEP = 10

norm_eps = 1e-06
beta_one = 0.9
beta_two = 0.95
adam_eps = 1e-08
weight_decay = 0.1
matrix_rate = 0.06
vector_rate = 1.0
gate_scale = 8.0

bf16, f32 = jnp.bfloat16, jnp.float32
MESH = pl.DeviceIdType.MESH
DIM = 2560
COLS = 3968
FIRST, SPLIT = 640, 1664
TRIPLE = 768
EXT = 2560 + 128
NT = (((1,), (1,)), ((), ()))
TN = (((0,), (0,)), ((), ()))


def dot(a, b):
    return jnp.dot(a, b, preferred_element_type=f32)


def dot_nt(a, b):
    return lax.dot_general(a, b, NT, preferred_element_type=f32)


def dot_tn(a, b):
    return lax.dot_general(a, b, TN, preferred_element_type=f32)


def many(n, fn):
    def one(i, carry):
        fn(i)
        return carry

    lax.fori_loop(0, n, one, 0)


class Place:
    def __init__(self):
        self.x = lax.axis_index("fsdp")
        self.c = lax.axis_index("context")
        self.t = lax.axis_index("tensor")
        self.y, self.z = lax.div(self.c, 4), lax.rem(self.c, 4)

    def ctx(self, dy, dz):
        return lax.rem(self.y + dy + 4, 4) * 4 + lax.rem(self.z + dz + 4, 4)

    def xs(self, d):
        return lax.rem(self.x + d + 4, 4)

    def along(self, half, d1, d2):
        return self.ctx(d2, d1) if half == 0 else self.ctx(d1, d2)

    def chain(self, d):
        return lax.rem(self.c + d + 16, 16)


class Wire:
    def __init__(self, place, ss, rs):
        self.place, self.ss, self.rs = place, ss, rs
        self.n, self.sent = 0, []

    def send(self, src, dst, **to):
        n = self.n
        self.n += 1
        copy = pltpu.make_async_remote_copy(
            src_ref=src, dst_ref=dst, send_sem=self.ss.at[n], recv_sem=self.rs.at[n],
            device_id=to, device_id_type=MESH,
        )
        copy.start()
        self.sent.append(copy)
        return n

    def recv(self, n, ref):
        pltpu.make_async_remote_copy(
            src_ref=ref, dst_ref=ref, send_sem=self.ss.at[n], recv_sem=self.rs.at[n],
            device_id={"fsdp": self.place.x}, device_id_type=MESH,
        ).wait_recv()

    def finish(self):
        for copy in self.sent:
            copy.wait_send()


class Local:
    def __init__(self, sems):
        self.sems, self.n, self.open = sems, 0, []

    def start(self, src, dst):
        copy = pltpu.make_async_copy(src, dst, self.sems.at[self.n])
        self.n += 1
        copy.start()
        self.open.append(copy)
        return copy

    def wait(self, copy):
        copy.wait()
        self.open = [other for other in self.open if other is not copy]

    def finish(self):
        for copy in self.open:
            copy.wait()


def greet(place, xs=(), ctx=(), chain=(), core=False, between=None):
    bar = pltpu.get_barrier_semaphore()
    n = 0
    for d in xs:
        pl.semaphore_signal(bar, inc=1, device_id={"fsdp": place.xs(d)}, device_id_type=MESH)
        n += 1
    for dy, dz in ctx:
        pl.semaphore_signal(bar, inc=1, device_id={"context": place.ctx(dy, dz)}, device_id_type=MESH)
        n += 1
    for d in chain:
        pl.semaphore_signal(bar, inc=1, device_id={"context": place.chain(d)}, device_id_type=MESH)
        n += 1
    if core:
        pl.semaphore_signal(bar, inc=1, device_id={"tensor": 1 - place.t}, device_id_type=MESH)
        n += 1
    if between is not None:
        between()
    pl.semaphore_wait(bar, n)


def chunk_rows(index, half):
    return pl.ds(pl.multiple_of(index * 160 + 80 * half, 16), 80)


def line_of(ref, place, half, d, cols):
    grid = ref.reshape(4, 4, 160, ref.shape[1])
    rows = pl.ds(80 * half, 80)
    if half == 0:
        return grid.at[:, lax.rem(place.z + d + 4, 4), rows, cols]
    return grid.at[lax.rem(place.y + d + 4, 4), :, rows, cols]


def gather_steps(wire, buf, own, at):
    place = wire.place
    width = own.shape[1]
    mid = width // 256 * 128
    FULL = pl.ds(at, width)
    part = {1: pl.ds(at, mid), -1: pl.ds(at + mid, width - mid)}

    def ref(h, d, cols):
        return buf.at[chunk_rows(place.along(h, d, 0), h), cols]

    def second_line(h, d, cols):
        grid = buf.reshape(4, 4, 160, buf.shape[1])
        rows = pl.ds(80 * h, 80)
        if h == 0:
            return grid.at[lax.rem(place.y + d + 4, 4), :, rows, cols]
        return grid.at[:, lax.rem(place.z + d + 4, 4), rows, cols]

    st = {}
    for h in (0, 1):
        for d in (1, -1):
            st[h, 1, d] = wire.send(own.at[pl.ds(80 * h, 80), :], ref(h, 0, FULL), context=place.along(h, d, 0))
    yield
    for d in (1, -1):
        for h in (0, 1):
            wire.recv(st[h, 1, d], ref(h, -d, FULL))
            st[h, 2, d] = wire.send(ref(h, -d, part[d]), ref(h, -d, part[d]), context=place.along(h, d, 0))
    yield
    for h in (0, 1):
        for d in (1, -1):
            wire.recv(st[h, 2, d], ref(h, 2, part[d]))
        for k in (1, -1):
            for d in (1, -1):
                cols = part[k * d]
                st[h, 3, d, k] = wire.send(second_line(h, 0, cols), second_line(h, 0, cols), context=place.along(h, 0, d))
    yield
    for h in (0, 1):
        for d in (1, -1):
            wire.recv(st[h, 3, d, 1], second_line(h, -d, part[d]))
            st[h, 4, d] = wire.send(second_line(h, -d, part[d]), second_line(h, -d, part[d]), context=place.along(h, 0, d))
    yield
    for h in (0, 1):
        for d in (1, -1):
            wire.recv(st[h, 3, d, -1], second_line(h, -d, part[-d]))
    for h in (0, 1):
        for d in (1, -1):
            wire.recv(st[h, 4, d], second_line(h, 2, part[d]))
    yield


def rows_gather_steps(wire, src, out, loc):
    place = wire.place
    x, t = place.x, place.t
    width = src.shape[1]
    h = width // 256 * 128
    LO, HI = pl.ds(0, h), pl.ds(h, width - h)
    xp, xm, xo = place.xs(1), place.xs(-1), place.xs(2)
    def hop(ref, piece, cols, d):
        return wire.send(ref, out.at[piece, t, :, cols], fsdp=place.xs(d))

    a = hop(src.at[:, LO], x, LO, 1)
    b = hop(src.at[:, HI], x, HI, -1)
    aa = hop(src.at[:, HI], x, HI, 1)
    bb = hop(src.at[:, LO], x, LO, -1)
    cores = [(x, wire.send(src, out.at[x, t], tensor=1 - t))]
    own = loc.start(src, out.at[x, t])
    yield
    wire.recv(a, out.at[xm, t, :, LO])
    e = hop(out.at[xm, t, :, LO], xm, LO, 1)
    wire.recv(b, out.at[xp, t, :, HI])
    f = hop(out.at[xp, t, :, HI], xp, HI, -1)
    yield
    wire.recv(aa, out.at[xm, t, :, HI])
    cores.append((xm, wire.send(out.at[xm, t], out.at[xm, t], tensor=1 - t)))
    wire.recv(bb, out.at[xp, t, :, LO])
    cores.append((xp, wire.send(out.at[xp, t], out.at[xp, t], tensor=1 - t)))
    yield
    wire.recv(e, out.at[xo, t, :, LO])
    wire.recv(f, out.at[xo, t, :, HI])
    cores.append((xo, wire.send(out.at[xo, t], out.at[xo, t], tensor=1 - t)))
    yield
    for k, n in cores:
        wire.recv(n, out.at[k, 1 - t])
    loc.wait(own)
    yield


class RowsScatter:
    def __init__(self, wire, part, crecv, sums, r1, r2, piece=512, own=None):
        self.wire, self.part, self.crecv, self.sums, self.r1, self.r2 = wire, part, crecv, sums, r1, r2
        self.piece, self.n = piece, {}
        place = wire.place
        self.x, self.t = place.x, place.t
        self.own = own if own is not None else part.at[:, self.t]
        self.xp, self.xm, self.xo = place.xs(1), place.xs(-1), place.xs(2)

    def cut(self, i):
        at, half = i * self.piece, self.piece // 2
        return pl.ds(at, self.piece), pl.ds(at, half), pl.ds(at + half, half)

    def rows(self, fn):
        for i in (0, 1):
            fn(pl.ds(32 * i, 32))

    def put(self, n, k, cols, extra=None):
        def fn(r):
            v = self.own[k, r, cols].astype(f32) + self.crecv[k, r, cols].astype(f32)
            if extra is not None:
                v = v + self.r1[extra, r, cols].astype(f32)
            self.sums[n, r, cols] = v.astype(bf16)

        self.rows(fn)

    def a(self, i):
        cols = self.cut(i)[0]
        self.n["a", i] = self.wire.send(self.part.at[:, 1 - self.t, :, cols], self.crecv.at[:, :, cols], tensor=1 - self.t)

    def b(self, i):
        cols, lo, hi = self.cut(i)
        self.wire.recv(self.n["a", i], self.crecv.at[:, :, cols])
        self.put(0, self.xo, cols)
        self.n["b", i] = self.wire.send(self.sums.at[0, :, lo], self.r1.at[0, :, lo], fsdp=self.xp)
        self.n["c", i] = self.wire.send(self.sums.at[0, :, hi], self.r1.at[1, :, hi], fsdp=self.xm)

    def c(self, i):
        cols, lo, hi = self.cut(i)
        self.wire.recv(self.n["b", i], self.r1.at[0, :, lo])
        self.put(1, self.xp, lo, 0)
        self.put(1, self.xp, hi)
        self.n["d", i] = self.wire.send(self.sums.at[1, :, cols], self.r2.at[0, :, cols], fsdp=self.xp)
        self.wire.recv(self.n["c", i], self.r1.at[1, :, hi])
        self.put(2, self.xm, lo)
        self.put(2, self.xm, hi, 1)
        self.n["e", i] = self.wire.send(self.sums.at[2, :, cols], self.r2.at[1, :, cols], fsdp=self.xm)

    def d(self, i, done):
        cols = self.cut(i)[0]
        self.wire.recv(self.n["d", i], self.r2.at[0, :, cols])
        self.wire.recv(self.n["e", i], self.r2.at[1, :, cols])

        def total(r):
            done(
                cols,
                r,
                self.own[self.x, r, cols].astype(f32)
                + self.crecv[self.x, r, cols].astype(f32)
                + self.r2[0, r, cols].astype(f32)
                + self.r2[1, r, cols].astype(f32),
            )

        self.rows(total)

    def steps(self, compute, done):
        count = self.sums.shape[2] // self.piece
        for i in range(count + 3):
            if i < count:
                compute(i)
                self.a(i)
            if 0 <= i - 1 < count:
                self.b(i - 1)
            if 0 <= i - 2 < count:
                self.c(i - 2)
            if 0 <= i - 3 < count:
                self.d(i - 3, done)
            yield


def drain(steps):
    for _ in steps:
        pass


def pump(steps, n=1):
    for _ in range(n):
        next(steps, None)


def gelu(v):
    return 0.5 * v * (1.0 + jnp.tanh(0.7978845608028654 * (v + 0.044715 * v * v * v)))


def gelu_and_slope(v):
    u = jnp.tanh(0.7978845608028654 * (v + 0.044715 * v * v * v))
    slope = 0.5 * (1.0 + u) + 0.5 * v * (1.0 - u * u) * (
        0.7978845608028654 * (1.0 + 3 * 0.044715 * v * v)
    )
    return 0.5 * v * (1.0 + u), slope


def one_less_exp(v):
    series = 1.0 + v * (1.0 / 7.0)
    for k in (6.0, 5.0, 4.0, 3.0, 2.0):
        series = 1.0 + v * (1.0 / k) * series
    return jnp.where(v > -0.35, -v * series, 1.0 - jnp.exp(v))


def sigmoid(v):
    return 1.0 / (1.0 + jnp.exp(-v))


def shifted(block, edge, k):
    moved = pltpu.roll(block, k, 0)
    first = jnp.where(
        lax.broadcasted_iota(jnp.int32, edge.shape, 0) < k, pltpu.roll(edge, k, 0), moved[:8]
    )
    return jnp.concatenate([first, moved[8:]], axis=0)


def scan_down(a, b):
    rows = lax.broadcasted_iota(jnp.int32, a.shape, 0)
    s = 1
    while s < a.shape[0]:
        earlier = rows >= s
        pa = jnp.where(earlier, pltpu.roll(a, s, 0), 1.0)
        pb = jnp.where(earlier, pltpu.roll(b, s, 0), 0.0)
        b = b + a * pb
        a = a * pa
        s *= 2
    return a, b


def scan_up(a, b):
    rows = lax.broadcasted_iota(jnp.int32, a.shape, 0)
    n = a.shape[0]
    s = 1
    while s < n:
        later = rows < n - s
        pa = jnp.where(later, pltpu.roll(a, n - s, 0), 1.0)
        pb = jnp.where(later, pltpu.roll(b, n - s, 0), 0.0)
        b = b + a * pb
        a = a * pa
        s *= 2
    return a, b


def selector(g):
    i = lax.broadcasted_iota(jnp.int32, (256, 512), 0)
    j = lax.broadcasted_iota(jnp.int32, (256, 512), 1)
    xx, cc, r = i // 64, (i // 4) % 16, i % 4
    return (j == cc * 32 + xx * 8 + g * 4 + r).astype(f32).astype(bf16)


def gate_matrix(packed, g):
    return dot(selector(g), packed).astype(bf16)


def column(tile, tiles=1):
    return pl.ds(pl.multiple_of(128 + 256 * tile, 128), 256 * tiles)


def triple(j):
    return column(jnp.where(j == 3, 3, 6 + 3 * j), 3)


def head_count(x):
    return jnp.where(x == 0, 2, 1).astype(jnp.int32)


def lanes(h):
    return pl.ds(pl.multiple_of(h * 256, 256), 256)


def token_rows(g):
    return pl.ds(pl.multiple_of(g * 128, 128), 128)


def recur_terms(lx, la, cl, sp, keep):
    sx, sa = sigmoid(lx), sigmoid(la)
    log_decay = (-gate_scale) * sa * sp
    grown = one_less_exp(2.0 * log_decay)
    root = jnp.sqrt(grown)
    factor = root * keep + 1.0 - keep
    return sx, sa, log_decay, root, factor


HEAD_START = (0, 2, 3, 4)
HEADS_OF = (2, 1, 1, 1)
FF_START = (0, 768, 1792, 2816)
TILE_ORDER = ((0, 1, 2), (3, 0, 1, 2), (3, 0, 1, 2), (3, 0, 1, 2))


def restored_granule(m):
    return 4 * (m % 16) + m // 16


def permuted_granule(m):
    return 16 * (m % 4) + m // 4


def moved_tile(get, q, shape, granule):
    lane = lax.broadcasted_iota(jnp.int32, shape, len(shape) - 1)
    out = jnp.zeros(shape, f32)
    at = 128 * q
    while at < 128 * q + 128:
        m = at // 40
        source = 40 * granule(m) + at - 40 * m
        p = source // 128
        stop = min(40 * m + 40, 128 * q + 128, at + 128 * p + 128 - source)
        turn = (at - 128 * q - (source - 128 * p)) % 128
        v = get(p)
        if turn:
            v = pltpu.roll(v, turn, len(shape) - 1)
        out = jnp.where((lane >= at - 128 * q) & (lane < stop - 128 * q), v, out)
        at = stop
    return out


def segment_of(place, ends):
    return sum((place >= e).astype(jnp.int32) for e in ends)


def forward_kernel(
    seq_ref, tokens, cotangent, gains, rec_ref, inp, blocks, outp, inner, down,
    w_out, act_out, gl_out, tok_out, gains_out, lx_out, la_out, hid_out, py_out, low_out, cg_out, nm_out, resid_out,
    xbuf, wide, chunk0, chunk1, chunk2, w1, act, lx_s, la_s, hid_s, py_s, low_s, halo, cum_s, cg, cin,
    part, crecv, sums, r1, r2, normed, resid, packed, gates,
    p_ref, n_ref, cot_ref, tok_ref, gain_ref,
    ss, rs, ls,
):
    place = Place()
    x, c, t = place.x, place.c, place.t
    wire, loc = Wire(place, ss, rs), Local(ls)
    nh = head_count(x)

    def weight_tile(k, tile):
        heads = HEADS_OF[k]
        if tile < 3 * heads:
            at = 256 * (HEAD_START[k] + tile % heads)
            ref = (inp.at[0], inp.at[1], outp)[tile // heads]
        else:
            kind = (tile - 6) % 3 if tile >= 6 else tile - 3
            j = (tile - 6) // 3 if tile >= 6 else 3
            at = FF_START[k] + 256 * j
            ref = (inner.at[0], inner.at[1], down)[kind]
        return ref[:, pl.ds(at, 256)]

    def pack(first, count):
        for k in range(4):
            for tile in range(first, first + count):
                v = jnp.concatenate([weight_tile(k, tile), jnp.zeros((8, 256), f32)], axis=0)
                p_ref[k, :, pl.ds(128 + 256 * tile, 256)] = v.astype(bf16)

    def pack_first():
        for k in range(4):
            heads = HEADS_OF[k]
            rows = [
                jnp.concatenate([blocks[g, HEAD_START[k] + h] for h in range(heads)] + [jnp.zeros((4, 512 - 256 * heads), f32)] * (heads < 2), axis=1)
                for g in (0, 1)
            ]
            gate = jnp.concatenate([jnp.concatenate(rows, axis=0), jnp.zeros((8, 128), f32)], axis=1)
            main = jnp.concatenate([jnp.zeros((40, 128), f32), weight_tile(k, 0), weight_tile(k, 1)], axis=1)
            p_ref[k, :, pl.ds(0, FIRST)] = jnp.concatenate([main, gate], axis=0).astype(bf16)

    def prepare():
        pack_first()
        for n in (0, 1):
            for q in range(20):
                gain_ref[pl.ds(n, 1), pl.ds(128 * q, 128)] = moved_tile(
                    lambda p: gains[pl.ds(n, 1), pl.ds(128 * p, 128)], q, (1, 128), permuted_granule
                )
        ends = [seq_ref[0, 0]]
        for k in (1, 2):
            ends.append(ends[-1] + seq_ref[0, k])

        def rows(i):
            src = pl.ds(pl.multiple_of(t * 64 + 16 * i, 16), 16)
            r = pl.ds(pl.multiple_of(16 * i, 16), 16)
            where = c * 128 + t * 64 + 16 * i + lax.broadcasted_iota(jnp.int32, (16, 128), 0)
            lane = lax.broadcasted_iota(jnp.int32, (16, 128), 1)
            here = segment_of(where, ends)
            valid = (here < 3).astype(f32)
            fresh = (where == 0).astype(f32)
            for e in ends:
                fresh = jnp.maximum(fresh, (where == e).astype(f32))
            back = where - (lane - 1)
            same = (segment_of(back, ends) == here).astype(f32) * (back >= 0).astype(f32) * (lane < 5).astype(f32)
            flag = jnp.where(lane == 0, valid, jnp.where(lane == 1, 1.0 - fresh, same))
            n_ref[r, pl.ds(DIM, 128)] = flag.astype(bf16)
            for q in range(20):
                cols = pl.ds(128 * q, 128)
                tok_ref[r, cols] = moved_tile(lambda p: tokens[src, pl.ds(128 * p, 128)].astype(f32), q, (16, 128), permuted_granule)
                cot = moved_tile(lambda p: cotangent[src, pl.ds(128 * p, 128)].astype(f32), q, (16, 128), permuted_granule)
                cot_ref[r, cols] = (cot * valid).astype(bf16)
            v = tok_ref[r, :]
            inv = lax.rsqrt(jnp.mean(v * v, axis=-1, keepdims=True) + norm_eps)
            n_ref[r, pl.ds(0, DIM)] = (v * inv * gain_ref[pl.ds(0, 1), :]).astype(bf16)

        many(4, rows)

    greet(
        place, xs=(1, 2, 3), ctx=((1, 0), (2, 0), (3, 0), (0, 1), (0, 2), (0, 3)), chain=(1, -1), core=True, between=prepare
    )
    loc.start(tok_ref, tok_out)
    loc.start(gain_ref, gains_out)

    stages = ((0, FIRST, chunk0), (FIRST, SPLIT, chunk1), (SPLIT, COLS, chunk2))
    came = {}

    def spread(s):
        c0, c1, _ = stages[s]
        cs = pl.ds(c0, c1 - c0)
        for d in (2, 1, 3):
            came[s, d] = wire.send(p_ref.at[place.xs(d), :, cs], xbuf.at[x, :, cs], fsdp=place.xs(d))

    def arrange(s):
        c0, c1, chunk = stages[s]
        cs = pl.ds(c0, c1 - c0)
        for d in (1, 3, 2):
            wire.recv(came[s, d], xbuf.at[place.xs(-d), :, cs])

        for k in range(4):
            def take(src, k=k):
                v = src[k, :, cs].astype(f32)
                wide[pl.ds(40 * k, 40), cs] = v[:40]

            pl.when(x == k)(functools.partial(take, p_ref))
            pl.when(x != k)(functools.partial(take, xbuf))
        if s == 0:
            for k in range(4):
                def gate(src, k=k):
                    v = src[k, :, pl.ds(0, 512)].astype(f32)
                    for b in range(4):
                        wide[pl.ds(32 * b + 8 * k, 8), pl.ds(0, 128)] = v[40:, 128 * b : 128 * b + 128]

                pl.when(x == k)(functools.partial(gate, p_ref))
                pl.when(x != k)(functools.partial(gate, xbuf))
        chunk[...] = wide[:, cs].astype(bf16)

    mine = pl.ds(pl.multiple_of(c * 160, 16), 160)
    spread(0)
    pack(2, 4)
    spread(1)
    pack(6, 9)
    arrange(0)
    own0 = loc.start(chunk0, w1.at[mine, pl.ds(0, FIRST)])
    one = gather_steps(wire, w1, chunk0, 0)
    pump(one)
    rows = rows_gather_steps(wire, n_ref, act, loc)
    pump(rows)
    pump(one)
    arrange(1)
    own1 = loc.start(chunk1, w1.at[mine, pl.ds(FIRST, SPLIT - FIRST)])
    two = gather_steps(wire, w1, chunk1, FIRST)
    pump(two)
    loc.wait(own0)
    pump(one)
    spread(2)
    pump(rows)
    pump(two)
    pump(one)
    pump(rows)
    loc.wait(own1)
    pump(two)
    pump(rows)
    drain(one)
    drain(rows)
    loc.start(act, act_out)
    later = rows_gather_steps(wire, cot_ref, gl_out, loc)

    def project_x(h):
        ni = act[:, :, :, pl.ds(0, DIM)].reshape(512, DIM)
        low_s[0, :, lanes(h)] = dot(ni, w1[:, column(h)]).astype(bf16)

    many(nh, project_x)
    before = low_s.at[0].reshape(4, 128, 512)
    hn = wire.send(before.at[:, pl.ds(112, 16), :], halo, context=place.chain(1))
    for cc in range(16):
        for b in range(4):
            packed[pl.ds(32 * cc, 32), pl.ds(128 * b, 128)] = w1[pl.ds(160 * cc + 32 * b, 32), pl.ds(0, 128)]
    for g in (0, 1):
        gates[g] = gate_matrix(packed[...], g)
    wire.recv(hn, halo)

    def flags(g, k):
        v = act[pl.ds(g, 1), :, :, pl.ds(DIM, 128)].reshape(128, 128).astype(f32)
        return v[:, k : k + 1]

    cg[c] = jnp.zeros((2, 8, 512), f32)

    def conv(h):
        def group(g):
            bx = low_s[0, token_rows(g), lanes(h)].astype(f32)
            edge = halo[g, :, lanes(h)].astype(f32)[8:]
            out = rec_ref[pl.ds(4, 1), lanes(h)] + rec_ref[pl.ds(0, 1), lanes(h)] * bx
            for k in (1, 2, 3):
                out = out + rec_ref[pl.ds(k, 1), lanes(h)] * (flags(g, 1 + k) * shifted(bx, edge, k))
            low_s[1, token_rows(g), lanes(h)] = out.astype(bf16)

        many(4, group)
        cl = low_s[1, :, lanes(h)]
        lx_s[:, lanes(h)] = dot(cl, gates[0, :, lanes(h)]) + rec_ref[pl.ds(5, 1), lanes(h)]
        la_s[:, lanes(h)] = dot(cl, gates[1, :, lanes(h)]) + rec_ref[pl.ds(6, 1), lanes(h)]

    many(nh, conv)
    loc.start(lx_s, lx_out)
    loc.start(la_s, la_out)
    pump(later)
    pump(two)
    arrange(2)
    own2 = loc.start(chunk2, w_out.at[mine, pl.ds(SPLIT, COLS - SPLIT)])
    three = gather_steps(wire, w_out, chunk2, SPLIT)
    pump(three)

    def scan(q):
        cols = pl.ds(pl.multiple_of(q * 128, 128), 128)
        for g in range(4):
            r = pl.ds(128 * g, 128)
            keep = flags(g, 1)
            cl = low_s[1, r, cols].astype(f32)
            sx, sa, log_decay, root, factor = recur_terms(
                lx_s[r, cols], la_s[r, cols], cl, rec_ref[pl.ds(7, 1), cols], keep
            )
            a, b = scan_down(jnp.exp(log_decay) * keep, factor * sx * cl)
            cum_s[r, cols] = a
            hid_s[r, cols] = b
            cg[c, 0, pl.ds(g, 1), cols] = a[127:]
            cg[c, 1, pl.ds(g, 1), cols] = b[127:]

    many(2 * nh, scan)
    ns = [wire.send(cg.at[c], cg.at[c], context=place.ctx(0, d)) for d in (1, 2, 3)]
    for d, n in zip((1, 2, 3), ns):
        wire.recv(n, cg.at[place.ctx(0, -d)])
    line = pl.ds(place.y * 4, 4)
    ns = [wire.send(cg.at[line], cg.at[line], context=place.ctx(d, 0)) for d in (1, 2, 3)]
    for d, n in zip((1, 2, 3), ns):
        wire.recv(n, cg.at[pl.ds(lax.rem(place.y + 4 - d, 4) * 4, 4)])

    def enter(s, state):
        return cg[s, 0] * state + cg[s, 1]

    cin[...] = lax.fori_loop(0, c, enter, jnp.zeros((8, 512), f32))
    loc.start(cg, cg_out)

    pump(later)
    drain(two)
    pump(three)
    loc.start(w1, w_out.at[:, pl.ds(0, SPLIT)])
    two = three

    def project_y(h):
        ni = act[:, :, :, pl.ds(0, DIM)].reshape(512, DIM)
        py_s[:, lanes(h)] = dot(ni, w1[:, column(nh + h)])

    many(nh, project_y)
    loc.start(py_s, py_out)
    pump(later)

    def mix(h):
        for g in range(4):
            r = pl.ds(128 * g, 128)
            hid = hid_s[r, lanes(h)] + cum_s[r, lanes(h)] * cin[pl.ds(g, 1), lanes(h)]
            hid_s[r, lanes(h)] = hid
            low_s[2, r, lanes(h)] = (hid * gelu(py_s[r, lanes(h)])).astype(bf16)

    many(nh, mix)
    loc.start(hid_s, hid_out)
    loc.start(low_s, low_out)
    loc.wait(own2)
    pump(two)

    drain(later)

    def project_out(n, heads):
        r = pl.ds(512 * n, 512)
        v = dot_nt(low_s[2, :, pl.ds(0, 256 * heads)], w1[r, pl.ds(128 + 512 * heads, 256 * heads)])
        part[:, :, :, r] = v.astype(bf16).reshape(4, 2, 64, 512)

    def project_piece(n):
        pl.when(x == 0)(lambda: project_out(n, 2))
        pl.when(x != 0)(lambda: project_out(n, 1))

    def add_resid(cols, r, total):
        resid[r, cols] = tok_ref[r, cols] + total

    drain(RowsScatter(wire, part, crecv, sums, r1, r2).steps(project_piece, add_resid))
    pump(two)
    loc.start(resid, resid_out)

    def norm(i):
        r = pl.ds(pl.multiple_of(i * 16, 16), 16)
        v = resid[r, :]
        inv = lax.rsqrt(jnp.mean(v * v, axis=-1, keepdims=True) + norm_eps)
        normed[r, :] = (v * inv * gain_ref[pl.ds(1, 1), :]).astype(bf16)

    many(4, norm)
    drain(rows_gather_steps(wire, normed, nm_out, loc))
    drain(two)
    wire.finish()
    loc.finish()


def vm(shape, dtype):
    return pltpu.VMEM(shape, dtype)


PLANE = ((1, 0), (3, 0), (0, 1), (0, 3))
ANY = pl.BlockSpec(memory_space=pl.ANY)
VM = pl.BlockSpec(memory_space=pltpu.VMEM)


def forward_call(seq, tokens, cotangent, gains, rec, inp, blocks, outp, inner, down):
    S = jax.ShapeDtypeStruct
    R = (64, DIM)
    F = (512, 512)
    return pl.pallas_call(
        forward_kernel,
        name="recurrent_forward",
        out_shape=(
            S((DIM, COLS), bf16), S((4, 2, 64, EXT), bf16), S((4, 2) + R, bf16), S(R, f32), S((2, DIM), f32),
            S(F, f32), S(F, f32), S(F, f32), S(F, f32),
            S((3,) + F, bf16), S((16, 2, 8, 512), f32), S((4, 2) + R, bf16), S(R, f32),
        ),
        in_specs=[pl.BlockSpec(memory_space=pltpu.SMEM)] + [VM] * 9,
        out_specs=[ANY] * 13,
        scratch_shapes=[
            vm((4, 48, COLS), bf16), vm((160, COLS), f32), vm((160, FIRST), bf16), vm((160, SPLIT - FIRST), bf16), vm((160, COLS - SPLIT), bf16),
            vm((DIM, SPLIT), bf16), vm((4, 2, 64, EXT), bf16),
            vm(F, f32), vm(F, f32), vm(F, f32), vm(F, f32),
            vm((3,) + F, bf16), vm((4, 16, 512), bf16), vm(F, f32), vm((16, 2, 8, 512), f32), vm((8, 512), f32),
            vm((4, 2) + R, bf16), vm((4,) + R, bf16), vm((3,) + R, bf16), vm((2,) + R, bf16), vm((2,) + R, bf16),
            vm(R, bf16), vm(R, f32), vm(F, bf16), vm((2, 256, 512), bf16),
            vm((4, 48, COLS), bf16), vm((64, EXT), bf16), vm(R, bf16), vm(R, f32), vm((2, DIM), f32),
            pltpu.SemaphoreType.DMA((160,)), pltpu.SemaphoreType.DMA((160,)), pltpu.SemaphoreType.DMA((20,)),
        ],
        compiler_params=pltpu.CompilerParams(collective_id=0, has_side_effects=True, vmem_limit_bytes=60 << 20),
    )(seq, tokens, cotangent, gains, rec, inp, blocks, outp, inner, down)


def transpose_rows(src, dst):
    def block(n):
        cols = pl.ds(pl.multiple_of(n * 256, 256), 256)
        dst[cols, :] = src[:, :, :, cols].reshape(512, 256).T

    many(10, block)


def add_sublanes(v):
    return v[:8] + v[8:]


def norm_back(total, value, gain):
    inv = lax.rsqrt(jnp.mean(value * value, axis=-1, keepdims=True) + norm_eps)
    xhat = value * inv
    weighted = total * gain
    inner = jnp.mean(weighted * xhat, axis=-1, keepdims=True)
    return inv * (weighted - xhat * inner), add_sublanes(total * xhat)


def ffn_kernel(
    w_ref, gl_ref, nm, resid, gain_ref,
    g_out, ahead_out, gm_out, gres_out, gain_out, first_out, second_out,
    gl, nmt, glt, wt, gfirst, gsecond, pre, lowi, lowg, parts, crecv, sums, r1, r2, normed, own_low, gsum,
    a2, a3, a4, a5, a6, a7, d2, d3, d4, d5, d6, d7,
    ss, rs, ls, ws, gs,
):
    place = Place()
    x, t = place.x, place.t
    wire, loc = Wire(place, ss, rs), Local(ls)
    nf = 5 - head_count(x)

    def load(j):
        return pltpu.make_async_copy(w_ref.at[:, triple(j)], wt.at[j], ws.at[j])

    def store(j):
        return pltpu.make_async_copy(wt.at[j], g_out.at[:, triple(j)], gs.at[j])

    glc = loc.start(gl_ref, gl)
    for j in range(3):
        load(j).start()
    pl.when(x != 0)(lambda: load(3).start())
    olc = loc.start(gl_ref.at[x, t], own_low)
    greet(place, xs=(1, -1), ctx=PLANE, core=True)
    transpose_rows(nm, nmt)
    loc.wait(glc)
    loc.wait(olc)
    transpose_rows(gl, glt)

    def tile(j):
        load(j).wait()
        pre[:, pl.ds(0, 512)] = dot(nm[...].reshape(512, DIM), wt[j, :, pl.ds(0, 512)])
        pre[:, pl.ds(512, 256)] = dot(gl[...].reshape(512, DIM), wt[j, :, pl.ds(512, 256)])

        def point(i):
            r = pl.ds(pl.multiple_of(i * 32, 32), 32)
            gated, slope = gelu_and_slope(pre[r, pl.ds(0, 256)])
            up, gi = pre[r, pl.ds(256, 256)], pre[r, pl.ds(512, 256)]
            lowi[j, r, :] = (gated * up).astype(bf16)
            lowg[j, r, pl.ds(0, 256)] = (gi * up * slope).astype(bf16)
            lowg[j, r, pl.ds(256, 256)] = (gi * gated).astype(bf16)

        many(16, point)

    def gradient(j, dst):
        def block(n):
            r = pl.ds(pl.multiple_of(n * 512, 512), 512)
            dst[r, pl.ds(0, 512)] = dot(nmt[r, :], lowg[j]).astype(bf16)
            dst[r, pl.ds(512, 256)] = dot(glt[r, :], lowi[j]).astype(bf16)

        many(5, block)

    tile(0)
    gradient(0, gfirst)
    first = scatter_steps(wire, loc, gfirst, 0, (None, None, a2, a3, a4, a5, a6, a7), first_out, False, True, False)
    pump(first, 1)
    tile(1)
    many(nf - 2, lambda j: tile(j + 2))

    def contract(dst, low, cols, n):
        r = pl.ds(512 * n, 512)

        def total(count):
            v = dot_nt(low[0], wt[0, r, cols])
            for j in range(1, count):
                v = v + dot_nt(low[j], wt[j, r, cols])
            dst[:, :, :, r] = v.astype(bf16).reshape(4, 2, 64, 512)

        pl.when(x == 0)(lambda: total(3))
        pl.when(x != 0)(lambda: total(4))

    def keep_sum(cols, r, total):
        gsum[r, cols] = total

    back = RowsScatter(wire, parts, crecv, sums, r1, r2).steps(
        lambda n: contract(parts, lowg, pl.ds(0, 512), n), keep_sum
    )
    pump(first, 4)
    pump(back, 5)
    gradient(1, gsecond)
    second = scatter_steps(wire, loc, gsecond, 0, (None, None, d2, d3, d4, d5, d6, d7), second_out, False, True, False)
    pump(second, 1)
    for n in range(5):
        contract(gl, lowi, pl.ds(512, 256), n)
        if n % 2 == 1:
            pump(back, 1)
    loc.start(gl, ahead_out)
    pump(first, 4)
    gradient(2, wt.at[2])
    store(2).start()
    drain(back)
    gain_out[...] = jnp.zeros_like(gain_out)

    def resid_back(i):
        r = pl.ds(pl.multiple_of(i * 16, 16), 16)
        gx, gain = norm_back(gsum[r, :], resid[r, :], gain_ref[pl.ds(1, 1), :])
        gr = own_low[r, :].astype(f32) + gx
        gres_out[r, :] = gr
        normed[r, :] = gr.astype(bf16)
        gain_out[...] += gain

    many(4, resid_back)
    rows = rows_gather_steps(wire, normed, gm_out, loc)
    pump(rows, 1)
    pump(second, 4)
    pump(rows, 1)

    @pl.when(x != 0)
    def _():
        gradient(3, wt.at[3])
        store(3).start()

    pump(rows, 1)
    pump(first, 1)
    drain(rows)
    pump(second, 4)
    pump(first, 1)
    pump(second, 1)
    drain(first)
    drain(second)
    store(2).wait()
    pl.when(x != 0)(lambda: store(3).wait())
    wire.finish()
    loc.finish()


def ffn_call(w, gl, nm, resid, gain):
    S = jax.ShapeDtypeStruct
    R = (64, DIM)
    slices = scatter_scratch(TRIPLE)[2:]
    return pl.pallas_call(
        ffn_kernel,
        name="feed_forward",
        out_shape=(
            S((DIM, COLS), bf16), S((4, 2) + R, bf16), S((4, 2) + R, bf16), S(R, f32), S((8, DIM), f32),
            S((4, 48, TRIPLE), bf16), S((4, 48, TRIPLE), bf16),
        ),
        in_specs=[ANY, ANY, VM, VM, VM],
        out_specs=[ANY, ANY, ANY, VM, VM, ANY, ANY],
        scratch_shapes=[
            vm((4, 2) + R, bf16), vm((DIM, 512), bf16), vm((DIM, 512), bf16), vm((4, DIM, TRIPLE), bf16), vm((DIM, TRIPLE), bf16), vm((DIM, TRIPLE), bf16),
            vm((512, TRIPLE), f32), vm((4, 512, 256), bf16), vm((4, 512, 512), bf16),
            vm((4, 2) + R, bf16), vm((4,) + R, bf16), vm((3,) + R, bf16), vm((2,) + R, bf16), vm((2,) + R, bf16),
            vm(R, bf16), vm(R, bf16), vm(R, f32),
        ] + slices + slices + [
            pltpu.SemaphoreType.DMA((170,)), pltpu.SemaphoreType.DMA((170,)), pltpu.SemaphoreType.DMA((12,)),
            pltpu.SemaphoreType.DMA((4,)), pltpu.SemaphoreType.DMA((4,)),
        ],
        compiler_params=pltpu.CompilerParams(collective_id=1, has_side_effects=True, vmem_limit_bytes=60 << 20),
    )(w, gl, nm, resid, gain)


def scatter_steps(wire, loc, g_ref, at, bufs, out_ref, gates, resident=False, spread=True):
    gvn, gvo, r1, r2, r3, r4, wide, obuf = bufs
    place = wire.place
    x, c = place.x, place.c
    width = wide.shape[1]
    mid = width // 256 * 128
    LO, HI, FULL = (0, mid), (mid, width), (0, width)
    zero = {1: LO, -1: HI}
    other = {1: HI, -1: LO}

    def cut(k):
        return pl.ds(k[0], k[1] - k[0])

    def short(k):
        return pl.ds(0, k[1] - k[0])

    def wide_cut(k):
        return pl.ds(at + k[0], k[1] - k[0])

    def group(h, d, k):
        return line_of(g_ref, place, h, d, wide_cut(k))

    def index(h, d, q):
        return q * 4 + lax.rem(place.z + d + 4, 4) if h == 0 else lax.rem(place.y + d + 4, 4) * 4 + q

    side = {1: 0, -1: 1}
    ends = {0: place.y, 1: place.z}
    st, loads = {}, {}

    class Piece:
        def __init__(self, h, d, k, ref):
            self.h, self.d, self.k, self.ref = h, d, k, ref

        def at(self, q, half):
            c0, c1 = self.k
            if half is not None:
                c0, c1 = (c0, mid) if half == 0 else (mid, c1)
            if resident:
                return g_ref, chunk_rows(index(self.h, self.d, q), self.h), wide_cut((c0, c1))
            return self.ref.at[q], pl.ds(0, 80), (short((c0, c1)) if self.d else cut((c0, c1)))

    def add_near(piece, got):
        def one(q):
            ref, r, cols = piece.at(q, None)
            ref[r, cols] = ref[r, cols] + got[q]

        many(4, one)

    def add_own(piece, srcs):
        def one(q):
            for half in (0, 1):
                ref, r, cols = piece.at(q, half)
                v = ref[r, cols].astype(f32)
                for s in srcs:
                    v = v + s[q, :, cut((LO, HI)[half])].astype(f32)
                ref[r, cols] = v.astype(bf16)

        many(4, one)

    def mine_at(h, q, k):
        if resident:
            return g_ref.at[chunk_rows(index(h, 0, q), h), wide_cut(k)]
        return gvo.at[h, q, :, cut(k)]

    for h in (0, 1):
        for d in (1, -1):
            k = zero[d]
            st[h, 1, d] = wire.send(group(h, 2, k), r1.at[h, side[d], :, :, short(k)], context=place.along(h, d, 0))
    if not resident:
        for h in (0, 1):
            for d in (1, -1):
                loads[h, d] = loc.start(group(h, d, zero[d]), gvn.at[h, side[d], :, :, short(zero[d])])
        for h in (0, 1):
            loads[h, 0] = loc.start(group(h, 0, FULL), gvo.at[h])
    for h in (0, 1):
        for d in (1, -1):
            k = other[d]
            st[h, 2, d] = wire.send(group(h, d, k), r2.at[h, side[d], :, :, cut(k)], context=place.along(h, d, 0))
    yield

    def add(dst, srcs):
        def one(i):
            r = pl.ds(pl.multiple_of(i * 16, 16), 16)
            v = srcs[0][r, :].astype(f32)
            for s in srcs[1:]:
                v = v + s[r, :].astype(f32)
            dst[r, :] = v.astype(dst.dtype)

        many(5, one)

    for h in (0, 1):
        for d in (1, -1):
            k = zero[d]
            if not resident:
                loc.wait(loads[h, d])
            got = r1.at[h, side[d], :, :, short(k)]
            wire.recv(st[h, 1, d], got)
            piece = Piece(h, d, k, None if resident else gvn.at[h, side[d]])
            add_near(piece, got)
            src = group(h, d, k) if resident else gvn.at[h, side[d], :, :, short(k)]
            st[h, 3, d] = wire.send(src, r2.at[h, side[d], :, :, cut(k)], context=place.along(h, d, 0))
            yield
    for h in (0, 1):
        if not resident:
            loc.wait(loads[h, 0])
        for d in (1, -1):
            wire.recv(st[h, 2, d], r2.at[h, side[d], :, :, cut(other[d])])
            wire.recv(st[h, 3, d], r2.at[h, side[d], :, :, cut(zero[d])])
        add_own(Piece(h, 0, FULL, None if resident else gvo.at[h]), [r2.at[h, 0], r2.at[h, 1]])
        far = lax.rem(ends[h] + 2, 4)
        for d in (1, -1):
            st[h, 4, d] = wire.send(
                mine_at(h, far, zero[d]), r3.at[h, side[d], :, short(zero[d])], context=place.along(h, 0, d)
            )
        for d in (1, -1):
            near = lax.rem(ends[h] + d + 4, 4)
            st[h, 5, d] = wire.send(
                mine_at(h, near, other[d]), r4.at[h, side[d], :, cut(other[d])], context=place.along(h, 0, d)
            )
        yield
        yield
    for h in (0, 1):
        for d in (1, -1):
            k = zero[d]
            mine = mine_at(h, lax.rem(ends[h] + d + 4, 4), k)
            got = r3.at[h, side[d], :, short(k)]
            wire.recv(st[h, 4, d], got)
            add(mine, [mine, got])
            st[h, 6, d] = wire.send(mine, r4.at[h, side[d], :, cut(k)], context=place.along(h, 0, d))
    yield
    for h in (0, 1):
        for d in (1, -1):
            wire.recv(st[h, 5, d], r4.at[h, side[d], :, cut(other[d])])
            wire.recv(st[h, 6, d], r4.at[h, side[d], :, cut(zero[d])])
        add(wide.at[pl.ds(80 * h, 80), :], [mine_at(h, ends[h], FULL), r4.at[h, 0], r4.at[h, 1]])
    for k in range(4):
        obuf[k] = jnp.concatenate([wide[pl.ds(40 * k, 40), :], jnp.zeros((8, width), f32)], axis=0).astype(bf16)
        if gates:
            tail = jnp.concatenate([wide[pl.ds(32 * b + 8 * k, 8), pl.ds(0, 128)] for b in range(4)], axis=1)
            obuf[k, :, pl.ds(0, 512)] = jnp.concatenate([wide[pl.ds(40 * k, 40), pl.ds(0, 512)], tail], axis=0).astype(bf16)
    if not spread:
        own = loc.start(obuf, out_ref)
        yield
        loc.wait(own)
        yield
        return
    sent = [(d, wire.send(obuf.at[place.xs(d)], out_ref.at[x], fsdp=place.xs(d))) for d in (1, 3, 2)]
    own = loc.start(obuf.at[x], out_ref.at[x])
    yield
    for d, n in sent:
        wire.recv(n, out_ref.at[place.xs(-d)])
    loc.wait(own)
    yield


def scatter_scratch(width):
    hi = width - width // 256 * 128
    return [
        vm((2, 2, 4, 80, hi), bf16), vm((2, 4, 80, width), bf16), vm((2, 2, 4, 80, hi), bf16), vm((2, 2, 4, 80, width), bf16),
        vm((2, 2, 80, hi), bf16), vm((2, 2, 80, width), bf16), vm((160, width), f32), vm((4, 48, width), bf16),
    ]


def small_steps(wire, mine, zin, yin, xin, corein):
    place = wire.place
    x = place.x
    ns = [wire.send(mine.at[0], zin.at[d - 1], context=place.ctx(0, d)) for d in (1, 2, 3)]
    yield
    for d, n in zip((1, 2, 3), ns):
        wire.recv(n, zin.at[d - 1])
    mine[1] = mine[0] + zin[0] + zin[1] + zin[2]
    ns = [wire.send(mine.at[1], yin.at[d - 1], context=place.ctx(d, 0)) for d in (1, 2, 3)]
    yield
    for d, n in zip((1, 2, 3), ns):
        wire.recv(n, yin.at[d - 1])
    total = mine[1] + yin[0] + yin[1] + yin[2]
    mine[2] = total
    xin[x] = total
    ns = [wire.send(mine.at[2], xin.at[x], fsdp=place.xs(d)) for d in (1, 2, 3)]
    yield
    for d, n in zip((1, 2, 3), ns):
        wire.recv(n, xin.at[place.xs(-d)])
    mine[3] = xin[0] + xin[1] + xin[2] + xin[3]
    n = wire.send(mine.at[3], corein, tensor=1 - place.t)
    yield
    wire.recv(n, corein)
    yield


def fold(dst, row, at):
    for i in range(20):
        dst[pl.ds(i // 3, 1), pl.ds(at + 128 * (i % 3), 128)] = row[:, 128 * i : 128 * i + 128]


def backward_kernel(
    g_ref, w_ref, act_ref, gm_ref, first_ref, second_ref, ahead_ref,
    lx_ref, la_ref, hid_ref, py_ref, low_ref, cg, tok_ref, gres, resid, gain_ref, rec_ref, gain_two,
    t0_out, t1_out, t2_out, mid_out, last_out, mixed_out, tgrad_out, recur_out, gains_out,
    a0, a1, a2, a3, a4, a5, a6, a7, b2, b3, b4, b5, b6, b7, c2, c3, c4, c5, c6, c7,
    w1, acts, turned, flag_s, gmx, gpy, bc, bp, bg, cin, cback, glow, edge, edge_in, edge_out, gpx, gates, packed, dgates,
    gain_acc, crecv, sums, r1, r2, own_f, crecv_f, sums_f, r1_f, r2_f,
    small, zin, yin, xin, corein, late, zin_l, yin_l, xin_l, corein_l,
    lx_s, la_s, hid_s, py_s, low_s, glast,
    ss, rs, ls, ws,
):
    part, gconv, gdir = acts, gmx, bc
    place = Place()
    x, c, t = place.x, place.c, place.t
    wire, loc = Wire(place, ss, rs), Local(ls)
    nh = head_count(x)
    rest = pl.ds(FIRST + 256, TRIPLE)
    both = pl.ds(0, FIRST + 256)
    lg = loc.start(gm_ref, acts)
    lw = loc.start(w_ref.at[:, both], w1.at[:, both])
    load_w = pltpu.make_async_copy(w_ref.at[:, rest], w1.at[:, rest], ws.at[0])
    load_g = pltpu.make_async_copy(g_ref.at[:, rest], w1.at[:, rest], ws.at[1])
    pl.when(x == 0)(lambda: load_w.start())
    pl.when(x != 0)(lambda: load_g.start())
    lf = loc.start(act_ref.at[:, :, :, pl.ds(DIM, 128)], flag_s)
    li = [loc.start(a, b) for a, b in ((low_ref, low_s), (py_ref, py_s), (hid_ref, hid_s), (la_ref, la_s), (lx_ref, lx_s))]
    lo = loc.start(ahead_ref.at[:, t], own_f)
    greet(place, xs=(1, 2, 3), ctx=((1, 0), (2, 0), (3, 0), (0, 1), (0, 2), (0, 3)), chain=(1, -1), core=True)
    big = scatter_steps(wire, loc, g_ref, SPLIT + 2 * TRIPLE, (a0, a1, a2, a3, a4, a5, a6, a7), t2_out, False)
    pump(big, 1)

    def keep_mixed(cols, r, total):
        mixed_out[t, r, cols] = (resid[r, cols] + total).astype(bf16)

    ahead = RowsScatter(wire, ahead_ref, crecv_f, sums_f, r1_f, r2_f, own=own_f).steps(lambda n: None, keep_mixed)
    fro = []
    for src, dst in ((first_ref, t0_out), (second_ref, t1_out)):
        for d in (2, 1, 3):
            fro.append((d, dst, wire.send(src.at[place.xs(d)], dst.at[x], fsdp=place.xs(d))))
        loc.start(src.at[x], dst.at[x])
    for copy in li:
        loc.wait(copy)
    before = low_s.at[0].reshape(4, 128, 512)
    hn = wire.send(before.at[:, pl.ds(112, 16), :], edge_in, context=place.chain(1))
    loc.wait(lg)
    loc.wait(lw)
    loc.wait(lf)
    loc.wait(lo)
    pl.when(x == 0)(lambda: load_w.wait())
    pl.when(x != 0)(lambda: load_g.wait())
    for cc in range(16):
        for b in range(4):
            packed[pl.ds(32 * cc, 32), pl.ds(128 * b, 128)] = w1[pl.ds(160 * cc + 32 * b, 32), pl.ds(0, 128)]
    small[...] = jnp.zeros_like(small)
    late[...] = jnp.zeros_like(late)
    fold(small.at[0], jnp.sum(gain_two[...], axis=0, keepdims=True), 512)

    def flags(g, k):
        return flag_s[pl.ds(g, 1)].reshape(128, 128).astype(f32)[:, k : k + 1]

    def put_tile(rhs, dst, cols):
        def block(n):
            r = pl.ds(pl.multiple_of(n * 512, 512), 512)
            dst[r, cols] = dot(turned[r, :], rhs).astype(bf16)

        many(5, block)

    def mixed_back(h):
        gmx[:, lanes(h)] = dot(acts[...].reshape(512, DIM), w1[:, column(2 * nh + h)])

    many(nh, mixed_back)

    bg[c] = jnp.zeros((8, 512), f32)

    def scan(q):
        cols = pl.ds(pl.multiple_of(q * 128, 128), 128)
        for g in range(4):
            r = pl.ds(128 * g, 128)
            gated, slope = gelu_and_slope(py_s[r, cols])
            grad = gmx[r, cols]
            gpy[r, cols] = (grad * hid_s[r, cols] * slope).astype(bf16)
            keep = flags(g, 1)
            dec = jnp.exp((-gate_scale) * sigmoid(la_s[r, cols]) * rec_ref[pl.ds(7, 1), cols]) * keep
            last = lax.broadcasted_iota(jnp.int32, dec.shape, 0) == 127
            a, b = scan_up(jnp.where(last, 1.0, pltpu.roll(dec, 127, 0)), grad * gated)
            bc[r, cols] = a
            bp[r, cols] = b
            bg[c, pl.ds(g, 1), cols] = dec[:1] * b[:1]

    many(2 * nh, scan)
    ns = [wire.send(bg.at[c], bg.at[c], context=place.ctx(0, d)) for d in (1, 2, 3)]
    transpose_rows(acts, turned)
    ln = loc.start(act_ref.at[:, :, :, pl.ds(0, DIM)], acts)

    many(nh, lambda h: put_tile(low_s[2, :, lanes(h)], w1, column(2 * nh + h)))
    pump(ahead, 2)
    pump(big, 4)
    for d, n in zip((1, 2, 3), ns):
        wire.recv(n, bg.at[place.ctx(0, -d)])
    line = pl.ds(place.y * 4, 4)
    ns = [wire.send(bg.at[line], bg.at[line], context=place.ctx(d, 0)) for d in (1, 2, 3)]
    for g in (0, 1):
        gates[g] = gate_matrix(packed[...], g)
    loc.wait(ln)
    transpose_rows(acts, turned)

    def norm_grad_y(heads):
        def block(n):
            r = pl.ds(pl.multiple_of(n * 512, 512), 512)
            v = dot_nt(gpy[:, pl.ds(0, 256 * heads)], w1[r, pl.ds(128 + 256 * heads, 256 * heads)])
            part[:, :, :, r] = v.astype(bf16).reshape(4, 2, 64, 512)

        many(5, block)

    pl.when(x == 0)(lambda: norm_grad_y(2))
    pl.when(x != 0)(lambda: norm_grad_y(1))
    pl.when(x == 0)(lambda: many(2, lambda h: put_tile(gpy[:, lanes(h)], w1, column(2 + h))))
    pl.when(x != 0)(lambda: put_tile(gpy[:, pl.ds(0, 256)], glast, pl.ds(384, 256)))
    mid = scatter_steps(wire, loc, w1, FIRST, (None, None, b2, b3, b4, b5, b6, b7), mid_out, False, True)
    pump(mid, 1)
    pump(ahead, 2)
    for d, n in zip((1, 2, 3), ns):
        wire.recv(n, bg.at[pl.ds(lax.rem(place.y + 4 - d, 4) * 4, 4)])

    def enter(s, state):
        return cg[s, 0] * state + cg[s, 1]

    cin[...] = lax.fori_loop(0, c, enter, jnp.zeros((8, 512), f32))

    def leave(s, state):
        k = 15 - s
        return cg[k, 0] * state + bg[k]

    cback[...] = lax.fori_loop(0, 15 - c, leave, jnp.zeros((8, 512), f32))
    def terms(q):
        cols = pl.ds(pl.multiple_of(q * 128, 128), 128)
        sums_x = jnp.zeros((1, 128), f32)
        sums_a = jnp.zeros((1, 128), f32)
        sums_l = jnp.zeros((1, 128), f32)
        for g in range(4):
            r = pl.ds(128 * g, 128)
            keep = flags(g, 1)
            cl = low_s[1, r, cols].astype(f32)
            sp, dsp = rec_ref[pl.ds(7, 1), cols], rec_ref[pl.ds(8, 1), cols]
            sx, sa, log_decay, root, factor = recur_terms(lx_s[r, cols], la_s[r, cols], cl, sp, keep)
            adj = bp[r, cols] + bc[r, cols] * cback[pl.ds(g, 1), cols]
            hid = hid_s[r, cols]
            first = lax.broadcasted_iota(jnp.int32, hid.shape, 0) == 0
            prev = jnp.where(first, cin[pl.ds(g, 1), cols], pltpu.roll(hid, 1, 0))
            grown = jnp.exp(log_decay)
            gld = keep * grown * (adj * prev - adj * sx * cl * grown / root)
            glx = (adj * factor * cl * sx * (1.0 - sx)).astype(bf16)
            gla = (gld * ((-gate_scale) * sp) * sa * (1.0 - sa)).astype(bf16)
            glow[0, r, cols] = glx
            glow[1, r, cols] = gla
            gdir[r, cols] = adj * factor * sx
            sums_x += jnp.sum(glx.astype(f32), axis=0, keepdims=True)
            sums_a += jnp.sum(gla.astype(f32), axis=0, keepdims=True)
            sums_l += jnp.sum(gld * sa, axis=0, keepdims=True) * (gate_scale * dsp)
        small[0, pl.ds(5, 1), cols] = sums_x
        small[0, pl.ds(6, 1), cols] = sums_a
        small[0, pl.ds(7, 1), cols] = sums_l

    many(2 * nh, terms)
    wire.recv(hn, edge_in)

    def conv_back(h):
        cl = low_s[1, :, lanes(h)]
        lx, la = glow[0, :, lanes(h)], glow[1, :, lanes(h)]
        gconv[:, lanes(h)] = (
            gdir[:, lanes(h)] + dot_nt(lx, gates[0, :, lanes(h)]) + dot_nt(la, gates[1, :, lanes(h)])
        )

        def group(g, taps):
            gc = gconv[token_rows(g), lanes(h)]
            bx = low_s[0, token_rows(g), lanes(h)].astype(f32)
            ahead = edge_in[g, :, lanes(h)].astype(f32)[8:]
            rows = lax.broadcasted_iota(jnp.int32, gc.shape, 0)
            low_rows = lax.broadcasted_iota(jnp.int32, (8, 256), 0)
            out = rec_ref[pl.ds(0, 1), lanes(h)] * gc
            over = jnp.zeros((8, 256), f32)
            new = [taps[0] + jnp.sum(bx * gc, axis=0, keepdims=True)]
            for k in (1, 2, 3):
                masked = flags(g, 1 + k) * gc
                new.append(taps[k] + jnp.sum(shifted(bx, ahead, k) * masked, axis=0, keepdims=True))
                scaled = rec_ref[pl.ds(k, 1), lanes(h)] * masked
                out = out + jnp.where(rows < 128 - k, pltpu.roll(scaled, 128 - k, 0), 0.0)
                over = over + jnp.where(low_rows >= 8 - k, pltpu.roll(scaled[:8], 8 - k, 0), 0.0)
            new.append(taps[4] + jnp.sum(gc, axis=0, keepdims=True))
            gdir[token_rows(g), lanes(h)] = out
            edge[g, :, lanes(h)] = over
            return tuple(new)

        taps = lax.fori_loop(0, 4, group, tuple(jnp.zeros((1, 256), f32) for _ in range(5)))
        for k in range(5):
            small[0, pl.ds(k, 1), lanes(h)] = taps[k]

    many(nh, conv_back)
    en = wire.send(edge, edge_out, context=place.chain(-1))

    early = small_steps(wire, small, zin, yin, xin, corein)
    pump(early)
    pump(big, 4)
    pump(ahead, 2)

    def gate_back(h):
        cl = low_s[1, :, lanes(h)]
        dgates[0, :, lanes(h)] = dot_tn(cl, glow[0, :, lanes(h)]).astype(bf16)
        dgates[1, :, lanes(h)] = dot_tn(cl, glow[1, :, lanes(h)]).astype(bf16)

    many(nh, gate_back)
    wire.recv(en, edge_out)

    def narrow(h):
        for g in range(4):
            v = gdir[pl.ds(128 * g, 128), lanes(h)]
            tail = v[120:] + edge_out[g, :, lanes(h)]
            gpx[pl.ds(128 * g, 128), lanes(h)] = jnp.concatenate([v[:120], tail], axis=0).astype(bf16)

    many(nh, narrow)

    def norm_grad(n, heads):
        r = pl.ds(512 * n, 512)
        v = dot_nt(gpx[:, pl.ds(0, 256 * heads)], w1[r, pl.ds(128, 256 * heads)])
        v = v + part[:, :, :, r].reshape(512, 512).astype(f32)
        part[:, :, :, r] = v.astype(bf16).reshape(4, 2, 64, 512)

    def norm_piece(n):
        pl.when(x == 0)(lambda: norm_grad(n, 2))
        pl.when(x != 0)(lambda: norm_grad(n, 1))

    def keep_sum(cols, r, total):
        tgrad_out[t, r, cols] = total

    pump(mid, 4)
    many(nh, lambda h: put_tile(gpx[:, lanes(h)], glast, column(h)))
    back = (dot_tn(selector(0), dgates[0]) + dot_tn(selector(1), dgates[1])).astype(bf16)
    glast[:, pl.ds(0, 128)] = jnp.zeros((DIM, 128), bf16)
    for cc in range(16):
        for b in range(4):
            glast[pl.ds(160 * cc + 32 * b, 32), pl.ds(0, 128)] = back[32 * cc : 32 * cc + 32, 128 * b : 128 * b + 128]
    last = scatter_steps(wire, loc, glast, 0, (None, None, c2, c3, c4, c5, c6, c7), last_out, True, True)
    pump(last, 1)
    final = RowsScatter(wire, part, crecv, sums, r1, r2).steps(norm_piece, keep_sum)
    pump(final, 5)
    pump(early)
    pump(big, 1)
    pump(final, 1)
    pump(last, 4)
    pump(early)
    pump(final, 1)
    drain(final)
    gain_acc[...] = jnp.zeros_like(gain_acc)

    def finish(i):
        r = pl.ds(pl.multiple_of(i * 16, 16), 16)
        gx, gain = norm_back(tgrad_out[t, r, :], tok_ref[r, :], gain_ref[pl.ds(0, 1), :])
        tgrad_out[t, r, :] = gres[r, :] + gx
        gain_acc[...] += gain

    many(4, finish)
    tn = wire.send(tgrad_out.at[t], tgrad_out.at[t], tensor=1 - t)
    fold(late.at[0], jnp.sum(gain_acc[...], axis=0, keepdims=True), 0)
    tail = small_steps(wire, late, zin_l, yin_l, xin_l, corein_l)
    pump(tail)
    pump(mid, 4)
    pump(early)
    pump(tail)
    pump(last, 4)
    pump(big, 1)
    pump(tail)
    pump(mid, 1)
    pump(early)
    pump(last, 1)
    pump(tail)
    drain(ahead)
    mn = wire.send(mixed_out.at[t], mixed_out.at[t], tensor=1 - t)
    pump(mid, 1)
    pump(last, 1)
    drain(big)
    drain(mid)
    drain(tail)
    drain(early)
    for k in range(4):
        recur_out[k] = xin[k, :, pl.ds(0, 512)]
    gains_out[0] = late[3] + corein_l[...]
    gains_out[1] = small[3, :, pl.ds(512, 384)] + corein[:, pl.ds(512, 384)]
    drain(last)
    for d, dst, n in fro:
        wire.recv(n, dst.at[place.xs(-d)])
    wire.recv(mn, mixed_out.at[1 - t])
    wire.recv(tn, tgrad_out.at[1 - t])
    wire.finish()
    loc.finish()


def backward_call(g, w, act, gm, first, second, ahead, lx, la, hid, py, low, cg, tok, gres, resid, gain, rec, gain_two):
    S = jax.ShapeDtypeStruct
    R = (64, DIM)
    F = (512, 512)
    E, L = (8, 896), (8, 384)
    slices = lambda n: S((4, 48, n), bf16)
    return pl.pallas_call(
        backward_kernel,
        name="recurrent_backward",
        out_shape=(
            slices(TRIPLE), slices(TRIPLE), slices(TRIPLE), slices(SPLIT - FIRST), slices(FIRST),
            S((2,) + R, bf16), S((2,) + R, f32), S((4, 8, 512), f32), S((2,) + L, f32),
        ),
        in_specs=[ANY] * 12 + [VM] * 7,
        out_specs=[ANY, ANY, ANY, ANY, ANY, VM, VM, VM, VM],
        scratch_shapes=scatter_scratch(TRIPLE) + scatter_scratch(SPLIT - FIRST)[2:] + scatter_scratch(FIRST)[2:] + [
            vm((DIM, SPLIT), bf16), vm((4, 2) + R, bf16), vm((DIM, 512), bf16), vm((4, 2, 64, 128), bf16),
            vm(F, f32), vm(F, bf16), vm(F, f32), vm(F, f32), vm((16, 8, 512), f32), vm((8, 512), f32), vm((8, 512), f32),
            vm((2,) + F, bf16), vm((4, 8, 512), f32), vm((4, 16, 512), bf16), vm((4, 8, 512), f32), vm(F, bf16),
            vm((2, 256, 512), bf16), vm(F, bf16), vm((2, 256, 512), bf16), vm((8, DIM), f32),
            vm((4,) + R, bf16), vm((3,) + R, bf16), vm((2,) + R, bf16), vm((2,) + R, bf16),
            vm((4,) + R, bf16), vm((4,) + R, bf16), vm((3,) + R, bf16), vm((2,) + R, bf16), vm((2,) + R, bf16),
            vm((4,) + E, f32), vm((3,) + E, f32), vm((3,) + E, f32), vm((4,) + E, f32), vm(E, f32),
            vm((4,) + L, f32), vm((3,) + L, f32), vm((3,) + L, f32), vm((4,) + L, f32), vm(L, f32),
            vm(F, f32), vm(F, f32), vm(F, f32), vm(F, f32), vm((3,) + F, bf16), vm((DIM, FIRST), bf16),
            pltpu.SemaphoreType.DMA((310,)), pltpu.SemaphoreType.DMA((310,)), pltpu.SemaphoreType.DMA((60,)),
            pltpu.SemaphoreType.DMA((2,)),
        ],
        compiler_params=pltpu.CompilerParams(collective_id=2, has_side_effects=True, vmem_limit_bytes=62 << 20),
    )(g, w, act, gm, first, second, ahead, lx, la, hid, py, low, cg, tok, gres, resid, gain, rec, gain_two)


def adam_update(weight, moment, square, gradient, rate, shrink):
    moment = beta_one * moment + (1.0 - beta_one) * gradient
    square = beta_two * square + (1.0 - beta_two) * gradient * gradient
    normed = (moment * (1.0 / (1.0 - beta_one**STEP))) / (jnp.sqrt(square * (1.0 / (1.0 - beta_two**STEP))) + adam_eps)
    return (weight - rate * (normed + shrink * weight), moment, square)


def update_kernel(
    last, mid, t0, t1, t2, recur, gains, mixed, tgrad, *refs,
):
    ins, outs, held, fresh, ls, ss = refs[:21], refs[21:44], refs[44:56], refs[56:68], refs[68], refs[69]
    mixed_out, tgrad_out = outs[:2]
    big = (2, 5, 4, 6)
    loads, stores = {}, {}
    for i, n in enumerate(big):
        for k in range(3):
            loads[n, k] = pltpu.make_async_copy(ins[3 * n + k], held[3 * i + k], ls.at[3 * i + k])
            loads[n, k].start()
            stores[n, k] = pltpu.make_async_copy(fresh[3 * i + k], outs[2 + 3 * n + k], ss.at[3 * i + k])

    def group(n):
        if n in big:
            i = big.index(n)
            return held[3 * i : 3 * i + 3], fresh[3 * i : 3 * i + 3]
        return ins[3 * n : 3 * n + 3], outs[2 + 3 * n : 5 + 3 * n]

    def ready(n):
        for k in range(3):
            loads[n, k].wait()

    def leave(n):
        for k in range(3):
            stores[n, k].start()

    def update(n, index, grad, rate=matrix_rate, shrink=weight_decay):
        old, new = group(n)
        values = adam_update(*(ref[index] for ref in old), grad, rate, shrink)
        for ref, value in zip(new, values):
            ref[index] = value

    def piece(k, tile):
        if tile < 2:
            ref, at = last, 128 + 256 * tile
        elif tile < 6:
            ref, at = mid, 256 * (tile - 2)
        else:
            ref, at = (t0, t1, t2)[(tile - 6) // 3], 256 * ((tile - 6) % 3)
        return ref[k, :, pl.ds(at, 256)].astype(f32)

    ready(2)
    for k in range(4):
        for h in range(HEADS_OF[k]):
            nh = HEADS_OF[k]
            at = 256 * (HEAD_START[k] + h)
            update(2, (0, slice(None), pl.ds(at, 256)), piece(k, h)[:40])
            update(2, (1, slice(None), pl.ds(at, 256)), piece(k, nh + h)[:40])
            b = last[k, :, pl.ds(256 * h, 256)].astype(f32)[40:]
            for g in (0, 1):
                update(3, (g, HEAD_START[k] + h), b[4 * g : 4 * g + 4])
        n = 256 * HEADS_OF[k]
        update(1, (slice(None), pl.ds(256 * HEAD_START[k], n)), recur[k, :, pl.ds(0, n)], vector_rate, 0.0)
    leave(2)
    ready(5)
    for k in range(4):
        for j in TILE_ORDER[k]:
            tile = 3 if j == 3 else 6 + 3 * j
            at = FF_START[k] + 256 * j
            update(5, (0, slice(None), pl.ds(at, 256)), piece(k, tile)[:40])
            update(5, (1, slice(None), pl.ds(at, 256)), piece(k, tile + 1)[:40])
    leave(5)
    ready(4)
    for k in range(4):
        for h in range(HEADS_OF[k]):
            at = 256 * (HEAD_START[k] + h)
            update(4, (slice(None), pl.ds(at, 256)), piece(k, 2 * HEADS_OF[k] + h)[:40])
    leave(4)
    ready(6)
    for k in range(4):
        for j in TILE_ORDER[k]:
            tile = 3 if j == 3 else 6 + 3 * j
            update(6, (slice(None), pl.ds(FF_START[k] + 256 * j, 256)), piece(k, tile + 2)[:40])
    leave(6)

    for n in (0, 1):
        for q in range(20):
            grad = moved_tile(lambda p: gains[n, pl.ds(p // 3, 1), pl.ds(128 * (p % 3), 128)], q, (1, 128), restored_granule)
            update(0, (pl.ds(n, 1), pl.ds(128 * q, 128)), grad, vector_rate, 0.0)

    def restore(i):
        t = i // 4
        r = pl.ds(pl.multiple_of((i % 4) * 16, 16), 16)
        dst = pl.ds(pl.multiple_of(i * 16, 16), 16)
        for q in range(20):
            cols = pl.ds(128 * q, 128)
            mixed_out[dst, cols] = moved_tile(lambda p: mixed[t, r, pl.ds(128 * p, 128)].astype(f32), q, (16, 128), restored_granule).astype(bf16)
            tgrad_out[dst, cols] = moved_tile(lambda p: tgrad[t, r, pl.ds(128 * p, 128)], q, (16, 128), restored_granule)

    many(8, restore)
    for n in big:
        for k in range(3):
            stores[n, k].wait()


def update_call(pieces, recur, gains, mixed, tgrad, params):
    shapes = [jax.ShapeDtypeStruct(v.shape, v.dtype) for v in params]
    outs = [jax.ShapeDtypeStruct((128, DIM), bf16), jax.ShapeDtypeStruct((128, DIM), f32)] + shapes
    place = [VM if n in (0, 1, 3) else ANY for n in range(7) for _ in range(3)]
    held = [vm(params[3 * n + k].shape, f32) for n in (2, 5, 4, 6) for k in range(3)]
    return pl.pallas_call(
        update_kernel,
        name="optimizer_step",
        out_shape=tuple(outs),
        in_specs=[VM] * 9 + place,
        out_specs=tuple([VM, VM] + place),
        scratch_shapes=held + held + [pltpu.SemaphoreType.DMA((12,)), pltpu.SemaphoreType.DMA((12,))],
        compiler_params=pltpu.CompilerParams(vmem_limit_bytes=56 << 20),
    )(*pieces, recur, gains, mixed, tgrad, *params)


def recurrent_rows(recur_params):
    x = lax.axis_index("fsdp")
    start = jnp.where(x == 0, 0, x + 1) * 256
    rec = lax.dynamic_slice_in_dim(jnp.pad(recur_params, ((0, 0), (0, 256))), start, 512, 1)
    return jnp.concatenate(
        [rec[:7], jax.nn.softplus(-rec[7:]), jax.nn.sigmoid(-rec[7:]), jnp.zeros((7, 512), f32)], axis=0
    )


def on_device(
    tokens, cotangent, seq_lengths,
    norm_gains, gains_moment, gains_square, recur_params, recur_moment, recur_square,
    input_proj, input_moment, input_square, gate_blocks, blocks_moment, blocks_square,
    output_proj, output_moment, output_square, inner_proj, inner_moment, inner_square,
    down_proj, down_moment, down_square,
):
    rec = recurrent_rows(recur_params)
    w, act, gl, tok, gains, lx, la, hid, py, low, cg, nm, resid = forward_call(
        seq_lengths, tokens, cotangent, norm_gains, rec, input_proj, gate_blocks, output_proj.T, inner_proj, down_proj.T
    )
    g, ahead, gm, gres, gain_two, first, second = ffn_call(w, gl, nm, resid, gains)
    t0, t1, t2, mid, last, mixed, tgrad, recur, gsum = backward_call(
        g, w, act, gm, first, second, ahead, lx, la, hid, py, low, cg, tok, gres, resid, gains, rec, gain_two
    )
    params = (
        norm_gains, gains_moment, gains_square, recur_params, recur_moment, recur_square,
        input_proj, input_moment, input_square, gate_blocks, blocks_moment, blocks_square,
        output_proj.T, output_moment.T, output_square.T, inner_proj, inner_moment, inner_square,
        down_proj.T, down_moment.T, down_square.T,
    )
    out = update_call((last, mid, t0, t1, t2), recur, gsum, mixed, tgrad, params)
    return out[:14] + tuple(v.T for v in out[14:17]) + out[17:20] + tuple(v.T for v in out[20:])


def solution(mesh):
    row = P(("fsdp", "context"), None)
    wide_spec = P(None, ("fsdp", "context"), "tensor")
    tall = P("tensor", ("fsdp", "context"))
    block = P(None, "tensor", ("fsdp", "context"), None)
    params = (P(),) * 3 + (P(None, "tensor"),) * 3 + (wide_spec,) * 3 + (block,) * 3 + (tall,) * 3 + (wide_spec,) * 3 + (tall,) * 3
    return jax.shard_map(
        on_device, mesh=mesh, in_specs=(row, row, P("fsdp", None)) + params, out_specs=(row, row) + params, check_vma=False
    )
```

```python
import functools

import jax
import jax.numpy as jnp
from jax import lax
from jax.experimental import pallas as pl
from jax.experimental.pallas import tpu as pltpu
from jax.sharding import PartitionSpec as P

STEP = 10

norm_eps = 1e-06
beta_one = 0.9
beta_two = 0.95
adam_eps = 1e-08
weight_decay = 0.1
matrix_rate = 0.06
vector_rate = 1.0
gate_scale = 8.0

bf16, f32 = jnp.bfloat16, jnp.float32
MESH = pl.DeviceIdType.MESH
DIM = 2560
COLS = 3968
FIRST, SPLIT = 640, 1664
TRIPLE = 768
EXT = 2560 + 128
NT = (((1,), (1,)), ((), ()))
TN = (((0,), (0,)), ((), ()))


def dot(a, b):
    return jnp.dot(a, b, preferred_element_type=f32)


def dot_nt(a, b):
    return lax.dot_general(a, b, NT, preferred_element_type=f32)


def dot_tn(a, b):
    return lax.dot_general(a, b, TN, preferred_element_type=f32)


def many(n, fn):
    def one(i, carry):
        fn(i)
        return carry

    lax.fori_loop(0, n, one, 0)


class Place:
    def __init__(self):
        self.x = lax.axis_index("fsdp")
        self.c = lax.axis_index("context")
        self.t = lax.axis_index("tensor")
        self.y, self.z = lax.div(self.c, 4), lax.rem(self.c, 4)

    def ctx(self, dy, dz):
        return lax.rem(self.y + dy + 4, 4) * 4 + lax.rem(self.z + dz + 4, 4)

    def xs(self, d):
        return lax.rem(self.x + d + 4, 4)

    def along(self, half, d1, d2):
        return self.ctx(d2, d1) if half == 0 else self.ctx(d1, d2)

    def chain(self, d):
        return lax.rem(self.c + d + 16, 16)


class Wire:
    def __init__(self, place, ss, rs):
        self.place, self.ss, self.rs = place, ss, rs
        self.n, self.sent = 0, []

    def send(self, src, dst, **to):
        n = self.n
        self.n += 1
        copy = pltpu.make_async_remote_copy(
            src_ref=src, dst_ref=dst, send_sem=self.ss.at[n], recv_sem=self.rs.at[n],
            device_id=to, device_id_type=MESH,
        )
        copy.start()
        self.sent.append(copy)
        return n

    def recv(self, n, ref):
        pltpu.make_async_remote_copy(
            src_ref=ref, dst_ref=ref, send_sem=self.ss.at[n], recv_sem=self.rs.at[n],
            device_id={"fsdp": self.place.x}, device_id_type=MESH,
        ).wait_recv()

    def finish(self):
        for copy in self.sent:
            copy.wait_send()


class Local:
    def __init__(self, sems):
        self.sems, self.n, self.open = sems, 0, []

    def start(self, src, dst):
        copy = pltpu.make_async_copy(src, dst, self.sems.at[self.n])
        self.n += 1
        copy.start()
        self.open.append(copy)
        return copy

    def wait(self, copy):
        copy.wait()
        self.open = [other for other in self.open if other is not copy]

    def finish(self):
        for copy in self.open:
            copy.wait()


def greet(place, xs=(), ctx=(), chain=(), core=False, between=None):
    bar = pltpu.get_barrier_semaphore()
    n = 0
    for d in xs:
        pl.semaphore_signal(bar, inc=1, device_id={"fsdp": place.xs(d)}, device_id_type=MESH)
        n += 1
    for dy, dz in ctx:
        pl.semaphore_signal(bar, inc=1, device_id={"context": place.ctx(dy, dz)}, device_id_type=MESH)
        n += 1
    for d in chain:
        pl.semaphore_signal(bar, inc=1, device_id={"context": place.chain(d)}, device_id_type=MESH)
        n += 1
    if core:
        pl.semaphore_signal(bar, inc=1, device_id={"tensor": 1 - place.t}, device_id_type=MESH)
        n += 1
    if between is not None:
        between()
    pl.semaphore_wait(bar, n)


def chunk_rows(index, half):
    return pl.ds(pl.multiple_of(index * 160 + 80 * half, 16), 80)


def line_of(ref, place, half, d, cols):
    grid = ref.reshape(4, 4, 160, ref.shape[1])
    rows = pl.ds(80 * half, 80)
    if half == 0:
        return grid.at[:, lax.rem(place.z + d + 4, 4), rows, cols]
    return grid.at[lax.rem(place.y + d + 4, 4), :, rows, cols]


def gather_steps(wire, buf, own, at):
    place = wire.place
    width = own.shape[1]
    mid = width // 256 * 128
    FULL = pl.ds(at, width)
    part = {1: pl.ds(at, mid), -1: pl.ds(at + mid, width - mid)}

    def ref(h, d, cols):
        return buf.at[chunk_rows(place.along(h, d, 0), h), cols]

    def second_line(h, d, cols):
        grid = buf.reshape(4, 4, 160, buf.shape[1])
        rows = pl.ds(80 * h, 80)
        if h == 0:
            return grid.at[lax.rem(place.y + d + 4, 4), :, rows, cols]
        return grid.at[:, lax.rem(place.z + d + 4, 4), rows, cols]

    st = {}
    for h in (0, 1):
        for d in (1, -1):
            st[h, 1, d] = wire.send(own.at[pl.ds(80 * h, 80), :], ref(h, 0, FULL), context=place.along(h, d, 0))
    yield
    for d in (1, -1):
        for h in (0, 1):
            wire.recv(st[h, 1, d], ref(h, -d, FULL))
            st[h, 2, d] = wire.send(ref(h, -d, part[d]), ref(h, -d, part[d]), context=place.along(h, d, 0))
    yield
    for h in (0, 1):
        for d in (1, -1):
            wire.recv(st[h, 2, d], ref(h, 2, part[d]))
        for k in (1, -1):
            for d in (1, -1):
                cols = part[k * d]
                st[h, 3, d, k] = wire.send(second_line(h, 0, cols), second_line(h, 0, cols), context=place.along(h, 0, d))
    yield
    for h in (0, 1):
        for d in (1, -1):
            wire.recv(st[h, 3, d, 1], second_line(h, -d, part[d]))
            st[h, 4, d] = wire.send(second_line(h, -d, part[d]), second_line(h, -d, part[d]), context=place.along(h, 0, d))
    yield
    for h in (0, 1):
        for d in (1, -1):
            wire.recv(st[h, 3, d, -1], second_line(h, -d, part[-d]))
    for h in (0, 1):
        for d in (1, -1):
            wire.recv(st[h, 4, d], second_line(h, 2, part[d]))
    yield


def rows_gather_steps(wire, src, out, loc):
    place = wire.place
    x, t = place.x, place.t
    width = src.shape[1]
    h = width // 256 * 128
    LO, HI = pl.ds(0, h), pl.ds(h, width - h)
    xp, xm, xo = place.xs(1), place.xs(-1), place.xs(2)
    def hop(ref, piece, cols, d):
        return wire.send(ref, out.at[piece, t, :, cols], fsdp=place.xs(d))

    a = hop(src.at[:, LO], x, LO, 1)
    b = hop(src.at[:, HI], x, HI, -1)
    aa = hop(src.at[:, HI], x, HI, 1)
    bb = hop(src.at[:, LO], x, LO, -1)
    cores = [(x, wire.send(src, out.at[x, t], tensor=1 - t))]
    own = loc.start(src, out.at[x, t])
    yield
    wire.recv(a, out.at[xm, t, :, LO])
    e = hop(out.at[xm, t, :, LO], xm, LO, 1)
    wire.recv(b, out.at[xp, t, :, HI])
    f = hop(out.at[xp, t, :, HI], xp, HI, -1)
    yield
    wire.recv(aa, out.at[xm, t, :, HI])
    cores.append((xm, wire.send(out.at[xm, t], out.at[xm, t], tensor=1 - t)))
    wire.recv(bb, out.at[xp, t, :, LO])
    cores.append((xp, wire.send(out.at[xp, t], out.at[xp, t], tensor=1 - t)))
    yield
    wire.recv(e, out.at[xo, t, :, LO])
    wire.recv(f, out.at[xo, t, :, HI])
    cores.append((xo, wire.send(out.at[xo, t], out.at[xo, t], tensor=1 - t)))
    yield
    for k, n in cores:
        wire.recv(n, out.at[k, 1 - t])
    loc.wait(own)
    yield


class RowsScatter:
    def __init__(self, wire, part, crecv, sums, r1, r2, piece=512, own=None):
        self.wire, self.part, self.crecv, self.sums, self.r1, self.r2 = wire, part, crecv, sums, r1, r2
        self.piece, self.n = piece, {}
        place = wire.place
        self.x, self.t = place.x, place.t
        self.own = own if own is not None else part.at[:, self.t]
        self.xp, self.xm, self.xo = place.xs(1), place.xs(-1), place.xs(2)

    def cut(self, i):
        at, half = i * self.piece, self.piece // 2
        return pl.ds(at, self.piece), pl.ds(at, half), pl.ds(at + half, half)

    def rows(self, fn):
        for i in (0, 1):
            fn(pl.ds(32 * i, 32))

    def put(self, n, k, cols, extra=None):
        def fn(r):
            v = self.own[k, r, cols].astype(f32) + self.crecv[k, r, cols].astype(f32)
            if extra is not None:
                v = v + self.r1[extra, r, cols].astype(f32)
            self.sums[n, r, cols] = v.astype(bf16)

        self.rows(fn)

    def a(self, i):
        cols = self.cut(i)[0]
        self.n["a", i] = self.wire.send(self.part.at[:, 1 - self.t, :, cols], self.crecv.at[:, :, cols], tensor=1 - self.t)

    def b(self, i):
        cols, lo, hi = self.cut(i)
        self.wire.recv(self.n["a", i], self.crecv.at[:, :, cols])
        self.put(0, self.xo, cols)
        self.n["b", i] = self.wire.send(self.sums.at[0, :, lo], self.r1.at[0, :, lo], fsdp=self.xp)
        self.n["c", i] = self.wire.send(self.sums.at[0, :, hi], self.r1.at[1, :, hi], fsdp=self.xm)

    def c(self, i):
        cols, lo, hi = self.cut(i)
        self.wire.recv(self.n["b", i], self.r1.at[0, :, lo])
        self.put(1, self.xp, lo, 0)
        self.put(1, self.xp, hi)
        self.n["d", i] = self.wire.send(self.sums.at[1, :, cols], self.r2.at[0, :, cols], fsdp=self.xp)
        self.wire.recv(self.n["c", i], self.r1.at[1, :, hi])
        self.put(2, self.xm, lo)
        self.put(2, self.xm, hi, 1)
        self.n["e", i] = self.wire.send(self.sums.at[2, :, cols], self.r2.at[1, :, cols], fsdp=self.xm)

    def d(self, i, done):
        cols = self.cut(i)[0]
        self.wire.recv(self.n["d", i], self.r2.at[0, :, cols])
        self.wire.recv(self.n["e", i], self.r2.at[1, :, cols])

        def total(r):
            done(
                cols,
                r,
                self.own[self.x, r, cols].astype(f32)
                + self.crecv[self.x, r, cols].astype(f32)
                + self.r2[0, r, cols].astype(f32)
                + self.r2[1, r, cols].astype(f32),
            )

        self.rows(total)

    def steps(self, compute, done):
        count = self.sums.shape[2] // self.piece
        for i in range(count + 3):
            if i < count:
                compute(i)
                self.a(i)
            if 0 <= i - 1 < count:
                self.b(i - 1)
            if 0 <= i - 2 < count:
                self.c(i - 2)
            if 0 <= i - 3 < count:
                self.d(i - 3, done)
            yield


def drain(steps):
    for _ in steps:
        pass


def pump(steps, n=1):
    for _ in range(n):
        next(steps, None)


def gelu(v):
    return 0.5 * v * (1.0 + jnp.tanh(0.7978845608028654 * (v + 0.044715 * v * v * v)))


def gelu_and_slope(v):
    u = jnp.tanh(0.7978845608028654 * (v + 0.044715 * v * v * v))
    slope = 0.5 * (1.0 + u) + 0.5 * v * (1.0 - u * u) * (
        0.7978845608028654 * (1.0 + 3 * 0.044715 * v * v)
    )
    return 0.5 * v * (1.0 + u), slope


def one_less_exp(v):
    series = 1.0 + v * (1.0 / 7.0)
    for k in (6.0, 5.0, 4.0, 3.0, 2.0):
        series = 1.0 + v * (1.0 / k) * series
    return jnp.where(v > -0.35, -v * series, 1.0 - jnp.exp(v))


def sigmoid(v):
    return 1.0 / (1.0 + jnp.exp(-v))


def shifted(block, edge, k):
    moved = pltpu.roll(block, k, 0)
    first = jnp.where(
        lax.broadcasted_iota(jnp.int32, edge.shape, 0) < k, pltpu.roll(edge, k, 0), moved[:8]
    )
    return jnp.concatenate([first, moved[8:]], axis=0)


def scan_down(a, b):
    rows = lax.broadcasted_iota(jnp.int32, a.shape, 0)
    s = 1
    while s < a.shape[0]:
        earlier = rows >= s
        pa = jnp.where(earlier, pltpu.roll(a, s, 0), 1.0)
        pb = jnp.where(earlier, pltpu.roll(b, s, 0), 0.0)
        b = b + a * pb
        a = a * pa
        s *= 2
    return a, b


def scan_up(a, b):
    rows = lax.broadcasted_iota(jnp.int32, a.shape, 0)
    n = a.shape[0]
    s = 1
    while s < n:
        later = rows < n - s
        pa = jnp.where(later, pltpu.roll(a, n - s, 0), 1.0)
        pb = jnp.where(later, pltpu.roll(b, n - s, 0), 0.0)
        b = b + a * pb
        a = a * pa
        s *= 2
    return a, b


def selector(g):
    i = lax.broadcasted_iota(jnp.int32, (256, 512), 0)
    j = lax.broadcasted_iota(jnp.int32, (256, 512), 1)
    xx, cc, r = i // 64, (i // 4) % 16, i % 4
    return (j == cc * 32 + xx * 8 + g * 4 + r).astype(f32).astype(bf16)


def gate_matrix(packed, g):
    return dot(selector(g), packed).astype(bf16)


def column(tile, tiles=1):
    return pl.ds(pl.multiple_of(128 + 256 * tile, 128), 256 * tiles)


def triple(j):
    return column(jnp.where(j == 3, 3, 6 + 3 * j), 3)


def head_count(x):
    return jnp.where(x == 0, 2, 1).astype(jnp.int32)


def lanes(h):
    return pl.ds(pl.multiple_of(h * 256, 256), 256)


def token_rows(g):
    return pl.ds(pl.multiple_of(g * 128, 128), 128)


def recur_terms(lx, la, cl, sp, keep):
    sx, sa = sigmoid(lx), sigmoid(la)
    log_decay = (-gate_scale) * sa * sp
    grown = one_less_exp(2.0 * log_decay)
    root = jnp.sqrt(grown)
    factor = root * keep + 1.0 - keep
    return sx, sa, log_decay, root, factor


HEAD_START = (0, 2, 3, 4)
HEADS_OF = (2, 1, 1, 1)
FF_START = (0, 768, 1792, 2816)
TILE_ORDER = ((0, 1, 2), (3, 0, 1, 2), (3, 0, 1, 2), (3, 0, 1, 2))


def restored_granule(m):
    return 4 * (m % 16) + m // 16


def permuted_granule(m):
    return 16 * (m % 4) + m // 4


def moved_tile(get, q, shape, granule):
    lane = lax.broadcasted_iota(jnp.int32, shape, len(shape) - 1)
    out = jnp.zeros(shape, f32)
    at = 128 * q
    while at < 128 * q + 128:
        m = at // 40
        source = 40 * granule(m) + at - 40 * m
        p = source // 128
        stop = min(40 * m + 40, 128 * q + 128, at + 128 * p + 128 - source)
        turn = (at - 128 * q - (source - 128 * p)) % 128
        v = get(p)
        if turn:
            v = pltpu.roll(v, turn, len(shape) - 1)
        out = jnp.where((lane >= at - 128 * q) & (lane < stop - 128 * q), v, out)
        at = stop
    return out


def segment_of(place, ends):
    return sum((place >= e).astype(jnp.int32) for e in ends)


def forward_kernel(
    seq_ref, tokens, cotangent, gains, recur, inp, blocks, outp, inner, down,
    w_out, act_out, gl_out, tok_out, gains_out, rec_out, lx_out, la_out, hid_out, py_out, low_out, cg_out, nm_out, resid_out,
    xbuf, wide, chunk0, chunk1, chunk2, w1, act, lx_s, la_s, hid_s, py_s, low_s, halo, cum_s, cg, cin,
    part, crecv, sums, r1, r2, normed, resid, packed, gates,
    p_ref, n_ref, cot_ref, tok_ref, gain_ref, rec_ref,
    ss, rs, ls,
):
    place = Place()
    x, c, t = place.x, place.c, place.t
    wire, loc = Wire(place, ss, rs), Local(ls)
    nh = head_count(x)

    def weight_tile(k, tile):
        heads = HEADS_OF[k]
        if tile < 3 * heads:
            at = 256 * (HEAD_START[k] + tile % heads)
            ref = (inp.at[0], inp.at[1], outp)[tile // heads]
        else:
            kind = (tile - 6) % 3 if tile >= 6 else tile - 3
            j = (tile - 6) // 3 if tile >= 6 else 3
            at = FF_START[k] + 256 * j
            ref = (inner.at[0], inner.at[1], down)[kind]
        return ref[:, pl.ds(at, 256)]

    def pack(first, count):
        for k in range(4):
            for tile in range(first, first + count):
                v = jnp.concatenate([weight_tile(k, tile), jnp.zeros((8, 256), f32)], axis=0)
                p_ref[k, :, pl.ds(128 + 256 * tile, 256)] = v.astype(bf16)

    def pack_first():
        for k in range(4):
            heads = HEADS_OF[k]
            rows = [
                jnp.concatenate([blocks[g, HEAD_START[k] + h] for h in range(heads)] + [jnp.zeros((4, 512 - 256 * heads), f32)] * (heads < 2), axis=1)
                for g in (0, 1)
            ]
            gate = jnp.concatenate([jnp.concatenate(rows, axis=0), jnp.zeros((8, 128), f32)], axis=1)
            main = jnp.concatenate([jnp.zeros((40, 128), f32), weight_tile(k, 0), weight_tile(k, 1)], axis=1)
            p_ref[k, :, pl.ds(0, FIRST)] = jnp.concatenate([main, gate], axis=0).astype(bf16)

    def recurrent_rows(k):
        n = 256 * HEADS_OF[k]
        cols = pl.ds(0, n)
        v = recur[:, pl.ds(256 * HEAD_START[k], n)]
        u = jnp.exp(-v[7:])
        z = u / (2.0 + u)
        zz = z * z
        series = 2.0 * z * (1.0 + zz * (1.0 / 3.0 + zz * (1.0 / 5.0 + zz * (1.0 / 7.0))))
        rec_ref[pl.ds(0, 8), cols] = v
        rec_ref[pl.ds(7, 1), cols] = jnp.where(u < 0.1, series, jnp.log(1.0 + u))
        rec_ref[pl.ds(8, 1), cols] = u / (1.0 + u)

    def prepare():
        pack_first()
        rec_ref[...] = jnp.zeros_like(rec_ref)
        for k in range(4):
            pl.when(x == k)(functools.partial(recurrent_rows, k))
        for n in (0, 1):
            for q in range(20):
                gain_ref[pl.ds(n, 1), pl.ds(128 * q, 128)] = moved_tile(
                    lambda p: gains[pl.ds(n, 1), pl.ds(128 * p, 128)], q, (1, 128), permuted_granule
                )
        ends = [seq_ref[0, 0]]
        for k in (1, 2):
            ends.append(ends[-1] + seq_ref[0, k])

        def rows(i):
            src = pl.ds(pl.multiple_of(t * 64 + 16 * i, 16), 16)
            r = pl.ds(pl.multiple_of(16 * i, 16), 16)
            where = c * 128 + t * 64 + 16 * i + lax.broadcasted_iota(jnp.int32, (16, 128), 0)
            lane = lax.broadcasted_iota(jnp.int32, (16, 128), 1)
            here = segment_of(where, ends)
            valid = (here < 3).astype(f32)
            fresh = (where == 0).astype(f32)
            for e in ends:
                fresh = jnp.maximum(fresh, (where == e).astype(f32))
            back = where - (lane - 1)
            same = (segment_of(back, ends) == here).astype(f32) * (back >= 0).astype(f32) * (lane < 5).astype(f32)
            flag = jnp.where(lane == 0, valid, jnp.where(lane == 1, 1.0 - fresh, same))
            n_ref[r, pl.ds(DIM, 128)] = flag.astype(bf16)
            for q in range(20):
                cols = pl.ds(128 * q, 128)
                tok_ref[r, cols] = moved_tile(lambda p: tokens[src, pl.ds(128 * p, 128)].astype(f32), q, (16, 128), permuted_granule)
                cot = moved_tile(lambda p: cotangent[src, pl.ds(128 * p, 128)].astype(f32), q, (16, 128), permuted_granule)
                cot_ref[r, cols] = (cot * valid).astype(bf16)
            v = tok_ref[r, :]
            inv = lax.rsqrt(jnp.mean(v * v, axis=-1, keepdims=True) + norm_eps)
            n_ref[r, pl.ds(0, DIM)] = (v * inv * gain_ref[pl.ds(0, 1), :]).astype(bf16)

        many(4, rows)

    greet(
        place, xs=(1, 2, 3), ctx=((1, 0), (2, 0), (3, 0), (0, 1), (0, 2), (0, 3)), chain=(1, -1), core=True, between=prepare
    )
    loc.start(tok_ref, tok_out)
    loc.start(gain_ref, gains_out)
    loc.start(rec_ref, rec_out)

    stages = ((0, FIRST, chunk0), (FIRST, SPLIT, chunk1), (SPLIT, COLS, chunk2))
    came = {}

    def spread(s):
        c0, c1, _ = stages[s]
        cs = pl.ds(c0, c1 - c0)
        for d in (2, 1, 3):
            came[s, d] = wire.send(p_ref.at[place.xs(d), :, cs], xbuf.at[x, :, cs], fsdp=place.xs(d))

    def arrange(s):
        c0, c1, chunk = stages[s]
        cs = pl.ds(c0, c1 - c0)
        for d in (1, 3, 2):
            wire.recv(came[s, d], xbuf.at[place.xs(-d), :, cs])

        for k in range(4):
            def take(src, k=k):
                v = src[k, :, cs].astype(f32)
                wide[pl.ds(40 * k, 40), cs] = v[:40]

            pl.when(x == k)(functools.partial(take, p_ref))
            pl.when(x != k)(functools.partial(take, xbuf))
        if s == 0:
            for k in range(4):
                def gate(src, k=k):
                    v = src[k, :, pl.ds(0, 512)].astype(f32)
                    for b in range(4):
                        wide[pl.ds(32 * b + 8 * k, 8), pl.ds(0, 128)] = v[40:, 128 * b : 128 * b + 128]

                pl.when(x == k)(functools.partial(gate, p_ref))
                pl.when(x != k)(functools.partial(gate, xbuf))
        chunk[...] = wide[:, cs].astype(bf16)

    mine = pl.ds(pl.multiple_of(c * 160, 16), 160)
    spread(0)
    pack(2, 4)
    spread(1)
    pack(6, 9)
    arrange(0)
    own0 = loc.start(chunk0, w1.at[mine, pl.ds(0, FIRST)])
    one = gather_steps(wire, w1, chunk0, 0)
    pump(one)
    rows = rows_gather_steps(wire, n_ref, act, loc)
    pump(rows)
    pump(one)
    arrange(1)
    own1 = loc.start(chunk1, w1.at[mine, pl.ds(FIRST, SPLIT - FIRST)])
    two = gather_steps(wire, w1, chunk1, FIRST)
    pump(two)
    loc.wait(own0)
    pump(one)
    spread(2)
    pump(rows)
    pump(two)
    pump(one)
    pump(rows)
    loc.wait(own1)
    pump(two)
    pump(rows)
    drain(one)
    drain(rows)
    loc.start(act, act_out)
    later = rows_gather_steps(wire, cot_ref, gl_out, loc)

    def project_x(h):
        ni = act[:, :, :, pl.ds(0, DIM)].reshape(512, DIM)
        low_s[0, :, lanes(h)] = dot(ni, w1[:, column(h)]).astype(bf16)

    many(nh, project_x)
    before = low_s.at[0].reshape(4, 128, 512)
    hn = wire.send(before.at[:, pl.ds(112, 16), :], halo, context=place.chain(1))
    for cc in range(16):
        for b in range(4):
            packed[pl.ds(32 * cc, 32), pl.ds(128 * b, 128)] = w1[pl.ds(160 * cc + 32 * b, 32), pl.ds(0, 128)]
    for g in (0, 1):
        gates[g] = gate_matrix(packed[...], g)
    wire.recv(hn, halo)

    def flags(g, k):
        v = act[pl.ds(g, 1), :, :, pl.ds(DIM, 128)].reshape(128, 128).astype(f32)
        return v[:, k : k + 1]

    cg[c] = jnp.zeros((2, 8, 512), f32)

    def conv(h):
        def group(g):
            bx = low_s[0, token_rows(g), lanes(h)].astype(f32)
            edge = halo[g, :, lanes(h)].astype(f32)[8:]
            out = rec_ref[pl.ds(4, 1), lanes(h)] + rec_ref[pl.ds(0, 1), lanes(h)] * bx
            for k in (1, 2, 3):
                out = out + rec_ref[pl.ds(k, 1), lanes(h)] * (flags(g, 1 + k) * shifted(bx, edge, k))
            low_s[1, token_rows(g), lanes(h)] = out.astype(bf16)

        many(4, group)
        cl = low_s[1, :, lanes(h)]
        lx_s[:, lanes(h)] = dot(cl, gates[0, :, lanes(h)]) + rec_ref[pl.ds(5, 1), lanes(h)]
        la_s[:, lanes(h)] = dot(cl, gates[1, :, lanes(h)]) + rec_ref[pl.ds(6, 1), lanes(h)]

    many(nh, conv)
    loc.start(lx_s, lx_out)
    loc.start(la_s, la_out)
    pump(later)
    pump(two)
    arrange(2)
    own2 = loc.start(chunk2, w_out.at[mine, pl.ds(SPLIT, COLS - SPLIT)])
    three = gather_steps(wire, w_out, chunk2, SPLIT)
    pump(three)

    def scan(q):
        cols = pl.ds(pl.multiple_of(q * 128, 128), 128)
        for g in range(4):
            r = pl.ds(128 * g, 128)
            keep = flags(g, 1)
            cl = low_s[1, r, cols].astype(f32)
            sx, sa, log_decay, root, factor = recur_terms(
                lx_s[r, cols], la_s[r, cols], cl, rec_ref[pl.ds(7, 1), cols], keep
            )
            a, b = scan_down(jnp.exp(log_decay) * keep, factor * sx * cl)
            cum_s[r, cols] = a
            hid_s[r, cols] = b
            cg[c, 0, pl.ds(g, 1), cols] = a[127:]
            cg[c, 1, pl.ds(g, 1), cols] = b[127:]

    many(2 * nh, scan)
    ns = [wire.send(cg.at[c], cg.at[c], context=place.ctx(0, d)) for d in (1, 2, 3)]
    for d, n in zip((1, 2, 3), ns):
        wire.recv(n, cg.at[place.ctx(0, -d)])
    line = pl.ds(place.y * 4, 4)
    ns = [wire.send(cg.at[line], cg.at[line], context=place.ctx(d, 0)) for d in (1, 2, 3)]
    for d, n in zip((1, 2, 3), ns):
        wire.recv(n, cg.at[pl.ds(lax.rem(place.y + 4 - d, 4) * 4, 4)])

    def enter(s, state):
        return cg[s, 0] * state + cg[s, 1]

    cin[...] = lax.fori_loop(0, c, enter, jnp.zeros((8, 512), f32))
    loc.start(cg, cg_out)

    pump(later)
    drain(two)
    pump(three)
    loc.start(w1, w_out.at[:, pl.ds(0, SPLIT)])
    two = three

    def project_y(h):
        ni = act[:, :, :, pl.ds(0, DIM)].reshape(512, DIM)
        py_s[:, lanes(h)] = dot(ni, w1[:, column(nh + h)])

    many(nh, project_y)
    loc.start(py_s, py_out)
    pump(later)

    def mix(h):
        for g in range(4):
            r = pl.ds(128 * g, 128)
            hid = hid_s[r, lanes(h)] + cum_s[r, lanes(h)] * cin[pl.ds(g, 1), lanes(h)]
            hid_s[r, lanes(h)] = hid
            low_s[2, r, lanes(h)] = (hid * gelu(py_s[r, lanes(h)])).astype(bf16)

    many(nh, mix)
    loc.start(hid_s, hid_out)
    loc.start(low_s, low_out)
    loc.wait(own2)
    pump(two)

    drain(later)

    def project_out(n, heads):
        r = pl.ds(512 * n, 512)
        v = dot_nt(low_s[2, :, pl.ds(0, 256 * heads)], w1[r, pl.ds(128 + 512 * heads, 256 * heads)])
        part[:, :, :, r] = v.astype(bf16).reshape(4, 2, 64, 512)

    def project_piece(n):
        pl.when(x == 0)(lambda: project_out(n, 2))
        pl.when(x != 0)(lambda: project_out(n, 1))

    def add_resid(cols, r, total):
        resid[r, cols] = tok_ref[r, cols] + total

    drain(RowsScatter(wire, part, crecv, sums, r1, r2).steps(project_piece, add_resid))
    pump(two)
    loc.start(resid, resid_out)

    def norm(i):
        r = pl.ds(pl.multiple_of(i * 16, 16), 16)
        v = resid[r, :]
        inv = lax.rsqrt(jnp.mean(v * v, axis=-1, keepdims=True) + norm_eps)
        normed[r, :] = (v * inv * gain_ref[pl.ds(1, 1), :]).astype(bf16)

    many(4, norm)
    drain(rows_gather_steps(wire, normed, nm_out, loc))
    drain(two)
    wire.finish()
    loc.finish()


def vm(shape, dtype):
    return pltpu.VMEM(shape, dtype)


PLANE = ((1, 0), (3, 0), (0, 1), (0, 3))
ANY = pl.BlockSpec(memory_space=pl.ANY)
VM = pl.BlockSpec(memory_space=pltpu.VMEM)


def forward_call(seq, tokens, cotangent, gains, recur, inp, blocks, outp, inner, down):
    S = jax.ShapeDtypeStruct
    R = (64, DIM)
    F = (512, 512)
    return pl.pallas_call(
        forward_kernel,
        name="recurrent_forward",
        out_shape=(
            S((DIM, COLS), bf16), S((4, 2, 64, EXT), bf16), S((4, 2) + R, bf16), S(R, f32), S((2, DIM), f32), S((16, 512), f32),
            S(F, f32), S(F, f32), S(F, f32), S(F, f32),
            S((3,) + F, bf16), S((16, 2, 8, 512), f32), S((4, 2) + R, bf16), S(R, f32),
        ),
        in_specs=[pl.BlockSpec(memory_space=pltpu.SMEM)] + [VM] * 9,
        out_specs=[ANY] * 14,
        scratch_shapes=[
            vm((4, 48, COLS), bf16), vm((160, COLS), f32), vm((160, FIRST), bf16), vm((160, SPLIT - FIRST), bf16), vm((160, COLS - SPLIT), bf16),
            vm((DIM, SPLIT), bf16), vm((4, 2, 64, EXT), bf16),
            vm(F, f32), vm(F, f32), vm(F, f32), vm(F, f32),
            vm((3,) + F, bf16), vm((4, 16, 512), bf16), vm(F, f32), vm((16, 2, 8, 512), f32), vm((8, 512), f32),
            vm((4, 2) + R, bf16), vm((4,) + R, bf16), vm((3,) + R, bf16), vm((2,) + R, bf16), vm((2,) + R, bf16),
            vm(R, bf16), vm(R, f32), vm(F, bf16), vm((2, 256, 512), bf16),
            vm((4, 48, COLS), bf16), vm((64, EXT), bf16), vm(R, bf16), vm(R, f32), vm((2, DIM), f32), vm((16, 512), f32),
            pltpu.SemaphoreType.DMA((160,)), pltpu.SemaphoreType.DMA((160,)), pltpu.SemaphoreType.DMA((20,)),
        ],
        compiler_params=pltpu.CompilerParams(collective_id=0, has_side_effects=True, vmem_limit_bytes=60 << 20),
    )(seq, tokens, cotangent, gains, recur, inp, blocks, outp, inner, down)


def transpose_rows(src, dst):
    def block(n):
        cols = pl.ds(pl.multiple_of(n * 256, 256), 256)
        dst[cols, :] = src[:, :, :, cols].reshape(512, 256).T

    many(10, block)


def add_sublanes(v):
    return v[:8] + v[8:]


def norm_back(total, value, gain):
    inv = lax.rsqrt(jnp.mean(value * value, axis=-1, keepdims=True) + norm_eps)
    xhat = value * inv
    weighted = total * gain
    inner = jnp.mean(weighted * xhat, axis=-1, keepdims=True)
    return inv * (weighted - xhat * inner), add_sublanes(total * xhat)


def ffn_kernel(
    w_ref, gl_ref, nm, resid, gain_ref,
    g_out, ahead_out, gm_out, gres_out, gain_out, first_out, second_out,
    gl, nmt, glt, wt, gfirst, gsecond, pre, lowi, lowg, parts, crecv, sums, r1, r2, normed, own_low, gsum,
    a2, a3, a4, a5, a6, a7, d2, d3, d4, d5, d6, d7,
    ss, rs, ls, ws, gs,
):
    place = Place()
    x, t = place.x, place.t
    wire, loc = Wire(place, ss, rs), Local(ls)
    nf = 5 - head_count(x)

    def load(j):
        return pltpu.make_async_copy(w_ref.at[:, triple(j)], wt.at[j], ws.at[j])

    def store(j):
        return pltpu.make_async_copy(wt.at[j], g_out.at[:, triple(j)], gs.at[j])

    glc = loc.start(gl_ref, gl)
    for j in range(3):
        load(j).start()
    pl.when(x != 0)(lambda: load(3).start())
    olc = loc.start(gl_ref.at[x, t], own_low)
    greet(place, xs=(1, -1), ctx=PLANE, core=True)
    transpose_rows(nm, nmt)
    loc.wait(glc)
    loc.wait(olc)
    transpose_rows(gl, glt)

    def tile(j):
        load(j).wait()
        pre[:, pl.ds(0, 512)] = dot(nm[...].reshape(512, DIM), wt[j, :, pl.ds(0, 512)])
        pre[:, pl.ds(512, 256)] = dot(gl[...].reshape(512, DIM), wt[j, :, pl.ds(512, 256)])

        def point(i):
            r = pl.ds(pl.multiple_of(i * 32, 32), 32)
            gated, slope = gelu_and_slope(pre[r, pl.ds(0, 256)])
            up, gi = pre[r, pl.ds(256, 256)], pre[r, pl.ds(512, 256)]
            lowi[j, r, :] = (gated * up).astype(bf16)
            lowg[j, r, pl.ds(0, 256)] = (gi * up * slope).astype(bf16)
            lowg[j, r, pl.ds(256, 256)] = (gi * gated).astype(bf16)

        many(16, point)

    def gradient(j, dst):
        def block(n):
            r = pl.ds(pl.multiple_of(n * 512, 512), 512)
            dst[r, pl.ds(0, 512)] = dot(nmt[r, :], lowg[j]).astype(bf16)
            dst[r, pl.ds(512, 256)] = dot(glt[r, :], lowi[j]).astype(bf16)

        many(5, block)

    tile(0)
    gradient(0, gfirst)
    first = scatter_steps(wire, loc, gfirst, 0, (None, None, a2, a3, a4, a5, a6, a7), first_out, False, True, False)
    pump(first, 1)
    tile(1)
    many(nf - 2, lambda j: tile(j + 2))

    def contract(dst, low, cols, n):
        r = pl.ds(512 * n, 512)

        def total(count):
            v = dot_nt(low[0], wt[0, r, cols])
            for j in range(1, count):
                v = v + dot_nt(low[j], wt[j, r, cols])
            dst[:, :, :, r] = v.astype(bf16).reshape(4, 2, 64, 512)

        pl.when(x == 0)(lambda: total(3))
        pl.when(x != 0)(lambda: total(4))

    def keep_sum(cols, r, total):
        gsum[r, cols] = total

    back = RowsScatter(wire, parts, crecv, sums, r1, r2).steps(
        lambda n: contract(parts, lowg, pl.ds(0, 512), n), keep_sum
    )
    pump(first, 4)
    pump(back, 5)
    gradient(1, gsecond)
    second = scatter_steps(wire, loc, gsecond, 0, (None, None, d2, d3, d4, d5, d6, d7), second_out, False, True, False)
    pump(second, 1)
    for n in range(5):
        contract(gl, lowi, pl.ds(512, 256), n)
        if n % 2 == 1:
            pump(back, 1)
    loc.start(gl, ahead_out)
    pump(first, 4)
    gradient(2, wt.at[2])
    store(2).start()
    drain(back)
    gain_out[...] = jnp.zeros_like(gain_out)

    def resid_back(i):
        r = pl.ds(pl.multiple_of(i * 16, 16), 16)
        gx, gain = norm_back(gsum[r, :], resid[r, :], gain_ref[pl.ds(1, 1), :])
        gr = own_low[r, :].astype(f32) + gx
        gres_out[r, :] = gr
        normed[r, :] = gr.astype(bf16)
        gain_out[...] += gain

    many(4, resid_back)
    rows = rows_gather_steps(wire, normed, gm_out, loc)
    pump(rows, 1)
    pump(second, 4)
    pump(rows, 1)

    @pl.when(x != 0)
    def _():
        gradient(3, wt.at[3])
        store(3).start()

    pump(rows, 1)
    pump(first, 1)
    drain(rows)
    pump(second, 4)
    pump(first, 1)
    pump(second, 1)
    drain(first)
    drain(second)
    store(2).wait()
    pl.when(x != 0)(lambda: store(3).wait())
    wire.finish()
    loc.finish()


def ffn_call(w, gl, nm, resid, gain):
    S = jax.ShapeDtypeStruct
    R = (64, DIM)
    slices = scatter_scratch(TRIPLE)[2:]
    return pl.pallas_call(
        ffn_kernel,
        name="feed_forward",
        out_shape=(
            S((DIM, COLS), bf16), S((4, 2) + R, bf16), S((4, 2) + R, bf16), S(R, f32), S((8, DIM), f32),
            S((4, 48, TRIPLE), bf16), S((4, 48, TRIPLE), bf16),
        ),
        in_specs=[ANY, ANY, VM, VM, VM],
        out_specs=[ANY, ANY, ANY, VM, VM, ANY, ANY],
        scratch_shapes=[
            vm((4, 2) + R, bf16), vm((DIM, 512), bf16), vm((DIM, 512), bf16), vm((4, DIM, TRIPLE), bf16), vm((DIM, TRIPLE), bf16), vm((DIM, TRIPLE), bf16),
            vm((512, TRIPLE), f32), vm((4, 512, 256), bf16), vm((4, 512, 512), bf16),
            vm((4, 2) + R, bf16), vm((4,) + R, bf16), vm((3,) + R, bf16), vm((2,) + R, bf16), vm((2,) + R, bf16),
            vm(R, bf16), vm(R, bf16), vm(R, f32),
        ] + slices + slices + [
            pltpu.SemaphoreType.DMA((170,)), pltpu.SemaphoreType.DMA((170,)), pltpu.SemaphoreType.DMA((12,)),
            pltpu.SemaphoreType.DMA((4,)), pltpu.SemaphoreType.DMA((4,)),
        ],
        compiler_params=pltpu.CompilerParams(collective_id=1, has_side_effects=True, vmem_limit_bytes=60 << 20),
    )(w, gl, nm, resid, gain)


def scatter_steps(wire, loc, g_ref, at, bufs, out_ref, gates, resident=False, spread=True):
    gvn, gvo, r1, r2, r3, r4, wide, obuf = bufs
    place = wire.place
    x, c = place.x, place.c
    width = wide.shape[1]
    mid = width // 256 * 128
    LO, HI, FULL = (0, mid), (mid, width), (0, width)
    zero = {1: LO, -1: HI}
    other = {1: HI, -1: LO}

    def cut(k):
        return pl.ds(k[0], k[1] - k[0])

    def short(k):
        return pl.ds(0, k[1] - k[0])

    def wide_cut(k):
        return pl.ds(at + k[0], k[1] - k[0])

    def group(h, d, k):
        return line_of(g_ref, place, h, d, wide_cut(k))

    def index(h, d, q):
        return q * 4 + lax.rem(place.z + d + 4, 4) if h == 0 else lax.rem(place.y + d + 4, 4) * 4 + q

    side = {1: 0, -1: 1}
    ends = {0: place.y, 1: place.z}
    st, loads = {}, {}

    class Piece:
        def __init__(self, h, d, k, ref):
            self.h, self.d, self.k, self.ref = h, d, k, ref

        def at(self, q, half):
            c0, c1 = self.k
            if half is not None:
                c0, c1 = (c0, mid) if half == 0 else (mid, c1)
            if resident:
                return g_ref, chunk_rows(index(self.h, self.d, q), self.h), wide_cut((c0, c1))
            return self.ref.at[q], pl.ds(0, 80), (short((c0, c1)) if self.d else cut((c0, c1)))

    def add_near(piece, got):
        def one(q):
            ref, r, cols = piece.at(q, None)
            ref[r, cols] = ref[r, cols] + got[q]

        many(4, one)

    def add_own(piece, srcs):
        def one(q):
            for half in (0, 1):
                ref, r, cols = piece.at(q, half)
                v = ref[r, cols].astype(f32)
                for s in srcs:
                    v = v + s[q, :, cut((LO, HI)[half])].astype(f32)
                ref[r, cols] = v.astype(bf16)

        many(4, one)

    def mine_at(h, q, k):
        if resident:
            return g_ref.at[chunk_rows(index(h, 0, q), h), wide_cut(k)]
        return gvo.at[h, q, :, cut(k)]

    for h in (0, 1):
        for d in (1, -1):
            k = zero[d]
            st[h, 1, d] = wire.send(group(h, 2, k), r1.at[h, side[d], :, :, short(k)], context=place.along(h, d, 0))
    if not resident:
        for h in (0, 1):
            for d in (1, -1):
                loads[h, d] = loc.start(group(h, d, zero[d]), gvn.at[h, side[d], :, :, short(zero[d])])
        for h in (0, 1):
            loads[h, 0] = loc.start(group(h, 0, FULL), gvo.at[h])
    for h in (0, 1):
        for d in (1, -1):
            k = other[d]
            st[h, 2, d] = wire.send(group(h, d, k), r2.at[h, side[d], :, :, cut(k)], context=place.along(h, d, 0))
    yield

    def add(dst, srcs):
        def one(i):
            r = pl.ds(pl.multiple_of(i * 16, 16), 16)
            v = srcs[0][r, :].astype(f32)
            for s in srcs[1:]:
                v = v + s[r, :].astype(f32)
            dst[r, :] = v.astype(dst.dtype)

        many(5, one)

    for h in (0, 1):
        for d in (1, -1):
            k = zero[d]
            if not resident:
                loc.wait(loads[h, d])
            got = r1.at[h, side[d], :, :, short(k)]
            wire.recv(st[h, 1, d], got)
            piece = Piece(h, d, k, None if resident else gvn.at[h, side[d]])
            add_near(piece, got)
            src = group(h, d, k) if resident else gvn.at[h, side[d], :, :, short(k)]
            st[h, 3, d] = wire.send(src, r2.at[h, side[d], :, :, cut(k)], context=place.along(h, d, 0))
            yield
    for h in (0, 1):
        if not resident:
            loc.wait(loads[h, 0])
        for d in (1, -1):
            wire.recv(st[h, 2, d], r2.at[h, side[d], :, :, cut(other[d])])
            wire.recv(st[h, 3, d], r2.at[h, side[d], :, :, cut(zero[d])])
        add_own(Piece(h, 0, FULL, None if resident else gvo.at[h]), [r2.at[h, 0], r2.at[h, 1]])
        far = lax.rem(ends[h] + 2, 4)
        for d in (1, -1):
            st[h, 4, d] = wire.send(
                mine_at(h, far, zero[d]), r3.at[h, side[d], :, short(zero[d])], context=place.along(h, 0, d)
            )
        for d in (1, -1):
            near = lax.rem(ends[h] + d + 4, 4)
            st[h, 5, d] = wire.send(
                mine_at(h, near, other[d]), r4.at[h, side[d], :, cut(other[d])], context=place.along(h, 0, d)
            )
        yield
        yield
    for h in (0, 1):
        for d in (1, -1):
            k = zero[d]
            mine = mine_at(h, lax.rem(ends[h] + d + 4, 4), k)
            got = r3.at[h, side[d], :, short(k)]
            wire.recv(st[h, 4, d], got)
            add(mine, [mine, got])
            st[h, 6, d] = wire.send(mine, r4.at[h, side[d], :, cut(k)], context=place.along(h, 0, d))
    yield
    for h in (0, 1):
        for d in (1, -1):
            wire.recv(st[h, 5, d], r4.at[h, side[d], :, cut(other[d])])
            wire.recv(st[h, 6, d], r4.at[h, side[d], :, cut(zero[d])])
        add(wide.at[pl.ds(80 * h, 80), :], [mine_at(h, ends[h], FULL), r4.at[h, 0], r4.at[h, 1]])
    for k in range(4):
        obuf[k] = jnp.concatenate([wide[pl.ds(40 * k, 40), :], jnp.zeros((8, width), f32)], axis=0).astype(bf16)
        if gates:
            tail = jnp.concatenate([wide[pl.ds(32 * b + 8 * k, 8), pl.ds(0, 128)] for b in range(4)], axis=1)
            obuf[k, :, pl.ds(0, 512)] = jnp.concatenate([wide[pl.ds(40 * k, 40), pl.ds(0, 512)], tail], axis=0).astype(bf16)
    if not spread:
        own = loc.start(obuf, out_ref)
        yield
        loc.wait(own)
        yield
        return
    sent = [(d, wire.send(obuf.at[place.xs(d)], out_ref.at[x], fsdp=place.xs(d))) for d in (1, 3, 2)]
    own = loc.start(obuf.at[x], out_ref.at[x])
    yield
    for d, n in sent:
        wire.recv(n, out_ref.at[place.xs(-d)])
    loc.wait(own)
    yield


def scatter_scratch(width):
    hi = width - width // 256 * 128
    return [
        vm((2, 2, 4, 80, hi), bf16), vm((2, 4, 80, width), bf16), vm((2, 2, 4, 80, hi), bf16), vm((2, 2, 4, 80, width), bf16),
        vm((2, 2, 80, hi), bf16), vm((2, 2, 80, width), bf16), vm((160, width), f32), vm((4, 48, width), bf16),
    ]


def small_steps(wire, mine, zin, yin, xin, corein):
    place = wire.place
    x = place.x
    ns = [wire.send(mine.at[0], zin.at[d - 1], context=place.ctx(0, d)) for d in (1, 2, 3)]
    yield
    for d, n in zip((1, 2, 3), ns):
        wire.recv(n, zin.at[d - 1])
    mine[1] = mine[0] + zin[0] + zin[1] + zin[2]
    ns = [wire.send(mine.at[1], yin.at[d - 1], context=place.ctx(d, 0)) for d in (1, 2, 3)]
    yield
    for d, n in zip((1, 2, 3), ns):
        wire.recv(n, yin.at[d - 1])
    total = mine[1] + yin[0] + yin[1] + yin[2]
    mine[2] = total
    xin[x] = total
    ns = [wire.send(mine.at[2], xin.at[x], fsdp=place.xs(d)) for d in (1, 2, 3)]
    yield
    for d, n in zip((1, 2, 3), ns):
        wire.recv(n, xin.at[place.xs(-d)])
    mine[3] = xin[0] + xin[1] + xin[2] + xin[3]
    n = wire.send(mine.at[3], corein, tensor=1 - place.t)
    yield
    wire.recv(n, corein)
    yield


def fold(dst, row, at):
    for i in range(20):
        dst[pl.ds(i // 3, 1), pl.ds(at + 128 * (i % 3), 128)] = row[:, 128 * i : 128 * i + 128]


def backward_kernel(
    g_ref, w_ref, act_ref, gm_ref, first_ref, second_ref, ahead_ref,
    lx_ref, la_ref, hid_ref, py_ref, low_ref, cg, tok_ref, gres, resid, gain_ref, rec_ref, gain_two,
    t0_out, t1_out, t2_out, mid_out, last_out, mixed_out, tgrad_out, recur_out, gains_out,
    a0, a1, a2, a3, a4, a5, a6, a7, b2, b3, b4, b5, b6, b7, c2, c3, c4, c5, c6, c7,
    w1, acts, turned, flag_s, gmx, gpy, bc, bp, bg, cin, cback, glow, edge, edge_in, edge_out, gpx, gates, packed, dgates,
    gain_acc, crecv, sums, r1, r2, own_f, crecv_f, sums_f, r1_f, r2_f,
    small, zin, yin, xin, corein, late, zin_l, yin_l, xin_l, corein_l,
    lx_s, la_s, hid_s, py_s, low_s, glast,
    ss, rs, ls, ws,
):
    part, gconv, gdir = acts, gmx, bc
    place = Place()
    x, c, t = place.x, place.c, place.t
    wire, loc = Wire(place, ss, rs), Local(ls)
    nh = head_count(x)
    rest = pl.ds(FIRST + 256, TRIPLE)
    both = pl.ds(0, FIRST + 256)
    lg = loc.start(gm_ref, acts)
    lw = loc.start(w_ref.at[:, both], w1.at[:, both])
    load_w = pltpu.make_async_copy(w_ref.at[:, rest], w1.at[:, rest], ws.at[0])
    load_g = pltpu.make_async_copy(g_ref.at[:, rest], w1.at[:, rest], ws.at[1])
    pl.when(x == 0)(lambda: load_w.start())
    pl.when(x != 0)(lambda: load_g.start())
    lf = loc.start(act_ref.at[:, :, :, pl.ds(DIM, 128)], flag_s)
    li = [loc.start(a, b) for a, b in ((low_ref, low_s), (py_ref, py_s), (hid_ref, hid_s), (la_ref, la_s), (lx_ref, lx_s))]
    lo = loc.start(ahead_ref.at[:, t], own_f)
    greet(place, xs=(1, 2, 3), ctx=((1, 0), (2, 0), (3, 0), (0, 1), (0, 2), (0, 3)), chain=(1, -1), core=True)
    big = scatter_steps(wire, loc, g_ref, SPLIT + 2 * TRIPLE, (a0, a1, a2, a3, a4, a5, a6, a7), t2_out, False)
    pump(big, 1)

    def keep_mixed(cols, r, total):
        mixed_out[t, r, cols] = (resid[r, cols] + total).astype(bf16)

    ahead = RowsScatter(wire, ahead_ref, crecv_f, sums_f, r1_f, r2_f, own=own_f).steps(lambda n: None, keep_mixed)
    fro = []
    for src, dst in ((first_ref, t0_out), (second_ref, t1_out)):
        for d in (2, 1, 3):
            fro.append((d, dst, wire.send(src.at[place.xs(d)], dst.at[x], fsdp=place.xs(d))))
        loc.start(src.at[x], dst.at[x])
    for copy in li:
        loc.wait(copy)
    before = low_s.at[0].reshape(4, 128, 512)
    hn = wire.send(before.at[:, pl.ds(112, 16), :], edge_in, context=place.chain(1))
    loc.wait(lg)
    loc.wait(lw)
    loc.wait(lf)
    loc.wait(lo)
    pl.when(x == 0)(lambda: load_w.wait())
    pl.when(x != 0)(lambda: load_g.wait())
    for cc in range(16):
        for b in range(4):
            packed[pl.ds(32 * cc, 32), pl.ds(128 * b, 128)] = w1[pl.ds(160 * cc + 32 * b, 32), pl.ds(0, 128)]
    small[...] = jnp.zeros_like(small)
    late[...] = jnp.zeros_like(late)
    fold(small.at[0], jnp.sum(gain_two[...], axis=0, keepdims=True), 512)

    def flags(g, k):
        return flag_s[pl.ds(g, 1)].reshape(128, 128).astype(f32)[:, k : k + 1]

    def put_tile(rhs, dst, cols):
        def block(n):
            r = pl.ds(pl.multiple_of(n * 512, 512), 512)
            dst[r, cols] = dot(turned[r, :], rhs).astype(bf16)

        many(5, block)

    def mixed_back(h):
        gmx[:, lanes(h)] = dot(acts[...].reshape(512, DIM), w1[:, column(2 * nh + h)])

    many(nh, mixed_back)

    bg[c] = jnp.zeros((8, 512), f32)

    def scan(q):
        cols = pl.ds(pl.multiple_of(q * 128, 128), 128)
        for g in range(4):
            r = pl.ds(128 * g, 128)
            gated, slope = gelu_and_slope(py_s[r, cols])
            grad = gmx[r, cols]
            gpy[r, cols] = (grad * hid_s[r, cols] * slope).astype(bf16)
            keep = flags(g, 1)
            dec = jnp.exp((-gate_scale) * sigmoid(la_s[r, cols]) * rec_ref[pl.ds(7, 1), cols]) * keep
            last = lax.broadcasted_iota(jnp.int32, dec.shape, 0) == 127
            a, b = scan_up(jnp.where(last, 1.0, pltpu.roll(dec, 127, 0)), grad * gated)
            bc[r, cols] = a
            bp[r, cols] = b
            bg[c, pl.ds(g, 1), cols] = dec[:1] * b[:1]

    many(2 * nh, scan)
    ns = [wire.send(bg.at[c], bg.at[c], context=place.ctx(0, d)) for d in (1, 2, 3)]
    transpose_rows(acts, turned)
    ln = loc.start(act_ref.at[:, :, :, pl.ds(0, DIM)], acts)

    many(nh, lambda h: put_tile(low_s[2, :, lanes(h)], w1, column(2 * nh + h)))
    pump(ahead, 2)
    pump(big, 4)
    for d, n in zip((1, 2, 3), ns):
        wire.recv(n, bg.at[place.ctx(0, -d)])
    line = pl.ds(place.y * 4, 4)
    ns = [wire.send(bg.at[line], bg.at[line], context=place.ctx(d, 0)) for d in (1, 2, 3)]
    for g in (0, 1):
        gates[g] = gate_matrix(packed[...], g)
    loc.wait(ln)
    transpose_rows(acts, turned)

    def norm_grad_y(heads):
        def block(n):
            r = pl.ds(pl.multiple_of(n * 512, 512), 512)
            v = dot_nt(gpy[:, pl.ds(0, 256 * heads)], w1[r, pl.ds(128 + 256 * heads, 256 * heads)])
            part[:, :, :, r] = v.astype(bf16).reshape(4, 2, 64, 512)

        many(5, block)

    pl.when(x == 0)(lambda: norm_grad_y(2))
    pl.when(x != 0)(lambda: norm_grad_y(1))
    pl.when(x == 0)(lambda: many(2, lambda h: put_tile(gpy[:, lanes(h)], w1, column(2 + h))))
    pl.when(x != 0)(lambda: put_tile(gpy[:, pl.ds(0, 256)], glast, pl.ds(384, 256)))
    mid = scatter_steps(wire, loc, w1, FIRST, (None, None, b2, b3, b4, b5, b6, b7), mid_out, False, True)
    pump(mid, 1)
    pump(ahead, 2)
    for d, n in zip((1, 2, 3), ns):
        wire.recv(n, bg.at[pl.ds(lax.rem(place.y + 4 - d, 4) * 4, 4)])

    def enter(s, state):
        return cg[s, 0] * state + cg[s, 1]

    cin[...] = lax.fori_loop(0, c, enter, jnp.zeros((8, 512), f32))

    def leave(s, state):
        k = 15 - s
        return cg[k, 0] * state + bg[k]

    cback[...] = lax.fori_loop(0, 15 - c, leave, jnp.zeros((8, 512), f32))
    def terms(q):
        cols = pl.ds(pl.multiple_of(q * 128, 128), 128)
        sums_x = jnp.zeros((1, 128), f32)
        sums_a = jnp.zeros((1, 128), f32)
        sums_l = jnp.zeros((1, 128), f32)
        for g in range(4):
            r = pl.ds(128 * g, 128)
            keep = flags(g, 1)
            cl = low_s[1, r, cols].astype(f32)
            sp, dsp = rec_ref[pl.ds(7, 1), cols], rec_ref[pl.ds(8, 1), cols]
            sx, sa, log_decay, root, factor = recur_terms(lx_s[r, cols], la_s[r, cols], cl, sp, keep)
            adj = bp[r, cols] + bc[r, cols] * cback[pl.ds(g, 1), cols]
            hid = hid_s[r, cols]
            first = lax.broadcasted_iota(jnp.int32, hid.shape, 0) == 0
            prev = jnp.where(first, cin[pl.ds(g, 1), cols], pltpu.roll(hid, 1, 0))
            grown = jnp.exp(log_decay)
            gld = keep * grown * (adj * prev - adj * sx * cl * grown / root)
            glx = (adj * factor * cl * sx * (1.0 - sx)).astype(bf16)
            gla = (gld * ((-gate_scale) * sp) * sa * (1.0 - sa)).astype(bf16)
            glow[0, r, cols] = glx
            glow[1, r, cols] = gla
            gdir[r, cols] = adj * factor * sx
            sums_x += jnp.sum(glx.astype(f32), axis=0, keepdims=True)
            sums_a += jnp.sum(gla.astype(f32), axis=0, keepdims=True)
            sums_l += jnp.sum(gld * sa, axis=0, keepdims=True) * (gate_scale * dsp)
        small[0, pl.ds(5, 1), cols] = sums_x
        small[0, pl.ds(6, 1), cols] = sums_a
        small[0, pl.ds(7, 1), cols] = sums_l

    many(2 * nh, terms)
    wire.recv(hn, edge_in)

    def conv_back(h):
        cl = low_s[1, :, lanes(h)]
        lx, la = glow[0, :, lanes(h)], glow[1, :, lanes(h)]
        gconv[:, lanes(h)] = (
            gdir[:, lanes(h)] + dot_nt(lx, gates[0, :, lanes(h)]) + dot_nt(la, gates[1, :, lanes(h)])
        )

        def group(g, taps):
            gc = gconv[token_rows(g), lanes(h)]
            bx = low_s[0, token_rows(g), lanes(h)].astype(f32)
            ahead = edge_in[g, :, lanes(h)].astype(f32)[8:]
            rows = lax.broadcasted_iota(jnp.int32, gc.shape, 0)
            low_rows = lax.broadcasted_iota(jnp.int32, (8, 256), 0)
            out = rec_ref[pl.ds(0, 1), lanes(h)] * gc
            over = jnp.zeros((8, 256), f32)
            new = [taps[0] + jnp.sum(bx * gc, axis=0, keepdims=True)]
            for k in (1, 2, 3):
                masked = flags(g, 1 + k) * gc
                new.append(taps[k] + jnp.sum(shifted(bx, ahead, k) * masked, axis=0, keepdims=True))
                scaled = rec_ref[pl.ds(k, 1), lanes(h)] * masked
                out = out + jnp.where(rows < 128 - k, pltpu.roll(scaled, 128 - k, 0), 0.0)
                over = over + jnp.where(low_rows >= 8 - k, pltpu.roll(scaled[:8], 8 - k, 0), 0.0)
            new.append(taps[4] + jnp.sum(gc, axis=0, keepdims=True))
            gdir[token_rows(g), lanes(h)] = out
            edge[g, :, lanes(h)] = over
            return tuple(new)

        taps = lax.fori_loop(0, 4, group, tuple(jnp.zeros((1, 256), f32) for _ in range(5)))
        for k in range(5):
            small[0, pl.ds(k, 1), lanes(h)] = taps[k]

    many(nh, conv_back)
    en = wire.send(edge, edge_out, context=place.chain(-1))

    early = small_steps(wire, small, zin, yin, xin, corein)
    pump(early)
    pump(big, 4)
    pump(ahead, 2)

    def gate_back(h):
        cl = low_s[1, :, lanes(h)]
        dgates[0, :, lanes(h)] = dot_tn(cl, glow[0, :, lanes(h)]).astype(bf16)
        dgates[1, :, lanes(h)] = dot_tn(cl, glow[1, :, lanes(h)]).astype(bf16)

    many(nh, gate_back)
    wire.recv(en, edge_out)

    def narrow(h):
        for g in range(4):
            v = gdir[pl.ds(128 * g, 128), lanes(h)]
            tail = v[120:] + edge_out[g, :, lanes(h)]
            gpx[pl.ds(128 * g, 128), lanes(h)] = jnp.concatenate([v[:120], tail], axis=0).astype(bf16)

    many(nh, narrow)

    def norm_grad(n, heads):
        r = pl.ds(512 * n, 512)
        v = dot_nt(gpx[:, pl.ds(0, 256 * heads)], w1[r, pl.ds(128, 256 * heads)])
        v = v + part[:, :, :, r].reshape(512, 512).astype(f32)
        part[:, :, :, r] = v.astype(bf16).reshape(4, 2, 64, 512)

    def norm_piece(n):
        pl.when(x == 0)(lambda: norm_grad(n, 2))
        pl.when(x != 0)(lambda: norm_grad(n, 1))

    def keep_sum(cols, r, total):
        tgrad_out[t, r, cols] = total

    pump(mid, 4)
    many(nh, lambda h: put_tile(gpx[:, lanes(h)], glast, column(h)))
    back = (dot_tn(selector(0), dgates[0]) + dot_tn(selector(1), dgates[1])).astype(bf16)
    glast[:, pl.ds(0, 128)] = jnp.zeros((DIM, 128), bf16)
    for cc in range(16):
        for b in range(4):
            glast[pl.ds(160 * cc + 32 * b, 32), pl.ds(0, 128)] = back[32 * cc : 32 * cc + 32, 128 * b : 128 * b + 128]
    last = scatter_steps(wire, loc, glast, 0, (None, None, c2, c3, c4, c5, c6, c7), last_out, True, True)
    pump(last, 1)
    final = RowsScatter(wire, part, crecv, sums, r1, r2).steps(norm_piece, keep_sum)
    pump(final, 5)
    pump(early)
    pump(big, 1)
    pump(final, 1)
    pump(last, 4)
    pump(early)
    pump(final, 1)
    drain(final)
    gain_acc[...] = jnp.zeros_like(gain_acc)

    def finish(i):
        r = pl.ds(pl.multiple_of(i * 16, 16), 16)
        gx, gain = norm_back(tgrad_out[t, r, :], tok_ref[r, :], gain_ref[pl.ds(0, 1), :])
        tgrad_out[t, r, :] = gres[r, :] + gx
        gain_acc[...] += gain

    many(4, finish)
    tn = wire.send(tgrad_out.at[t], tgrad_out.at[t], tensor=1 - t)
    fold(late.at[0], jnp.sum(gain_acc[...], axis=0, keepdims=True), 0)
    tail = small_steps(wire, late, zin_l, yin_l, xin_l, corein_l)
    pump(tail)
    pump(mid, 4)
    pump(early)
    pump(tail)
    pump(last, 4)
    pump(big, 1)
    pump(tail)
    pump(mid, 1)
    pump(early)
    pump(last, 1)
    pump(tail)
    drain(ahead)
    mn = wire.send(mixed_out.at[t], mixed_out.at[t], tensor=1 - t)
    pump(mid, 1)
    pump(last, 1)
    drain(big)
    drain(mid)
    drain(tail)
    drain(early)
    for k in range(4):
        recur_out[k] = xin[k, :, pl.ds(0, 512)]
    gains_out[0] = late[3] + corein_l[...]
    gains_out[1] = small[3, :, pl.ds(512, 384)] + corein[:, pl.ds(512, 384)]
    drain(last)
    for d, dst, n in fro:
        wire.recv(n, dst.at[place.xs(-d)])
    wire.recv(mn, mixed_out.at[1 - t])
    wire.recv(tn, tgrad_out.at[1 - t])
    wire.finish()
    loc.finish()


def backward_call(g, w, act, gm, first, second, ahead, lx, la, hid, py, low, cg, tok, gres, resid, gain, rec, gain_two):
    S = jax.ShapeDtypeStruct
    R = (64, DIM)
    F = (512, 512)
    E, L = (8, 896), (8, 384)
    slices = lambda n: S((4, 48, n), bf16)
    return pl.pallas_call(
        backward_kernel,
        name="recurrent_backward",
        out_shape=(
            slices(TRIPLE), slices(TRIPLE), slices(TRIPLE), slices(SPLIT - FIRST), slices(FIRST),
            S((2,) + R, bf16), S((2,) + R, f32), S((4, 8, 512), f32), S((2,) + L, f32),
        ),
        in_specs=[ANY] * 12 + [VM] * 7,
        out_specs=[ANY, ANY, ANY, ANY, ANY, VM, VM, VM, VM],
        scratch_shapes=scatter_scratch(TRIPLE) + scatter_scratch(SPLIT - FIRST)[2:] + scatter_scratch(FIRST)[2:] + [
            vm((DIM, SPLIT), bf16), vm((4, 2) + R, bf16), vm((DIM, 512), bf16), vm((4, 2, 64, 128), bf16),
            vm(F, f32), vm(F, bf16), vm(F, f32), vm(F, f32), vm((16, 8, 512), f32), vm((8, 512), f32), vm((8, 512), f32),
            vm((2,) + F, bf16), vm((4, 8, 512), f32), vm((4, 16, 512), bf16), vm((4, 8, 512), f32), vm(F, bf16),
            vm((2, 256, 512), bf16), vm(F, bf16), vm((2, 256, 512), bf16), vm((8, DIM), f32),
            vm((4,) + R, bf16), vm((3,) + R, bf16), vm((2,) + R, bf16), vm((2,) + R, bf16),
            vm((4,) + R, bf16), vm((4,) + R, bf16), vm((3,) + R, bf16), vm((2,) + R, bf16), vm((2,) + R, bf16),
            vm((4,) + E, f32), vm((3,) + E, f32), vm((3,) + E, f32), vm((4,) + E, f32), vm(E, f32),
            vm((4,) + L, f32), vm((3,) + L, f32), vm((3,) + L, f32), vm((4,) + L, f32), vm(L, f32),
            vm(F, f32), vm(F, f32), vm(F, f32), vm(F, f32), vm((3,) + F, bf16), vm((DIM, FIRST), bf16),
            pltpu.SemaphoreType.DMA((310,)), pltpu.SemaphoreType.DMA((310,)), pltpu.SemaphoreType.DMA((60,)),
            pltpu.SemaphoreType.DMA((2,)),
        ],
        compiler_params=pltpu.CompilerParams(collective_id=2, has_side_effects=True, vmem_limit_bytes=62 << 20),
    )(g, w, act, gm, first, second, ahead, lx, la, hid, py, low, cg, tok, gres, resid, gain, rec, gain_two)


def adam_update(weight, moment, square, gradient, rate, shrink):
    moment = beta_one * moment + (1.0 - beta_one) * gradient
    square = beta_two * square + (1.0 - beta_two) * gradient * gradient
    normed = (moment * (1.0 / (1.0 - beta_one**STEP))) / (jnp.sqrt(square * (1.0 / (1.0 - beta_two**STEP))) + adam_eps)
    return (weight - rate * (normed + shrink * weight), moment, square)


def update_kernel(
    last, mid, t0, t1, t2, recur, gains, mixed, tgrad, *refs,
):
    ins, outs, held, fresh, ls, ss = refs[:21], refs[21:44], refs[44:56], refs[56:68], refs[68], refs[69]
    mixed_out, tgrad_out = outs[:2]
    big = (2, 5, 4, 6)
    loads, stores = {}, {}
    for i, n in enumerate(big):
        for k in range(3):
            loads[n, k] = pltpu.make_async_copy(ins[3 * n + k], held[3 * i + k], ls.at[3 * i + k])
            loads[n, k].start()
            stores[n, k] = pltpu.make_async_copy(fresh[3 * i + k], outs[2 + 3 * n + k], ss.at[3 * i + k])

    def group(n):
        if n in big:
            i = big.index(n)
            return held[3 * i : 3 * i + 3], fresh[3 * i : 3 * i + 3]
        return ins[3 * n : 3 * n + 3], outs[2 + 3 * n : 5 + 3 * n]

    def ready(n):
        for k in range(3):
            loads[n, k].wait()

    def leave(n):
        for k in range(3):
            stores[n, k].start()

    def update(n, index, grad, rate=matrix_rate, shrink=weight_decay):
        old, new = group(n)
        values = adam_update(*(ref[index] for ref in old), grad, rate, shrink)
        for ref, value in zip(new, values):
            ref[index] = value

    def piece(k, tile):
        if tile < 2:
            ref, at = last, 128 + 256 * tile
        elif tile < 6:
            ref, at = mid, 256 * (tile - 2)
        else:
            ref, at = (t0, t1, t2)[(tile - 6) // 3], 256 * ((tile - 6) % 3)
        return ref[k, :, pl.ds(at, 256)].astype(f32)

    ready(2)
    for k in range(4):
        for h in range(HEADS_OF[k]):
            nh = HEADS_OF[k]
            at = 256 * (HEAD_START[k] + h)
            update(2, (0, slice(None), pl.ds(at, 256)), piece(k, h)[:40])
            update(2, (1, slice(None), pl.ds(at, 256)), piece(k, nh + h)[:40])
            b = last[k, :, pl.ds(256 * h, 256)].astype(f32)[40:]
            for g in (0, 1):
                update(3, (g, HEAD_START[k] + h), b[4 * g : 4 * g + 4])
        n = 256 * HEADS_OF[k]
        update(1, (slice(None), pl.ds(256 * HEAD_START[k], n)), recur[k, :, pl.ds(0, n)], vector_rate, 0.0)
    leave(2)
    ready(5)
    for k in range(4):
        for j in TILE_ORDER[k]:
            tile = 3 if j == 3 else 6 + 3 * j
            at = FF_START[k] + 256 * j
            update(5, (0, slice(None), pl.ds(at, 256)), piece(k, tile)[:40])
            update(5, (1, slice(None), pl.ds(at, 256)), piece(k, tile + 1)[:40])
    leave(5)
    ready(4)
    for k in range(4):
        for h in range(HEADS_OF[k]):
            at = 256 * (HEAD_START[k] + h)
            update(4, (slice(None), pl.ds(at, 256)), piece(k, 2 * HEADS_OF[k] + h)[:40])
    leave(4)
    ready(6)
    for k in range(4):
        for j in TILE_ORDER[k]:
            tile = 3 if j == 3 else 6 + 3 * j
            update(6, (slice(None), pl.ds(FF_START[k] + 256 * j, 256)), piece(k, tile + 2)[:40])
    leave(6)

    for n in (0, 1):
        for q in range(20):
            grad = moved_tile(lambda p: gains[n, pl.ds(p // 3, 1), pl.ds(128 * (p % 3), 128)], q, (1, 128), restored_granule)
            update(0, (pl.ds(n, 1), pl.ds(128 * q, 128)), grad, vector_rate, 0.0)

    def restore(i):
        t = i // 4
        r = pl.ds(pl.multiple_of((i % 4) * 16, 16), 16)
        dst = pl.ds(pl.multiple_of(i * 16, 16), 16)
        for q in range(20):
            cols = pl.ds(128 * q, 128)
            mixed_out[dst, cols] = moved_tile(lambda p: mixed[t, r, pl.ds(128 * p, 128)].astype(f32), q, (16, 128), restored_granule).astype(bf16)
            tgrad_out[dst, cols] = moved_tile(lambda p: tgrad[t, r, pl.ds(128 * p, 128)], q, (16, 128), restored_granule)

    many(8, restore)
    for n in big:
        for k in range(3):
            stores[n, k].wait()


def update_call(pieces, recur, gains, mixed, tgrad, params):
    shapes = [jax.ShapeDtypeStruct(v.shape, v.dtype) for v in params]
    outs = [jax.ShapeDtypeStruct((128, DIM), bf16), jax.ShapeDtypeStruct((128, DIM), f32)] + shapes
    place = [VM if n in (0, 1, 3) else ANY for n in range(7) for _ in range(3)]
    held = [vm(params[3 * n + k].shape, f32) for n in (2, 5, 4, 6) for k in range(3)]
    return pl.pallas_call(
        update_kernel,
        name="optimizer_step",
        out_shape=tuple(outs),
        in_specs=[VM] * 9 + place,
        out_specs=tuple([VM, VM] + place),
        scratch_shapes=held + held + [pltpu.SemaphoreType.DMA((12,)), pltpu.SemaphoreType.DMA((12,))],
        compiler_params=pltpu.CompilerParams(vmem_limit_bytes=56 << 20),
    )(*pieces, recur, gains, mixed, tgrad, *params)


def on_device(
    tokens, cotangent, seq_lengths,
    norm_gains, gains_moment, gains_square, recur_params, recur_moment, recur_square,
    input_proj, input_moment, input_square, gate_blocks, blocks_moment, blocks_square,
    output_proj, output_moment, output_square, inner_proj, inner_moment, inner_square,
    down_proj, down_moment, down_square,
):
    w, act, gl, tok, gains, rec, lx, la, hid, py, low, cg, nm, resid = forward_call(
        seq_lengths, tokens, cotangent, norm_gains, recur_params, input_proj, gate_blocks, output_proj.T, inner_proj, down_proj.T
    )
    g, ahead, gm, gres, gain_two, first, second = ffn_call(w, gl, nm, resid, gains)
    t0, t1, t2, mid, last, mixed, tgrad, recur, gsum = backward_call(
        g, w, act, gm, first, second, ahead, lx, la, hid, py, low, cg, tok, gres, resid, gains, rec, gain_two
    )
    params = (
        norm_gains, gains_moment, gains_square, recur_params, recur_moment, recur_square,
        input_proj, input_moment, input_square, gate_blocks, blocks_moment, blocks_square,
        output_proj.T, output_moment.T, output_square.T, inner_proj, inner_moment, inner_square,
        down_proj.T, down_moment.T, down_square.T,
    )
    out = update_call((last, mid, t0, t1, t2), recur, gsum, mixed, tgrad, params)
    return out[:14] + tuple(v.T for v in out[14:17]) + out[17:20] + tuple(v.T for v in out[20:])


def solution(mesh):
    row = P(("fsdp", "context"), None)
    wide_spec = P(None, ("fsdp", "context"), "tensor")
    tall = P("tensor", ("fsdp", "context"))
    block = P(None, "tensor", ("fsdp", "context"), None)
    params = (P(),) * 3 + (P(None, "tensor"),) * 3 + (wide_spec,) * 3 + (block,) * 3 + (tall,) * 3 + (wide_spec,) * 3 + (tall,) * 3
    return jax.shard_map(
        on_device, mesh=mesh, in_specs=(row, row, P("fsdp", None)) + params, out_specs=(row, row) + params, check_vma=False
    )
```
